32 devices in a mesh: seq: 4 (over y, core), fsdp: 8 (over z, x).
Axes of the slice: x: 2, y: 2, z: 4, core: 2. Of those that a mesh axis runs over, the one named last changes fastest.
Arguments:
- tokens: bfloat16 [32, 200, 768], P(('fsdp', 'seq')), may hold values from -6 to 6
- key_mask: int32 [32, 200], P('fsdp'), may hold values from 0 to 1, as said below
- expert_ids: int32 [32, 200, 2], P(('fsdp', 'seq')), may hold values from 0 to 3, all different within a row; in each aligned block of 200 rows (0 to 199, 200 to 399, ..., all dimensions but the last counted through in order) at most 142 rows name the same one
- cotangent: bfloat16 [32, 200, 768], P(('fsdp', 'seq')), may hold values from -6 to 6
- norm1_gain: bfloat16 [768], P('fsdp'), may hold values from 0.5 to 1.5
- norm1_bias: bfloat16 [768], P('fsdp'), may hold values from -1 to 1
- w_qkv: bfloat16 [768, 2304], P('fsdp'), may hold values from -0.21875 to 0.21875
- w_proj: bfloat16 [768, 768], P('fsdp'), may hold values from -1.75 to 1.75
- proj_bias: bfloat16 [768], P('fsdp'), may hold values from -1 to 1
- norm2_gain: bfloat16 [768], P('fsdp'), may hold values from 0.5 to 1.5
- norm2_bias: bfloat16 [768], P('fsdp'), may hold values from -1 to 1
- w_router: bfloat16 [768, 4], P('fsdp'), may hold values from -0.15625 to 0.15625
- w_in: bfloat16 [4, 768, 3072], P(None, 'fsdp'), may hold values from -0.21875 to 0.21875
- b_in: bfloat16 [4, 3072], P(None, 'fsdp'), may hold values from -1 to 1
- w_out: bfloat16 [4, 3072, 768], P(None, 'fsdp'), may hold values from -0.3125 to 0.3125
- b_out: bfloat16 [4, 768], P(None, 'fsdp'), may hold values from -1 to 1
Outputs:
- mixed: bfloat16 [32, 200, 768], P(('fsdp', 'seq'))
- token_grad: bfloat16 [32, 200, 768], P(('fsdp', 'seq'))
- norm1_gain_grad: float32 [768], P('fsdp')
- norm1_bias_grad: float32 [768], P('fsdp')
- w_qkv_grad: float32 [768, 2304], P('fsdp')
- w_proj_grad: float32 [768, 768], P('fsdp')
- proj_bias_grad: float32 [768], P('fsdp')
- norm2_gain_grad: float32 [768], P('fsdp')
- norm2_bias_grad: float32 [768], P('fsdp')
- w_router_grad: float32 [768, 4], P('fsdp')
- w_in_grad: float32 [4, 768, 3072], P(None, 'fsdp')
- b_in_grad: float32 [4, 3072], P(None, 'fsdp')
- w_out_grad: float32 [4, 3072, 768], P(None, 'fsdp')
- b_out_grad: float32 [4, 768], P(None, 'fsdp')
The draws below stay inside these ranges and needn't reach their ends.
Inputs may be any that keep to these rules, and one draw needn't show every extreme that they name: `expert_ids`: each token names two different experts. Among the 200 tokens of one device (aligned blocks of rows) no expert is named more than 142 times, and some expert of some device is named exactly 142 times. `key_mask`: each image's mask is 1 on a prefix of 160 to 200 tokens and 0 after it; both ends occur.
All inputs are finite; a program needn't handle non-finite values.
Results may differ from the reference program's by a relative error of at most 0.018.
Values may be sent and summed in bfloat16 or wider, within the bound.
A program may use at most 320 MiB of HBM per device.

```python
import math
import jax
import jax.numpy as jnp
import numpy as np
from jax import lax

D = 768
HEADS = 12
HEAD_DIM = 64
FF = 3072
EXPERTS = 4
SEQ = 200
IMG_DEV = 1
CAP = 142
IMAGES = 32
N_SEQ = 4
N_FSDP = 8


def draw_key_mask(key, part):
    key = jax.random.fold_in(key, 7)
    shortest = SEQ - SEQ // 5
    lengths = jax.random.randint(key, (IMAGES,), shortest, SEQ + 1, dtype=jnp.int32)
    lengths = lengths.at[0].set(shortest).at[1].set(SEQ)
    positions = jnp.arange(SEQ, dtype=jnp.int32)
    return (positions[None, :] < lengths[:, None]).astype(jnp.int32)


def block_levels(stream_key, dims, shards, low, top_value):
    loudness, own = 1.0, jax.random.fold_in(stream_key, 6)
    for axis_at, shards_of in shards:
        heights = jnp.exp(jax.random.uniform(jax.random.fold_in(own, axis_at), (shards_of,), jnp.float32, low / len(shards), top_value / len(shards)))
        loudness = loudness * jnp.repeat(heights, dims[axis_at] // shards_of).reshape([-1 if axis == axis_at else 1 for axis in range(len(dims))])
    return loudness


def deal_out(key, own, number, rows, count, top, bound, lean):
    ranking = jax.random.permutation(key, count)
    heavy_load, ordinary = shares(count, rows * top, bound, lean, True), shares(count, rows * top, bound, lean, False)
    places = jnp.arange(count)

    def named(sizes, rotation):
        used = int((sizes > 0).sum())
        fixed = max(1, used // 4)
        passed = fixed + (places - fixed + rotation * (used - fixed)) % max(1, count - fixed)
        return jnp.zeros((count,), jnp.int32).at[ranking[jnp.where(places < fixed, places, passed)]].set(jnp.asarray(sizes, jnp.int32))

    sizes = jnp.where(number % 4 == 0, named(heavy_load, number // 4), named(ordinary, number - number // 4 - 1))
    mixed = jax.random.permutation(jax.random.fold_in(own, 3), count)
    giver, sink = mixed[0:count // 2 * 2:2], mixed[1:count // 2 * 2:2]
    room = jnp.minimum(sizes[giver] - 1, bound - sizes[sink]) // 2
    room = jnp.where((giver == ranking[0]) | (sink == ranking[0]) | (sizes[sink] == 0), 0, jnp.maximum(room, 0))
    passed = jax.random.randint(jax.random.fold_in(own, 4), (count // 2,), 0, 1 << 20) % (room + 1)
    sizes = sizes.at[giver].add(-passed).at[sink].add(passed)
    members = jnp.searchsorted(jnp.cumsum(sizes), jnp.arange(rows * top), side="right").astype(jnp.int32)
    table = members.reshape(top, rows).T
    table = table[jax.random.permutation(jax.random.fold_in(own, 1), rows)]
    rotation = jax.random.randint(jax.random.fold_in(own, 2), (rows, 1), 0, top)
    return jnp.take_along_axis(table, (jnp.arange(top)[None, :] + rotation) % top, axis=1)


def shares(count, total, reach, slope, full):
    loads = [(1 << 20) // math.isqrt(grade ** slope) + 1 for grade in range(1, count + 1)]
    largest = reach if full else min(reach, max(-(-total // count), total * loads[0] // sum(loads)))
    least = 1 if total - largest >= count - 1 else 0
    counts, spare = [largest] + [least] * (count - 1), total - largest - least * (count - 1)
    while spare > 0:
        movable = [i for i in range(1, count) if counts[i] < largest] or [i for i in range(1, count) if counts[i] < reach]
        pool, left = sum([loads[i] for i in movable]), spare
        for i in movable:
            more = min(reach - counts[i], max(1, left * loads[i] // pool), spare)
            counts[i] = counts[i] + more
            spare = spare - more
    return np.array(counts)


def bell_draw(key, shape, width, reach, shards=(), kind=jnp.bfloat16):
    factor_of = block_levels(key, shape, shards, -0.22, 0.18) if shards else 1.0
    values = jax.random.normal(key, shape, jnp.float32) * width * factor_of
    return jnp.minimum(jnp.maximum(values, -reach), reach).astype(kind)


def setup_inputs(seed: int = 0) -> dict:
    arg_keys = jax.random.split(jax.random.key(seed), 17)
    tokens = bell_draw(arg_keys[0], (IMAGES, SEQ, D), 1.0, 6.0, ((0, 32),))
    key_mask = draw_key_mask(jax.random.fold_in(arg_keys[16], 71), 0)
    expert_ids_keys = jax.random.split(jax.random.fold_in(arg_keys[2], 1), IMAGES * SEQ // (IMG_DEV * SEQ))
    expert_ids_turns = jax.random.permutation(jax.random.fold_in(arg_keys[2], 3), IMAGES * SEQ // (IMG_DEV * SEQ))
    expert_ids = jax.vmap(lambda own, number: deal_out(jax.random.fold_in(arg_keys[2], 2), own, number, IMG_DEV * SEQ, EXPERTS, 2, CAP, 1))(expert_ids_keys, expert_ids_turns).reshape((IMAGES, SEQ, 2))
    cotangent = bell_draw(arg_keys[3], (IMAGES, SEQ, D), 1.0, 6.0, ((0, 32),))
    norm1_gain = jnp.clip(1.0 + 0.1 * jax.random.normal(arg_keys[4], (D,), jnp.float32), 0.5, 1.5).astype(jnp.bfloat16)
    norm1_bias = bell_draw(arg_keys[5], (D,), 0.2, 1.0, ((0, 8),))
    w_qkv = bell_draw(arg_keys[6], (D, 3 * D), D ** -0.5, 0.21875, ((0, 8),))
    w_proj = bell_draw(arg_keys[7], (D, D), (D // 64) ** -0.5, 1.75, ((0, 8),))
    proj_bias = bell_draw(arg_keys[8], (D,), 0.2, 1.0, ((0, 8),))
    norm2_gain = jnp.clip(1.0 + 0.1 * jax.random.normal(arg_keys[9], (D,), jnp.float32), 0.5, 1.5).astype(jnp.bfloat16)
    norm2_bias = bell_draw(arg_keys[10], (D,), 0.2, 1.0, ((0, 8),))
    w_router = bell_draw(arg_keys[11], (D, EXPERTS), (2 * D) ** -0.5, 0.15625, ((0, 8),))
    w_in = bell_draw(arg_keys[12], (EXPERTS, D, FF), D ** -0.5, 0.21875, ((1, 8),))
    b_in = bell_draw(arg_keys[13], (EXPERTS, FF), 0.2, 1.0, ((1, 8),))
    w_out = bell_draw(arg_keys[14], (EXPERTS, FF, D), (FF // 8) ** -0.5, 0.3125, ((1, 8),))
    b_out = bell_draw(arg_keys[15], (EXPERTS, D), 0.2, 1.0, ((1, 8),))
    return dict(tokens=tokens, key_mask=key_mask, expert_ids=expert_ids, cotangent=cotangent, norm1_gain=norm1_gain, norm1_bias=norm1_bias, w_qkv=w_qkv, w_proj=w_proj, proj_bias=proj_bias, norm2_gain=norm2_gain, norm2_bias=norm2_bias, w_router=w_router, w_in=w_in, b_in=b_in, w_out=w_out, b_out=b_out)


@jax.custom_vjp
def low(v):
    return lax.optimization_barrier(v.astype(jnp.bfloat16)).astype(jnp.float32)

@jax.custom_vjp
def low_back(v):
    return v

def low_keep(v):
    return (low(v), None)

def low_pass(kept, grad):
    return (grad,)

def back_keep(v):
    return (v, None)

def back_low(kept, grad):
    return (low(grad),)
low.defvjp(low_keep, low_pass)
low_back.defvjp(back_keep, back_low)
epsilon = 1e-06
highest = lax.Precision.HIGHEST
masked_score = -1e+30

def norm_rows(values, gain, offset):
    center = values - lax.optimization_barrier(jnp.mean(values, axis=-1, keepdims=True))
    spread = lax.optimization_barrier(jnp.mean(center * center, axis=-1, keepdims=True))
    return center * lax.rsqrt(spread + epsilon) * gain + offset

def softmax_rows(values):
    shifted = jnp.exp(values - lax.optimization_barrier(jnp.max(values, axis=-1, keepdims=True)))
    return shifted / lax.optimization_barrier(jnp.sum(shifted, axis=-1, keepdims=True))

def expert_slots(chosen):
    flat_ids = chosen.reshape(-1).astype(jnp.int32)
    onehot = (flat_ids[:, None] == jnp.arange(EXPERTS, dtype=jnp.int32)[None, :]).astype(jnp.int32)
    ranks = jnp.cumsum(onehot, axis=0, dtype=jnp.int32)
    slot_pos = lax.optimization_barrier(jnp.sum(onehot * ranks, axis=1, dtype=jnp.int32)) - 1
    return (flat_ids, slot_pos.astype(jnp.int32))

def expert_block(normed, chosen, routing, w_in, b_in, w_out, b_out):
    flat_ids, slot_pos = expert_slots(chosen)
    rows = jnp.repeat(normed, 2, axis=0)
    buffer = jnp.zeros((EXPERTS, CAP, D), jnp.float32).at[flat_ids, slot_pos].add(rows)
    pre_act = low_back(jnp.einsum('ecd,edf->ecf', buffer, w_in, precision=highest) + b_in[:, None, :])
    activated = low(jax.nn.gelu(pre_act, approximate=False))
    expert_out = low_back(jnp.einsum('ecf,efd->ecd', activated, w_out, precision=highest) + b_out[:, None, :])
    picked = expert_out[flat_ids, slot_pos].reshape(normed.shape[0], 2, D)
    gating = jnp.take_along_axis(routing, chosen, axis=1)
    return lax.optimization_barrier(jnp.sum(gating[:, :, None] * picked, axis=1))

def group_forward(tokens, key_mask, chosen, params):
    norm1_gain, norm1_bias, w_qkv, w_proj, proj_bias, norm2_gain, norm2_bias, w_router, w_in, b_in, w_out, b_out = params
    images = tokens.shape[0]
    normed_in = low(norm_rows(tokens, norm1_gain, norm1_bias))
    mixed_qkv = low(low_back(jnp.einsum('isd,de->ise', normed_in, w_qkv, precision=highest)))
    mixed_qkv = mixed_qkv.reshape(images, SEQ, 3, HEADS, HEAD_DIM)
    queries = mixed_qkv[:, :, 0]
    key_rows = mixed_qkv[:, :, 1]
    value_rows = mixed_qkv[:, :, 2]
    scores = low_back(jnp.einsum('iahd,ibhd->ihab', queries, key_rows, precision=highest) * HEAD_DIM ** (-0.5))
    scores = jnp.where((key_mask > 0)[:, None, None, :], scores, masked_score)
    attn_probs = low(softmax_rows(scores))
    attended = low(low_back(jnp.einsum('ihab,ibhd->iahd', attn_probs, value_rows, precision=highest)))
    attended = attended.reshape(images, SEQ, D)
    middle = tokens + low_back(jnp.einsum('isd,de->ise', attended, w_proj, precision=highest) + proj_bias)
    normed_mid = low(norm_rows(middle, norm2_gain, norm2_bias))
    routing = softmax_rows(low_back(jnp.einsum('isd,de->ise', normed_mid, w_router, precision=highest)))
    rows_block = images // N_SEQ * SEQ
    mixture = jax.vmap(expert_block, in_axes=(0, 0, 0, None, None, None, None))(normed_mid.reshape(N_SEQ, rows_block, D), chosen.reshape(N_SEQ, rows_block, 2), routing.reshape(N_SEQ, rows_block, EXPERTS), w_in, b_in, w_out, b_out)
    return (middle + mixture.reshape(images, SEQ, D)) * key_mask[:, :, None].astype(jnp.float32)

def reference(tokens, key_mask, expert_ids, cotangent, norm1_gain, norm1_bias, w_qkv, w_proj, proj_bias, norm2_gain, norm2_bias, w_router, w_in, b_in, w_out, b_out):
    per_group = N_SEQ * IMG_DEV
    params = tuple((item.astype(jnp.float32) for item in (norm1_gain, norm1_bias, w_qkv, w_proj, proj_bias, norm2_gain, norm2_bias, w_router, w_in, b_in, w_out, b_out)))
    stacked_mask = key_mask.reshape(N_FSDP, per_group, SEQ)
    stacked_ids = expert_ids.reshape(N_FSDP, per_group, SEQ, 2)

    def forward(values, *weights):

        def one_group(items):
            return group_forward(items[0], items[1], items[2], weights)
        stacked = (values.reshape(N_FSDP, per_group, SEQ, D), stacked_mask, stacked_ids)
        return lax.map(jax.checkpoint(one_group), stacked).reshape(IMAGES, SEQ, D)
    result, pull_back = jax.vjp(forward, tokens.astype(jnp.float32), *params)
    grads = pull_back(cotangent.astype(jnp.float32))
    return (result.astype(jnp.bfloat16), grads[0].astype(jnp.bfloat16), grads[1], grads[2], grads[3], grads[4], grads[5], grads[6], grads[7], grads[8], grads[9], grads[10], grads[11], grads[12])
```

```python
import jax
import jax.numpy as jnp
from jax import lax
from jax.sharding import PartitionSpec as P

HEADS = 12
CAP = 142


epsilon = 1e-06
masked_score = -1e30


def norm_rows(values, gain, offset):
    center = values - jnp.mean(values, axis=-1, keepdims=True)
    spread = jnp.mean(center * center, axis=-1, keepdims=True)
    return center * lax.rsqrt(spread + epsilon) * gain + offset


def softmax_rows(values):
    shifted = jnp.exp(values - jnp.max(values, axis=-1, keepdims=True))
    return shifted / jnp.sum(shifted, axis=-1, keepdims=True)


def exact_gelu(values):
    return jax.nn.gelu(values, approximate=False)


def expert_slots(chosen, experts):
    flat_ids = chosen.reshape(-1)
    onehot = (flat_ids[:, None] == jnp.arange(experts, dtype=jnp.int32)[None, :]).astype(jnp.int32)
    ranks = jnp.cumsum(onehot, axis=0, dtype=jnp.int32)
    slot_pos = jnp.sum(onehot * ranks, axis=1, dtype=jnp.int32) - 1
    return (flat_ids, slot_pos)


def gather_weights_plan(
    tokens,
    key_mask,
    expert_ids,
    cotangent,
    norm1_gain,
    norm1_bias,
    w_qkv,
    w_proj,
    proj_bias,
    norm2_gain,
    norm2_bias,
    w_router,
    w_in,
    b_in,
    w_out,
    b_out,
):
    images, seq_len, width = tokens.shape
    experts = w_in.shape[0]
    head_dim = width // HEADS
    scaling = head_dim ** (-0.5)
    row_count = images * seq_len
    dense_set = (
        lax.all_gather(norm1_gain, "fsdp", axis=0, tiled=True),
        lax.all_gather(norm1_bias, "fsdp", axis=0, tiled=True),
        lax.all_gather(w_qkv, "fsdp", axis=0, tiled=True),
        lax.all_gather(w_proj, "fsdp", axis=0, tiled=True),
        lax.all_gather(proj_bias, "fsdp", axis=0, tiled=True),
        lax.all_gather(norm2_gain, "fsdp", axis=0, tiled=True),
        lax.all_gather(norm2_bias, "fsdp", axis=0, tiled=True),
        lax.all_gather(w_router, "fsdp", axis=0, tiled=True),
    )
    gain_first = dense_set[0].astype(jnp.float32)
    bias_first = dense_set[1].astype(jnp.float32)
    full_qkv = dense_set[2]
    full_proj = dense_set[3]
    bias_proj = dense_set[4].astype(jnp.float32)
    gain_second = dense_set[5].astype(jnp.float32)
    bias_second = dense_set[6].astype(jnp.float32)
    full_router = dense_set[7]
    expert_set = (
        lax.all_gather(w_in, "fsdp", axis=1, tiled=True),
        lax.all_gather(b_in, "fsdp", axis=1, tiled=True),
        lax.all_gather(w_out, "fsdp", axis=1, tiled=True),
        lax.all_gather(b_out, "fsdp", axis=1, tiled=True),
    )
    inner_weight = expert_set[0]
    inner_bias = expert_set[1].astype(jnp.float32)
    outer_weight = expert_set[2]
    outer_bias = expert_set[3].astype(jnp.float32)
    own_mask = lax.dynamic_slice_in_dim(key_mask, lax.axis_index("seq") * images, images, 0)
    keep_rows = own_mask.reshape(row_count, 1).astype(jnp.float32)
    usable = (key_mask > 0)[:, None, None, :]
    flat_tokens = tokens.astype(jnp.float32).reshape(row_count, width)
    normed_in = norm_rows(flat_tokens, gain_first, bias_first).astype(jnp.bfloat16)
    mixed_qkv = jnp.dot(normed_in, full_qkv, preferred_element_type=jnp.float32).astype(
        jnp.bfloat16
    )
    mixed_qkv = mixed_qkv.reshape(images, seq_len, 3, HEADS, head_dim)
    head_qkv = lax.all_to_all(mixed_qkv, "seq", split_axis=3, concat_axis=0, tiled=True)
    queries = head_qkv[:, :, 0]
    key_rows = head_qkv[:, :, 1]
    value_rows = head_qkv[:, :, 2]

    def score_block():
        raw = (
            jnp.einsum("gahd,gbhd->ghab", queries, key_rows, preferred_element_type=jnp.float32)
            * scaling
        )
        return jnp.where(usable, raw, masked_score)

    scores = score_block()
    row_top = jnp.max(scores, axis=-1, keepdims=True)
    shifted = jnp.exp(scores - row_top)
    row_total = jnp.sum(shifted, axis=-1, keepdims=True)
    attn_probs = (shifted / row_total).astype(jnp.bfloat16)
    log_total = row_top + jnp.log(row_total)
    head_out = jnp.einsum(
        "ghab,gbhd->gahd", attn_probs, value_rows, preferred_element_type=jnp.float32
    ).astype(jnp.bfloat16)
    attended = lax.all_to_all(head_out, "seq", split_axis=0, concat_axis=2, tiled=True).reshape(
        row_count, width
    )
    middle = (
        flat_tokens + jnp.dot(attended, full_proj, preferred_element_type=jnp.float32) + bias_proj
    )
    normed_mid = norm_rows(middle, gain_second, bias_second).astype(jnp.bfloat16)
    routing = softmax_rows(jnp.dot(normed_mid, full_router, preferred_element_type=jnp.float32))
    chosen = expert_ids.reshape(row_count, 2)
    flat_ids, slot_pos = expert_slots(chosen, experts)
    gating = jnp.take_along_axis(routing, chosen, axis=1)
    buffer = (
        jnp.zeros((experts, CAP, width), jnp.bfloat16)
        .at[flat_ids, slot_pos]
        .set(jnp.repeat(normed_mid, 2, axis=0))
    )
    pre_act = (
        jnp.einsum("ecd,edf->ecf", buffer, inner_weight, preferred_element_type=jnp.float32)
        + inner_bias[:, None, :]
    )
    activated = exact_gelu(pre_act).astype(jnp.bfloat16)
    expert_out = (
        jnp.einsum("ecf,efd->ecd", activated, outer_weight, preferred_element_type=jnp.float32)
        + outer_bias[:, None, :]
    )
    picked = expert_out[flat_ids, slot_pos].reshape(row_count, 2, width)
    mixture = jnp.sum(gating[:, :, None] * picked, axis=1)
    mixed = (keep_rows * (middle + mixture)).astype(jnp.bfloat16).reshape(images, seq_len, width)
    grad_out = cotangent.astype(jnp.float32).reshape(row_count, width) * keep_rows
    grad_gate = jnp.sum(grad_out[:, None, :] * picked, axis=2)
    grad_picked = (
        (gating[:, :, None] * grad_out[:, None, :])
        .astype(jnp.bfloat16)
        .reshape(2 * row_count, width)
    )
    grad_expert_out = (
        jnp.zeros((experts, CAP, width), jnp.bfloat16).at[flat_ids, slot_pos].set(grad_picked)
    )
    grad_outer_bias = jnp.sum(grad_expert_out, axis=1, dtype=jnp.float32)
    hidden_pre = (
        jnp.einsum("ecd,edf->ecf", buffer, inner_weight, preferred_element_type=jnp.float32)
        + inner_bias[:, None, :]
    )
    hidden_act = exact_gelu(hidden_pre).astype(jnp.bfloat16)
    grad_outer_weight = jnp.einsum(
        "ecf,ecd->efd", hidden_act, grad_expert_out, preferred_element_type=jnp.float32
    )
    grad_act = jnp.einsum(
        "ecd,efd->ecf", grad_expert_out, outer_weight, preferred_element_type=jnp.float32
    )
    gelu_pull = jax.vjp(exact_gelu, hidden_pre)[1]
    grad_pre = gelu_pull(grad_act)[0].astype(jnp.bfloat16)
    grad_inner_bias = jnp.sum(grad_pre, axis=1, dtype=jnp.float32)
    grad_inner_weight = jnp.einsum(
        "ecd,ecf->edf", buffer, grad_pre, preferred_element_type=jnp.float32
    )
    grad_buffer = jnp.einsum(
        "ecf,edf->ecd", grad_pre, inner_weight, preferred_element_type=jnp.float32
    )
    grad_rows = jnp.sum(grad_buffer[flat_ids, slot_pos].reshape(row_count, 2, width), axis=1)
    expert_range = jnp.arange(experts, dtype=jnp.int32)[None, None, :]
    grad_route = jnp.sum(
        grad_gate[:, :, None] * (chosen[:, :, None] == expert_range).astype(jnp.float32), axis=1
    )
    grad_logits = (
        routing * (grad_route - jnp.sum(routing * grad_route, axis=-1, keepdims=True))
    ).astype(jnp.bfloat16)
    grad_router = jnp.einsum(
        "nd,ne->de", normed_mid, grad_logits, preferred_element_type=jnp.float32
    )
    grad_normed_mid = grad_rows + jnp.einsum(
        "ne,de->nd", grad_logits, full_router, preferred_element_type=jnp.float32
    )
    second_pull = jax.vjp(norm_rows, middle, gain_second, bias_second)[1]
    grad_mid_norm, grad_gain_second, grad_bias_second = second_pull(grad_normed_mid)
    grad_middle = grad_out + grad_mid_norm
    grad_proj = grad_middle.astype(jnp.bfloat16)
    grad_bias_proj = jnp.sum(grad_proj, axis=0, dtype=jnp.float32)
    grad_proj_weight = jnp.einsum(
        "nd,ne->de", attended, grad_proj, preferred_element_type=jnp.float32
    )
    grad_attended = jnp.einsum(
        "ne,de->nd", grad_proj, full_proj, preferred_element_type=jnp.float32
    ).astype(jnp.bfloat16)
    grad_head_out = lax.all_to_all(
        grad_attended.reshape(images, seq_len, HEADS, head_dim),
        "seq",
        split_axis=2,
        concat_axis=0,
        tiled=True,
    )
    recomputed = jnp.exp(score_block() - log_total)
    grad_values = jnp.einsum(
        "ghab,gahd->gbhd",
        recomputed.astype(jnp.bfloat16),
        grad_head_out,
        preferred_element_type=jnp.float32,
    )
    grad_probs = jnp.einsum(
        "gahd,gbhd->ghab", grad_head_out, value_rows, preferred_element_type=jnp.float32
    )
    grad_scores = (
        recomputed * (grad_probs - jnp.sum(recomputed * grad_probs, axis=-1, keepdims=True))
    ).astype(jnp.bfloat16)
    grad_queries = (
        jnp.einsum("ghab,gbhd->gahd", grad_scores, key_rows, preferred_element_type=jnp.float32)
        * scaling
    )
    grad_keys = (
        jnp.einsum("ghab,gahd->gbhd", grad_scores, queries, preferred_element_type=jnp.float32)
        * scaling
    )
    grad_head_qkv = jnp.stack([grad_queries, grad_keys, grad_values], axis=2).astype(jnp.bfloat16)
    grad_qkv = lax.all_to_all(
        grad_head_qkv, "seq", split_axis=0, concat_axis=3, tiled=True
    ).reshape(row_count, 3 * width)
    grad_qkv_weight = jnp.einsum(
        "nd,ne->de", normed_in, grad_qkv, preferred_element_type=jnp.float32
    )
    grad_normed_in = jnp.einsum("ne,de->nd", grad_qkv, full_qkv, preferred_element_type=jnp.float32)
    first_pull = jax.vjp(norm_rows, flat_tokens, gain_first, bias_first)[1]
    grad_first, grad_gain_first, grad_bias_first = first_pull(grad_normed_in)
    token_grad = (grad_middle + grad_first).astype(jnp.bfloat16).reshape(images, seq_len, width)
    shares = (
        lax.psum_scatter(grad_gain_first, "fsdp", scatter_dimension=0, tiled=True),
        lax.psum_scatter(grad_bias_first, "fsdp", scatter_dimension=0, tiled=True),
        lax.psum_scatter(grad_qkv_weight, "fsdp", scatter_dimension=0, tiled=True),
        lax.psum_scatter(grad_proj_weight, "fsdp", scatter_dimension=0, tiled=True),
        lax.psum_scatter(grad_bias_proj, "fsdp", scatter_dimension=0, tiled=True),
        lax.psum_scatter(grad_gain_second, "fsdp", scatter_dimension=0, tiled=True),
        lax.psum_scatter(grad_bias_second, "fsdp", scatter_dimension=0, tiled=True),
        lax.psum_scatter(grad_router, "fsdp", scatter_dimension=0, tiled=True),
        lax.psum_scatter(grad_inner_weight, "fsdp", scatter_dimension=1, tiled=True),
        lax.psum_scatter(grad_inner_bias, "fsdp", scatter_dimension=1, tiled=True),
        lax.psum_scatter(grad_outer_weight, "fsdp", scatter_dimension=1, tiled=True),
        lax.psum_scatter(grad_outer_bias, "fsdp", scatter_dimension=1, tiled=True),
    )
    parted = (
        lax.psum_scatter(
            shares[0].astype(jnp.bfloat16), "seq", scatter_dimension=0, tiled=True
        ).astype(jnp.float32),
        lax.psum_scatter(
            shares[1].astype(jnp.bfloat16), "seq", scatter_dimension=0, tiled=True
        ).astype(jnp.float32),
        lax.psum_scatter(
            shares[2].astype(jnp.bfloat16), "seq", scatter_dimension=0, tiled=True
        ).astype(jnp.float32),
        lax.psum_scatter(
            shares[3].astype(jnp.bfloat16), "seq", scatter_dimension=0, tiled=True
        ).astype(jnp.float32),
        lax.psum_scatter(
            shares[4].astype(jnp.bfloat16), "seq", scatter_dimension=0, tiled=True
        ).astype(jnp.float32),
        lax.psum_scatter(
            shares[5].astype(jnp.bfloat16), "seq", scatter_dimension=0, tiled=True
        ).astype(jnp.float32),
        lax.psum_scatter(
            shares[6].astype(jnp.bfloat16), "seq", scatter_dimension=0, tiled=True
        ).astype(jnp.float32),
        lax.psum_scatter(
            shares[7].astype(jnp.bfloat16), "seq", scatter_dimension=0, tiled=True
        ).astype(jnp.float32),
        lax.psum_scatter(
            shares[8].astype(jnp.bfloat16), "seq", scatter_dimension=1, tiled=True
        ).astype(jnp.float32),
        lax.psum_scatter(
            shares[9].astype(jnp.bfloat16), "seq", scatter_dimension=1, tiled=True
        ).astype(jnp.float32),
        lax.psum_scatter(
            shares[10].astype(jnp.bfloat16), "seq", scatter_dimension=1, tiled=True
        ).astype(jnp.float32),
        lax.psum_scatter(
            shares[11].astype(jnp.bfloat16), "seq", scatter_dimension=1, tiled=True
        ).astype(jnp.float32),
    )
    totals = (
        lax.all_gather(parted[0].astype(jnp.bfloat16), "seq", axis=0, tiled=True).astype(
            jnp.float32
        ),
        lax.all_gather(parted[1].astype(jnp.bfloat16), "seq", axis=0, tiled=True).astype(
            jnp.float32
        ),
        lax.all_gather(parted[2].astype(jnp.bfloat16), "seq", axis=0, tiled=True).astype(
            jnp.float32
        ),
        lax.all_gather(parted[3].astype(jnp.bfloat16), "seq", axis=0, tiled=True).astype(
            jnp.float32
        ),
        lax.all_gather(parted[4].astype(jnp.bfloat16), "seq", axis=0, tiled=True).astype(
            jnp.float32
        ),
        lax.all_gather(parted[5].astype(jnp.bfloat16), "seq", axis=0, tiled=True).astype(
            jnp.float32
        ),
        lax.all_gather(parted[6].astype(jnp.bfloat16), "seq", axis=0, tiled=True).astype(
            jnp.float32
        ),
        lax.all_gather(parted[7].astype(jnp.bfloat16), "seq", axis=0, tiled=True).astype(
            jnp.float32
        ),
        lax.all_gather(parted[8].astype(jnp.bfloat16), "seq", axis=1, tiled=True).astype(
            jnp.float32
        ),
        lax.all_gather(parted[9].astype(jnp.bfloat16), "seq", axis=1, tiled=True).astype(
            jnp.float32
        ),
        lax.all_gather(parted[10].astype(jnp.bfloat16), "seq", axis=1, tiled=True).astype(
            jnp.float32
        ),
        lax.all_gather(parted[11].astype(jnp.bfloat16), "seq", axis=1, tiled=True).astype(
            jnp.float32
        ),
    )
    return (
        mixed,
        token_grad,
        totals[0],
        totals[1],
        totals[2],
        totals[3],
        totals[4],
        totals[5],
        totals[6],
        totals[7],
        totals[8],
        totals[9],
        totals[10],
        totals[11],
    )


def z_shift(planes, step):
    return [(2 * z + x, 2 * ((z + step) % planes) + x) for z in range(planes) for x in range(2)]


def x_swap(planes):
    return [(2 * z + x, 2 * z + 1 - x) for z in range(planes) for x in range(2)]


core_swap = [(0, 1), (1, 0), (2, 3), (3, 2)]
y_swap = [(0, 2), (1, 3), (2, 0), (3, 1)]


def gather_fsdp(block, planes):
    column = jnp.stack(
        [block] + [lax.ppermute(block, "fsdp", z_shift(planes, k)) for k in range(1, planes)]
    )
    across = lax.ppermute(column, "fsdp", x_swap(planes))
    return jnp.stack([column, across], axis=1)


def gather_plane(block, planes):
    mine = gather_fsdp(block, planes)
    return jnp.stack([mine, lax.ppermute(mine, "seq", core_swap)])


def scatter_fsdp(parts, planes):
    add = lambda a, b: a.astype(jnp.float32) + b.astype(jnp.float32)
    column = add(parts[:, 0], lax.ppermute(parts[:, 1], "fsdp", x_swap(planes))).astype(
        jnp.bfloat16
    )
    total = column[0].astype(jnp.float32)
    for k in range(1, planes):
        total = total + lax.ppermute(column[k], "fsdp", z_shift(planes, -k)).astype(jnp.float32)
    return total


def scatter_plane(parts, planes):
    other = lax.ppermute(parts[1], "seq", core_swap)
    mine = (parts[0].astype(jnp.float32) + other.astype(jnp.float32)).astype(jnp.bfloat16)
    return scatter_fsdp(mine, planes)


def shard_order(planes):
    f = lax.axis_index("fsdp")
    z, x = f // 2, f % 2
    g = jnp.arange(2 * planes, dtype=jnp.int32)
    return ((z - g // 2) % planes) * 2 + (x ^ (g % 2))


def sum_everywhere(parts, planes):
    order = shard_order(planes)
    shards, rows, columns = parts.shape
    s = lax.axis_index("seq")
    y, c = s // 2, s % 2
    half, quarter = columns // 2, columns // 4
    keep = lax.dynamic_slice_in_dim(parts, c * half, half, 2)
    give = lax.dynamic_slice_in_dim(parts, (1 - c) * half, half, 2)
    got = lax.ppermute(give, "seq", core_swap)
    keep = (keep.astype(jnp.float32) + got.astype(jnp.float32)).astype(jnp.bfloat16)
    give = lax.dynamic_slice_in_dim(keep, (1 - y) * quarter, quarter, 2)
    keep = lax.dynamic_slice_in_dim(keep, y * quarter, quarter, 2)
    got = lax.ppermute(give, "seq", y_swap)
    keep = (keep.astype(jnp.float32) + got.astype(jnp.float32)).astype(jnp.bfloat16)
    place = jnp.take(keep, order, axis=0).reshape(planes, 2, rows, quarter)
    total = scatter_fsdp(place, planes).astype(jnp.bfloat16)
    other = lax.ppermute(total, "seq", y_swap)
    first, second = jnp.where(y == 0, total, other), jnp.where(y == 0, other, total)
    total = jnp.concatenate([first, second], axis=1)
    other = lax.ppermute(total, "seq", core_swap)
    first, second = jnp.where(c == 0, total, other), jnp.where(c == 0, other, total)
    return jnp.concatenate([first, second], axis=1).astype(jnp.float32)


def norm_parts(values):
    center = values - jnp.mean(values, axis=-1, keepdims=True)
    rstd = lax.rsqrt(jnp.mean(center * center, axis=-1, keepdims=True) + epsilon)
    return center * rstd, rstd


def norm_back(grad, normal, rstd, gain):
    scaled = grad * gain
    return rstd * (
        scaled
        - jnp.mean(scaled, axis=-1, keepdims=True)
        - normal * jnp.mean(scaled * normal, axis=-1, keepdims=True)
    )


def move_tokens_plan(
    tokens,
    key_mask,
    expert_ids,
    cotangent,
    norm1_gain,
    norm1_bias,
    w_qkv,
    w_proj,
    proj_bias,
    norm2_gain,
    norm2_bias,
    w_router,
    w_in,
    b_in,
    w_out,
    b_out,
):
    f32, bf16 = jnp.float32, jnp.bfloat16
    _, rows, width = tokens.shape
    experts, depth, hidden = w_in.shape
    slice_width = w_out.shape[1]
    planes = hidden // slice_width // 2
    own = experts // 2
    head_dim = width // HEADS
    scaling = head_dim ** (-0.5)
    s = lax.axis_index("seq")
    f = lax.axis_index("fsdp")
    core = s % 2
    z, x = f // 2, f % 2
    order = shard_order(planes)

    small = jnp.concatenate(
        [
            jnp.stack([norm1_gain, norm1_bias, proj_bias, norm2_gain, norm2_bias], axis=1),
            w_router,
            b_out.T,
        ],
        axis=1,
    )
    small = jnp.pad(small, ((0, 0), (0, 128 - small.shape[1])))
    dense = jnp.concatenate([small, w_qkv, w_proj], axis=1)
    dense = gather_fsdp(dense, planes).reshape(2 * planes, depth, dense.shape[1])
    dense = jnp.take(dense, order, axis=0).reshape(width, dense.shape[2])
    small, full_qkv, full_proj = jnp.split(dense, [128, 128 + w_qkv.shape[1]], axis=1)
    vectors = small[:, :5].T.astype(f32)
    gain_first, bias_first, bias_proj, gain_second, bias_second = [vectors[i] for i in range(5)]
    full_router = small[:, 5 : 5 + experts]
    full_b_out = small[:, 5 + experts : 5 + 2 * experts].T.astype(f32)

    own_mask = lax.dynamic_slice_in_dim(key_mask, s, 1, 0)
    keep_rows = own_mask.reshape(rows, 1).astype(f32)
    usable = (own_mask > 0)[:, None, :]
    chosen = expert_ids.reshape(rows, 2)
    selected = jnp.sum(
        (chosen[:, :, None] == jnp.arange(experts, dtype=jnp.int32)).astype(f32), axis=1
    )
    grad_out = cotangent.astype(f32).reshape(rows, width) * keep_rows
    packed = jnp.concatenate(
        [grad_out.astype(bf16), jnp.pad(selected, ((0, 0), (0, 128 - experts))).astype(bf16)],
        axis=1,
    )
    packed = gather_plane(packed, planes).reshape(-1, width + 128)
    all_grad_out, all_selected = packed[:, :width], packed[:, width : width + experts].astype(f32)

    mine_in = lax.dynamic_slice_in_dim(w_in, core * own, own, 0)
    mine_in = mine_in.reshape(own, depth, 2 * planes, slice_width).transpose(2, 0, 1, 3)
    mine_in = jnp.take(mine_in, order, axis=0).reshape(planes, 2, own, depth, slice_width)
    across = lax.ppermute(mine_in[:, 1], "fsdp", x_swap(planes))
    pairs = jnp.stack([mine_in[:, 0], across], axis=1)
    got = [pairs[0]] + [
        lax.ppermute(pairs[k], "fsdp", z_shift(planes, -k)) for k in range(1, planes)
    ]
    got = jnp.stack(got).reshape(2 * planes, own, depth, slice_width)
    up_order = ((jnp.arange(2 * planes, dtype=jnp.int32) // 2 - z) % planes) * 2 + (
        x ^ (jnp.arange(2 * planes, dtype=jnp.int32) % 2)
    )
    inner = jnp.take(got, up_order, axis=0).transpose(0, 2, 1, 3).reshape(width, own * slice_width)
    outer = lax.dynamic_slice_in_dim(w_out, core * own, own, 0).reshape(own * slice_width, width)
    inner_bias = lax.dynamic_slice_in_dim(b_in_slice(b_in), core * own, own, 0)
    inner_bias = inner_bias.reshape(1, own * slice_width).astype(f32)

    flat_tokens = tokens.astype(f32).reshape(rows, width)
    normal_first, rstd_first = norm_parts(flat_tokens)
    normed_in = (normal_first * gain_first + bias_first).astype(bf16)
    qkv = jnp.dot(normed_in, full_qkv, preferred_element_type=f32).astype(bf16)
    qkv = qkv.reshape(rows, 3, HEADS, head_dim).transpose(1, 2, 0, 3)
    queries, key_rows, value_rows = qkv[0], qkv[1], qkv[2]
    raw = jnp.einsum("had,hbd->hab", queries, key_rows, preferred_element_type=f32) * scaling
    scores = jnp.where(usable, raw, masked_score)
    shifted = jnp.exp(scores - jnp.max(scores, axis=-1, keepdims=True))
    probs = shifted / jnp.sum(shifted, axis=-1, keepdims=True)
    attended = jnp.einsum("hab,hbd->ahd", probs.astype(bf16), value_rows, preferred_element_type=f32)
    attended = attended.astype(bf16).reshape(rows, width)
    middle = flat_tokens + jnp.dot(attended, full_proj, preferred_element_type=f32) + bias_proj
    normal_mid, rstd_mid = norm_parts(middle)
    normed_mid = (normal_mid * gain_second + bias_second).astype(bf16)

    everyone = gather_plane(normed_mid, planes).reshape(-1, width)
    own_experts = core * own + jnp.arange(own, dtype=jnp.int32)
    pick = (own_experts[:, None] == jnp.arange(experts, dtype=jnp.int32)).astype(f32)
    routing = softmax_rows(jnp.dot(everyone, full_router, preferred_element_type=f32))
    gates = jnp.dot(routing * all_selected, pick.T, precision=lax.Precision.HIGHEST)
    spread_gates = jnp.repeat(gates, slice_width, axis=1)
    pre = jnp.dot(everyone, inner, preferred_element_type=f32) + inner_bias
    cdf = 0.5 * (1.0 + lax.erf(pre * (0.5**0.5)))
    slope = cdf + pre * jnp.exp(-0.5 * pre * pre) * 0.3989422804014327
    act = pre * cdf
    gated = (spread_gates * act).astype(bf16)
    mix_parts = jnp.dot(gated, outer, preferred_element_type=f32).astype(bf16)
    grad_act = jnp.einsum("nd,fd->nf", all_grad_out, outer, preferred_element_type=f32)
    grad_gate = jnp.sum((act * grad_act).reshape(-1, own, slice_width), axis=2)
    grad_pre32 = spread_gates * grad_act * slope
    grad_pre = grad_pre32.astype(bf16)
    outer_grad = jnp.einsum("nf,nd->fd", gated, all_grad_out, preferred_element_type=f32)
    inner_bias_grad = jnp.sum(grad_pre32, axis=0)
    inner_grad = jnp.einsum("nd,nf->df", everyone, grad_pre, preferred_element_type=f32)
    grad_gate = jnp.dot(grad_gate * all_select(all_selected, pick), pick, precision=lax.Precision.HIGHEST)
    grad_logits = (
        routing * (grad_gate - jnp.sum(routing * grad_gate, axis=-1, keepdims=True))
    ).astype(bf16)
    router_grad = jnp.einsum("nd,ne->de", everyone, grad_logits, preferred_element_type=f32)
    row_parts = jnp.einsum("nf,df->nd", grad_pre, inner, preferred_element_type=f32)
    row_parts = row_parts + jnp.einsum(
        "ne,de->nd", grad_logits, full_router, preferred_element_type=f32
    )
    row_parts = row_parts.astype(bf16)
    grad_rows = scatter_plane(row_parts.reshape(2, planes, 2, rows, width), planes)
    mixture = scatter_plane(mix_parts.reshape(2, planes, 2, rows, width), planes)

    own_routing = softmax_rows(jnp.dot(normed_mid, full_router, preferred_element_type=f32))
    own_gates = own_routing * selected
    mixture = mixture + jnp.dot(own_gates, full_b_out, precision=lax.Precision.HIGHEST)
    mixed = (keep_rows * (middle + mixture)).astype(bf16).reshape(1, rows, width)
    bias_gate = selected * jnp.einsum(
        "nd,ed->ne", grad_out, full_b_out, precision=lax.Precision.HIGHEST
    )
    bias_logits = (
        own_routing * (bias_gate - jnp.sum(own_routing * bias_gate, axis=-1, keepdims=True))
    ).astype(bf16)
    router_grad = router_grad + jnp.einsum(
        "nd,ne->de", normed_mid, bias_logits, preferred_element_type=f32
    )
    outer_bias_grad = jnp.einsum(
        "ne,nd->de", own_gates, grad_out, precision=lax.Precision.HIGHEST
    )
    grad_normed_mid = grad_rows + jnp.einsum(
        "ne,de->nd", bias_logits, full_router, preferred_element_type=f32
    )
    grad_gain_second = jnp.sum(grad_normed_mid * normal_mid, axis=0)
    grad_bias_second = jnp.sum(grad_normed_mid, axis=0)
    grad_middle = grad_out + norm_back(grad_normed_mid, normal_mid, rstd_mid, gain_second)
    grad_proj = grad_middle.astype(bf16)
    grad_bias_proj = jnp.sum(grad_proj, axis=0, dtype=f32)
    grad_proj_weight = jnp.einsum("nd,ne->de", attended, grad_proj, preferred_element_type=f32)
    vectors = jnp.concatenate(
        [
            jnp.stack([grad_gain_second, grad_bias_second, grad_bias_proj], axis=1),
            router_grad,
            outer_bias_grad,
        ],
        axis=1,
    )
    early = jnp.concatenate(
        [grad_proj_weight, jnp.pad(vectors, ((0, 0), (0, 256 - vectors.shape[1])))], axis=1
    ).astype(bf16)
    early = sum_everywhere(early.reshape(2 * planes, depth, width + 256), planes)
    grad_attended = jnp.einsum("ne,de->nd", grad_proj, full_proj, preferred_element_type=f32)
    grad_attended = grad_attended.astype(bf16).reshape(rows, HEADS, head_dim)
    grad_values = jnp.einsum(
        "hab,ahd->bhd", probs.astype(bf16), grad_attended, preferred_element_type=f32
    )
    grad_probs = jnp.einsum("ahd,hbd->hab", grad_attended, value_rows, preferred_element_type=f32)
    grad_scores = (
        probs * (grad_probs - jnp.sum(probs * grad_probs, axis=-1, keepdims=True))
    ).astype(bf16)
    grad_queries = (
        jnp.einsum("hab,hbd->ahd", grad_scores, key_rows, preferred_element_type=f32) * scaling
    )
    grad_keys = (
        jnp.einsum("hab,had->bhd", grad_scores, queries, preferred_element_type=f32) * scaling
    )
    grad_qkv = jnp.stack([grad_queries, grad_keys, grad_values], axis=1).astype(bf16)
    grad_qkv = grad_qkv.reshape(rows, 3 * width)
    grad_qkv_weight = jnp.einsum("nd,ne->de", normed_in, grad_qkv, preferred_element_type=f32)
    grad_normed_in = jnp.einsum("ne,de->nd", grad_qkv, full_qkv, preferred_element_type=f32)
    grad_gain_first = jnp.sum(grad_normed_in * normal_first, axis=0)
    grad_bias_first = jnp.sum(grad_normed_in, axis=0)
    token_grad = grad_middle + norm_back(grad_normed_in, normal_first, rstd_first, gain_first)
    token_grad = token_grad.astype(bf16).reshape(1, rows, width)
    vectors = jnp.stack([grad_gain_first, grad_bias_first], axis=1)
    late = jnp.concatenate(
        [grad_qkv_weight, jnp.pad(vectors, ((0, 0), (0, 256 - vectors.shape[1])))], axis=1
    ).astype(bf16)
    late = sum_everywhere(late.reshape(2 * planes, depth, 3 * width + 256), planes)

    def both_cores(mine):
        mine = mine.astype(bf16)
        other = lax.ppermute(mine, "seq", core_swap)
        first, second = jnp.where(core == 0, mine, other), jnp.where(core == 0, other, mine)
        return jnp.concatenate([first, second], axis=0).astype(f32)

    bias_row = jnp.pad(
        inner_bias_grad.reshape(own, 1, slice_width), ((0, 0), (0, 15), (0, width - slice_width))
    )
    outer_grad = jnp.concatenate([outer_grad.reshape(own, slice_width, width), bias_row], axis=1)
    outer_grad = outer_grad.astype(bf16)
    outer_grad = outer_grad.astype(f32) + lax.ppermute(outer_grad, "seq", y_swap).astype(f32)
    outer_grad = both_cores(outer_grad)
    inner_grad = inner_grad.astype(bf16).reshape(2 * planes, depth, own, slice_width)
    inner_grad = jnp.take(inner_grad, order, axis=0).reshape(planes, 2, depth, own, slice_width)
    across = lax.ppermute(inner_grad[:, 1], "fsdp", x_swap(planes))
    pairs = jnp.stack([inner_grad[:, 0], across], axis=1)
    got = [pairs[0]] + [
        lax.ppermute(pairs[k], "fsdp", z_shift(planes, -k)) for k in range(1, planes)
    ]
    got = jnp.stack(got).reshape(2 * planes, depth, own, slice_width)
    inner_grad = jnp.take(got, up_order, axis=0).transpose(2, 1, 0, 3).reshape(own, depth, hidden)
    inner_grad = inner_grad.astype(f32) + lax.ppermute(inner_grad, "seq", y_swap).astype(f32)
    inner_grad = both_cores(inner_grad)
    return (
        mixed,
        token_grad,
        late[:, 3 * width],
        late[:, 3 * width + 1],
        late[:, : 3 * width],
        early[:, :width],
        early[:, width + 2],
        early[:, width],
        early[:, width + 1],
        early[:, width + 3 : width + 3 + experts],
        inner_grad,
        outer_grad[:, slice_width, :slice_width],
        outer_grad[:, :slice_width],
        early[:, width + 3 + experts : width + 3 + 2 * experts].T,
    )


def b_in_slice(b_in):
    return b_in


def all_select(selected, pick):
    return jnp.dot(selected, pick.T, precision=lax.Precision.HIGHEST)


def solution(mesh):
    n_seq, n_fsdp = mesh.shape["seq"], mesh.shape["fsdp"]

    def per_device(*args):
        tokens, w_in, w_out = args[0], args[12], args[14]
        experts, _, hidden = w_in.shape
        lanes = hidden // n_fsdp
        whole_tiles = lanes % 128 == 0 and w_in.shape[1] % 16 == 0
        if n_seq == 4 and experts == n_seq and tokens.shape[0] == 1 and whole_tiles:
            return move_tokens_plan(*args)
        return gather_weights_plan(*args)

    return jax.shard_map(
        per_device,
        mesh=mesh,
        in_specs=(
            P(("fsdp", "seq"), None, None),
            P("fsdp", None),
            P(("fsdp", "seq"), None, None),
            P(("fsdp", "seq"), None, None),
            P("fsdp"),
            P("fsdp"),
            P("fsdp", None),
            P("fsdp", None),
            P("fsdp"),
            P("fsdp"),
            P("fsdp"),
            P("fsdp", None),
            P(None, "fsdp", None),
            P(None, "fsdp"),
            P(None, "fsdp", None),
            P(None, "fsdp"),
        ),
        out_specs=(
            P(("fsdp", "seq"), None, None),
            P(("fsdp", "seq"), None, None),
            P("fsdp"),
            P("fsdp"),
            P("fsdp", None),
            P("fsdp", None),
            P("fsdp"),
            P("fsdp"),
            P("fsdp"),
            P("fsdp", None),
            P(None, "fsdp", None),
            P(None, "fsdp"),
            P(None, "fsdp", None),
            P(None, "fsdp"),
        ),
        check_vma=False,
    )
```

```python
import functools

import jax
import jax.numpy as jnp
from jax import lax
from jax.experimental import pallas as pl
from jax.experimental.pallas import tpu as pltpu
from jax.sharding import PartitionSpec as P

HEADS = 12
CAP = 142


epsilon = 1e-06
masked_score = -1e30


def norm_rows(values, gain, offset):
    center = values - jnp.mean(values, axis=-1, keepdims=True)
    spread = jnp.mean(center * center, axis=-1, keepdims=True)
    return center * lax.rsqrt(spread + epsilon) * gain + offset


def softmax_rows(values):
    shifted = jnp.exp(values - jnp.max(values, axis=-1, keepdims=True))
    return shifted / jnp.sum(shifted, axis=-1, keepdims=True)


def exact_gelu(values):
    return jax.nn.gelu(values, approximate=False)


def expert_slots(chosen, experts):
    flat_ids = chosen.reshape(-1)
    onehot = (flat_ids[:, None] == jnp.arange(experts, dtype=jnp.int32)[None, :]).astype(jnp.int32)
    ranks = jnp.cumsum(onehot, axis=0, dtype=jnp.int32)
    slot_pos = jnp.sum(onehot * ranks, axis=1, dtype=jnp.int32) - 1
    return (flat_ids, slot_pos)


def gather_weights_plan(
    tokens,
    key_mask,
    expert_ids,
    cotangent,
    norm1_gain,
    norm1_bias,
    w_qkv,
    w_proj,
    proj_bias,
    norm2_gain,
    norm2_bias,
    w_router,
    w_in,
    b_in,
    w_out,
    b_out,
):
    images, seq_len, width = tokens.shape
    experts = w_in.shape[0]
    head_dim = width // HEADS
    scaling = head_dim ** (-0.5)
    row_count = images * seq_len
    dense_set = (
        lax.all_gather(norm1_gain, "fsdp", axis=0, tiled=True),
        lax.all_gather(norm1_bias, "fsdp", axis=0, tiled=True),
        lax.all_gather(w_qkv, "fsdp", axis=0, tiled=True),
        lax.all_gather(w_proj, "fsdp", axis=0, tiled=True),
        lax.all_gather(proj_bias, "fsdp", axis=0, tiled=True),
        lax.all_gather(norm2_gain, "fsdp", axis=0, tiled=True),
        lax.all_gather(norm2_bias, "fsdp", axis=0, tiled=True),
        lax.all_gather(w_router, "fsdp", axis=0, tiled=True),
    )
    gain_first = dense_set[0].astype(jnp.float32)
    bias_first = dense_set[1].astype(jnp.float32)
    full_qkv = dense_set[2]
    full_proj = dense_set[3]
    bias_proj = dense_set[4].astype(jnp.float32)
    gain_second = dense_set[5].astype(jnp.float32)
    bias_second = dense_set[6].astype(jnp.float32)
    full_router = dense_set[7]
    expert_set = (
        lax.all_gather(w_in, "fsdp", axis=1, tiled=True),
        lax.all_gather(b_in, "fsdp", axis=1, tiled=True),
        lax.all_gather(w_out, "fsdp", axis=1, tiled=True),
        lax.all_gather(b_out, "fsdp", axis=1, tiled=True),
    )
    inner_weight = expert_set[0]
    inner_bias = expert_set[1].astype(jnp.float32)
    outer_weight = expert_set[2]
    outer_bias = expert_set[3].astype(jnp.float32)
    own_mask = lax.dynamic_slice_in_dim(key_mask, lax.axis_index("seq") * images, images, 0)
    keep_rows = own_mask.reshape(row_count, 1).astype(jnp.float32)
    usable = (key_mask > 0)[:, None, None, :]
    flat_tokens = tokens.astype(jnp.float32).reshape(row_count, width)
    normed_in = norm_rows(flat_tokens, gain_first, bias_first).astype(jnp.bfloat16)
    mixed_qkv = jnp.dot(normed_in, full_qkv, preferred_element_type=jnp.float32).astype(
        jnp.bfloat16
    )
    mixed_qkv = mixed_qkv.reshape(images, seq_len, 3, HEADS, head_dim)
    head_qkv = lax.all_to_all(mixed_qkv, "seq", split_axis=3, concat_axis=0, tiled=True)
    queries = head_qkv[:, :, 0]
    key_rows = head_qkv[:, :, 1]
    value_rows = head_qkv[:, :, 2]

    def score_block():
        raw = (
            jnp.einsum("gahd,gbhd->ghab", queries, key_rows, preferred_element_type=jnp.float32)
            * scaling
        )
        return jnp.where(usable, raw, masked_score)

    scores = score_block()
    row_top = jnp.max(scores, axis=-1, keepdims=True)
    shifted = jnp.exp(scores - row_top)
    row_total = jnp.sum(shifted, axis=-1, keepdims=True)
    attn_probs = (shifted / row_total).astype(jnp.bfloat16)
    log_total = row_top + jnp.log(row_total)
    head_out = jnp.einsum(
        "ghab,gbhd->gahd", attn_probs, value_rows, preferred_element_type=jnp.float32
    ).astype(jnp.bfloat16)
    attended = lax.all_to_all(head_out, "seq", split_axis=0, concat_axis=2, tiled=True).reshape(
        row_count, width
    )
    middle = (
        flat_tokens + jnp.dot(attended, full_proj, preferred_element_type=jnp.float32) + bias_proj
    )
    normed_mid = norm_rows(middle, gain_second, bias_second).astype(jnp.bfloat16)
    routing = softmax_rows(jnp.dot(normed_mid, full_router, preferred_element_type=jnp.float32))
    chosen = expert_ids.reshape(row_count, 2)
    flat_ids, slot_pos = expert_slots(chosen, experts)
    gating = jnp.take_along_axis(routing, chosen, axis=1)
    buffer = (
        jnp.zeros((experts, CAP, width), jnp.bfloat16)
        .at[flat_ids, slot_pos]
        .set(jnp.repeat(normed_mid, 2, axis=0))
    )
    pre_act = (
        jnp.einsum("ecd,edf->ecf", buffer, inner_weight, preferred_element_type=jnp.float32)
        + inner_bias[:, None, :]
    )
    activated = exact_gelu(pre_act).astype(jnp.bfloat16)
    expert_out = (
        jnp.einsum("ecf,efd->ecd", activated, outer_weight, preferred_element_type=jnp.float32)
        + outer_bias[:, None, :]
    )
    picked = expert_out[flat_ids, slot_pos].reshape(row_count, 2, width)
    mixture = jnp.sum(gating[:, :, None] * picked, axis=1)
    mixed = (keep_rows * (middle + mixture)).astype(jnp.bfloat16).reshape(images, seq_len, width)
    grad_out = cotangent.astype(jnp.float32).reshape(row_count, width) * keep_rows
    grad_gate = jnp.sum(grad_out[:, None, :] * picked, axis=2)
    grad_picked = (
        (gating[:, :, None] * grad_out[:, None, :])
        .astype(jnp.bfloat16)
        .reshape(2 * row_count, width)
    )
    grad_expert_out = (
        jnp.zeros((experts, CAP, width), jnp.bfloat16).at[flat_ids, slot_pos].set(grad_picked)
    )
    grad_outer_bias = jnp.sum(grad_expert_out, axis=1, dtype=jnp.float32)
    hidden_pre = (
        jnp.einsum("ecd,edf->ecf", buffer, inner_weight, preferred_element_type=jnp.float32)
        + inner_bias[:, None, :]
    )
    hidden_act = exact_gelu(hidden_pre).astype(jnp.bfloat16)
    grad_outer_weight = jnp.einsum(
        "ecf,ecd->efd", hidden_act, grad_expert_out, preferred_element_type=jnp.float32
    )
    grad_act = jnp.einsum(
        "ecd,efd->ecf", grad_expert_out, outer_weight, preferred_element_type=jnp.float32
    )
    gelu_pull = jax.vjp(exact_gelu, hidden_pre)[1]
    grad_pre = gelu_pull(grad_act)[0].astype(jnp.bfloat16)
    grad_inner_bias = jnp.sum(grad_pre, axis=1, dtype=jnp.float32)
    grad_inner_weight = jnp.einsum(
        "ecd,ecf->edf", buffer, grad_pre, preferred_element_type=jnp.float32
    )
    grad_buffer = jnp.einsum(
        "ecf,edf->ecd", grad_pre, inner_weight, preferred_element_type=jnp.float32
    )
    grad_rows = jnp.sum(grad_buffer[flat_ids, slot_pos].reshape(row_count, 2, width), axis=1)
    expert_range = jnp.arange(experts, dtype=jnp.int32)[None, None, :]
    grad_route = jnp.sum(
        grad_gate[:, :, None] * (chosen[:, :, None] == expert_range).astype(jnp.float32), axis=1
    )
    grad_logits = (
        routing * (grad_route - jnp.sum(routing * grad_route, axis=-1, keepdims=True))
    ).astype(jnp.bfloat16)
    grad_router = jnp.einsum(
        "nd,ne->de", normed_mid, grad_logits, preferred_element_type=jnp.float32
    )
    grad_normed_mid = grad_rows + jnp.einsum(
        "ne,de->nd", grad_logits, full_router, preferred_element_type=jnp.float32
    )
    second_pull = jax.vjp(norm_rows, middle, gain_second, bias_second)[1]
    grad_mid_norm, grad_gain_second, grad_bias_second = second_pull(grad_normed_mid)
    grad_middle = grad_out + grad_mid_norm
    grad_proj = grad_middle.astype(jnp.bfloat16)
    grad_bias_proj = jnp.sum(grad_proj, axis=0, dtype=jnp.float32)
    grad_proj_weight = jnp.einsum(
        "nd,ne->de", attended, grad_proj, preferred_element_type=jnp.float32
    )
    grad_attended = jnp.einsum(
        "ne,de->nd", grad_proj, full_proj, preferred_element_type=jnp.float32
    ).astype(jnp.bfloat16)
    grad_head_out = lax.all_to_all(
        grad_attended.reshape(images, seq_len, HEADS, head_dim),
        "seq",
        split_axis=2,
        concat_axis=0,
        tiled=True,
    )
    recomputed = jnp.exp(score_block() - log_total)
    grad_values = jnp.einsum(
        "ghab,gahd->gbhd",
        recomputed.astype(jnp.bfloat16),
        grad_head_out,
        preferred_element_type=jnp.float32,
    )
    grad_probs = jnp.einsum(
        "gahd,gbhd->ghab", grad_head_out, value_rows, preferred_element_type=jnp.float32
    )
    grad_scores = (
        recomputed * (grad_probs - jnp.sum(recomputed * grad_probs, axis=-1, keepdims=True))
    ).astype(jnp.bfloat16)
    grad_queries = (
        jnp.einsum("ghab,gbhd->gahd", grad_scores, key_rows, preferred_element_type=jnp.float32)
        * scaling
    )
    grad_keys = (
        jnp.einsum("ghab,gahd->gbhd", grad_scores, queries, preferred_element_type=jnp.float32)
        * scaling
    )
    grad_head_qkv = jnp.stack([grad_queries, grad_keys, grad_values], axis=2).astype(jnp.bfloat16)
    grad_qkv = lax.all_to_all(
        grad_head_qkv, "seq", split_axis=0, concat_axis=3, tiled=True
    ).reshape(row_count, 3 * width)
    grad_qkv_weight = jnp.einsum(
        "nd,ne->de", normed_in, grad_qkv, preferred_element_type=jnp.float32
    )
    grad_normed_in = jnp.einsum("ne,de->nd", grad_qkv, full_qkv, preferred_element_type=jnp.float32)
    first_pull = jax.vjp(norm_rows, flat_tokens, gain_first, bias_first)[1]
    grad_first, grad_gain_first, grad_bias_first = first_pull(grad_normed_in)
    token_grad = (grad_middle + grad_first).astype(jnp.bfloat16).reshape(images, seq_len, width)
    shares = (
        lax.psum_scatter(grad_gain_first, "fsdp", scatter_dimension=0, tiled=True),
        lax.psum_scatter(grad_bias_first, "fsdp", scatter_dimension=0, tiled=True),
        lax.psum_scatter(grad_qkv_weight, "fsdp", scatter_dimension=0, tiled=True),
        lax.psum_scatter(grad_proj_weight, "fsdp", scatter_dimension=0, tiled=True),
        lax.psum_scatter(grad_bias_proj, "fsdp", scatter_dimension=0, tiled=True),
        lax.psum_scatter(grad_gain_second, "fsdp", scatter_dimension=0, tiled=True),
        lax.psum_scatter(grad_bias_second, "fsdp", scatter_dimension=0, tiled=True),
        lax.psum_scatter(grad_router, "fsdp", scatter_dimension=0, tiled=True),
        lax.psum_scatter(grad_inner_weight, "fsdp", scatter_dimension=1, tiled=True),
        lax.psum_scatter(grad_inner_bias, "fsdp", scatter_dimension=1, tiled=True),
        lax.psum_scatter(grad_outer_weight, "fsdp", scatter_dimension=1, tiled=True),
        lax.psum_scatter(grad_outer_bias, "fsdp", scatter_dimension=1, tiled=True),
    )
    parted = (
        lax.psum_scatter(
            shares[0].astype(jnp.bfloat16), "seq", scatter_dimension=0, tiled=True
        ).astype(jnp.float32),
        lax.psum_scatter(
            shares[1].astype(jnp.bfloat16), "seq", scatter_dimension=0, tiled=True
        ).astype(jnp.float32),
        lax.psum_scatter(
            shares[2].astype(jnp.bfloat16), "seq", scatter_dimension=0, tiled=True
        ).astype(jnp.float32),
        lax.psum_scatter(
            shares[3].astype(jnp.bfloat16), "seq", scatter_dimension=0, tiled=True
        ).astype(jnp.float32),
        lax.psum_scatter(
            shares[4].astype(jnp.bfloat16), "seq", scatter_dimension=0, tiled=True
        ).astype(jnp.float32),
        lax.psum_scatter(
            shares[5].astype(jnp.bfloat16), "seq", scatter_dimension=0, tiled=True
        ).astype(jnp.float32),
        lax.psum_scatter(
            shares[6].astype(jnp.bfloat16), "seq", scatter_dimension=0, tiled=True
        ).astype(jnp.float32),
        lax.psum_scatter(
            shares[7].astype(jnp.bfloat16), "seq", scatter_dimension=0, tiled=True
        ).astype(jnp.float32),
        lax.psum_scatter(
            shares[8].astype(jnp.bfloat16), "seq", scatter_dimension=1, tiled=True
        ).astype(jnp.float32),
        lax.psum_scatter(
            shares[9].astype(jnp.bfloat16), "seq", scatter_dimension=1, tiled=True
        ).astype(jnp.float32),
        lax.psum_scatter(
            shares[10].astype(jnp.bfloat16), "seq", scatter_dimension=1, tiled=True
        ).astype(jnp.float32),
        lax.psum_scatter(
            shares[11].astype(jnp.bfloat16), "seq", scatter_dimension=1, tiled=True
        ).astype(jnp.float32),
    )
    totals = (
        lax.all_gather(parted[0].astype(jnp.bfloat16), "seq", axis=0, tiled=True).astype(
            jnp.float32
        ),
        lax.all_gather(parted[1].astype(jnp.bfloat16), "seq", axis=0, tiled=True).astype(
            jnp.float32
        ),
        lax.all_gather(parted[2].astype(jnp.bfloat16), "seq", axis=0, tiled=True).astype(
            jnp.float32
        ),
        lax.all_gather(parted[3].astype(jnp.bfloat16), "seq", axis=0, tiled=True).astype(
            jnp.float32
        ),
        lax.all_gather(parted[4].astype(jnp.bfloat16), "seq", axis=0, tiled=True).astype(
            jnp.float32
        ),
        lax.all_gather(parted[5].astype(jnp.bfloat16), "seq", axis=0, tiled=True).astype(
            jnp.float32
        ),
        lax.all_gather(parted[6].astype(jnp.bfloat16), "seq", axis=0, tiled=True).astype(
            jnp.float32
        ),
        lax.all_gather(parted[7].astype(jnp.bfloat16), "seq", axis=0, tiled=True).astype(
            jnp.float32
        ),
        lax.all_gather(parted[8].astype(jnp.bfloat16), "seq", axis=1, tiled=True).astype(
            jnp.float32
        ),
        lax.all_gather(parted[9].astype(jnp.bfloat16), "seq", axis=1, tiled=True).astype(
            jnp.float32
        ),
        lax.all_gather(parted[10].astype(jnp.bfloat16), "seq", axis=1, tiled=True).astype(
            jnp.float32
        ),
        lax.all_gather(parted[11].astype(jnp.bfloat16), "seq", axis=1, tiled=True).astype(
            jnp.float32
        ),
    )
    return (
        mixed,
        token_grad,
        totals[0],
        totals[1],
        totals[2],
        totals[3],
        totals[4],
        totals[5],
        totals[6],
        totals[7],
        totals[8],
        totals[9],
        totals[10],
        totals[11],
    )


def z_shift(planes, step):
    return [(2 * z + x, 2 * ((z + step) % planes) + x) for z in range(planes) for x in range(2)]


def x_swap(planes):
    return [(2 * z + x, 2 * z + 1 - x) for z in range(planes) for x in range(2)]


core_swap = [(0, 1), (1, 0), (2, 3), (3, 2)]
y_swap = [(0, 2), (1, 3), (2, 0), (3, 1)]


def gather_fsdp(block, planes):
    column = jnp.stack(
        [block] + [lax.ppermute(block, "fsdp", z_shift(planes, k)) for k in range(1, planes)]
    )
    across = lax.ppermute(column, "fsdp", x_swap(planes))
    return jnp.stack([column, across], axis=1)


def gather_plane(block, planes):
    mine = gather_fsdp(block, planes)
    return jnp.stack([mine, lax.ppermute(mine, "seq", core_swap)], axis=1)


def scatter_fsdp(parts, planes):
    add = lambda a, b: a.astype(jnp.float32) + b.astype(jnp.float32)
    column = add(parts[:, 0], lax.ppermute(parts[:, 1], "fsdp", x_swap(planes))).astype(
        jnp.bfloat16
    )
    total = column[0].astype(jnp.float32)
    for k in range(1, planes):
        total = total + lax.ppermute(column[k], "fsdp", z_shift(planes, -k)).astype(jnp.float32)
    return total


def scatter_plane(parts, planes):
    other = lax.ppermute(parts[:, 1], "seq", core_swap)
    mine = (parts[:, 0].astype(jnp.float32) + other.astype(jnp.float32)).astype(jnp.bfloat16)
    return scatter_fsdp(mine, planes)


def shard_order(planes):
    f = lax.axis_index("fsdp")
    z, x = f // 2, f % 2
    g = jnp.arange(2 * planes, dtype=jnp.int32)
    return ((z - g // 2) % planes) * 2 + (x ^ (g % 2))


def sum_everywhere(parts, planes):
    order = shard_order(planes)
    shards, rows, columns = parts.shape
    s = lax.axis_index("seq")
    y, c = s // 2, s % 2
    half, quarter = columns // 2, columns // 4
    keep = lax.dynamic_slice_in_dim(parts, c * half, half, 2)
    give = lax.dynamic_slice_in_dim(parts, (1 - c) * half, half, 2)
    got = lax.ppermute(give, "seq", core_swap)
    keep = (keep.astype(jnp.float32) + got.astype(jnp.float32)).astype(jnp.bfloat16)
    give = lax.dynamic_slice_in_dim(keep, (1 - y) * quarter, quarter, 2)
    keep = lax.dynamic_slice_in_dim(keep, y * quarter, quarter, 2)
    got = lax.ppermute(give, "seq", y_swap)
    keep = (keep.astype(jnp.float32) + got.astype(jnp.float32)).astype(jnp.bfloat16)
    place = jnp.take(keep, order, axis=0).reshape(planes, 2, rows, quarter)
    total = scatter_fsdp(place, planes).astype(jnp.bfloat16)
    other = lax.ppermute(total, "seq", y_swap)
    first, second = jnp.where(y == 0, total, other), jnp.where(y == 0, other, total)
    total = jnp.concatenate([first, second], axis=1)
    other = lax.ppermute(total, "seq", core_swap)
    first, second = jnp.where(c == 0, total, other), jnp.where(c == 0, other, total)
    return jnp.concatenate([first, second], axis=1).astype(jnp.float32)


MESH = pl.DeviceIdType.MESH
NT = (((1,), (1,)), ((), ()))
TN = (((0,), (0,)), ((), ()))


def dot(a, b):
    return jnp.dot(a, b, preferred_element_type=jnp.float32)


class Place:
    def __init__(self, planes):
        self.planes = planes
        s, f = lax.axis_index("seq"), lax.axis_index("fsdp")
        self.y, self.c, self.z, self.x = s // 2, s % 2, f // 2, f % 2

    def at(self, y, c, z, x):
        return (y * 2 + c, z * 2 + x)

    def other_core(self):
        return self.at(self.y, 1 - self.c, self.z, self.x)

    def other_x(self):
        return self.at(self.y, self.c, self.z, 1 - self.x)

    def other_y(self):
        return self.at(1 - self.y, self.c, self.z, self.x)

    def level(self, k):
        return self.at(self.y, self.c, lax.rem(self.z + k + self.planes, self.planes), self.x)


def greet(partners):
    barrier = pltpu.get_barrier_semaphore()
    for partner in partners:
        pl.semaphore_signal(barrier, inc=1, device_id=partner, device_id_type=MESH)
    pl.semaphore_wait(barrier, len(partners))


def expert_kernel(
    planes,
    own,
    rows,
    normed_ref,
    grads_ref,
    select_ref,
    inner_ref,
    inner_t_ref,
    outer_ref,
    outer_t_ref,
    bias_ref,
    router_ref,
    router_t_ref,
    mix_ref,
    out_ref,
    inner_grad_ref,
    outer_grad_ref,
    bias_grad_ref,
    router_grad_ref,
    tokens,
    part,
    from_core,
    from_x,
    from_z,
    hidden,
    hidden_grad,
    logit_grad,
    inner_acc,
    outer_acc,
    z_send,
    z_recv,
    x_send,
    x_recv,
    c_send,
    c_recv,
    sum_c_send,
    sum_c_recv,
    sum_x_send,
    sum_x_recv,
    sum_z_send,
    sum_z_recv,
):
    f32, bf16 = jnp.float32, jnp.bfloat16
    place = Place(planes)
    width = normed_ref.shape[1]
    lanes = inner_ref.shape[1] // own

    def remote(src, dst, send, recv, device):
        return pltpu.make_async_remote_copy(
            src_ref=src, dst_ref=dst, send_sem=send, recv_sem=recv, device_id=device, device_id_type=MESH
        )

    def slot(buffer, k, at, count=1):
        return buffer.at[k, pl.ds(at * rows, count * rows)]

    def z_copy(k):
        return remote(slot(tokens, 0, 0), slot(tokens, k, 0), z_send.at[k], z_recv.at[k], place.level(k))

    def x_copy(k):
        return remote(slot(tokens, k, 0), slot(tokens, k, 1), x_send.at[k], x_recv.at[k], place.other_x())

    def c_copy(k, r):
        return remote(
            slot(tokens, k, r), slot(tokens, k, 2 + r), c_send.at[k, r], c_recv.at[k, r], place.other_core()
        )

    def sum_c_copy(k):
        return remote(slot(part, k, 2, 2), from_core.at[k], sum_c_send.at[k], sum_c_recv.at[k], place.other_core())

    def sum_x_copy(k):
        return remote(slot(part, k, 1), from_x.at[k], sum_x_send.at[k], sum_x_recv.at[k], place.other_x())

    def sum_z_copy(k):
        return remote(slot(part, k, 0), from_z.at[k], sum_z_send.at[k], sum_z_recv.at[k], place.level(-k))

    greet([place.other_core(), place.other_x()] + [place.level(k) for k in range(1, planes)])
    tokens[0, 0:rows, :] = normed_ref[...]
    c_copy(0, 0).start()
    x_copy(0).start()
    for k in range(1, planes):
        z_copy(k).start()
    inner_acc[...] = jnp.zeros_like(inner_acc)
    outer_acc[...] = jnp.zeros_like(outer_acc)
    bias_grad_ref[...] = jnp.zeros_like(bias_grad_ref)
    router_grad_ref[...] = jnp.zeros_like(router_grad_ref)

    def tile(k, t):
        here = pl.ds(pl.multiple_of(t * rows, 16), rows)
        normed, grad_out = tokens[k, here, :], grads_ref[k, here, :]
        select = select_ref[k, here, :].astype(f32)
        lane = lax.broadcasted_iota(jnp.int32, select.shape, 1)
        logits = dot(normed, router_ref[...])
        logits = jnp.where(lane < 2 * own, logits, -1e30)
        routing = jnp.exp(logits - jnp.max(logits, axis=1, keepdims=True))
        routing = routing / jnp.sum(routing, axis=1, keepdims=True)
        gates = routing * select
        gate_grads = jnp.zeros_like(gates)
        for i in range(own):
            mine = lane == place.c * own + i
            units = slice(i * lanes, (i + 1) * lanes)
            gate = jnp.sum(jnp.where(mine, gates, 0.0), axis=1, keepdims=True)
            pre = dot(normed, inner_ref[:, units]) + bias_ref[:, units]
            grad_act = dot(grad_out, outer_t_ref[:, units])
            cdf = 0.5 * (1.0 + lax.erf(pre * (0.5**0.5)))
            act = pre * cdf
            hidden[here, units] = (gate * act).astype(bf16)
            gate_grad = jnp.sum(act * grad_act, axis=1, keepdims=True)
            gate_grads = gate_grads + jnp.where(mine, gate_grad * select, 0.0)
            slope = cdf + pre * jnp.exp(-0.5 * pre * pre) * 0.3989422804014327
            grad_pre = gate * grad_act * slope
            bias_grad_ref[:, units] += jnp.sum(grad_pre, axis=0, keepdims=True)
            hidden_grad[here, units] = grad_pre.astype(bf16)
        grad_logits = routing * (gate_grads - jnp.sum(routing * gate_grads, axis=1, keepdims=True))
        logit_grad[here, :] = grad_logits.astype(bf16)
        mix_ref[k, here, :] = dot(hidden[here, :], outer_ref[...]).astype(bf16)
        row_grad = dot(hidden_grad[here, :], inner_t_ref[...])
        row_grad = row_grad + dot(logit_grad[here, :], router_t_ref[...])
        part[k, here, :] = row_grad.astype(bf16)

    def add_core(k):
        sum_c_copy(k).wait_recv()
        total = slot(part, k, 1)[...].astype(f32) + from_core[k, rows : 2 * rows, :].astype(f32)
        part[k, rows : 2 * rows, :] = total.astype(bf16)
        sum_x_copy(k).start()

    def add_x(k):
        sum_x_copy(k).wait_recv()
        total = part[k, 0:rows, :].astype(f32) + from_core[k, 0:rows, :].astype(f32)
        total = total + from_x[k].astype(f32)
        part[k, 0:rows, :] = total.astype(bf16)

        @pl.when(k > 0)
        def _():
            sum_z_copy(k).start()

    def step(k, carry):
        x_copy(k).wait_recv()
        c_copy(k, 1).start()

        @pl.when(k + 1 < planes)
        def _():
            z_copy(k + 1).wait_recv()
            c_copy(k + 1, 0).start()
            x_copy(k + 1).start()

        c_copy(k, 0).wait_recv()
        c_copy(k, 1).wait_recv()

        def one(t, carry):
            tile(k, t)
            return carry

        lax.fori_loop(0, 4, one, 0)
        sum_c_copy(k).start()

        @pl.when(k > 0)
        def _():
            add_core(k - 1)

        @pl.when(k > 1)
        def _():
            add_x(k - 2)

        def columns(j, carry):
            some = pl.ds(pl.multiple_of(j * 256, 256), 256)
            outer_acc[:, some] += lax.dot_general(
                hidden[...], grads_ref[k, :, some], TN, preferred_element_type=f32
            )
            inner_acc[:, some] += lax.dot_general(
                tokens[k], hidden_grad[:, some], TN, preferred_element_type=f32
            )
            return carry

        lax.fori_loop(0, width // 256, columns, 0)
        router_grad_ref[...] += lax.dot_general(tokens[k], logit_grad[...], TN, preferred_element_type=f32)
        return carry

    lax.fori_loop(0, planes, step, 0)
    add_core(planes - 1)
    add_x(planes - 2)
    add_x(planes - 1)
    inner_grad_ref[...] = inner_acc[...].astype(bf16)
    outer_grad_ref[...] = outer_acc[...].astype(bf16)
    total = part[0, 0:rows, :].astype(f32)
    for k in range(1, planes):
        sum_z_copy(k).wait_recv()
        total = total + from_z[k].astype(f32)
    out_ref[...] = total
    for k in range(planes):
        x_copy(k).wait_send()
        c_copy(k, 0).wait_send()
        c_copy(k, 1).wait_send()
        sum_c_copy(k).wait_send()
        sum_x_copy(k).wait_send()
        if k > 0:
            z_copy(k).wait_send()
            sum_z_copy(k).wait_send()


def experts_of_the_plane(planes, own, normed, grads, select, inner, outer, bias, router):
    f32, bf16 = jnp.float32, jnp.bfloat16
    rows, width = normed.shape
    chunk = 4 * rows
    units = inner.shape[1]
    vmem = pl.BlockSpec(memory_space=pltpu.VMEM)
    dma = pltpu.SemaphoreType.DMA
    flops = 12 * planes * chunk * width * units
    return pl.pallas_call(
        functools.partial(expert_kernel, planes, own, rows),
        out_shape=[
            jax.ShapeDtypeStruct((planes, chunk, width), bf16),
            jax.ShapeDtypeStruct((rows, width), f32),
            jax.ShapeDtypeStruct((width, units), bf16),
            jax.ShapeDtypeStruct((units, width), bf16),
            jax.ShapeDtypeStruct((1, units), f32),
            jax.ShapeDtypeStruct((width, 128), f32),
        ],
        in_specs=[vmem] * 10,
        out_specs=[vmem] * 6,
        scratch_shapes=[
            pltpu.VMEM((planes, chunk, width), bf16),
            pltpu.VMEM((planes, chunk, width), bf16),
            pltpu.VMEM((planes, 2 * rows, width), bf16),
            pltpu.VMEM((planes, rows, width), bf16),
            pltpu.VMEM((planes, rows, width), bf16),
            pltpu.VMEM((chunk, units), bf16),
            pltpu.VMEM((chunk, units), bf16),
            pltpu.VMEM((chunk, 128), bf16),
            pltpu.VMEM((width, units), f32),
            pltpu.VMEM((units, width), f32),
        ]
        + [dma((planes,))] * 4
        + [dma((planes, 2))] * 2
        + [dma((planes,))] * 6,
        compiler_params=pltpu.CompilerParams(
            collective_id=1, has_side_effects=True, vmem_limit_bytes=60 * 2**20
        ),
        cost_estimate=pl.CostEstimate(flops=flops, bytes_accessed=40 * 2**20, transcendentals=0),
        name="experts_of_the_plane",
    )(normed, grads, select, inner, inner.T, outer, outer.T, bias, router, router.T)


def norm_parts(values):
    center = values - jnp.mean(values, axis=-1, keepdims=True)
    rstd = lax.rsqrt(jnp.mean(center * center, axis=-1, keepdims=True) + epsilon)
    return center * rstd, rstd


def norm_back(grad, normal, rstd, gain):
    scaled = grad * gain
    return rstd * (
        scaled
        - jnp.mean(scaled, axis=-1, keepdims=True)
        - normal * jnp.mean(scaled * normal, axis=-1, keepdims=True)
    )


def move_tokens_plan(
    tokens,
    key_mask,
    expert_ids,
    cotangent,
    norm1_gain,
    norm1_bias,
    w_qkv,
    w_proj,
    proj_bias,
    norm2_gain,
    norm2_bias,
    w_router,
    w_in,
    b_in,
    w_out,
    b_out,
):
    f32, bf16 = jnp.float32, jnp.bfloat16
    _, rows, width = tokens.shape
    experts, depth, hidden = w_in.shape
    slice_width = w_out.shape[1]
    planes = hidden // slice_width // 2
    own = experts // 2
    head_dim = width // HEADS
    scaling = head_dim ** (-0.5)
    s = lax.axis_index("seq")
    f = lax.axis_index("fsdp")
    core = s % 2
    z, x = f // 2, f % 2
    order = shard_order(planes)

    small = jnp.concatenate(
        [
            jnp.stack([norm1_gain, norm1_bias, proj_bias, norm2_gain, norm2_bias], axis=1),
            w_router,
            b_out.T,
        ],
        axis=1,
    )
    small = jnp.pad(small, ((0, 0), (0, 128 - small.shape[1])))
    dense = jnp.concatenate([small, w_qkv, w_proj], axis=1)
    dense = gather_fsdp(dense, planes).reshape(2 * planes, depth, dense.shape[1])
    dense = jnp.take(dense, order, axis=0).reshape(width, dense.shape[2])
    small, full_qkv, full_proj = jnp.split(dense, [128, 128 + w_qkv.shape[1]], axis=1)
    vectors = small[:, :5].T.astype(f32)
    gain_first, bias_first, bias_proj, gain_second, bias_second = [vectors[i] for i in range(5)]
    full_router = small[:, 5 : 5 + experts]
    full_b_out = small[:, 5 + experts : 5 + 2 * experts].T.astype(f32)

    own_mask = lax.dynamic_slice_in_dim(key_mask, s, 1, 0)
    keep_rows = own_mask.reshape(rows, 1).astype(f32)
    usable = (own_mask > 0)[:, None, :]
    chosen = expert_ids.reshape(rows, 2)
    selected = jnp.sum(
        (chosen[:, :, None] == jnp.arange(experts, dtype=jnp.int32)).astype(f32), axis=1
    )
    grad_out = cotangent.astype(f32).reshape(rows, width) * keep_rows
    padded = (rows + 15) // 16 * 16
    extra = ((0, padded - rows), (0, 0))
    packed = jnp.concatenate(
        [grad_out.astype(bf16), jnp.pad(selected, ((0, 0), (0, 128 - experts))).astype(bf16)],
        axis=1,
    )
    packed = gather_plane(jnp.pad(packed, extra), planes)
    packed = packed.reshape(planes, 4 * padded, width + 128)
    all_grad_out, all_selected = packed[..., :width], packed[..., width:]

    mine_in = lax.dynamic_slice_in_dim(w_in, core * own, own, 0)
    mine_in = mine_in.reshape(own, depth, 2 * planes, slice_width).transpose(2, 0, 1, 3)
    mine_in = jnp.take(mine_in, order, axis=0).reshape(planes, 2, own, depth, slice_width)
    across = lax.ppermute(mine_in[:, 1], "fsdp", x_swap(planes))
    pairs = jnp.stack([mine_in[:, 0], across], axis=1)
    got = [pairs[0]] + [
        lax.ppermute(pairs[k], "fsdp", z_shift(planes, -k)) for k in range(1, planes)
    ]
    got = jnp.stack(got).reshape(2 * planes, own, depth, slice_width)
    up_order = ((jnp.arange(2 * planes, dtype=jnp.int32) // 2 - z) % planes) * 2 + (
        x ^ (jnp.arange(2 * planes, dtype=jnp.int32) % 2)
    )
    inner = jnp.take(got, up_order, axis=0).transpose(0, 2, 1, 3).reshape(width, own * slice_width)
    outer = lax.dynamic_slice_in_dim(w_out, core * own, own, 0).reshape(own * slice_width, width)
    inner_bias = lax.dynamic_slice_in_dim(b_in, core * own, own, 0)
    inner_bias = inner_bias.reshape(1, own * slice_width).astype(f32)

    flat_tokens = tokens.astype(f32).reshape(rows, width)
    normal_first, rstd_first = norm_parts(flat_tokens)
    normed_in = (normal_first * gain_first + bias_first).astype(bf16)
    qkv = jnp.dot(normed_in, full_qkv, preferred_element_type=f32).astype(bf16)
    qkv = qkv.reshape(rows, 3, HEADS, head_dim).transpose(1, 2, 0, 3)
    queries, key_rows, value_rows = qkv[0], qkv[1], qkv[2]
    raw = jnp.einsum("had,hbd->hab", queries, key_rows, preferred_element_type=f32) * scaling
    scores = jnp.where(usable, raw, masked_score)
    shifted = jnp.exp(scores - jnp.max(scores, axis=-1, keepdims=True))
    probs = shifted / jnp.sum(shifted, axis=-1, keepdims=True)
    attended = jnp.einsum("hab,hbd->ahd", probs.astype(bf16), value_rows, preferred_element_type=f32)
    attended = attended.astype(bf16).reshape(rows, width)
    middle = flat_tokens + jnp.dot(attended, full_proj, preferred_element_type=f32) + bias_proj
    normal_mid, rstd_mid = norm_parts(middle)
    normed_mid = (normal_mid * gain_second + bias_second).astype(bf16)

    wide_router = jnp.pad(full_router, ((0, 0), (0, 128 - experts)))
    mix_parts, grad_rows, inner_grad, outer_grad, inner_bias_grad, router_grad = experts_of_the_plane(
        planes,
        own,
        jnp.pad(normed_mid, extra),
        all_grad_out,
        all_selected,
        inner,
        outer,
        inner_bias,
        wide_router,
    )
    grad_rows = grad_rows[:rows]
    router_grad = router_grad[:, :experts]
    mixture = scatter_plane(mix_parts.reshape(planes, 2, 2, padded, width), planes)[:rows]

    own_routing = softmax_rows(jnp.dot(normed_mid, full_router, preferred_element_type=f32))
    own_gates = own_routing * selected
    mixture = mixture + jnp.dot(own_gates, full_b_out, precision=lax.Precision.HIGHEST)
    mixed = (keep_rows * (middle + mixture)).astype(bf16).reshape(1, rows, width)
    bias_gate = selected * jnp.einsum(
        "nd,ed->ne", grad_out, full_b_out, precision=lax.Precision.HIGHEST
    )
    bias_logits = (
        own_routing * (bias_gate - jnp.sum(own_routing * bias_gate, axis=-1, keepdims=True))
    ).astype(bf16)
    router_grad = router_grad + jnp.einsum(
        "nd,ne->de", normed_mid, bias_logits, preferred_element_type=f32
    )
    outer_bias_grad = jnp.einsum(
        "ne,nd->de", own_gates, grad_out, precision=lax.Precision.HIGHEST
    )
    grad_normed_mid = grad_rows + jnp.einsum(
        "ne,de->nd", bias_logits, full_router, preferred_element_type=f32
    )
    grad_gain_second = jnp.sum(grad_normed_mid * normal_mid, axis=0)
    grad_bias_second = jnp.sum(grad_normed_mid, axis=0)
    grad_middle = grad_out + norm_back(grad_normed_mid, normal_mid, rstd_mid, gain_second)
    grad_proj = grad_middle.astype(bf16)
    grad_bias_proj = jnp.sum(grad_proj, axis=0, dtype=f32)
    grad_proj_weight = jnp.einsum("nd,ne->de", attended, grad_proj, preferred_element_type=f32)
    vectors = jnp.concatenate(
        [
            jnp.stack([grad_gain_second, grad_bias_second, grad_bias_proj], axis=1),
            router_grad,
            outer_bias_grad,
        ],
        axis=1,
    )
    early = jnp.concatenate(
        [grad_proj_weight, jnp.pad(vectors, ((0, 0), (0, 256 - vectors.shape[1])))], axis=1
    ).astype(bf16)
    early = sum_everywhere(early.reshape(2 * planes, depth, width + 256), planes)
    grad_attended = jnp.einsum("ne,de->nd", grad_proj, full_proj, preferred_element_type=f32)
    grad_attended = grad_attended.astype(bf16).reshape(rows, HEADS, head_dim)
    grad_values = jnp.einsum(
        "hab,ahd->bhd", probs.astype(bf16), grad_attended, preferred_element_type=f32
    )
    grad_probs = jnp.einsum("ahd,hbd->hab", grad_attended, value_rows, preferred_element_type=f32)
    grad_scores = (
        probs * (grad_probs - jnp.sum(probs * grad_probs, axis=-1, keepdims=True))
    ).astype(bf16)
    grad_queries = (
        jnp.einsum("hab,hbd->ahd", grad_scores, key_rows, preferred_element_type=f32) * scaling
    )
    grad_keys = (
        jnp.einsum("hab,had->bhd", grad_scores, queries, preferred_element_type=f32) * scaling
    )
    grad_qkv = jnp.stack([grad_queries, grad_keys, grad_values], axis=1).astype(bf16)
    grad_qkv = grad_qkv.reshape(rows, 3 * width)
    grad_qkv_weight = jnp.einsum("nd,ne->de", normed_in, grad_qkv, preferred_element_type=f32)
    grad_normed_in = jnp.einsum("ne,de->nd", grad_qkv, full_qkv, preferred_element_type=f32)
    grad_gain_first = jnp.sum(grad_normed_in * normal_first, axis=0)
    grad_bias_first = jnp.sum(grad_normed_in, axis=0)
    token_grad = grad_middle + norm_back(grad_normed_in, normal_first, rstd_first, gain_first)
    token_grad = token_grad.astype(bf16).reshape(1, rows, width)
    vectors = jnp.stack([grad_gain_first, grad_bias_first], axis=1)
    late = jnp.concatenate(
        [grad_qkv_weight, jnp.pad(vectors, ((0, 0), (0, 256 - vectors.shape[1])))], axis=1
    ).astype(bf16)
    late = sum_everywhere(late.reshape(2 * planes, depth, 3 * width + 256), planes)

    def both_cores(mine):
        mine = mine.astype(bf16)
        other = lax.ppermute(mine, "seq", core_swap)
        first, second = jnp.where(core == 0, mine, other), jnp.where(core == 0, other, mine)
        return jnp.concatenate([first, second], axis=0).astype(f32)

    bias_row = jnp.pad(
        inner_bias_grad.reshape(own, 1, slice_width), ((0, 0), (0, 15), (0, width - slice_width))
    )
    outer_grad = jnp.concatenate([outer_grad.reshape(own, slice_width, width), bias_row], axis=1)
    outer_grad = outer_grad.astype(bf16)
    outer_grad = outer_grad.astype(f32) + lax.ppermute(outer_grad, "seq", y_swap).astype(f32)
    outer_grad = both_cores(outer_grad)
    inner_grad = inner_grad.astype(bf16).reshape(2 * planes, depth, own, slice_width)
    inner_grad = jnp.take(inner_grad, order, axis=0).reshape(planes, 2, depth, own, slice_width)
    across = lax.ppermute(inner_grad[:, 1], "fsdp", x_swap(planes))
    pairs = jnp.stack([inner_grad[:, 0], across], axis=1)
    got = [pairs[0]] + [
        lax.ppermute(pairs[k], "fsdp", z_shift(planes, -k)) for k in range(1, planes)
    ]
    got = jnp.stack(got).reshape(2 * planes, depth, own, slice_width)
    inner_grad = jnp.take(got, up_order, axis=0).transpose(2, 1, 0, 3).reshape(own, depth, hidden)
    inner_grad = inner_grad.astype(f32) + lax.ppermute(inner_grad, "seq", y_swap).astype(f32)
    inner_grad = both_cores(inner_grad)
    return (
        mixed,
        token_grad,
        late[:, 3 * width],
        late[:, 3 * width + 1],
        late[:, : 3 * width],
        early[:, :width],
        early[:, width + 2],
        early[:, width],
        early[:, width + 1],
        early[:, width + 3 : width + 3 + experts],
        inner_grad,
        outer_grad[:, slice_width, :slice_width],
        outer_grad[:, :slice_width],
        early[:, width + 3 + experts : width + 3 + 2 * experts].T,
    )


def solution(mesh):
    n_seq, n_fsdp = mesh.shape["seq"], mesh.shape["fsdp"]

    def per_device(*args):
        tokens, w_in, w_out = args[0], args[12], args[14]
        experts, _, hidden = w_in.shape
        lanes = hidden // n_fsdp
        whole_tiles = lanes % 128 == 0 and w_in.shape[1] % 16 == 0
        if n_seq == 4 and experts == n_seq and tokens.shape[0] == 1 and whole_tiles:
            return move_tokens_plan(*args)
        return gather_weights_plan(*args)

    return jax.shard_map(
        per_device,
        mesh=mesh,
        in_specs=(
            P(("fsdp", "seq"), None, None),
            P("fsdp", None),
            P(("fsdp", "seq"), None, None),
            P(("fsdp", "seq"), None, None),
            P("fsdp"),
            P("fsdp"),
            P("fsdp", None),
            P("fsdp", None),
            P("fsdp"),
            P("fsdp"),
            P("fsdp"),
            P("fsdp", None),
            P(None, "fsdp", None),
            P(None, "fsdp"),
            P(None, "fsdp", None),
            P(None, "fsdp"),
        ),
        out_specs=(
            P(("fsdp", "seq"), None, None),
            P(("fsdp", "seq"), None, None),
            P("fsdp"),
            P("fsdp"),
            P("fsdp", None),
            P("fsdp", None),
            P("fsdp"),
            P("fsdp"),
            P("fsdp"),
            P("fsdp", None),
            P(None, "fsdp", None),
            P(None, "fsdp"),
            P(None, "fsdp", None),
            P(None, "fsdp"),
        ),
        check_vma=False,
    )
```

```python
import functools

import jax
import jax.numpy as jnp
from jax import lax
from jax.experimental import pallas as pl
from jax.experimental.pallas import tpu as pltpu
from jax.sharding import PartitionSpec as P

HEADS = 12
CAP = 142


epsilon = 1e-06
masked_score = -1e30


def norm_rows(values, gain, offset):
    center = values - jnp.mean(values, axis=-1, keepdims=True)
    spread = jnp.mean(center * center, axis=-1, keepdims=True)
    return center * lax.rsqrt(spread + epsilon) * gain + offset


def softmax_rows(values):
    shifted = jnp.exp(values - jnp.max(values, axis=-1, keepdims=True))
    return shifted / jnp.sum(shifted, axis=-1, keepdims=True)


def exact_gelu(values):
    return jax.nn.gelu(values, approximate=False)


def expert_slots(chosen, experts):
    flat_ids = chosen.reshape(-1)
    onehot = (flat_ids[:, None] == jnp.arange(experts, dtype=jnp.int32)[None, :]).astype(jnp.int32)
    ranks = jnp.cumsum(onehot, axis=0, dtype=jnp.int32)
    slot_pos = jnp.sum(onehot * ranks, axis=1, dtype=jnp.int32) - 1
    return (flat_ids, slot_pos)


def gather_weights_plan(
    tokens,
    key_mask,
    expert_ids,
    cotangent,
    norm1_gain,
    norm1_bias,
    w_qkv,
    w_proj,
    proj_bias,
    norm2_gain,
    norm2_bias,
    w_router,
    w_in,
    b_in,
    w_out,
    b_out,
):
    images, seq_len, width = tokens.shape
    experts = w_in.shape[0]
    head_dim = width // HEADS
    scaling = head_dim ** (-0.5)
    row_count = images * seq_len
    dense_set = (
        lax.all_gather(norm1_gain, "fsdp", axis=0, tiled=True),
        lax.all_gather(norm1_bias, "fsdp", axis=0, tiled=True),
        lax.all_gather(w_qkv, "fsdp", axis=0, tiled=True),
        lax.all_gather(w_proj, "fsdp", axis=0, tiled=True),
        lax.all_gather(proj_bias, "fsdp", axis=0, tiled=True),
        lax.all_gather(norm2_gain, "fsdp", axis=0, tiled=True),
        lax.all_gather(norm2_bias, "fsdp", axis=0, tiled=True),
        lax.all_gather(w_router, "fsdp", axis=0, tiled=True),
    )
    gain_first = dense_set[0].astype(jnp.float32)
    bias_first = dense_set[1].astype(jnp.float32)
    full_qkv = dense_set[2]
    full_proj = dense_set[3]
    bias_proj = dense_set[4].astype(jnp.float32)
    gain_second = dense_set[5].astype(jnp.float32)
    bias_second = dense_set[6].astype(jnp.float32)
    full_router = dense_set[7]
    expert_set = (
        lax.all_gather(w_in, "fsdp", axis=1, tiled=True),
        lax.all_gather(b_in, "fsdp", axis=1, tiled=True),
        lax.all_gather(w_out, "fsdp", axis=1, tiled=True),
        lax.all_gather(b_out, "fsdp", axis=1, tiled=True),
    )
    inner_weight = expert_set[0]
    inner_bias = expert_set[1].astype(jnp.float32)
    outer_weight = expert_set[2]
    outer_bias = expert_set[3].astype(jnp.float32)
    own_mask = lax.dynamic_slice_in_dim(key_mask, lax.axis_index("seq") * images, images, 0)
    keep_rows = own_mask.reshape(row_count, 1).astype(jnp.float32)
    usable = (key_mask > 0)[:, None, None, :]
    flat_tokens = tokens.astype(jnp.float32).reshape(row_count, width)
    normed_in = norm_rows(flat_tokens, gain_first, bias_first).astype(jnp.bfloat16)
    mixed_qkv = jnp.dot(normed_in, full_qkv, preferred_element_type=jnp.float32).astype(
        jnp.bfloat16
    )
    mixed_qkv = mixed_qkv.reshape(images, seq_len, 3, HEADS, head_dim)
    head_qkv = lax.all_to_all(mixed_qkv, "seq", split_axis=3, concat_axis=0, tiled=True)
    queries = head_qkv[:, :, 0]
    key_rows = head_qkv[:, :, 1]
    value_rows = head_qkv[:, :, 2]

    def score_block():
        raw = (
            jnp.einsum("gahd,gbhd->ghab", queries, key_rows, preferred_element_type=jnp.float32)
            * scaling
        )
        return jnp.where(usable, raw, masked_score)

    scores = score_block()
    row_top = jnp.max(scores, axis=-1, keepdims=True)
    shifted = jnp.exp(scores - row_top)
    row_total = jnp.sum(shifted, axis=-1, keepdims=True)
    attn_probs = (shifted / row_total).astype(jnp.bfloat16)
    log_total = row_top + jnp.log(row_total)
    head_out = jnp.einsum(
        "ghab,gbhd->gahd", attn_probs, value_rows, preferred_element_type=jnp.float32
    ).astype(jnp.bfloat16)
    attended = lax.all_to_all(head_out, "seq", split_axis=0, concat_axis=2, tiled=True).reshape(
        row_count, width
    )
    middle = (
        flat_tokens + jnp.dot(attended, full_proj, preferred_element_type=jnp.float32) + bias_proj
    )
    normed_mid = norm_rows(middle, gain_second, bias_second).astype(jnp.bfloat16)
    routing = softmax_rows(jnp.dot(normed_mid, full_router, preferred_element_type=jnp.float32))
    chosen = expert_ids.reshape(row_count, 2)
    flat_ids, slot_pos = expert_slots(chosen, experts)
    gating = jnp.take_along_axis(routing, chosen, axis=1)
    buffer = (
        jnp.zeros((experts, CAP, width), jnp.bfloat16)
        .at[flat_ids, slot_pos]
        .set(jnp.repeat(normed_mid, 2, axis=0))
    )
    pre_act = (
        jnp.einsum("ecd,edf->ecf", buffer, inner_weight, preferred_element_type=jnp.float32)
        + inner_bias[:, None, :]
    )
    activated = exact_gelu(pre_act).astype(jnp.bfloat16)
    expert_out = (
        jnp.einsum("ecf,efd->ecd", activated, outer_weight, preferred_element_type=jnp.float32)
        + outer_bias[:, None, :]
    )
    picked = expert_out[flat_ids, slot_pos].reshape(row_count, 2, width)
    mixture = jnp.sum(gating[:, :, None] * picked, axis=1)
    mixed = (keep_rows * (middle + mixture)).astype(jnp.bfloat16).reshape(images, seq_len, width)
    grad_out = cotangent.astype(jnp.float32).reshape(row_count, width) * keep_rows
    grad_gate = jnp.sum(grad_out[:, None, :] * picked, axis=2)
    grad_picked = (
        (gating[:, :, None] * grad_out[:, None, :])
        .astype(jnp.bfloat16)
        .reshape(2 * row_count, width)
    )
    grad_expert_out = (
        jnp.zeros((experts, CAP, width), jnp.bfloat16).at[flat_ids, slot_pos].set(grad_picked)
    )
    grad_outer_bias = jnp.sum(grad_expert_out, axis=1, dtype=jnp.float32)
    hidden_pre = (
        jnp.einsum("ecd,edf->ecf", buffer, inner_weight, preferred_element_type=jnp.float32)
        + inner_bias[:, None, :]
    )
    hidden_act = exact_gelu(hidden_pre).astype(jnp.bfloat16)
    grad_outer_weight = jnp.einsum(
        "ecf,ecd->efd", hidden_act, grad_expert_out, preferred_element_type=jnp.float32
    )
    grad_act = jnp.einsum(
        "ecd,efd->ecf", grad_expert_out, outer_weight, preferred_element_type=jnp.float32
    )
    gelu_pull = jax.vjp(exact_gelu, hidden_pre)[1]
    grad_pre = gelu_pull(grad_act)[0].astype(jnp.bfloat16)
    grad_inner_bias = jnp.sum(grad_pre, axis=1, dtype=jnp.float32)
    grad_inner_weight = jnp.einsum(
        "ecd,ecf->edf", buffer, grad_pre, preferred_element_type=jnp.float32
    )
    grad_buffer = jnp.einsum(
        "ecf,edf->ecd", grad_pre, inner_weight, preferred_element_type=jnp.float32
    )
    grad_rows = jnp.sum(grad_buffer[flat_ids, slot_pos].reshape(row_count, 2, width), axis=1)
    expert_range = jnp.arange(experts, dtype=jnp.int32)[None, None, :]
    grad_route = jnp.sum(
        grad_gate[:, :, None] * (chosen[:, :, None] == expert_range).astype(jnp.float32), axis=1
    )
    grad_logits = (
        routing * (grad_route - jnp.sum(routing * grad_route, axis=-1, keepdims=True))
    ).astype(jnp.bfloat16)
    grad_router = jnp.einsum(
        "nd,ne->de", normed_mid, grad_logits, preferred_element_type=jnp.float32
    )
    grad_normed_mid = grad_rows + jnp.einsum(
        "ne,de->nd", grad_logits, full_router, preferred_element_type=jnp.float32
    )
    second_pull = jax.vjp(norm_rows, middle, gain_second, bias_second)[1]
    grad_mid_norm, grad_gain_second, grad_bias_second = second_pull(grad_normed_mid)
    grad_middle = grad_out + grad_mid_norm
    grad_proj = grad_middle.astype(jnp.bfloat16)
    grad_bias_proj = jnp.sum(grad_proj, axis=0, dtype=jnp.float32)
    grad_proj_weight = jnp.einsum(
        "nd,ne->de", attended, grad_proj, preferred_element_type=jnp.float32
    )
    grad_attended = jnp.einsum(
        "ne,de->nd", grad_proj, full_proj, preferred_element_type=jnp.float32
    ).astype(jnp.bfloat16)
    grad_head_out = lax.all_to_all(
        grad_attended.reshape(images, seq_len, HEADS, head_dim),
        "seq",
        split_axis=2,
        concat_axis=0,
        tiled=True,
    )
    recomputed = jnp.exp(score_block() - log_total)
    grad_values = jnp.einsum(
        "ghab,gahd->gbhd",
        recomputed.astype(jnp.bfloat16),
        grad_head_out,
        preferred_element_type=jnp.float32,
    )
    grad_probs = jnp.einsum(
        "gahd,gbhd->ghab", grad_head_out, value_rows, preferred_element_type=jnp.float32
    )
    grad_scores = (
        recomputed * (grad_probs - jnp.sum(recomputed * grad_probs, axis=-1, keepdims=True))
    ).astype(jnp.bfloat16)
    grad_queries = (
        jnp.einsum("ghab,gbhd->gahd", grad_scores, key_rows, preferred_element_type=jnp.float32)
        * scaling
    )
    grad_keys = (
        jnp.einsum("ghab,gahd->gbhd", grad_scores, queries, preferred_element_type=jnp.float32)
        * scaling
    )
    grad_head_qkv = jnp.stack([grad_queries, grad_keys, grad_values], axis=2).astype(jnp.bfloat16)
    grad_qkv = lax.all_to_all(
        grad_head_qkv, "seq", split_axis=0, concat_axis=3, tiled=True
    ).reshape(row_count, 3 * width)
    grad_qkv_weight = jnp.einsum(
        "nd,ne->de", normed_in, grad_qkv, preferred_element_type=jnp.float32
    )
    grad_normed_in = jnp.einsum("ne,de->nd", grad_qkv, full_qkv, preferred_element_type=jnp.float32)
    first_pull = jax.vjp(norm_rows, flat_tokens, gain_first, bias_first)[1]
    grad_first, grad_gain_first, grad_bias_first = first_pull(grad_normed_in)
    token_grad = (grad_middle + grad_first).astype(jnp.bfloat16).reshape(images, seq_len, width)
    shares = (
        lax.psum_scatter(grad_gain_first, "fsdp", scatter_dimension=0, tiled=True),
        lax.psum_scatter(grad_bias_first, "fsdp", scatter_dimension=0, tiled=True),
        lax.psum_scatter(grad_qkv_weight, "fsdp", scatter_dimension=0, tiled=True),
        lax.psum_scatter(grad_proj_weight, "fsdp", scatter_dimension=0, tiled=True),
        lax.psum_scatter(grad_bias_proj, "fsdp", scatter_dimension=0, tiled=True),
        lax.psum_scatter(grad_gain_second, "fsdp", scatter_dimension=0, tiled=True),
        lax.psum_scatter(grad_bias_second, "fsdp", scatter_dimension=0, tiled=True),
        lax.psum_scatter(grad_router, "fsdp", scatter_dimension=0, tiled=True),
        lax.psum_scatter(grad_inner_weight, "fsdp", scatter_dimension=1, tiled=True),
        lax.psum_scatter(grad_inner_bias, "fsdp", scatter_dimension=1, tiled=True),
        lax.psum_scatter(grad_outer_weight, "fsdp", scatter_dimension=1, tiled=True),
        lax.psum_scatter(grad_outer_bias, "fsdp", scatter_dimension=1, tiled=True),
    )
    parted = (
        lax.psum_scatter(
            shares[0].astype(jnp.bfloat16), "seq", scatter_dimension=0, tiled=True
        ).astype(jnp.float32),
        lax.psum_scatter(
            shares[1].astype(jnp.bfloat16), "seq", scatter_dimension=0, tiled=True
        ).astype(jnp.float32),
        lax.psum_scatter(
            shares[2].astype(jnp.bfloat16), "seq", scatter_dimension=0, tiled=True
        ).astype(jnp.float32),
        lax.psum_scatter(
            shares[3].astype(jnp.bfloat16), "seq", scatter_dimension=0, tiled=True
        ).astype(jnp.float32),
        lax.psum_scatter(
            shares[4].astype(jnp.bfloat16), "seq", scatter_dimension=0, tiled=True
        ).astype(jnp.float32),
        lax.psum_scatter(
            shares[5].astype(jnp.bfloat16), "seq", scatter_dimension=0, tiled=True
        ).astype(jnp.float32),
        lax.psum_scatter(
            shares[6].astype(jnp.bfloat16), "seq", scatter_dimension=0, tiled=True
        ).astype(jnp.float32),
        lax.psum_scatter(
            shares[7].astype(jnp.bfloat16), "seq", scatter_dimension=0, tiled=True
        ).astype(jnp.float32),
        lax.psum_scatter(
            shares[8].astype(jnp.bfloat16), "seq", scatter_dimension=1, tiled=True
        ).astype(jnp.float32),
        lax.psum_scatter(
            shares[9].astype(jnp.bfloat16), "seq", scatter_dimension=1, tiled=True
        ).astype(jnp.float32),
        lax.psum_scatter(
            shares[10].astype(jnp.bfloat16), "seq", scatter_dimension=1, tiled=True
        ).astype(jnp.float32),
        lax.psum_scatter(
            shares[11].astype(jnp.bfloat16), "seq", scatter_dimension=1, tiled=True
        ).astype(jnp.float32),
    )
    totals = (
        lax.all_gather(parted[0].astype(jnp.bfloat16), "seq", axis=0, tiled=True).astype(
            jnp.float32
        ),
        lax.all_gather(parted[1].astype(jnp.bfloat16), "seq", axis=0, tiled=True).astype(
            jnp.float32
        ),
        lax.all_gather(parted[2].astype(jnp.bfloat16), "seq", axis=0, tiled=True).astype(
            jnp.float32
        ),
        lax.all_gather(parted[3].astype(jnp.bfloat16), "seq", axis=0, tiled=True).astype(
            jnp.float32
        ),
        lax.all_gather(parted[4].astype(jnp.bfloat16), "seq", axis=0, tiled=True).astype(
            jnp.float32
        ),
        lax.all_gather(parted[5].astype(jnp.bfloat16), "seq", axis=0, tiled=True).astype(
            jnp.float32
        ),
        lax.all_gather(parted[6].astype(jnp.bfloat16), "seq", axis=0, tiled=True).astype(
            jnp.float32
        ),
        lax.all_gather(parted[7].astype(jnp.bfloat16), "seq", axis=0, tiled=True).astype(
            jnp.float32
        ),
        lax.all_gather(parted[8].astype(jnp.bfloat16), "seq", axis=1, tiled=True).astype(
            jnp.float32
        ),
        lax.all_gather(parted[9].astype(jnp.bfloat16), "seq", axis=1, tiled=True).astype(
            jnp.float32
        ),
        lax.all_gather(parted[10].astype(jnp.bfloat16), "seq", axis=1, tiled=True).astype(
            jnp.float32
        ),
        lax.all_gather(parted[11].astype(jnp.bfloat16), "seq", axis=1, tiled=True).astype(
            jnp.float32
        ),
    )
    return (
        mixed,
        token_grad,
        totals[0],
        totals[1],
        totals[2],
        totals[3],
        totals[4],
        totals[5],
        totals[6],
        totals[7],
        totals[8],
        totals[9],
        totals[10],
        totals[11],
    )


MESH = pl.DeviceIdType.MESH
NT = (((1,), (1,)), ((), ()))
TN = (((0,), (0,)), ((), ()))


def dot(a, b):
    return jnp.dot(a, b, preferred_element_type=jnp.float32)


class Place:
    def __init__(self, planes):
        self.planes = planes
        s, f = lax.axis_index("seq"), lax.axis_index("fsdp")
        self.y, self.c, self.z, self.x = s // 2, s % 2, f // 2, f % 2

    def at(self, y, c, z, x):
        return (y * 2 + c, z * 2 + x)

    def other_core(self):
        return self.at(self.y, 1 - self.c, self.z, self.x)

    def other_x(self):
        return self.at(self.y, self.c, self.z, 1 - self.x)

    def other_y(self):
        return self.at(1 - self.y, self.c, self.z, self.x)

    def level(self, k):
        return self.at(self.y, self.c, lax.rem(self.z + k + self.planes, self.planes), self.x)


def greet(partners):
    barrier = pltpu.get_barrier_semaphore()
    for partner in partners:
        pl.semaphore_signal(barrier, inc=1, device_id=partner, device_id_type=MESH)
    pl.semaphore_wait(barrier, len(partners))


def expert_kernel(
    planes,
    own,
    rows,
    packed_ref,
    inner_ref,
    outer_ref,
    bias_ref,
    small_ref,
    mix_ref,
    out_ref,
    inner_grad_ref,
    outer_grad_ref,
    router_grad_ref,
    inner_t_ref,
    outer_t_ref,
    router_ref,
    router_t_ref,
    bias_grad_ref,
    tokens,
    part,
    from_core,
    from_x,
    from_z,
    hidden,
    hidden_grad,
    logit_grad,
    inner_acc,
    outer_acc,
    z_send,
    z_recv,
    x_send,
    x_recv,
    c_send,
    c_recv,
    sum_c_send,
    sum_c_recv,
    sum_x_send,
    sum_x_recv,
    sum_z_send,
    sum_z_recv,
):
    f32, bf16 = jnp.float32, jnp.bfloat16
    place = Place(planes)
    width = inner_ref.shape[0]
    lanes = inner_ref.shape[1] // own

    def remote(src, dst, send, recv, device):
        return pltpu.make_async_remote_copy(
            src_ref=src, dst_ref=dst, send_sem=send, recv_sem=recv, device_id=device, device_id_type=MESH
        )

    def slot(buffer, k, at, count=1):
        return buffer.at[k, pl.ds(at * rows, count * rows)]

    def z_copy(k):
        return remote(slot(tokens, 0, 0), slot(tokens, k, 0), z_send.at[k], z_recv.at[k], place.level(k))

    def x_copy(k):
        return remote(slot(tokens, k, 0), slot(tokens, k, 1), x_send.at[k], x_recv.at[k], place.other_x())

    def c_copy(k, r):
        return remote(
            slot(tokens, k, r), slot(tokens, k, 2 + r), c_send.at[k, r], c_recv.at[k, r], place.other_core()
        )

    def sum_c_copy(k):
        return remote(slot(part, k, 2, 2), from_core.at[k], sum_c_send.at[k], sum_c_recv.at[k], place.other_core())

    def sum_x_copy(k):
        return remote(slot(part, k, 1), from_x.at[k], sum_x_send.at[k], sum_x_recv.at[k], place.other_x())

    def sum_z_copy(k):
        return remote(slot(part, k, 0), from_z.at[k], sum_z_send.at[k], sum_z_recv.at[k], place.level(-k))

    greet([place.other_core(), place.other_x()] + [place.level(k) for k in range(1, planes)])
    tokens[0, 0:rows, :] = packed_ref[...]
    c_copy(0, 0).start()
    x_copy(0).start()
    for k in range(1, planes):
        z_copy(k).start()
    inner_t_ref[...] = jnp.transpose(inner_ref[...])
    outer_t_ref[...] = jnp.transpose(outer_ref[...])
    place_row = lax.broadcasted_iota(jnp.int32, (128, 128), 0)
    place_lane = lax.broadcasted_iota(jnp.int32, (128, 128), 1)
    take = (place_row == place_lane + 5) & (place_lane < 2 * own)
    router = dot(small_ref[...], take.astype(bf16))
    router_ref[...] = router.astype(bf16)
    router_t_ref[...] = jnp.transpose(router).astype(bf16)
    inner_acc[...] = jnp.zeros_like(inner_acc)
    outer_acc[...] = jnp.zeros_like(outer_acc)
    bias_grad_ref[...] = jnp.zeros_like(bias_grad_ref)
    router_grad_ref[...] = jnp.zeros_like(router_grad_ref)

    def tile(k, t):
        here = pl.ds(pl.multiple_of(t * rows, 16), rows)
        normed, grad_out = tokens[k, here, :width], tokens[k, here, width : 2 * width]
        select = tokens[k, here, 2 * width :].astype(f32)
        lane = lax.broadcasted_iota(jnp.int32, select.shape, 1)
        logits = dot(normed, router_ref[...])
        logits = jnp.where(lane < 2 * own, logits, -1e30)
        routing = jnp.exp(logits - jnp.max(logits, axis=1, keepdims=True))
        routing = routing / jnp.sum(routing, axis=1, keepdims=True)
        gates = routing * select
        gate_grads = jnp.zeros_like(gates)
        for i in range(own):
            mine = lane == place.c * own + i
            units = slice(i * lanes, (i + 1) * lanes)
            gate = jnp.sum(jnp.where(mine, gates, 0.0), axis=1, keepdims=True)
            pre = dot(normed, inner_ref[:, units]) + bias_ref[:, units]
            grad_act = dot(grad_out, outer_t_ref[:, units])
            cdf = 0.5 * (1.0 + lax.erf(pre * (0.5**0.5)))
            act = pre * cdf
            hidden[here, units] = (gate * act).astype(bf16)
            gate_grad = jnp.sum(act * grad_act, axis=1, keepdims=True)
            gate_grads = gate_grads + jnp.where(mine, gate_grad * select, 0.0)
            slope = cdf + pre * jnp.exp(-0.5 * pre * pre) * 0.3989422804014327
            grad_pre = gate * grad_act * slope
            bias_grad_ref[:, units] += jnp.sum(grad_pre, axis=0, keepdims=True)
            hidden_grad[here, units] = grad_pre.astype(bf16)
        grad_logits = routing * (gate_grads - jnp.sum(routing * gate_grads, axis=1, keepdims=True))
        logit_grad[here, :] = grad_logits.astype(bf16)
        mix_ref[k, here, :] = dot(hidden[here, :], outer_ref[...]).astype(bf16)
        row_grad = dot(hidden_grad[here, :], inner_t_ref[...])
        row_grad = row_grad + dot(logit_grad[here, :], router_t_ref[...])
        part[k, here, :] = row_grad.astype(bf16)

    def add_core(k):
        sum_c_copy(k).wait_recv()
        total = slot(part, k, 1)[...].astype(f32) + from_core[k, rows : 2 * rows, :].astype(f32)
        part[k, rows : 2 * rows, :] = total.astype(bf16)
        sum_x_copy(k).start()

    def add_x(k):
        sum_x_copy(k).wait_recv()
        total = part[k, 0:rows, :].astype(f32) + from_core[k, 0:rows, :].astype(f32)
        total = total + from_x[k].astype(f32)
        part[k, 0:rows, :] = total.astype(bf16)

        @pl.when(k > 0)
        def _():
            sum_z_copy(k).start()

    def step(k, carry):
        x_copy(k).wait_recv()
        c_copy(k, 1).start()

        @pl.when(k + 1 < planes)
        def _():
            z_copy(k + 1).wait_recv()
            c_copy(k + 1, 0).start()
            x_copy(k + 1).start()

        c_copy(k, 0).wait_recv()
        c_copy(k, 1).wait_recv()

        def one(t, carry):
            tile(k, t)
            return carry

        lax.fori_loop(0, 4, one, 0)
        sum_c_copy(k).start()

        @pl.when(k > 0)
        def _():
            add_core(k - 1)

        @pl.when(k > 1)
        def _():
            add_x(k - 2)

        def columns(j, carry):
            some = pl.ds(pl.multiple_of(j * 256, 256), 256)
            outer_acc[:, some] += lax.dot_general(
                hidden[...], tokens[k, :, pl.ds(pl.multiple_of(width + j * 256, 256), 256)], TN, preferred_element_type=f32
            )
            inner_acc[:, some] += lax.dot_general(
                tokens[k, :, :width], hidden_grad[:, some], TN, preferred_element_type=f32
            )
            return carry

        lax.fori_loop(0, width // 256, columns, 0)
        router_grad_ref[...] += lax.dot_general(tokens[k, :, :width], logit_grad[...], TN, preferred_element_type=f32)
        return carry

    lax.fori_loop(0, planes, step, 0)
    add_core(planes - 1)
    add_x(planes - 2)
    add_x(planes - 1)
    inner_grad_ref[...] = inner_acc[...].astype(bf16)
    units = outer_acc.shape[0]
    outer_grad_ref[0:units, :] = outer_acc[...].astype(bf16)
    outer_grad_ref[units : units + 16, :] = jnp.broadcast_to(bias_grad_ref[...], (16, width)).astype(bf16)
    total = part[0, 0:rows, :].astype(f32)
    for k in range(1, planes):
        sum_z_copy(k).wait_recv()
        total = total + from_z[k].astype(f32)
    out_ref[...] = total
    for k in range(planes):
        x_copy(k).wait_send()
        c_copy(k, 0).wait_send()
        c_copy(k, 1).wait_send()
        sum_c_copy(k).wait_send()
        sum_x_copy(k).wait_send()
        if k > 0:
            z_copy(k).wait_send()
            sum_z_copy(k).wait_send()


def experts_of_the_plane(planes, own, packed, inner, outer, bias, small):
    f32, bf16 = jnp.float32, jnp.bfloat16
    rows, wide = packed.shape
    chunk = 4 * rows
    width, units = inner.shape
    vmem = pl.BlockSpec(memory_space=pltpu.VMEM)
    dma = pltpu.SemaphoreType.DMA
    flops = 12 * planes * chunk * width * units
    return pl.pallas_call(
        functools.partial(expert_kernel, planes, own, rows),
        out_shape=[
            jax.ShapeDtypeStruct((planes, chunk, width), bf16),
            jax.ShapeDtypeStruct((rows, width), f32),
            jax.ShapeDtypeStruct((width, units), bf16),
            jax.ShapeDtypeStruct((units + 16, width), bf16),
            jax.ShapeDtypeStruct((width, 128), f32),
        ],
        in_specs=[vmem] * 5,
        out_specs=[vmem] * 5,
        scratch_shapes=[
            pltpu.VMEM((units, width), bf16),
            pltpu.VMEM((width, units), bf16),
            pltpu.VMEM((width, 128), bf16),
            pltpu.VMEM((128, width), bf16),
            pltpu.VMEM((1, units), f32),
            pltpu.VMEM((planes, chunk, wide), bf16),
            pltpu.VMEM((planes, chunk, width), bf16),
            pltpu.VMEM((planes, 2 * rows, width), bf16),
            pltpu.VMEM((planes, rows, width), bf16),
            pltpu.VMEM((planes, rows, width), bf16),
            pltpu.VMEM((chunk, units), bf16),
            pltpu.VMEM((chunk, units), bf16),
            pltpu.VMEM((chunk, 128), bf16),
            pltpu.VMEM((width, units), f32),
            pltpu.VMEM((units, width), f32),
        ]
        + [dma((planes,))] * 4
        + [dma((planes, 2))] * 2
        + [dma((planes,))] * 6,
        compiler_params=pltpu.CompilerParams(
            collective_id=1, has_side_effects=True, vmem_limit_bytes=60 * 2**20
        ),
        cost_estimate=pl.CostEstimate(flops=flops, bytes_accessed=40 * 2**20, transcendentals=0),
        name="experts_of_the_plane",
    )(packed, inner, outer, bias, small)


def front_kernel(
    planes,
    heads,
    real,
    tokens_ref,
    keys_ref,
    keep_ref,
    cotangent_ref,
    select_ref,
    small_ref,
    qkv_part_ref,
    proj_part_ref,
    inner_part_ref,
    small_all,
    w_qkv_all,
    w_proj_all,
    inner_all,
    normed_in_ref,
    qkv_ref,
    attended_ref,
    middle_ref,
    packed_ref,
    up_send,
    up_recv,
    down_send,
    down_recv,
    x_send,
    x_recv,
    c_send,
    c_recv,
    spread_send,
    spread_recv,
    own_sem,
    y_send,
    y_recv,
):
    f32, bf16 = jnp.float32, jnp.bfloat16
    place = Place(planes)
    rows, width = tokens_ref.shape
    depth = small_ref.shape[0]
    half = depth // 2
    lanes = inner_part_ref.shape[2] // (2 * planes)
    head_dim = width // heads
    y, c, z, x = place.y, place.c, place.z, place.x
    gathered = [small_all, w_qkv_all, w_proj_all]

    def remote(src, dst, send, recv, device):
        return pltpu.make_async_remote_copy(
            src_ref=src, dst_ref=dst, send_sem=send, recv_sem=recv, device_id=device, device_id_type=MESH
        )

    def piece(j, level, across):
        start = (level * 2 + across) * depth + c * half
        return gathered[j].at[pl.ds(pl.multiple_of(start, 16), half)]

    def up_copy(j, level):
        here = piece(j, level, x)
        return remote(here, here, up_send.at[j, level], up_recv.at[j, level], place.at(y, c, z + 1, x))

    def down_copy(j, level):
        here = piece(j, level, x)
        return remote(here, here, down_send.at[j, level], down_recv.at[j, level], place.at(y, c, z - 1, x))

    def x_copy(j, level, across):
        here = piece(j, level, across)
        return remote(here, here, x_send.at[j, level], x_recv.at[j, level], place.other_x())

    def c_copy(j, level, across):
        here = piece(j, level, across)
        at = level * 2 + across
        return remote(here, here, c_send.at[j, at], c_recv.at[j, at], place.other_core())

    def sibling_piece(j, level, across):
        start = (level * 2 + across) * depth + (1 - c) * half
        here = gathered[j].at[pl.ds(pl.multiple_of(start, 16), half)]
        at = level * 2 + across
        return remote(here, here, c_send.at[j, at], c_recv.at[j, at], place.other_core())

    def columns_of(f):
        return pl.ds(pl.multiple_of(f * lanes, 128), lanes)

    here_rows = pl.ds(pl.multiple_of((z * 2 + x) * depth, 16), depth)
    my_units = pl.ds(pl.multiple_of(y * lanes, 128), lanes)

    def spread_copy(k, r):
        level, across = lax.rem(z + k, planes), (x + r) % 2
        return remote(
            inner_part_ref.at[c * 2 + y, :, columns_of(level * 2 + across)],
            inner_all.at[here_rows, my_units],
            spread_send.at[k, r],
            spread_recv.at[k, r],
            place.at(y, c, level, across),
        )

    own_copy = pltpu.make_async_copy(
        inner_part_ref.at[c * 2 + y, :, columns_of(z * 2 + x)], inner_all.at[here_rows, my_units], own_sem
    )
    y_copy = remote(inner_all.at[:, my_units], inner_all.at[:, my_units], y_send, y_recv, place.other_y())
    their_units = pl.ds(pl.multiple_of((1 - y) * lanes, 128), lanes)
    from_y = remote(inner_all.at[:, their_units], inner_all.at[:, their_units], y_send, y_recv, place.other_y())

    others = [(k, r) for k in range(planes) for r in range(2) if k or r]
    partners = [place.other_core(), place.other_y()]
    partners += [place.at(y, c, lax.rem(z + k, planes), (x + r) % 2) for k, r in others]
    greet(partners)

    small_all[here_rows, :] = small_ref[...]
    w_qkv_all[here_rows, :] = qkv_part_ref[...]
    w_proj_all[here_rows, :] = proj_part_ref[...]

    def forward(level, flows):
        for j in flows:
            x_copy(j, level, x).start()

    def line(flows):
        @pl.when(z < planes - 1)
        def _():
            for j in flows:
                up_copy(j, z).start()

        @pl.when(z > 0)
        def _():
            for j in flows:
                down_copy(j, z).start()

        forward(z, flows)

    def hops(flows):
        for h in range(1, planes):
            @pl.when(z >= h)
            def _():
                for j in flows:
                    up_copy(j, z - h).wait_recv()

                @pl.when(z < planes - 1)
                def _():
                    for j in flows:
                        up_copy(j, z - h).start()

                forward(z - h, flows)
                for j in flows:
                    c_copy(j, z - h, x).start()

            @pl.when(z + h < planes)
            def _():
                for j in flows:
                    down_copy(j, z + h).wait_recv()

                @pl.when(z > 0)
                def _():
                    for j in flows:
                        down_copy(j, z + h).start()

                forward(z + h, flows)
                for j in flows:
                    c_copy(j, z + h, x).start()

    def arrive(flows):
        for level in range(planes):
            for j in flows:
                x_copy(j, level, 1 - x).wait_recv()
                c_copy(j, level, 1 - x).start()

    def gather_done(flows):
        for level in range(planes):
            for j in flows:
                sibling_piece(j, level, 1 - x).wait_recv()

            @pl.when(level != z)
            def _():
                for j in flows:
                    sibling_piece(j, level, x).wait_recv()

    line([0, 1])
    line([2])
    values = tokens_ref[...].astype(f32)
    normal, _ = norm_parts(values)
    hops([0, 1])
    hops([2])
    own_copy.start()
    for k, r in others:
        spread_copy(k, r).start()
    arrive([0, 1])
    gather_done([0, 1])
    vectors = jnp.transpose(small_all[...].astype(f32))
    normed_in = (normal * vectors[0:1] + vectors[1:2]).astype(bf16)
    normed_in_ref[...] = normed_in
    for j in range(3):
        part = slice(j * width, (j + 1) * width)
        qkv_ref[:, part] = dot(normed_in, w_qkv_all[:, part]).astype(bf16)
    arrive([2])
    lane = lax.broadcasted_iota(jnp.int32, (rows, 2 * head_dim), 1)
    usable = keys_ref[...] > 0
    for pair in range(heads // 2):
        at = pair * 2 * head_dim
        queries = qkv_ref[:, at : at + 2 * head_dim]
        keys = qkv_ref[:, width + at : width + at + 2 * head_dim]
        held = qkv_ref[:, 2 * width + at : 2 * width + at + 2 * head_dim]
        outs = []
        for side in range(2):
            only = (lane < head_dim) if side == 0 else (lane >= head_dim)
            scores = lax.dot_general(
                jnp.where(only, queries, 0).astype(bf16), keys, NT, preferred_element_type=f32
            )
            scores = jnp.where(usable, scores * head_dim ** (-0.5), masked_score)
            shifted = jnp.exp(scores - jnp.max(scores, axis=1, keepdims=True))
            probs = (shifted / jnp.sum(shifted, axis=1, keepdims=True)).astype(bf16)
            outs.append(dot(probs, held))
        attended_ref[:, at : at + 2 * head_dim] = jnp.where(lane < head_dim, outs[0], outs[1]).astype(bf16)
    own_copy.wait()
    for k, r in others:
        spread_copy(k, r).wait_recv()
    y_copy.start()
    gather_done([2])
    middle = values + dot(attended_ref[...], w_proj_all[...]) + vectors[2:3]
    middle_ref[...] = middle
    normal_mid, _ = norm_parts(middle)
    normed = normal_mid * vectors[3:4] + vectors[4:5]
    row = lax.broadcasted_iota(jnp.int32, normed.shape, 0)
    packed_ref[:, :width] = jnp.where(row < real, normed, 0.0).astype(bf16)
    packed_ref[:, width : 2 * width] = (cotangent_ref[...].astype(f32) * keep_ref[...]).astype(bf16)
    packed_ref[:, 2 * width :] = select_ref[...]
    from_y.wait_recv()
    y_copy.wait_send()
    for k, r in others:
        spread_copy(k, r).wait_send()
    for j in range(3):
        for level in range(planes):
            x_copy(j, level, x).wait_send()
            c_copy(j, level, 1 - x).wait_send()

            @pl.when(level != z)
            def _():
                c_copy(j, level, x).wait_send()

            @pl.when((z >= level) & (z < planes - 1))
            def _():
                up_copy(j, level).wait_send()

            @pl.when((z <= level) & (z > 0))
            def _():
                down_copy(j, level).wait_send()


def front(planes, real, tokens, keys, keep, cotangent, select, small, w_qkv, w_proj, w_in):
    f32, bf16 = jnp.float32, jnp.bfloat16
    rows, width = tokens.shape
    lanes = w_in.shape[2] // (2 * planes)
    shape = jax.ShapeDtypeStruct
    vmem = pl.BlockSpec(memory_space=pltpu.VMEM)
    dma = pltpu.SemaphoreType.DMA
    return pl.pallas_call(
        functools.partial(front_kernel, planes, HEADS, real),
        out_shape=[
            shape((width, small.shape[1]), bf16),
            shape((width, 3 * width), bf16),
            shape((width, width), bf16),
            shape((width, 2 * lanes), bf16),
            shape((rows, width), bf16),
            shape((rows, 3 * width), bf16),
            shape((rows, width), bf16),
            shape((rows, width), f32),
            shape((rows, 2 * width + 128), bf16),
        ],
        in_specs=[vmem] * 8 + [pl.BlockSpec(memory_space=pl.ANY)],
        out_specs=[vmem] * 9,
        scratch_shapes=[dma((3, planes))] * 6
        + [dma((3, 2 * planes))] * 2
        + [dma((planes, 2))] * 2
        + [dma] * 3,
        compiler_params=pltpu.CompilerParams(
            collective_id=2, has_side_effects=True, vmem_limit_bytes=60 * 2**20
        ),
        cost_estimate=pl.CostEstimate(flops=2**32, bytes_accessed=40 * 2**20, transcendentals=0),
        name="dense_weights_and_attention",
    )(tokens, keys, keep, cotangent, select, small, w_qkv, w_proj, w_in)


def back_kernel(planes, heads, own, groups, real, *refs):
    (
        row_grad_ref,
        packed_ref,
        middle_ref,
        tokens_ref,
        normed_in_ref,
        qkv_ref,
        attended_ref,
        small_ref,
        w_qkv_ref,
        w_proj_ref,
        keys_ref,
        keep_ref,
        mix_ref,
        inner_ref,
        outer_ref,
        router_grad_ref,
    ) = refs[:16]
    mixed_ref, token_grad_ref, qkv_out, proj_out, small_out, inner_out, outer_out = refs[16:23]
    (
        grad_attended,
        grad_qkv,
        mix_x,
        mix_z,
        mix_from_core,
        mix_from_x,
        mix_from_z,
        inner_from_y,
        inner_sum,
        outer_from_y,
        held,
        held_small,
        from_core,
        from_core_small,
        from_x,
        from_x_small,
        from_z,
        from_z_small,
        plane_sum,
        plane_sum_small,
        from_y,
        from_y_small,
        final,
        final_small,
    ) = refs[23:47]
    (
        mix_c_sem,
        mix_x_sem,
        mix_z_send,
        mix_z_recv,
        inner_y_sem,
        spread_send,
        spread_recv,
        inner_back_sem,
        inner_core_sem,
        outer_y_sem,
        outer_c_sem,
        own_sem,
        flow_c_sem,
        flow_x_sem,
        flow_z_send,
        flow_z_recv,
        flow_y_sem,
        flow_end_sem,
    ) = refs[47:]
    f32, bf16 = jnp.float32, jnp.bfloat16
    place = Place(planes)
    y, c, z, x = place.y, place.c, place.z, place.x
    rows, width = middle_ref.shape
    depth = width // (2 * planes)
    half = depth // 2
    lanes = inner_ref.shape[1] // own
    head_dim = width // heads
    pair_width = 2 * head_dim
    small_at = groups + 1

    def remote(src, dst, send, recv, device):
        return pltpu.make_async_remote_copy(
            src_ref=src, dst_ref=dst, send_sem=send, recv_sem=recv, device_id=device, device_id_type=MESH
        )

    def swap(src, dst, sem, device):
        return remote(src, dst, sem.at[0], sem.at[1], device)

    def of_flow(j, many, alone):
        return alone if j == small_at else many.at[j]

    mine, theirs = pl.ds(pl.multiple_of(c * half, 16), half), pl.ds(pl.multiple_of((1 - c) * half, 16), half)

    def flow_c(j):
        source = of_flow(j, held, held_small)
        return swap(
            source.at[:, :, theirs], of_flow(j, from_core, from_core_small), flow_c_sem.at[j], place.other_core()
        )

    def flow_x(j):
        source = of_flow(j, held, held_small)
        return swap(source.at[:, 1 - x, mine], of_flow(j, from_x, from_x_small), flow_x_sem.at[j], place.other_x())

    def flow_z(j, k):
        level = lax.rem(z + k, planes)
        source = of_flow(j, held, held_small)
        return remote(
            source.at[level, x, mine],
            of_flow(j, from_z, from_z_small).at[k],
            flow_z_send.at[j, k],
            flow_z_recv.at[j, k],
            place.level(k),
        )

    def flow_y(j):
        return swap(
            of_flow(j, plane_sum, plane_sum_small),
            of_flow(j, from_y, from_y_small),
            flow_y_sem.at[j],
            place.other_y(),
        )

    def flow_end(j):
        here = of_flow(j, final, final_small).at[mine]
        return swap(here, here, flow_end_sem.at[j], place.other_core())

    def flow_core_sum(j):
        flow_c(j).wait_recv()
        kept = of_flow(j, held, held_small)
        total = kept[:, :, mine, :].astype(f32) + of_flow(j, from_core, from_core_small)[...].astype(f32)
        kept[:, :, mine, :] = total.astype(bf16)
        flow_x(j).start()

    def flow_x_sum(j):
        flow_x(j).wait_recv()
        kept = of_flow(j, held, held_small)
        total = kept[:, x, mine, :].astype(f32) + of_flow(j, from_x, from_x_small)[...].astype(f32)
        kept[:, x, mine, :] = total.astype(bf16)
        for k in range(1, planes):
            flow_z(j, k).start()

    def flow_z_sum(j):
        kept = of_flow(j, held, held_small)
        total = kept[z, x, mine, :].astype(f32)
        for k in range(1, planes):
            flow_z(j, k).wait_recv()
            total = total + of_flow(j, from_z, from_z_small)[k].astype(f32)
        of_flow(j, plane_sum, plane_sum_small)[...] = total.astype(bf16)
        flow_y(j).start()

    def flow_y_sum(j):
        flow_y(j).wait_recv()
        total = of_flow(j, plane_sum, plane_sum_small)[...].astype(f32)
        total = total + of_flow(j, from_y, from_y_small)[...].astype(f32)
        of_flow(j, final, final_small)[mine, :] = total.astype(bf16)
        flow_end(j).start()

    def mix_c():
        return swap(mix_ref.at[:, pl.ds(2 * rows, 2 * rows)], mix_from_core, mix_c_sem, place.other_core())

    def mix_to_x():
        return swap(mix_x, mix_from_x, mix_x_sem, place.other_x())

    def mix_to_z(k):
        return remote(mix_z.at[k], mix_from_z.at[k], mix_z_send.at[k], mix_z_recv.at[k], place.level(-k))

    def mix_core_sum():
        mix_c().wait_recv()
        for k in range(planes):
            total = mix_ref[k, rows : 2 * rows, :].astype(f32) + mix_from_core[k, rows:, :].astype(f32)
            mix_x[k] = total.astype(bf16)
        mix_to_x().start()
        for k in range(planes):
            total = mix_ref[k, :rows, :].astype(f32) + mix_from_core[k, :rows, :].astype(f32)
            mix_z[k] = total.astype(bf16)

    def mix_x_sum():
        mix_to_x().wait_recv()
        for k in range(planes):
            mix_z[k] = (mix_z[k].astype(f32) + mix_from_x[k].astype(f32)).astype(bf16)
            if k:
                mix_to_z(k).start()

    my_units = pl.ds(pl.multiple_of(y * lanes, 128), lanes)
    their_units = pl.ds(pl.multiple_of((1 - y) * lanes, 128), lanes)
    my_expert, their_expert = c * 2 + y, c * 2 + 1 - y
    my_columns = pl.ds(pl.multiple_of((z * 2 + x) * lanes, 128), lanes)

    def inner_y():
        return swap(inner_ref.at[:, their_units], inner_from_y, inner_y_sem, place.other_y())

    def shard_rows(f):
        return pl.ds(pl.multiple_of(f * depth, 16), depth)

    def spread(k, r):
        level, across = lax.rem(z + k, planes), (x + r) % 2
        return remote(
            inner_sum.at[shard_rows(level * 2 + across)],
            inner_out.at[my_expert, :, my_columns],
            spread_send.at[k, r],
            spread_recv.at[k, r],
            place.at(y, c, level, across),
        )

    own_copy = pltpu.make_async_copy(
        inner_sum.at[shard_rows(z * 2 + x)], inner_out.at[my_expert, :, my_columns], own_sem
    )

    def inner_back():
        here = inner_out.at[my_expert]
        return swap(here, here, inner_back_sem, place.other_y())

    def inner_core(expert, at):
        here = inner_out.at[expert]
        return swap(here, here, inner_core_sem.at[at], place.other_core())

    def outer_y():
        return swap(outer_ref, outer_from_y, outer_y_sem, place.other_y())

    def outer_c():
        here = outer_out.at[c]
        return swap(here, here, outer_c_sem, place.other_core())

    others = [(k, r) for k in range(planes) for r in range(2) if k or r]

    def inner_y_sum():
        inner_y().wait_recv()
        total = inner_ref[:, my_units].astype(f32) + inner_from_y[...].astype(f32)
        inner_sum[...] = total.astype(bf16)
        own_copy.start()
        for k, r in others:
            spread(k, r).start()
        outer_y().start()

    def inner_spread_done():
        own_copy.wait()
        for k, r in others:
            spread(k, r).wait_recv()
        inner_back().start()
        inner_core(my_expert, 0).start()

    def outer_y_sum():
        outer_y().wait_recv()
        total = outer_ref[...].astype(f32) + outer_from_y[...].astype(f32)
        outer_out[c] = total.astype(bf16)
        outer_c().start()

    partners = [place.other_core(), place.other_y()]
    partners += [place.at(y, c, lax.rem(z + k, planes), (x + r) % 2) for k, r in others]
    greet(partners)
    inner_y().start()
    mix_c().start()

    vectors = jnp.transpose(small_ref[...].astype(f32))
    gain_first, gain_second = vectors[0:1], vectors[3:4]
    place_row = lax.broadcasted_iota(jnp.int32, (128, 128), 0)
    place_lane = lax.broadcasted_iota(jnp.int32, (128, 128), 1)

    def lanes_from(first):
        take = (place_row == place_lane + first) & (place_lane < 2 * own)
        return dot(small_ref[...], take.astype(bf16)).astype(bf16)

    router, outer_bias = lanes_from(5), lanes_from(5 + 2 * own)
    normed_mid, grad_out = packed_ref[:, :width], packed_ref[:, width : 2 * width]
    select = packed_ref[:, 2 * width :].astype(f32)
    lane = lax.broadcasted_iota(jnp.int32, select.shape, 1)
    logits = jnp.where(lane < 2 * own, dot(normed_mid, router), -1e30)
    routing = jnp.exp(logits - jnp.max(logits, axis=1, keepdims=True))
    routing = routing / jnp.sum(routing, axis=1, keepdims=True)
    gates = routing * select
    bias_gate = select * dot(grad_out, outer_bias)
    bias_logits = routing * (bias_gate - jnp.sum(routing * bias_gate, axis=1, keepdims=True))
    bias_logits = bias_logits.astype(bf16)
    router_grad = router_grad_ref[...] + lax.dot_general(
        normed_mid, bias_logits, TN, preferred_element_type=f32
    )
    outer_bias_grad = lax.dot_general(gates.astype(bf16), grad_out, TN, preferred_element_type=f32)
    grad_normed_mid = row_grad_ref[...] + lax.dot_general(bias_logits, router, NT, preferred_element_type=f32)
    normal_mid, rstd_mid = norm_parts(middle_ref[...])
    gain_second_grad = jnp.sum(grad_normed_mid * normal_mid, axis=0, keepdims=True)
    bias_second_grad = jnp.sum(grad_normed_mid, axis=0, keepdims=True)
    grad_middle = grad_out.astype(f32) + norm_back(grad_normed_mid, normal_mid, rstd_mid, gain_second)
    grad_proj = grad_middle.astype(bf16)
    proj_bias_grad = jnp.sum(grad_proj.astype(f32), axis=0, keepdims=True)
    mix_core_sum()

    def hold(j, value):
        held[j] = value.astype(bf16).reshape(planes, 2, depth, width)
        flow_c(j).start()

    hold(0, lax.dot_general(attended_ref[...], grad_proj, TN, preferred_element_type=f32))
    grad_attended[...] = lax.dot_general(grad_proj, w_proj_ref[...], NT, preferred_element_type=f32).astype(bf16)
    flow_core_sum(0)

    pair_lane = lax.broadcasted_iota(jnp.int32, (rows, pair_width), 1)
    usable = keys_ref[...] > 0
    scaling = head_dim ** (-0.5)
    group_width = width // groups

    def pair_back(pair):
        at = pair * pair_width
        group, inside = at // group_width, at % group_width
        queries = qkv_ref[:, at : at + pair_width]
        keys = qkv_ref[:, width + at : width + at + pair_width]
        values = qkv_ref[:, 2 * width + at : 2 * width + at + pair_width]
        grads = grad_attended[:, at : at + pair_width]
        found = []
        for side in range(2):
            only = (pair_lane < head_dim) if side == 0 else (pair_lane >= head_dim)
            some_queries = jnp.where(only, queries, 0).astype(bf16)
            some_grads = jnp.where(only, grads, 0).astype(bf16)
            scores = lax.dot_general(some_queries, keys, NT, preferred_element_type=f32)
            scores = jnp.where(usable, scores * scaling, masked_score)
            shifted = jnp.exp(scores - jnp.max(scores, axis=1, keepdims=True))
            probs = shifted / jnp.sum(shifted, axis=1, keepdims=True)
            grad_probs = lax.dot_general(some_grads, values, NT, preferred_element_type=f32)
            grad_scores = probs * (grad_probs - jnp.sum(probs * grad_probs, axis=1, keepdims=True))
            grad_scores = grad_scores.astype(bf16)
            found.append(
                (
                    dot(grad_scores, keys),
                    lax.dot_general(grad_scores, some_queries, TN, preferred_element_type=f32),
                    lax.dot_general(probs.astype(bf16), some_grads, TN, preferred_element_type=f32),
                )
            )
        grad_queries = jnp.where(pair_lane < head_dim, found[0][0], found[1][0]) * scaling
        grad_keys = (found[0][1] + found[1][1]) * scaling
        grad_values = found[0][2] + found[1][2]
        for part, value in enumerate((grad_queries, grad_keys, grad_values)):
            start = part * group_width + inside
            grad_qkv[group, :, start : start + pair_width] = value.astype(bf16)

    def group_back(group):
        per_group = heads // 2 // groups
        for pair in range(group * per_group, (group + 1) * per_group):
            pair_back(pair)
        hold(
            1 + group,
            lax.dot_general(normed_in_ref[...], grad_qkv[group], TN, preferred_element_type=f32),
        )

    group_back(0)
    inner_y_sum()
    flow_core_sum(1)
    for group in range(1, groups):
        group_back(group)
        if group == 1:
            mix_x_sum()
            flow_x_sum(0)
        flow_core_sum(1 + group)
    flow_x_sum(1)

    grad_normed_in = jnp.zeros((rows, width), f32)
    for group in range(groups):
        for part in range(3):
            grad_normed_in = grad_normed_in + lax.dot_general(
                grad_qkv[group, :, part * group_width : (part + 1) * group_width],
                w_qkv_ref[:, part * width + group * group_width : part * width + (group + 1) * group_width],
                NT,
                preferred_element_type=f32,
            )
    normal_first, rstd_first = norm_parts(tokens_ref[...].astype(f32))
    gain_first_grad = jnp.sum(grad_normed_in * normal_first, axis=0, keepdims=True)
    bias_first_grad = jnp.sum(grad_normed_in, axis=0, keepdims=True)
    token_grad = grad_middle + norm_back(grad_normed_in, normal_first, rstd_first, gain_first)
    token_grad_ref[...] = token_grad.astype(bf16)[:real]
    vector_rows = jnp.concatenate(
        [
            gain_first_grad,
            bias_first_grad,
            proj_bias_grad,
            gain_second_grad,
            bias_second_grad,
            jnp.zeros((3, width), f32),
            outer_bias_grad[:8],
            jnp.zeros((112, width), f32),
        ],
        axis=0,
    )
    vector_grads = jnp.transpose(vector_rows) + pltpu.roll(router_grad, 16, 1)
    held_small[...] = vector_grads.astype(bf16).reshape(planes, 2, depth, 128)
    flow_c(small_at).start()
    inner_spread_done()
    flow_core_sum(small_at)
    outer_y_sum()
    for group in range(1, groups):
        flow_x_sum(1 + group)
    flow_z_sum(0)
    flow_x_sum(small_at)
    mixture = mix_z[0].astype(f32) + dot(gates.astype(bf16), jnp.transpose(outer_bias.astype(f32)).astype(bf16))
    for k in range(1, planes):
        mix_to_z(k).wait_recv()
        mixture = mixture + mix_from_z[k].astype(f32)
    mixed = (keep_ref[...] * (middle_ref[...] + mixture)).astype(bf16)
    mixed_ref[...] = mixed[:real]
    flow_y_sum(0)
    for group in range(groups):
        flow_z_sum(1 + group)
    flow_z_sum(small_at)
    inner_back().wait_recv()
    inner_core(their_expert, 1).start()
    for group in range(groups):
        flow_y_sum(1 + group)
    flow_y_sum(small_at)

    def arrived(j):
        here = of_flow(j, final, final_small).at[theirs]
        swap(here, here, flow_end_sem.at[j], place.other_core()).wait_recv()

    arrived(0)
    proj_out[...] = final[0]
    for group in range(groups):
        arrived(1 + group)
        for part in range(3):
            start = part * width + group * group_width
            qkv_out[:, start : start + group_width] = final[
                1 + group, :, part * group_width : (part + 1) * group_width
            ]
    arrived(small_at)
    small_out[...] = final_small[...].astype(f32)
    outer_theirs = outer_out.at[1 - c]
    swap(outer_theirs, outer_theirs, outer_c_sem, place.other_core()).wait_recv()
    for at, expert in enumerate(((1 - c) * 2 + y, (1 - c) * 2 + 1 - y)):
        inner_core(expert, at).wait_recv()

    mix_c().wait_send()
    mix_to_x().wait_send()
    inner_y().wait_send()
    inner_back().wait_send()
    inner_core(my_expert, 0).wait_send()
    inner_core(their_expert, 1).wait_send()
    outer_y().wait_send()
    outer_c().wait_send()
    for k, r in others:
        spread(k, r).wait_send()
    for k in range(1, planes):
        mix_to_z(k).wait_send()
    for j in range(groups + 2):
        flow_c(j).wait_send()
        flow_x(j).wait_send()
        for k in range(1, planes):
            flow_z(j, k).wait_send()
        flow_y(j).wait_send()
        flow_end(j).wait_send()


def back(planes, own, real, *args):
    f32, bf16 = jnp.float32, jnp.bfloat16
    (
        row_grad,
        packed,
        middle,
        tokens,
        normed_in,
        qkv,
        attended,
        small,
        w_qkv,
        w_proj,
        keys,
        keep,
        mix_parts,
        inner_grad,
        outer_grad,
        router_grad,
    ) = args
    rows, width = middle.shape
    depth = width // (2 * planes)
    half = depth // 2
    lanes = inner_grad.shape[1] // own
    tall = outer_grad.shape[0]
    pairs = HEADS // 2
    groups = 3 if pairs % 3 == 0 and (pairs // 3) * 2 * (width // HEADS) % 128 == 0 else 1
    flows = groups + 1
    shape = jax.ShapeDtypeStruct
    vmem = pl.BlockSpec(memory_space=pltpu.VMEM)
    dma = pltpu.SemaphoreType.DMA

    def both(*dims):
        return [pltpu.VMEM((flows, *dims, width), bf16), pltpu.VMEM((*dims, 128), bf16)]

    return pl.pallas_call(
        functools.partial(back_kernel, planes, HEADS, own, groups, real),
        out_shape=[
            shape((real, width), bf16),
            shape((real, width), bf16),
            shape((depth, 3 * width), bf16),
            shape((depth, width), bf16),
            shape((depth, 128), f32),
            shape((2 * own, depth, 2 * planes * lanes), bf16),
            shape((2, tall, width), bf16),
        ],
        in_specs=[vmem] * 16,
        out_specs=[vmem] * 7,
        scratch_shapes=[
            pltpu.VMEM((rows, width), bf16),
            pltpu.VMEM((groups, rows, 3 * width // groups), bf16),
            pltpu.VMEM((planes, rows, width), bf16),
            pltpu.VMEM((planes, rows, width), bf16),
            pltpu.VMEM((planes, 2 * rows, width), bf16),
            pltpu.VMEM((planes, rows, width), bf16),
            pltpu.VMEM((planes, rows, width), bf16),
            pltpu.VMEM((width, lanes), bf16),
            pltpu.VMEM((width, lanes), bf16),
            pltpu.VMEM((tall, width), bf16),
        ]
        + both(planes, 2, depth)
        + both(planes, 2, half)
        + both(planes, half)
        + both(planes, half)
        + both(half)
        + both(half)
        + both(depth)
        + [dma((2,))] * 2
        + [dma((planes,))] * 2
        + [dma((2,))]
        + [dma((planes, 2))] * 2
        + [dma((2,)), dma((2, 2)), dma((2,)), dma((2,)), dma]
        + [dma((flows + 1, 2))] * 2
        + [dma((flows + 1, planes))] * 2
        + [dma((flows + 1, 2))] * 2,
        compiler_params=pltpu.CompilerParams(
            collective_id=3, has_side_effects=True, vmem_limit_bytes=60 * 2**20
        ),
        cost_estimate=pl.CostEstimate(flops=2**33, bytes_accessed=40 * 2**20, transcendentals=0),
        name="attention_backward_and_sums",
    )(*args)


def norm_parts(values):
    center = values - jnp.mean(values, axis=-1, keepdims=True)
    rstd = lax.rsqrt(jnp.mean(center * center, axis=-1, keepdims=True) + epsilon)
    return center * rstd, rstd


def norm_back(grad, normal, rstd, gain):
    scaled = grad * gain
    return rstd * (
        scaled
        - jnp.mean(scaled, axis=-1, keepdims=True)
        - normal * jnp.mean(scaled * normal, axis=-1, keepdims=True)
    )


def move_tokens_plan(
    tokens,
    key_mask,
    expert_ids,
    cotangent,
    norm1_gain,
    norm1_bias,
    w_qkv,
    w_proj,
    proj_bias,
    norm2_gain,
    norm2_bias,
    w_router,
    w_in,
    b_in,
    w_out,
    b_out,
):
    f32, bf16 = jnp.float32, jnp.bfloat16
    _, rows, width = tokens.shape
    experts, depth, hidden = w_in.shape
    slice_width = w_out.shape[1]
    planes = hidden // slice_width // 2
    own = experts // 2
    s = lax.axis_index("seq")
    core = s % 2
    small = jnp.concatenate(
        [
            jnp.stack([norm1_gain, norm1_bias, proj_bias, norm2_gain, norm2_bias], axis=1),
            w_router,
            b_out.T,
        ],
        axis=1,
    )
    small = jnp.pad(small, ((0, 0), (0, 128 - small.shape[1])))
    own_mask = lax.dynamic_slice_in_dim(key_mask, s, 1, 0).astype(f32)
    selected = jnp.sum(
        (expert_ids[0][:, :, None] == jnp.arange(experts, dtype=jnp.int32)).astype(f32), axis=1
    )
    padded = (rows + 15) // 16 * 16
    extra = ((0, padded - rows), (0, 0))
    wide_tokens = jnp.pad(tokens[0], extra)
    keys = jnp.pad(own_mask, ((0, 0), (0, padded - rows)))
    keep = keys.reshape(padded, 1)
    small, full_qkv, full_proj, inner, normed_in, qkv, attended, middle, packed = front(
        planes,
        rows,
        wide_tokens,
        keys,
        keep,
        jnp.pad(cotangent[0], extra),
        jnp.pad(selected, ((0, padded - rows), (0, 128 - experts))).astype(bf16),
        small,
        w_qkv,
        w_proj,
        w_in,
    )
    outer = lax.dynamic_slice_in_dim(w_out, core * own, own, 0).reshape(own * slice_width, width)
    inner_bias = lax.dynamic_slice_in_dim(b_in, core * own, own, 0)
    inner_bias = inner_bias.reshape(1, own * slice_width).astype(f32)
    mix_parts, row_grad, inner_grad, outer_grad, router_grad = experts_of_the_plane(
        planes, own, packed, inner, outer, inner_bias, small
    )
    mixed, token_grad, qkv_grad, proj_grad, vector_grads, inner_grad, outer_grad = back(
        planes,
        own,
        rows,
        row_grad,
        packed,
        middle,
        wide_tokens,
        normed_in,
        qkv,
        attended,
        small,
        full_qkv,
        full_proj,
        keys,
        keep,
        mix_parts,
        inner_grad,
        outer_grad,
        router_grad,
    )
    units = own * slice_width
    return (
        mixed[None],
        token_grad[None],
        vector_grads[:, 0],
        vector_grads[:, 1],
        qkv_grad.astype(f32),
        proj_grad.astype(f32),
        vector_grads[:, 2],
        vector_grads[:, 3],
        vector_grads[:, 4],
        vector_grads[:, 16 : 16 + experts],
        inner_grad.astype(f32),
        outer_grad[:, units, :units].reshape(experts, slice_width).astype(f32),
        outer_grad[:, :units].reshape(experts, slice_width, width).astype(f32),
        vector_grads[:, 8 : 8 + experts].T,
    )


def solution(mesh):
    n_seq, n_fsdp = mesh.shape["seq"], mesh.shape["fsdp"]

    def per_device(*args):
        tokens, w_in, w_out = args[0], args[12], args[14]
        experts, _, hidden = w_in.shape
        lanes = hidden // n_fsdp
        whole_tiles = lanes % 128 == 0 and w_in.shape[1] % 32 == 0 and 2 * lanes <= tokens.shape[2]
        if n_seq == 4 and experts == n_seq and tokens.shape[0] == 1 and whole_tiles:
            return move_tokens_plan(*args)
        return gather_weights_plan(*args)

    return jax.shard_map(
        per_device,
        mesh=mesh,
        in_specs=(
            P(("fsdp", "seq"), None, None),
            P("fsdp", None),
            P(("fsdp", "seq"), None, None),
            P(("fsdp", "seq"), None, None),
            P("fsdp"),
            P("fsdp"),
            P("fsdp", None),
            P("fsdp", None),
            P("fsdp"),
            P("fsdp"),
            P("fsdp"),
            P("fsdp", None),
            P(None, "fsdp", None),
            P(None, "fsdp"),
            P(None, "fsdp", None),
            P(None, "fsdp"),
        ),
        out_specs=(
            P(("fsdp", "seq"), None, None),
            P(("fsdp", "seq"), None, None),
            P("fsdp"),
            P("fsdp"),
            P("fsdp", None),
            P("fsdp", None),
            P("fsdp"),
            P("fsdp"),
            P("fsdp"),
            P("fsdp", None),
            P(None, "fsdp", None),
            P(None, "fsdp"),
            P(None, "fsdp", None),
            P(None, "fsdp"),
        ),
        check_vma=False,
    )
```

```python
import functools

import jax
import jax.numpy as jnp
from jax import lax
from jax.experimental import pallas as pl
from jax.experimental.pallas import tpu as pltpu
from jax.sharding import PartitionSpec as P

HEADS = 12
CAP = 142


epsilon = 1e-06
masked_score = -1e30


def norm_rows(values, gain, offset):
    center = values - jnp.mean(values, axis=-1, keepdims=True)
    spread = jnp.mean(center * center, axis=-1, keepdims=True)
    return center * lax.rsqrt(spread + epsilon) * gain + offset


def softmax_rows(values):
    shifted = jnp.exp(values - jnp.max(values, axis=-1, keepdims=True))
    return shifted / jnp.sum(shifted, axis=-1, keepdims=True)


def exact_gelu(values):
    return jax.nn.gelu(values, approximate=False)


def expert_slots(chosen, experts):
    flat_ids = chosen.reshape(-1)
    onehot = (flat_ids[:, None] == jnp.arange(experts, dtype=jnp.int32)[None, :]).astype(jnp.int32)
    ranks = jnp.cumsum(onehot, axis=0, dtype=jnp.int32)
    slot_pos = jnp.sum(onehot * ranks, axis=1, dtype=jnp.int32) - 1
    return (flat_ids, slot_pos)


def gather_weights_plan(
    tokens,
    key_mask,
    expert_ids,
    cotangent,
    norm1_gain,
    norm1_bias,
    w_qkv,
    w_proj,
    proj_bias,
    norm2_gain,
    norm2_bias,
    w_router,
    w_in,
    b_in,
    w_out,
    b_out,
):
    images, seq_len, width = tokens.shape
    experts = w_in.shape[0]
    head_dim = width // HEADS
    scaling = head_dim ** (-0.5)
    row_count = images * seq_len
    dense_set = (
        lax.all_gather(norm1_gain, "fsdp", axis=0, tiled=True),
        lax.all_gather(norm1_bias, "fsdp", axis=0, tiled=True),
        lax.all_gather(w_qkv, "fsdp", axis=0, tiled=True),
        lax.all_gather(w_proj, "fsdp", axis=0, tiled=True),
        lax.all_gather(proj_bias, "fsdp", axis=0, tiled=True),
        lax.all_gather(norm2_gain, "fsdp", axis=0, tiled=True),
        lax.all_gather(norm2_bias, "fsdp", axis=0, tiled=True),
        lax.all_gather(w_router, "fsdp", axis=0, tiled=True),
    )
    gain_first = dense_set[0].astype(jnp.float32)
    bias_first = dense_set[1].astype(jnp.float32)
    full_qkv = dense_set[2]
    full_proj = dense_set[3]
    bias_proj = dense_set[4].astype(jnp.float32)
    gain_second = dense_set[5].astype(jnp.float32)
    bias_second = dense_set[6].astype(jnp.float32)
    full_router = dense_set[7]
    expert_set = (
        lax.all_gather(w_in, "fsdp", axis=1, tiled=True),
        lax.all_gather(b_in, "fsdp", axis=1, tiled=True),
        lax.all_gather(w_out, "fsdp", axis=1, tiled=True),
        lax.all_gather(b_out, "fsdp", axis=1, tiled=True),
    )
    inner_weight = expert_set[0]
    inner_bias = expert_set[1].astype(jnp.float32)
    outer_weight = expert_set[2]
    outer_bias = expert_set[3].astype(jnp.float32)
    own_mask = lax.dynamic_slice_in_dim(key_mask, lax.axis_index("seq") * images, images, 0)
    keep_rows = own_mask.reshape(row_count, 1).astype(jnp.float32)
    usable = (key_mask > 0)[:, None, None, :]
    flat_tokens = tokens.astype(jnp.float32).reshape(row_count, width)
    normed_in = norm_rows(flat_tokens, gain_first, bias_first).astype(jnp.bfloat16)
    mixed_qkv = jnp.dot(normed_in, full_qkv, preferred_element_type=jnp.float32).astype(
        jnp.bfloat16
    )
    mixed_qkv = mixed_qkv.reshape(images, seq_len, 3, HEADS, head_dim)
    head_qkv = lax.all_to_all(mixed_qkv, "seq", split_axis=3, concat_axis=0, tiled=True)
    queries = head_qkv[:, :, 0]
    key_rows = head_qkv[:, :, 1]
    value_rows = head_qkv[:, :, 2]

    def score_block():
        raw = (
            jnp.einsum("gahd,gbhd->ghab", queries, key_rows, preferred_element_type=jnp.float32)
            * scaling
        )
        return jnp.where(usable, raw, masked_score)

    scores = score_block()
    row_top = jnp.max(scores, axis=-1, keepdims=True)
    shifted = jnp.exp(scores - row_top)
    row_total = jnp.sum(shifted, axis=-1, keepdims=True)
    attn_probs = (shifted / row_total).astype(jnp.bfloat16)
    log_total = row_top + jnp.log(row_total)
    head_out = jnp.einsum(
        "ghab,gbhd->gahd", attn_probs, value_rows, preferred_element_type=jnp.float32
    ).astype(jnp.bfloat16)
    attended = lax.all_to_all(head_out, "seq", split_axis=0, concat_axis=2, tiled=True).reshape(
        row_count, width
    )
    middle = (
        flat_tokens + jnp.dot(attended, full_proj, preferred_element_type=jnp.float32) + bias_proj
    )
    normed_mid = norm_rows(middle, gain_second, bias_second).astype(jnp.bfloat16)
    routing = softmax_rows(jnp.dot(normed_mid, full_router, preferred_element_type=jnp.float32))
    chosen = expert_ids.reshape(row_count, 2)
    flat_ids, slot_pos = expert_slots(chosen, experts)
    gating = jnp.take_along_axis(routing, chosen, axis=1)
    buffer = (
        jnp.zeros((experts, CAP, width), jnp.bfloat16)
        .at[flat_ids, slot_pos]
        .set(jnp.repeat(normed_mid, 2, axis=0))
    )
    pre_act = (
        jnp.einsum("ecd,edf->ecf", buffer, inner_weight, preferred_element_type=jnp.float32)
        + inner_bias[:, None, :]
    )
    activated = exact_gelu(pre_act).astype(jnp.bfloat16)
    expert_out = (
        jnp.einsum("ecf,efd->ecd", activated, outer_weight, preferred_element_type=jnp.float32)
        + outer_bias[:, None, :]
    )
    picked = expert_out[flat_ids, slot_pos].reshape(row_count, 2, width)
    mixture = jnp.sum(gating[:, :, None] * picked, axis=1)
    mixed = (keep_rows * (middle + mixture)).astype(jnp.bfloat16).reshape(images, seq_len, width)
    grad_out = cotangent.astype(jnp.float32).reshape(row_count, width) * keep_rows
    grad_gate = jnp.sum(grad_out[:, None, :] * picked, axis=2)
    grad_picked = (
        (gating[:, :, None] * grad_out[:, None, :])
        .astype(jnp.bfloat16)
        .reshape(2 * row_count, width)
    )
    grad_expert_out = (
        jnp.zeros((experts, CAP, width), jnp.bfloat16).at[flat_ids, slot_pos].set(grad_picked)
    )
    grad_outer_bias = jnp.sum(grad_expert_out, axis=1, dtype=jnp.float32)
    hidden_pre = (
        jnp.einsum("ecd,edf->ecf", buffer, inner_weight, preferred_element_type=jnp.float32)
        + inner_bias[:, None, :]
    )
    hidden_act = exact_gelu(hidden_pre).astype(jnp.bfloat16)
    grad_outer_weight = jnp.einsum(
        "ecf,ecd->efd", hidden_act, grad_expert_out, preferred_element_type=jnp.float32
    )
    grad_act = jnp.einsum(
        "ecd,efd->ecf", grad_expert_out, outer_weight, preferred_element_type=jnp.float32
    )
    gelu_pull = jax.vjp(exact_gelu, hidden_pre)[1]
    grad_pre = gelu_pull(grad_act)[0].astype(jnp.bfloat16)
    grad_inner_bias = jnp.sum(grad_pre, axis=1, dtype=jnp.float32)
    grad_inner_weight = jnp.einsum(
        "ecd,ecf->edf", buffer, grad_pre, preferred_element_type=jnp.float32
    )
    grad_buffer = jnp.einsum(
        "ecf,edf->ecd", grad_pre, inner_weight, preferred_element_type=jnp.float32
    )
    grad_rows = jnp.sum(grad_buffer[flat_ids, slot_pos].reshape(row_count, 2, width), axis=1)
    expert_range = jnp.arange(experts, dtype=jnp.int32)[None, None, :]
    grad_route = jnp.sum(
        grad_gate[:, :, None] * (chosen[:, :, None] == expert_range).astype(jnp.float32), axis=1
    )
    grad_logits = (
        routing * (grad_route - jnp.sum(routing * grad_route, axis=-1, keepdims=True))
    ).astype(jnp.bfloat16)
    grad_router = jnp.einsum(
        "nd,ne->de", normed_mid, grad_logits, preferred_element_type=jnp.float32
    )
    grad_normed_mid = grad_rows + jnp.einsum(
        "ne,de->nd", grad_logits, full_router, preferred_element_type=jnp.float32
    )
    second_pull = jax.vjp(norm_rows, middle, gain_second, bias_second)[1]
    grad_mid_norm, grad_gain_second, grad_bias_second = second_pull(grad_normed_mid)
    grad_middle = grad_out + grad_mid_norm
    grad_proj = grad_middle.astype(jnp.bfloat16)
    grad_bias_proj = jnp.sum(grad_proj, axis=0, dtype=jnp.float32)
    grad_proj_weight = jnp.einsum(
        "nd,ne->de", attended, grad_proj, preferred_element_type=jnp.float32
    )
    grad_attended = jnp.einsum(
        "ne,de->nd", grad_proj, full_proj, preferred_element_type=jnp.float32
    ).astype(jnp.bfloat16)
    grad_head_out = lax.all_to_all(
        grad_attended.reshape(images, seq_len, HEADS, head_dim),
        "seq",
        split_axis=2,
        concat_axis=0,
        tiled=True,
    )
    recomputed = jnp.exp(score_block() - log_total)
    grad_values = jnp.einsum(
        "ghab,gahd->gbhd",
        recomputed.astype(jnp.bfloat16),
        grad_head_out,
        preferred_element_type=jnp.float32,
    )
    grad_probs = jnp.einsum(
        "gahd,gbhd->ghab", grad_head_out, value_rows, preferred_element_type=jnp.float32
    )
    grad_scores = (
        recomputed * (grad_probs - jnp.sum(recomputed * grad_probs, axis=-1, keepdims=True))
    ).astype(jnp.bfloat16)
    grad_queries = (
        jnp.einsum("ghab,gbhd->gahd", grad_scores, key_rows, preferred_element_type=jnp.float32)
        * scaling
    )
    grad_keys = (
        jnp.einsum("ghab,gahd->gbhd", grad_scores, queries, preferred_element_type=jnp.float32)
        * scaling
    )
    grad_head_qkv = jnp.stack([grad_queries, grad_keys, grad_values], axis=2).astype(jnp.bfloat16)
    grad_qkv = lax.all_to_all(
        grad_head_qkv, "seq", split_axis=0, concat_axis=3, tiled=True
    ).reshape(row_count, 3 * width)
    grad_qkv_weight = jnp.einsum(
        "nd,ne->de", normed_in, grad_qkv, preferred_element_type=jnp.float32
    )
    grad_normed_in = jnp.einsum("ne,de->nd", grad_qkv, full_qkv, preferred_element_type=jnp.float32)
    first_pull = jax.vjp(norm_rows, flat_tokens, gain_first, bias_first)[1]
    grad_first, grad_gain_first, grad_bias_first = first_pull(grad_normed_in)
    token_grad = (grad_middle + grad_first).astype(jnp.bfloat16).reshape(images, seq_len, width)
    shares = (
        lax.psum_scatter(grad_gain_first, "fsdp", scatter_dimension=0, tiled=True),
        lax.psum_scatter(grad_bias_first, "fsdp", scatter_dimension=0, tiled=True),
        lax.psum_scatter(grad_qkv_weight, "fsdp", scatter_dimension=0, tiled=True),
        lax.psum_scatter(grad_proj_weight, "fsdp", scatter_dimension=0, tiled=True),
        lax.psum_scatter(grad_bias_proj, "fsdp", scatter_dimension=0, tiled=True),
        lax.psum_scatter(grad_gain_second, "fsdp", scatter_dimension=0, tiled=True),
        lax.psum_scatter(grad_bias_second, "fsdp", scatter_dimension=0, tiled=True),
        lax.psum_scatter(grad_router, "fsdp", scatter_dimension=0, tiled=True),
        lax.psum_scatter(grad_inner_weight, "fsdp", scatter_dimension=1, tiled=True),
        lax.psum_scatter(grad_inner_bias, "fsdp", scatter_dimension=1, tiled=True),
        lax.psum_scatter(grad_outer_weight, "fsdp", scatter_dimension=1, tiled=True),
        lax.psum_scatter(grad_outer_bias, "fsdp", scatter_dimension=1, tiled=True),
    )
    parted = (
        lax.psum_scatter(
            shares[0].astype(jnp.bfloat16), "seq", scatter_dimension=0, tiled=True
        ).astype(jnp.float32),
        lax.psum_scatter(
            shares[1].astype(jnp.bfloat16), "seq", scatter_dimension=0, tiled=True
        ).astype(jnp.float32),
        lax.psum_scatter(
            shares[2].astype(jnp.bfloat16), "seq", scatter_dimension=0, tiled=True
        ).astype(jnp.float32),
        lax.psum_scatter(
            shares[3].astype(jnp.bfloat16), "seq", scatter_dimension=0, tiled=True
        ).astype(jnp.float32),
        lax.psum_scatter(
            shares[4].astype(jnp.bfloat16), "seq", scatter_dimension=0, tiled=True
        ).astype(jnp.float32),
        lax.psum_scatter(
            shares[5].astype(jnp.bfloat16), "seq", scatter_dimension=0, tiled=True
        ).astype(jnp.float32),
        lax.psum_scatter(
            shares[6].astype(jnp.bfloat16), "seq", scatter_dimension=0, tiled=True
        ).astype(jnp.float32),
        lax.psum_scatter(
            shares[7].astype(jnp.bfloat16), "seq", scatter_dimension=0, tiled=True
        ).astype(jnp.float32),
        lax.psum_scatter(
            shares[8].astype(jnp.bfloat16), "seq", scatter_dimension=1, tiled=True
        ).astype(jnp.float32),
        lax.psum_scatter(
            shares[9].astype(jnp.bfloat16), "seq", scatter_dimension=1, tiled=True
        ).astype(jnp.float32),
        lax.psum_scatter(
            shares[10].astype(jnp.bfloat16), "seq", scatter_dimension=1, tiled=True
        ).astype(jnp.float32),
        lax.psum_scatter(
            shares[11].astype(jnp.bfloat16), "seq", scatter_dimension=1, tiled=True
        ).astype(jnp.float32),
    )
    totals = (
        lax.all_gather(parted[0].astype(jnp.bfloat16), "seq", axis=0, tiled=True).astype(
            jnp.float32
        ),
        lax.all_gather(parted[1].astype(jnp.bfloat16), "seq", axis=0, tiled=True).astype(
            jnp.float32
        ),
        lax.all_gather(parted[2].astype(jnp.bfloat16), "seq", axis=0, tiled=True).astype(
            jnp.float32
        ),
        lax.all_gather(parted[3].astype(jnp.bfloat16), "seq", axis=0, tiled=True).astype(
            jnp.float32
        ),
        lax.all_gather(parted[4].astype(jnp.bfloat16), "seq", axis=0, tiled=True).astype(
            jnp.float32
        ),
        lax.all_gather(parted[5].astype(jnp.bfloat16), "seq", axis=0, tiled=True).astype(
            jnp.float32
        ),
        lax.all_gather(parted[6].astype(jnp.bfloat16), "seq", axis=0, tiled=True).astype(
            jnp.float32
        ),
        lax.all_gather(parted[7].astype(jnp.bfloat16), "seq", axis=0, tiled=True).astype(
            jnp.float32
        ),
        lax.all_gather(parted[8].astype(jnp.bfloat16), "seq", axis=1, tiled=True).astype(
            jnp.float32
        ),
        lax.all_gather(parted[9].astype(jnp.bfloat16), "seq", axis=1, tiled=True).astype(
            jnp.float32
        ),
        lax.all_gather(parted[10].astype(jnp.bfloat16), "seq", axis=1, tiled=True).astype(
            jnp.float32
        ),
        lax.all_gather(parted[11].astype(jnp.bfloat16), "seq", axis=1, tiled=True).astype(
            jnp.float32
        ),
    )
    return (
        mixed,
        token_grad,
        totals[0],
        totals[1],
        totals[2],
        totals[3],
        totals[4],
        totals[5],
        totals[6],
        totals[7],
        totals[8],
        totals[9],
        totals[10],
        totals[11],
    )


MESH = pl.DeviceIdType.MESH
NT = (((1,), (1,)), ((), ()))
TN = (((0,), (0,)), ((), ()))


def dot(a, b):
    return jnp.dot(a, b, preferred_element_type=jnp.float32)


class Place:
    def __init__(self, planes):
        self.planes = planes
        s, f = lax.axis_index("seq"), lax.axis_index("fsdp")
        self.y, self.c, self.z, self.x = s // 2, s % 2, f // 2, f % 2

    def at(self, y, c, z, x):
        return (y * 2 + c, z * 2 + x)

    def other_core(self):
        return self.at(self.y, 1 - self.c, self.z, self.x)

    def other_x(self):
        return self.at(self.y, self.c, self.z, 1 - self.x)

    def other_y(self):
        return self.at(1 - self.y, self.c, self.z, self.x)

    def level(self, k):
        return self.at(self.y, self.c, lax.rem(self.z + k + self.planes, self.planes), self.x)


def greet(partners):
    barrier = pltpu.get_barrier_semaphore()
    for partner in partners:
        pl.semaphore_signal(barrier, inc=1, device_id=partner, device_id_type=MESH)
    pl.semaphore_wait(barrier, len(partners))


def nearest(place, i):
    level = 0
    for z in range(place.planes):
        order = sorted(range(place.planes), key=lambda other: (abs(other - z), other))
        for at in range(place.planes):
            level = level + jnp.where((place.z == z) & (i == at), order[at], 0)
    return level


def expert_kernel(
    planes,
    own,
    rows,
    real,
    packed_ref,
    inner_ref,
    outer_all_ref,
    bias_all_ref,
    small_ref,
    mix_ref,
    out_ref,
    inner_grad_ref,
    outer_grad_ref,
    bias_grad_ref,
    router_grad_ref,
    outer_ref,
    inner_t_ref,
    outer_t_ref,
    router_ref,
    router_t_ref,
    tokens,
    part,
    from_core,
    from_x,
    from_z,
    hidden,
    hidden_grad,
    logit_grad,
    inner_acc,
    outer_acc,
    outer_sem,
    z_send,
    z_recv,
    x_send,
    x_recv,
    c_send,
    c_recv,
    sum_c_send,
    sum_c_recv,
    sum_x_send,
    sum_x_recv,
    sum_z_send,
    sum_z_recv,
):
    f32, bf16 = jnp.float32, jnp.bfloat16
    place = Place(planes)
    y, c, z, x = place.y, place.c, place.z, place.x
    width = inner_ref.shape[0]
    lanes = inner_ref.shape[1] // own
    first = real % 16

    def remote(src, dst, send, recv, device):
        return pltpu.make_async_remote_copy(
            src_ref=src, dst_ref=dst, send_sem=send, recv_sem=recv, device_id=device, device_id_type=MESH
        )

    def slot(buffer, level, at, count=1):
        return buffer.at[level, pl.ds(at * rows, count * rows)]

    def up_copy(level):
        here = slot(tokens, level, 0)
        return remote(here, here, z_send.at[0, level], z_recv.at[0, level], place.at(y, c, z + 1, x))

    def down_copy(level):
        here = slot(tokens, level, 0)
        return remote(here, here, z_send.at[1, level], z_recv.at[1, level], place.at(y, c, z - 1, x))

    def x_copy(level):
        return remote(
            slot(tokens, level, 0), slot(tokens, level, 1), x_send.at[level], x_recv.at[level], place.other_x()
        )

    def c_copy(level, r):
        return remote(
            slot(tokens, level, r),
            slot(tokens, level, 2 + r),
            c_send.at[level, r],
            c_recv.at[level, r],
            place.other_core(),
        )

    def sum_c_copy(level):
        return remote(
            slot(part, level, 2, 2),
            from_core.at[level],
            sum_c_send.at[level],
            sum_c_recv.at[level],
            place.other_core(),
        )

    def sum_x_copy(level):
        return remote(
            slot(part, level, 1), from_x.at[level], sum_x_send.at[level], sum_x_recv.at[level], place.other_x()
        )

    def sum_z_copy(level, source):
        return remote(
            slot(part, level, 0),
            from_z.at[source],
            sum_z_send.at[level],
            sum_z_recv.at[source],
            place.at(y, c, level, x),
        )

    partners = [place.other_core(), place.other_x()] + [place.level(k) for k in range(1, planes)]
    greet(partners)
    tokens[z, 0:rows, :] = packed_ref[...]

    @pl.when(z < planes - 1)
    def _():
        up_copy(z).start()

    @pl.when(z > 0)
    def _():
        down_copy(z).start()

    c_copy(z, 0).start()
    x_copy(z).start()
    load = pltpu.make_async_copy(outer_all_ref.at[pl.ds(c * own, own)], outer_ref, outer_sem)
    load.start()
    inner_t_ref[...] = jnp.transpose(inner_ref[...])
    place_row = lax.broadcasted_iota(jnp.int32, (128, 128), 0)
    place_lane = lax.broadcasted_iota(jnp.int32, (128, 128), 1)
    take = (place_row - (5 + 2 * own) == place_lane - first) & (place_lane >= first)
    take = take & (place_lane < first + 2 * own)
    router = dot(small_ref[...], take.astype(bf16))
    router_ref[...] = router.astype(bf16)
    router_t_ref[...] = jnp.transpose(router).astype(bf16)
    inner_acc[...] = jnp.zeros_like(inner_acc)
    outer_acc[...] = jnp.zeros_like(outer_acc)
    bias_grad_ref[...] = jnp.zeros_like(bias_grad_ref)
    router_grad_ref[...] = jnp.zeros_like(router_grad_ref)
    load.wait()
    for i in range(own):
        outer_t_ref[:, i * lanes : (i + 1) * lanes] = jnp.transpose(outer_ref[i])

    def hop(h):
        @pl.when(z >= h)
        def _():
            up_copy(z - h).wait_recv()

            @pl.when(z < planes - 1)
            def _():
                up_copy(z - h).start()

            c_copy(z - h, 0).start()

        @pl.when(z + h < planes)
        def _():
            down_copy(z + h).wait_recv()

            @pl.when(z > 0)
            def _():
                down_copy(z + h).start()

            c_copy(z + h, 0).start()

    def tile(level, t):
        here = pl.ds(pl.multiple_of(t * rows, 16), rows)
        normed, grad_out = tokens[level, here, :width], tokens[level, here, width:]
        last = pl.ds(pl.multiple_of(t * rows + real - first, 16), 16)
        chosen = tokens[level, last, width : width + 256].astype(f32)
        chosen = jnp.concatenate([chosen, jnp.zeros((112, 256), f32)], axis=0)
        select = jnp.transpose(chosen)[:rows]
        lane = lax.broadcasted_iota(jnp.int32, select.shape, 1)
        named = (lane >= first) & (lane < first + 2 * own)
        select = jnp.where(named, select, 0.0)
        logits = jnp.where(named, dot(normed, router_ref[...]), -1e30)
        routing = jnp.exp(logits - jnp.max(logits, axis=1, keepdims=True))
        routing = routing / jnp.sum(routing, axis=1, keepdims=True)
        gates = routing * select
        gate_grads = jnp.zeros_like(gates)
        for i in range(own):
            mine = lane == first + c * own + i
            units = slice(i * lanes, (i + 1) * lanes)
            gate = jnp.sum(jnp.where(mine, gates, 0.0), axis=1, keepdims=True)
            bias = jnp.where(c == 0, bias_all_ref[i : i + 1, :], bias_all_ref[own + i : own + i + 1, :])
            pre = dot(normed, inner_ref[:, units]) + bias.astype(f32)
            grad_act = dot(grad_out, outer_t_ref[:, units])
            cdf = 0.5 * (1.0 + lax.erf(pre * (0.5**0.5)))
            act = pre * cdf
            hidden[here, units] = (gate * act).astype(bf16)
            gate_grad = jnp.sum(act * grad_act, axis=1, keepdims=True)
            gate_grads = gate_grads + jnp.where(mine, gate_grad * select, 0.0)
            slope = cdf + pre * jnp.exp(-0.5 * pre * pre) * 0.3989422804014327
            grad_pre = gate * grad_act * slope
            bias_grad_ref[0:1, units] += jnp.sum(grad_pre, axis=0, keepdims=True)
            hidden_grad[here, units] = grad_pre.astype(bf16)
        grad_logits = routing * (gate_grads - jnp.sum(routing * gate_grads, axis=1, keepdims=True))
        logit_grad[here, :] = grad_logits.astype(bf16)
        mixed = jnp.zeros((rows, width), f32)
        for i in range(own):
            mixed = mixed + dot(hidden[here, i * lanes : (i + 1) * lanes], outer_ref[i])
        mix_ref[level, here, :] = mixed.astype(bf16)
        row_grad = dot(hidden_grad[here, :], inner_t_ref[...])
        row_grad = row_grad + dot(logit_grad[here, :], router_t_ref[...])
        part[level, here, :] = row_grad.astype(bf16)

    def tiles(level, start):
        def one(t, carry):
            tile(level, 2 * t + start)
            return carry

        lax.fori_loop(0, 2, one, 0)

    def add_core(level):
        sum_c_copy(level).wait_recv()
        total = part[level, rows : 2 * rows, :].astype(f32) + from_core[level, rows : 2 * rows, :].astype(f32)
        part[level, rows : 2 * rows, :] = total.astype(bf16)
        sum_x_copy(level).start()

    def add_x(level):
        sum_x_copy(level).wait_recv()
        total = part[level, 0:rows, :].astype(f32) + from_core[level, 0:rows, :].astype(f32)
        total = total + from_x[level].astype(f32)
        part[level, 0:rows, :] = total.astype(bf16)

        @pl.when(level != z)
        def _():
            sum_z_copy(level, z).start()

    def step(i, carry):
        level, later, before = nearest(place, i), nearest(place, i + 1), nearest(place, i - 1)

        @pl.when(i > 0)
        def _():
            c_copy(level, 0).wait_recv()

        @pl.when(i == 0)
        def _():
            c_copy(z, 0).wait_recv()

        tiles(level, 0)

        @pl.when(i + 1 < planes)
        def _():
            hop(i + 1)

        x_copy(level).wait_recv()
        c_copy(level, 1).start()

        @pl.when(i + 1 < planes)
        def _():
            x_copy(later).start()

        c_copy(level, 1).wait_recv()
        tiles(level, 1)
        sum_c_copy(level).start()

        @pl.when(i > 0)
        def _():
            add_x(before)

        add_core(level)

        def columns(j, carry):
            some = pl.ds(pl.multiple_of(j * 256, 256), 256)
            outer_acc[:, some] += lax.dot_general(
                hidden[...],
                tokens[level, :, pl.ds(pl.multiple_of(width + j * 256, 256), 256)],
                TN,
                preferred_element_type=f32,
            )
            inner_acc[:, some] += lax.dot_general(
                tokens[level, :, :width], hidden_grad[:, some], TN, preferred_element_type=f32
            )
            return carry

        lax.fori_loop(0, width // 256, columns, 0)
        router_grad_ref[...] += lax.dot_general(
            tokens[level, :, :width], logit_grad[...], TN, preferred_element_type=f32
        )
        return carry

    lax.fori_loop(0, planes, step, 0)
    inner_grad_ref[...] = inner_acc[...].astype(bf16)
    outer_grad_ref[...] = outer_acc[...].astype(bf16)
    add_x(nearest(place, planes - 1))
    total = part[z, 0:rows, :].astype(f32)
    for k in range(1, planes):
        source = lax.rem(z + k, planes)
        sum_z_copy(z, source).wait_recv()
        total = total + from_z[source].astype(f32)
    out_ref[...] = total
    for level in range(planes):
        x_copy(level).wait_send()
        c_copy(level, 0).wait_send()
        c_copy(level, 1).wait_send()
        sum_c_copy(level).wait_send()
        sum_x_copy(level).wait_send()

        @pl.when(level != z)
        def _():
            sum_z_copy(level, z).wait_send()

        @pl.when((z >= level) & (z < planes - 1))
        def _():
            up_copy(level).wait_send()

        @pl.when((z <= level) & (z > 0))
        def _():
            down_copy(level).wait_send()


def experts_of_the_plane(planes, own, real, packed, inner, outer, bias, small):
    f32, bf16 = jnp.float32, jnp.bfloat16
    rows, wide = packed.shape
    chunk = 4 * rows
    width, units = inner.shape
    shape = jax.ShapeDtypeStruct
    vmem = pl.BlockSpec(memory_space=pltpu.VMEM)
    dma = pltpu.SemaphoreType.DMA
    flops = 12 * planes * chunk * width * units
    return pl.pallas_call(
        functools.partial(expert_kernel, planes, own, rows, real),
        out_shape=[
            shape((planes, chunk, width), bf16),
            shape((rows, width), f32),
            shape((width, units), bf16),
            shape((units, width), bf16),
            shape((8, units), f32),
            shape((width, 128), f32),
        ],
        in_specs=[vmem] * 2 + [pl.BlockSpec(memory_space=pl.ANY)] + [vmem] * 2,
        out_specs=[vmem] * 6,
        scratch_shapes=[
            pltpu.VMEM((own, units // own, width), bf16),
            pltpu.VMEM((units, width), bf16),
            pltpu.VMEM((width, units), bf16),
            pltpu.VMEM((width, 128), bf16),
            pltpu.VMEM((128, width), bf16),
            pltpu.VMEM((planes, chunk, wide), bf16),
            pltpu.VMEM((planes, chunk, width), bf16),
            pltpu.VMEM((planes, 2 * rows, width), bf16),
            pltpu.VMEM((planes, rows, width), bf16),
            pltpu.VMEM((planes, rows, width), bf16),
            pltpu.VMEM((chunk, units), bf16),
            pltpu.VMEM((chunk, units), bf16),
            pltpu.VMEM((chunk, 128), bf16),
            pltpu.VMEM((width, units), f32),
            pltpu.VMEM((units, width), f32),
            dma,
        ]
        + [dma((2, planes))] * 2
        + [dma((planes,))] * 2
        + [dma((planes, 2))] * 2
        + [dma((planes,))] * 6,
        compiler_params=pltpu.CompilerParams(
            collective_id=1, has_side_effects=True, vmem_limit_bytes=60 * 2**20
        ),
        cost_estimate=pl.CostEstimate(flops=flops, bytes_accessed=40 * 2**20, transcendentals=0),
        name="experts_of_the_plane",
    )(packed, inner, outer, bias, small)


def front_kernel(
    planes,
    heads,
    real,
    tokens_ref,
    mask_ref,
    ids_ref,
    cotangent_ref,
    *refs,
):
    vector_refs, refs = refs[:5], refs[5:]
    (
        router_part_ref,
        outer_bias_ref,
        qkv_part_ref,
    proj_part_ref,
    inner_part_ref,
    small_all,
    w_qkv_all,
    w_proj_all,
    inner_all,
    normed_in_ref,
    qkv_ref,
    attended_ref,
    middle_ref,
    packed_ref,
    wide_ref,
    select_ref,
    keys_ref,
    keep_ref,
    up_send,
    up_recv,
    down_send,
    down_recv,
    x_send,
    x_recv,
    c_send,
    c_recv,
    spread_send,
    spread_recv,
    own_sem,
    y_send,
    y_recv,
    ) = refs
    f32, bf16 = jnp.float32, jnp.bfloat16
    place = Place(planes)
    rows, width = wide_ref.shape
    depth = qkv_part_ref.shape[0]
    experts = inner_part_ref.shape[0]
    half = depth // 2
    lanes = inner_part_ref.shape[2] // (2 * planes)
    head_dim = width // heads
    y, c, z, x = place.y, place.c, place.z, place.x
    gathered = [small_all, w_qkv_all, w_proj_all]

    def remote(src, dst, send, recv, device):
        return pltpu.make_async_remote_copy(
            src_ref=src, dst_ref=dst, send_sem=send, recv_sem=recv, device_id=device, device_id_type=MESH
        )

    def piece(j, level, across):
        start = (level * 2 + across) * depth + c * half
        return gathered[j].at[pl.ds(pl.multiple_of(start, 16), half)]

    def up_copy(j, level):
        here = piece(j, level, x)
        return remote(here, here, up_send.at[j, level], up_recv.at[j, level], place.at(y, c, z + 1, x))

    def down_copy(j, level):
        here = piece(j, level, x)
        return remote(here, here, down_send.at[j, level], down_recv.at[j, level], place.at(y, c, z - 1, x))

    def x_copy(j, level, across):
        here = piece(j, level, across)
        return remote(here, here, x_send.at[j, level], x_recv.at[j, level], place.other_x())

    def c_copy(j, level, across):
        here = piece(j, level, across)
        at = level * 2 + across
        return remote(here, here, c_send.at[j, at], c_recv.at[j, at], place.other_core())

    def sibling_piece(j, level, across):
        start = (level * 2 + across) * depth + (1 - c) * half
        here = gathered[j].at[pl.ds(pl.multiple_of(start, 16), half)]
        at = level * 2 + across
        return remote(here, here, c_send.at[j, at], c_recv.at[j, at], place.other_core())

    def columns_of(f):
        return pl.ds(pl.multiple_of(f * lanes, 128), lanes)

    here_rows = pl.ds(pl.multiple_of((z * 2 + x) * depth, 16), depth)
    my_units = pl.ds(pl.multiple_of(y * lanes, 128), lanes)

    def spread_copy(k, r):
        level, across = lax.rem(z + k, planes), (x + r) % 2
        return remote(
            inner_part_ref.at[c * 2 + y, :, columns_of(level * 2 + across)],
            inner_all.at[here_rows, my_units],
            spread_send.at[k, r],
            spread_recv.at[k, r],
            place.at(y, c, level, across),
        )

    own_copy = pltpu.make_async_copy(
        inner_part_ref.at[c * 2 + y, :, columns_of(z * 2 + x)], inner_all.at[here_rows, my_units], own_sem
    )
    y_copy = remote(inner_all.at[:, my_units], inner_all.at[:, my_units], y_send, y_recv, place.other_y())
    their_units = pl.ds(pl.multiple_of((1 - y) * lanes, 128), lanes)
    from_y = remote(inner_all.at[:, their_units], inner_all.at[:, their_units], y_send, y_recv, place.other_y())

    others = [(k, r) for k in range(planes) for r in range(2) if k or r]
    partners = [place.other_core(), place.other_y()]
    partners += [place.at(y, c, lax.rem(z + k, planes), (x + r) % 2) for k, r in others]
    greet(partners)

    w_qkv_all[here_rows, :] = qkv_part_ref[...]

    def forward(level, flows):
        for j in flows:
            x_copy(j, level, x).start()

    def line(flows):
        @pl.when(z < planes - 1)
        def _():
            for j in flows:
                up_copy(j, z).start()

        @pl.when(z > 0)
        def _():
            for j in flows:
                down_copy(j, z).start()

        forward(z, flows)

    def hops(flows):
        for h in range(1, planes):
            @pl.when(z >= h)
            def _():
                for j in flows:
                    up_copy(j, z - h).wait_recv()

                @pl.when(z < planes - 1)
                def _():
                    for j in flows:
                        up_copy(j, z - h).start()

                forward(z - h, flows)
                for j in flows:
                    c_copy(j, z - h, x).start()

            @pl.when(z + h < planes)
            def _():
                for j in flows:
                    down_copy(j, z + h).wait_recv()

                @pl.when(z > 0)
                def _():
                    for j in flows:
                        down_copy(j, z + h).start()

                forward(z + h, flows)
                for j in flows:
                    c_copy(j, z + h, x).start()

    def arrive(flows):
        for level in range(planes):
            for j in flows:
                x_copy(j, level, 1 - x).wait_recv()
                c_copy(j, level, 1 - x).start()

    def gather_done(flows):
        for level in range(planes):
            for j in flows:
                sibling_piece(j, level, 1 - x).wait_recv()

            @pl.when(level != z)
            def _():
                for j in flows:
                    sibling_piece(j, level, x).wait_recv()

    line([1])
    lined = [ref[...].astype(f32) for ref in vector_refs] + [outer_bias_ref[...].astype(f32)]
    lined = jnp.concatenate(lined, axis=0)
    lined = jnp.concatenate([lined, jnp.zeros((128 - lined.shape[0], depth), f32)], axis=0)
    lined = jnp.concatenate([lined, jnp.zeros((128, 128 - depth), f32)], axis=1)
    routed = jnp.concatenate([router_part_ref[...].astype(f32), jnp.zeros((depth, 128 - experts), f32)], axis=1)
    small = jnp.transpose(lined)[:depth] + pltpu.roll(routed, 5 + experts, 1)
    small_all[here_rows, :] = small.astype(bf16)
    line([0])
    w_proj_all[here_rows, :] = proj_part_ref[...]
    line([2])
    spare = jnp.zeros((rows - real, width), f32)
    values = jnp.concatenate([tokens_ref[...].astype(f32), spare], axis=0)
    wide_ref[...] = values.astype(bf16)
    normal, _ = norm_parts(values)
    mask = mask_ref[pl.ds(y * 2 + c, 1), :].astype(f32)
    keys = jnp.concatenate([mask, jnp.zeros((1, rows - real), f32)], axis=1)
    keys_ref[...] = keys
    keep = lax.broadcasted_iota(jnp.int32, (rows, rows), 0) == lax.broadcasted_iota(jnp.int32, (rows, rows), 1)
    keep = jnp.sum(jnp.where(keep, keys, 0.0), axis=1, keepdims=True)
    keep_ref[...] = keep
    ids = ids_ref[...]
    number = lax.broadcasted_iota(jnp.int32, (real, 128), 1)
    select = ((number == ids[:, 0:1]) | (number == ids[:, 1:2])).astype(f32)
    select = jnp.concatenate([select, jnp.zeros((rows - real, 128), f32)], axis=0)
    select_ref[...] = select.astype(bf16)
    chosen = jnp.transpose(jnp.concatenate([select, jnp.zeros((256 - rows, 128), f32)], axis=0))[:8]
    chosen = jnp.concatenate([chosen, jnp.zeros((8, width - 256), f32)], axis=1)
    if rows - real > 8:
        chosen = jnp.concatenate([chosen, jnp.zeros((rows - real - 8, width), f32)], axis=0)
    grad_out = cotangent_ref[...].astype(f32) * keep[:real]
    packed_ref[:, width:] = jnp.concatenate([grad_out, chosen], axis=0).astype(bf16)
    hops([0, 1])
    hops([2])
    own_copy.start()
    for k, r in others:
        spread_copy(k, r).start()
    arrive([0, 1])
    gather_done([0, 1])
    vectors = jnp.transpose(small_all[...].astype(f32))
    normed_in = (normal * vectors[0:1] + vectors[1:2]).astype(bf16)
    normed_in_ref[...] = normed_in
    for j in range(3):
        part = slice(j * width, (j + 1) * width)
        qkv_ref[:, part] = dot(normed_in, w_qkv_all[:, part]).astype(bf16)
    arrive([2])
    lane = lax.broadcasted_iota(jnp.int32, (rows, 2 * head_dim), 1)
    usable = keys_ref[...] > 0
    for pair in range(heads // 2):
        at = pair * 2 * head_dim
        queries = qkv_ref[:, at : at + 2 * head_dim]
        keys = qkv_ref[:, width + at : width + at + 2 * head_dim]
        held = qkv_ref[:, 2 * width + at : 2 * width + at + 2 * head_dim]
        outs = []
        for side in range(2):
            only = (lane < head_dim) if side == 0 else (lane >= head_dim)
            scores = lax.dot_general(
                jnp.where(only, queries, 0).astype(bf16), keys, NT, preferred_element_type=f32
            )
            scores = jnp.where(usable, scores * head_dim ** (-0.5), masked_score)
            shifted = jnp.exp(scores - jnp.max(scores, axis=1, keepdims=True))
            probs = (shifted / jnp.sum(shifted, axis=1, keepdims=True)).astype(bf16)
            outs.append(dot(probs, held))
        attended_ref[:, at : at + 2 * head_dim] = jnp.where(lane < head_dim, outs[0], outs[1]).astype(bf16)
    own_copy.wait()
    for k, r in others:
        spread_copy(k, r).wait_recv()
    y_copy.start()
    gather_done([2])
    middle = values + dot(attended_ref[...], w_proj_all[...]) + vectors[2:3]
    middle_ref[...] = middle
    normal_mid, _ = norm_parts(middle)
    normed = normal_mid * vectors[3:4] + vectors[4:5]
    row = lax.broadcasted_iota(jnp.int32, normed.shape, 0)
    packed_ref[:, :width] = jnp.where(row < real, normed, 0.0).astype(bf16)
    from_y.wait_recv()
    y_copy.wait_send()
    for k, r in others:
        spread_copy(k, r).wait_send()
    for j in range(3):
        for level in range(planes):
            x_copy(j, level, x).wait_send()
            c_copy(j, level, 1 - x).wait_send()

            @pl.when(level != z)
            def _():
                c_copy(j, level, x).wait_send()

            @pl.when((z >= level) & (z < planes - 1))
            def _():
                up_copy(j, level).wait_send()

            @pl.when((z <= level) & (z > 0))
            def _():
                down_copy(j, level).wait_send()


def front(planes, rows, tokens, mask, ids, cotangent, vectors, router, outer_bias, w_qkv, w_proj, w_in):
    f32, bf16 = jnp.float32, jnp.bfloat16
    real, width = tokens.shape
    lanes = w_in.shape[2] // (2 * planes)
    shape = jax.ShapeDtypeStruct
    vmem = pl.BlockSpec(memory_space=pltpu.VMEM)
    dma = pltpu.SemaphoreType.DMA
    return pl.pallas_call(
        functools.partial(front_kernel, planes, HEADS, real),
        out_shape=[
            shape((width, 128), bf16),
            shape((width, 3 * width), bf16),
            shape((width, width), bf16),
            shape((width, 2 * lanes), bf16),
            shape((rows, width), bf16),
            shape((rows, 3 * width), bf16),
            shape((rows, width), bf16),
            shape((rows, width), f32),
            shape((rows, 2 * width), bf16),
            shape((rows, width), bf16),
            shape((rows, 128), bf16),
            shape((1, rows), f32),
            shape((rows, 1), f32),
        ],
        in_specs=[vmem] * (6 + len(vectors)) + [vmem] * 2 + [pl.BlockSpec(memory_space=pl.ANY)],
        out_specs=[vmem] * 13,
        scratch_shapes=[dma((3, planes))] * 6
        + [dma((3, 2 * planes))] * 2
        + [dma((planes, 2))] * 2
        + [dma] * 3,
        compiler_params=pltpu.CompilerParams(
            collective_id=2, has_side_effects=True, vmem_limit_bytes=60 * 2**20
        ),
        cost_estimate=pl.CostEstimate(flops=2**32, bytes_accessed=40 * 2**20, transcendentals=0),
        name="dense_weights_and_attention",
    )(tokens, mask, ids, cotangent, *vectors, router, outer_bias, w_qkv, w_proj, w_in)


def back_kernel(planes, heads, own, groups, real, *refs):
    (
        row_grad_ref,
        packed_ref,
        middle_ref,
        tokens_ref,
        normed_in_ref,
        qkv_ref,
        attended_ref,
        small_ref,
        w_qkv_ref,
        w_proj_ref,
        keys_ref,
        keep_ref,
        select_ref,
        mix_ref,
        inner_ref,
        outer_ref,
        bias_ref,
        router_grad_ref,
    ) = refs[:18]
    mixed_ref, token_grad_ref, qkv_out, proj_out, small_out, inner_out, outer_out, bias_out = refs[18:26]
    refs = refs[26:]
    (
        grad_attended,
        grad_qkv,
        mix_x,
        mix_z,
        mix_from_core,
        mix_from_x,
        mix_from_z,
        inner_from_y,
        inner_sum,
        outer_from_y,
        bias_from_y,
        held,
        held_small,
        from_core,
        from_core_small,
        from_x,
        from_x_small,
        from_z,
        from_z_small,
        plane_sum,
        plane_sum_small,
        from_y,
        from_y_small,
        final,
        final_small,
    ) = refs[:25]
    (
        mix_c_sem,
        mix_x_send,
        mix_x_recv,
        mix_z_send,
        mix_z_recv,
        inner_y_sem,
        spread_send,
        spread_recv,
        inner_back_sem,
        inner_core_sem,
        outer_y_sem,
        outer_c_sem,
        bias_y_sem,
        bias_c_sem,
        own_sem,
        flow_c_sem,
        flow_x_sem,
        flow_z_send,
        flow_z_recv,
        flow_y_sem,
        flow_end_sem,
    ) = refs[25:]
    f32, bf16 = jnp.float32, jnp.bfloat16
    place = Place(planes)
    y, c, z, x = place.y, place.c, place.z, place.x
    rows, width = middle_ref.shape
    depth = width // (2 * planes)
    half = depth // 2
    lanes = inner_ref.shape[1] // own
    head_dim = width // heads
    pair_width = 2 * head_dim
    small_at = groups + 1

    def remote(src, dst, send, recv, device):
        return pltpu.make_async_remote_copy(
            src_ref=src, dst_ref=dst, send_sem=send, recv_sem=recv, device_id=device, device_id_type=MESH
        )

    def swap(src, dst, sem, device):
        return remote(src, dst, sem.at[0], sem.at[1], device)

    def of_flow(j, many, alone):
        return alone if j == small_at else many.at[j]

    mine, theirs = pl.ds(pl.multiple_of(c * half, 16), half), pl.ds(pl.multiple_of((1 - c) * half, 16), half)

    def flow_c(j):
        source = of_flow(j, held, held_small)
        return swap(
            source.at[:, :, theirs], of_flow(j, from_core, from_core_small), flow_c_sem.at[j], place.other_core()
        )

    def flow_x(j):
        source = of_flow(j, held, held_small)
        return swap(source.at[:, 1 - x, mine], of_flow(j, from_x, from_x_small), flow_x_sem.at[j], place.other_x())

    def flow_z(j, k):
        level = lax.rem(z + k, planes)
        source = of_flow(j, held, held_small)
        return remote(
            source.at[level, x, mine],
            of_flow(j, from_z, from_z_small).at[k],
            flow_z_send.at[j, k],
            flow_z_recv.at[j, k],
            place.level(k),
        )

    def flow_y(j):
        return swap(
            of_flow(j, plane_sum, plane_sum_small),
            of_flow(j, from_y, from_y_small),
            flow_y_sem.at[j],
            place.other_y(),
        )

    def flow_end(j):
        here = of_flow(j, final, final_small).at[mine]
        return swap(here, here, flow_end_sem.at[j], place.other_core())

    def flow_core_sum(j):
        flow_c(j).wait_recv()
        kept = of_flow(j, held, held_small)
        total = kept[:, :, mine, :].astype(f32) + of_flow(j, from_core, from_core_small)[...].astype(f32)
        kept[:, :, mine, :] = total.astype(bf16)
        flow_x(j).start()

    def flow_x_sum(j):
        flow_x(j).wait_recv()
        kept = of_flow(j, held, held_small)
        total = kept[:, x, mine, :].astype(f32) + of_flow(j, from_x, from_x_small)[...].astype(f32)
        kept[:, x, mine, :] = total.astype(bf16)
        for k in range(1, planes):
            flow_z(j, k).start()

    def flow_z_sum(j):
        kept = of_flow(j, held, held_small)
        total = kept[z, x, mine, :].astype(f32)
        for k in range(1, planes):
            flow_z(j, k).wait_recv()
            total = total + of_flow(j, from_z, from_z_small)[k].astype(f32)
        of_flow(j, plane_sum, plane_sum_small)[...] = total.astype(bf16)
        flow_y(j).start()

    def flow_y_sum(j):
        flow_y(j).wait_recv()
        total = of_flow(j, plane_sum, plane_sum_small)[...].astype(f32)
        total = total + of_flow(j, from_y, from_y_small)[...].astype(f32)
        of_flow(j, final, final_small)[mine, :] = total.astype(bf16)
        flow_end(j).start()

    def mix_c():
        return swap(mix_ref.at[:, pl.ds(2 * rows, 2 * rows)], mix_from_core, mix_c_sem, place.other_core())

    def mix_to_x(level):
        return remote(mix_x.at[level], mix_from_x.at[level], mix_x_send.at[level], mix_x_recv.at[level], place.other_x())

    def mix_to_z(level, source):
        return remote(
            mix_z.at[level], mix_from_z.at[source], mix_z_send.at[level], mix_z_recv.at[source], place.at(y, c, level, x)
        )

    def mix_core_sum():
        mix_c().wait_recv()
        for k in range(1, planes + 1):
            level = lax.rem(z + k, planes)
            total = mix_ref[level, rows : 2 * rows, :].astype(f32) + mix_from_core[level, rows:, :].astype(f32)
            mix_x[level] = total.astype(bf16)
            mix_to_x(level).start()
        for level in range(planes):
            total = mix_ref[level, :rows, :].astype(f32) + mix_from_core[level, :rows, :].astype(f32)
            mix_z[level] = total.astype(bf16)

    def mix_x_sum(k):
        level = lax.rem(z + k, planes)
        mix_to_x(level).wait_recv()
        mix_z[level] = (mix_z[level].astype(f32) + mix_from_x[level].astype(f32)).astype(bf16)
        if k < planes:
            mix_to_z(level, z).start()

    my_units = pl.ds(pl.multiple_of(y * lanes, 128), lanes)
    their_units = pl.ds(pl.multiple_of((1 - y) * lanes, 128), lanes)
    my_expert, their_expert = c * 2 + y, c * 2 + 1 - y
    my_columns = pl.ds(pl.multiple_of((z * 2 + x) * lanes, 128), lanes)

    def inner_y():
        return swap(inner_ref.at[:, their_units], inner_from_y, inner_y_sem, place.other_y())

    def shard_rows(f):
        return pl.ds(pl.multiple_of(f * depth, 16), depth)

    def spread(k, r):
        level, across = lax.rem(z + k, planes), (x + r) % 2
        return remote(
            inner_sum.at[shard_rows(level * 2 + across)],
            inner_out.at[my_expert, :, my_columns],
            spread_send.at[k, r],
            spread_recv.at[k, r],
            place.at(y, c, level, across),
        )

    own_copy = pltpu.make_async_copy(
        inner_sum.at[shard_rows(z * 2 + x)], inner_out.at[my_expert, :, my_columns], own_sem
    )

    def inner_back():
        here = inner_out.at[my_expert]
        return swap(here, here, inner_back_sem, place.other_y())

    def inner_core(expert, at):
        here = inner_out.at[expert]
        return swap(here, here, inner_core_sem.at[at], place.other_core())

    def outer_y():
        return swap(outer_ref, outer_from_y, outer_y_sem, place.other_y())

    def outer_c():
        here = outer_out.at[c]
        return swap(here, here, outer_c_sem, place.other_core())

    def bias_y():
        return swap(bias_ref, bias_from_y, bias_y_sem, place.other_y())

    def bias_c():
        here = bias_out.at[c]
        return swap(here, here, bias_c_sem, place.other_core())

    others = [(k, r) for k in range(planes) for r in range(2) if k or r]

    def inner_y_sum():
        inner_y().wait_recv()
        total = inner_ref[:, my_units].astype(f32) + inner_from_y[...].astype(f32)
        inner_sum[...] = total.astype(bf16)
        own_copy.start()
        for k, r in others:
            spread(k, r).start()
        outer_y().start()

    def inner_spread_done():
        own_copy.wait()
        for k, r in others:
            spread(k, r).wait_recv()
        inner_back().start()
        inner_core(my_expert, 0).start()

    def outer_y_sum():
        outer_y().wait_recv()
        total = outer_ref[...].astype(f32) + outer_from_y[...].astype(f32)
        outer_out[c] = total.astype(bf16)
        outer_c().start()
        bias_y().wait_recv()
        bias_out[c] = bias_ref[...] + bias_from_y[...]
        bias_c().start()

    partners = [place.other_core(), place.other_y()]
    partners += [place.at(y, c, lax.rem(z + k, planes), (x + r) % 2) for k, r in others]
    greet(partners)
    inner_y().start()
    bias_y().start()
    mix_c().start()

    vectors = jnp.transpose(small_ref[...].astype(f32))
    gain_first, gain_second = vectors[0:1], vectors[3:4]
    place_row = lax.broadcasted_iota(jnp.int32, (128, 128), 0)
    place_lane = lax.broadcasted_iota(jnp.int32, (128, 128), 1)

    def lanes_from(first):
        take = (place_row == place_lane + first) & (place_lane < 2 * own)
        return dot(small_ref[...], take.astype(bf16)).astype(bf16)

    outer_bias, router = lanes_from(5), lanes_from(5 + 2 * own)
    normed_mid, grad_out = packed_ref[:, :width], packed_ref[:, width:]
    real_row = lax.broadcasted_iota(jnp.int32, grad_out.shape, 0) < real
    grad_out = jnp.where(real_row, grad_out, 0).astype(bf16)
    select = select_ref[...].astype(f32)
    lane = lax.broadcasted_iota(jnp.int32, select.shape, 1)
    logits = jnp.where(lane < 2 * own, dot(normed_mid, router), -1e30)
    routing = jnp.exp(logits - jnp.max(logits, axis=1, keepdims=True))
    routing = routing / jnp.sum(routing, axis=1, keepdims=True)
    gates = routing * select
    bias_gate = select * dot(grad_out, outer_bias)
    bias_logits = routing * (bias_gate - jnp.sum(routing * bias_gate, axis=1, keepdims=True))
    bias_logits = bias_logits.astype(bf16)
    router_grad = lax.dot_general(normed_mid, bias_logits, TN, preferred_element_type=f32)
    router_grad = pltpu.roll(router_grad, 16, 1) + pltpu.roll(router_grad_ref[...], 16 - real % 16, 1)
    outer_bias_grad = lax.dot_general(gates.astype(bf16), grad_out, TN, preferred_element_type=f32)
    grad_normed_mid = row_grad_ref[...] + lax.dot_general(bias_logits, router, NT, preferred_element_type=f32)
    normal_mid, rstd_mid = norm_parts(middle_ref[...])
    gain_second_grad = jnp.sum(grad_normed_mid * normal_mid, axis=0, keepdims=True)
    bias_second_grad = jnp.sum(grad_normed_mid, axis=0, keepdims=True)
    grad_middle = grad_out.astype(f32) + norm_back(grad_normed_mid, normal_mid, rstd_mid, gain_second)
    grad_proj = grad_middle.astype(bf16)
    proj_bias_grad = jnp.sum(grad_proj.astype(f32), axis=0, keepdims=True)
    mix_core_sum()

    def hold(j, value):
        held[j] = value.astype(bf16).reshape(planes, 2, depth, width)
        flow_c(j).start()

    hold(0, lax.dot_general(attended_ref[...], grad_proj, TN, preferred_element_type=f32))
    grad_attended[...] = lax.dot_general(grad_proj, w_proj_ref[...], NT, preferred_element_type=f32).astype(bf16)
    flow_core_sum(0)

    pair_lane = lax.broadcasted_iota(jnp.int32, (rows, pair_width), 1)
    usable = keys_ref[...] > 0
    scaling = head_dim ** (-0.5)
    group_width = width // groups

    def pair_back(pair):
        at = pair * pair_width
        group, inside = at // group_width, at % group_width
        queries = qkv_ref[:, at : at + pair_width]
        keys = qkv_ref[:, width + at : width + at + pair_width]
        values = qkv_ref[:, 2 * width + at : 2 * width + at + pair_width]
        grads = grad_attended[:, at : at + pair_width]
        found = []
        for side in range(2):
            only = (pair_lane < head_dim) if side == 0 else (pair_lane >= head_dim)
            some_queries = jnp.where(only, queries, 0).astype(bf16)
            some_grads = jnp.where(only, grads, 0).astype(bf16)
            scores = lax.dot_general(some_queries, keys, NT, preferred_element_type=f32)
            scores = jnp.where(usable, scores * scaling, masked_score)
            shifted = jnp.exp(scores - jnp.max(scores, axis=1, keepdims=True))
            probs = shifted / jnp.sum(shifted, axis=1, keepdims=True)
            grad_probs = lax.dot_general(some_grads, values, NT, preferred_element_type=f32)
            grad_scores = probs * (grad_probs - jnp.sum(probs * grad_probs, axis=1, keepdims=True))
            grad_scores = grad_scores.astype(bf16)
            found.append(
                (
                    dot(grad_scores, keys),
                    lax.dot_general(grad_scores, some_queries, TN, preferred_element_type=f32),
                    lax.dot_general(probs.astype(bf16), some_grads, TN, preferred_element_type=f32),
                )
            )
        grad_queries = jnp.where(pair_lane < head_dim, found[0][0], found[1][0]) * scaling
        grad_keys = (found[0][1] + found[1][1]) * scaling
        grad_values = found[0][2] + found[1][2]
        for part, value in enumerate((grad_queries, grad_keys, grad_values)):
            start = part * group_width + inside
            grad_qkv[group, :, start : start + pair_width] = value.astype(bf16)

    def group_back(group):
        per_group = heads // 2 // groups
        for pair in range(group * per_group, (group + 1) * per_group):
            pair_back(pair)
        hold(
            1 + group,
            lax.dot_general(normed_in_ref[...], grad_qkv[group], TN, preferred_element_type=f32),
        )

    group_back(0)
    inner_y_sum()
    flow_core_sum(1)
    mix_x_sum(1)
    for group in range(1, groups):
        group_back(group)
        flow_core_sum(1 + group)
        if group == 1:
            mix_x_sum(2)

    grad_normed_in = jnp.zeros((rows, width), f32)
    for group in range(groups):
        for part in range(3):
            grad_normed_in = grad_normed_in + lax.dot_general(
                grad_qkv[group, :, part * group_width : (part + 1) * group_width],
                w_qkv_ref[:, part * width + group * group_width : part * width + (group + 1) * group_width],
                NT,
                preferred_element_type=f32,
            )
    normal_first, rstd_first = norm_parts(tokens_ref[...].astype(f32))
    gain_first_grad = jnp.sum(grad_normed_in * normal_first, axis=0, keepdims=True)
    bias_first_grad = jnp.sum(grad_normed_in, axis=0, keepdims=True)
    token_grad = grad_middle + norm_back(grad_normed_in, normal_first, rstd_first, gain_first)
    token_grad_ref[...] = token_grad.astype(bf16)[:real]
    vector_rows = jnp.concatenate(
        [
            gain_first_grad,
            bias_first_grad,
            proj_bias_grad,
            gain_second_grad,
            bias_second_grad,
            jnp.zeros((3, width), f32),
            outer_bias_grad[:8],
            jnp.zeros((112, width), f32),
        ],
        axis=0,
    )
    vector_grads = jnp.transpose(vector_rows) + router_grad
    held_small[...] = vector_grads.astype(bf16).reshape(planes, 2, depth, 128)
    flow_c(small_at).start()
    flow_core_sum(small_at)
    for k in range(3, planes):
        mix_x_sum(k)
    inner_spread_done()
    flow_x_sum(0)
    flow_x_sum(1)
    mix_x_sum(planes)
    outer_y_sum()
    for group in range(1, groups):
        flow_x_sum(1 + group)
    flow_z_sum(0)
    flow_x_sum(small_at)
    mixture = mix_z[z].astype(f32) + dot(gates.astype(bf16), jnp.transpose(outer_bias.astype(f32)).astype(bf16))
    for k in range(1, planes):
        source = lax.rem(z + k, planes)
        mix_to_z(z, source).wait_recv()
        mixture = mixture + mix_from_z[source].astype(f32)
    mixed = (keep_ref[...] * (middle_ref[...] + mixture)).astype(bf16)
    mixed_ref[...] = mixed[:real]
    flow_y_sum(0)
    for group in range(groups):
        flow_z_sum(1 + group)
    flow_z_sum(small_at)
    inner_back().wait_recv()
    inner_core(their_expert, 1).start()
    for group in range(groups):
        flow_y_sum(1 + group)
    flow_y_sum(small_at)

    def arrived(j):
        here = of_flow(j, final, final_small).at[theirs]
        swap(here, here, flow_end_sem.at[j], place.other_core()).wait_recv()

    arrived(0)
    proj_out[...] = final[0]
    for group in range(groups):
        arrived(1 + group)
        for part in range(3):
            start = part * width + group * group_width
            qkv_out[:, start : start + group_width] = final[
                1 + group, :, part * group_width : (part + 1) * group_width
            ]
    arrived(small_at)
    small_out[...] = final_small[...].astype(f32)
    outer_theirs = outer_out.at[1 - c]
    swap(outer_theirs, outer_theirs, outer_c_sem, place.other_core()).wait_recv()
    bias_theirs = bias_out.at[1 - c]
    swap(bias_theirs, bias_theirs, bias_c_sem, place.other_core()).wait_recv()
    for at, expert in enumerate(((1 - c) * 2 + y, (1 - c) * 2 + 1 - y)):
        inner_core(expert, at).wait_recv()

    mix_c().wait_send()
    inner_y().wait_send()
    inner_back().wait_send()
    inner_core(my_expert, 0).wait_send()
    inner_core(their_expert, 1).wait_send()
    outer_y().wait_send()
    outer_c().wait_send()
    bias_y().wait_send()
    bias_c().wait_send()
    for k, r in others:
        spread(k, r).wait_send()
    for k in range(1, planes + 1):
        level = lax.rem(z + k, planes)
        mix_to_x(level).wait_send()
        if k < planes:
            mix_to_z(level, z).wait_send()
    for j in range(groups + 2):
        flow_c(j).wait_send()
        flow_x(j).wait_send()
        for k in range(1, planes):
            flow_z(j, k).wait_send()
        flow_y(j).wait_send()
        flow_end(j).wait_send()


def back(planes, own, real, *args):
    f32, bf16 = jnp.float32, jnp.bfloat16
    (
        row_grad,
        packed,
        middle,
        tokens,
        normed_in,
        qkv,
        attended,
        small,
        w_qkv,
        w_proj,
        keys,
        keep,
        select,
        mix_parts,
        inner_grad,
        outer_grad,
        bias_grad,
        router_grad,
    ) = args
    rows, width = middle.shape
    depth = width // (2 * planes)
    half = depth // 2
    lanes = inner_grad.shape[1] // own
    tall = outer_grad.shape[0]
    pairs = HEADS // 2
    groups = 3 if pairs % 3 == 0 and (pairs // 3) * 2 * (width // HEADS) % 128 == 0 else 1
    flows = groups + 1
    shape = jax.ShapeDtypeStruct
    vmem = pl.BlockSpec(memory_space=pltpu.VMEM)
    dma = pltpu.SemaphoreType.DMA

    def both(*dims):
        return [pltpu.VMEM((flows, *dims, width), bf16), pltpu.VMEM((*dims, 128), bf16)]

    return pl.pallas_call(
        functools.partial(back_kernel, planes, HEADS, own, groups, real),
        out_shape=[
            shape((real, width), bf16),
            shape((real, width), bf16),
            shape((depth, 3 * width), bf16),
            shape((depth, width), bf16),
            shape((depth, 128), f32),
            shape((2 * own, depth, 2 * planes * lanes), bf16),
            shape((2, tall, width), bf16),
            shape((2, *bias_grad.shape), f32),
        ],
        in_specs=[vmem] * 18,
        out_specs=[vmem] * 8,
        scratch_shapes=[
            pltpu.VMEM((rows, width), bf16),
            pltpu.VMEM((groups, rows, 3 * width // groups), bf16),
            pltpu.VMEM((planes, rows, width), bf16),
            pltpu.VMEM((planes, rows, width), bf16),
            pltpu.VMEM((planes, 2 * rows, width), bf16),
            pltpu.VMEM((planes, rows, width), bf16),
            pltpu.VMEM((planes, rows, width), bf16),
            pltpu.VMEM((width, lanes), bf16),
            pltpu.VMEM((width, lanes), bf16),
            pltpu.VMEM((tall, width), bf16),
            pltpu.VMEM(bias_grad.shape, f32),
        ]
        + both(planes, 2, depth)
        + both(planes, 2, half)
        + both(planes, half)
        + both(planes, half)
        + both(half)
        + both(half)
        + both(depth)
        + [dma((2,))]
        + [dma((planes,))] * 4
        + [dma((2,))]
        + [dma((planes, 2))] * 2
        + [dma((2,)), dma((2, 2)), dma((2,)), dma((2,)), dma((2,)), dma((2,)), dma]
        + [dma((flows + 1, 2))] * 2
        + [dma((flows + 1, planes))] * 2
        + [dma((flows + 1, 2))] * 2,
        compiler_params=pltpu.CompilerParams(
            collective_id=3, has_side_effects=True, vmem_limit_bytes=60 * 2**20
        ),
        cost_estimate=pl.CostEstimate(flops=2**33, bytes_accessed=40 * 2**20, transcendentals=0),
        name="attention_backward_and_sums",
    )(*args)


def norm_parts(values):
    center = values - jnp.mean(values, axis=-1, keepdims=True)
    rstd = lax.rsqrt(jnp.mean(center * center, axis=-1, keepdims=True) + epsilon)
    return center * rstd, rstd


def norm_back(grad, normal, rstd, gain):
    scaled = grad * gain
    return rstd * (
        scaled
        - jnp.mean(scaled, axis=-1, keepdims=True)
        - normal * jnp.mean(scaled * normal, axis=-1, keepdims=True)
    )


def move_tokens_plan(
    tokens,
    key_mask,
    expert_ids,
    cotangent,
    norm1_gain,
    norm1_bias,
    w_qkv,
    w_proj,
    proj_bias,
    norm2_gain,
    norm2_bias,
    w_router,
    w_in,
    b_in,
    w_out,
    b_out,
):
    f32 = jnp.float32
    _, rows, width = tokens.shape
    experts, depth, hidden = w_in.shape
    slice_width = w_out.shape[1]
    planes = hidden // slice_width // 2
    own = experts // 2
    padded = (rows + experts + 15) // 16 * 16
    vectors = [v[None] for v in (norm1_gain, norm1_bias, proj_bias, norm2_gain, norm2_bias)]
    small, full_qkv, full_proj, inner, normed_in, qkv, attended, middle, packed, wide, select, keys, keep = front(
        planes,
        padded,
        tokens[0],
        key_mask,
        expert_ids[0],
        cotangent[0],
        vectors,
        w_router,
        b_out,
        w_qkv,
        w_proj,
        w_in,
    )
    mix_parts, row_grad, inner_grad, outer_grad, bias_grad, router_grad = experts_of_the_plane(
        planes, own, rows, packed, inner, w_out, b_in, small
    )
    mixed, token_grad, qkv_grad, proj_grad, vector_grads, inner_grad, outer_grad, bias_grad = back(
        planes,
        own,
        rows,
        row_grad,
        packed,
        middle,
        wide,
        normed_in,
        qkv,
        attended,
        small,
        full_qkv,
        full_proj,
        keys,
        keep,
        select,
        mix_parts,
        inner_grad,
        outer_grad,
        bias_grad,
        router_grad,
    )
    return (
        mixed[None],
        token_grad[None],
        vector_grads[:, 0],
        vector_grads[:, 1],
        qkv_grad.astype(f32),
        proj_grad.astype(f32),
        vector_grads[:, 2],
        vector_grads[:, 3],
        vector_grads[:, 4],
        vector_grads[:, 16 : 16 + experts],
        inner_grad.astype(f32),
        bias_grad[:, 0].reshape(experts, slice_width),
        outer_grad.reshape(experts, slice_width, width).astype(f32),
        vector_grads[:, 8 : 8 + experts].T,
    )


def solution(mesh):
    n_seq, n_fsdp = mesh.shape["seq"], mesh.shape["fsdp"]

    def per_device(*args):
        tokens, w_in, w_out = args[0], args[12], args[14]
        experts, _, hidden = w_in.shape
        lanes = hidden // n_fsdp
        whole_tiles = lanes % 128 == 0 and w_in.shape[1] % 32 == 0 and 2 * lanes <= tokens.shape[2]
        if n_seq == 4 and experts == n_seq and tokens.shape[0] == 1 and whole_tiles:
            return move_tokens_plan(*args)
        return gather_weights_plan(*args)

    return jax.shard_map(
        per_device,
        mesh=mesh,
        in_specs=(
            P(("fsdp", "seq"), None, None),
            P("fsdp", None),
            P(("fsdp", "seq"), None, None),
            P(("fsdp", "seq"), None, None),
            P("fsdp"),
            P("fsdp"),
            P("fsdp", None),
            P("fsdp", None),
            P("fsdp"),
            P("fsdp"),
            P("fsdp"),
            P("fsdp", None),
            P(None, "fsdp", None),
            P(None, "fsdp"),
            P(None, "fsdp", None),
            P(None, "fsdp"),
        ),
        out_specs=(
            P(("fsdp", "seq"), None, None),
            P(("fsdp", "seq"), None, None),
            P("fsdp"),
            P("fsdp"),
            P("fsdp", None),
            P("fsdp", None),
            P("fsdp"),
            P("fsdp"),
            P("fsdp"),
            P("fsdp", None),
            P(None, "fsdp", None),
            P(None, "fsdp"),
            P(None, "fsdp", None),
            P(None, "fsdp"),
        ),
        check_vma=False,
    )
```

```python
import functools

import jax
import jax.numpy as jnp
from jax import lax
from jax.experimental import pallas as pl
from jax.experimental.pallas import tpu as pltpu
from jax.sharding import PartitionSpec as P

HEADS = 12
CAP = 142


epsilon = 1e-06
masked_score = -1e30


def norm_rows(values, gain, offset):
    center = values - jnp.mean(values, axis=-1, keepdims=True)
    spread = jnp.mean(center * center, axis=-1, keepdims=True)
    return center * lax.rsqrt(spread + epsilon) * gain + offset


def softmax_rows(values):
    shifted = jnp.exp(values - jnp.max(values, axis=-1, keepdims=True))
    return shifted / jnp.sum(shifted, axis=-1, keepdims=True)


def exact_gelu(values):
    return jax.nn.gelu(values, approximate=False)


def expert_slots(chosen, experts):
    flat_ids = chosen.reshape(-1)
    onehot = (flat_ids[:, None] == jnp.arange(experts, dtype=jnp.int32)[None, :]).astype(jnp.int32)
    ranks = jnp.cumsum(onehot, axis=0, dtype=jnp.int32)
    slot_pos = jnp.sum(onehot * ranks, axis=1, dtype=jnp.int32) - 1
    return (flat_ids, slot_pos)


def gather_weights_plan(
    tokens,
    key_mask,
    expert_ids,
    cotangent,
    norm1_gain,
    norm1_bias,
    w_qkv,
    w_proj,
    proj_bias,
    norm2_gain,
    norm2_bias,
    w_router,
    w_in,
    b_in,
    w_out,
    b_out,
):
    images, seq_len, width = tokens.shape
    experts = w_in.shape[0]
    head_dim = width // HEADS
    scaling = head_dim ** (-0.5)
    row_count = images * seq_len
    dense_set = (
        lax.all_gather(norm1_gain, "fsdp", axis=0, tiled=True),
        lax.all_gather(norm1_bias, "fsdp", axis=0, tiled=True),
        lax.all_gather(w_qkv, "fsdp", axis=0, tiled=True),
        lax.all_gather(w_proj, "fsdp", axis=0, tiled=True),
        lax.all_gather(proj_bias, "fsdp", axis=0, tiled=True),
        lax.all_gather(norm2_gain, "fsdp", axis=0, tiled=True),
        lax.all_gather(norm2_bias, "fsdp", axis=0, tiled=True),
        lax.all_gather(w_router, "fsdp", axis=0, tiled=True),
    )
    gain_first = dense_set[0].astype(jnp.float32)
    bias_first = dense_set[1].astype(jnp.float32)
    full_qkv = dense_set[2]
    full_proj = dense_set[3]
    bias_proj = dense_set[4].astype(jnp.float32)
    gain_second = dense_set[5].astype(jnp.float32)
    bias_second = dense_set[6].astype(jnp.float32)
    full_router = dense_set[7]
    expert_set = (
        lax.all_gather(w_in, "fsdp", axis=1, tiled=True),
        lax.all_gather(b_in, "fsdp", axis=1, tiled=True),
        lax.all_gather(w_out, "fsdp", axis=1, tiled=True),
        lax.all_gather(b_out, "fsdp", axis=1, tiled=True),
    )
    inner_weight = expert_set[0]
    inner_bias = expert_set[1].astype(jnp.float32)
    outer_weight = expert_set[2]
    outer_bias = expert_set[3].astype(jnp.float32)
    own_mask = lax.dynamic_slice_in_dim(key_mask, lax.axis_index("seq") * images, images, 0)
    keep_rows = own_mask.reshape(row_count, 1).astype(jnp.float32)
    usable = (key_mask > 0)[:, None, None, :]
    flat_tokens = tokens.astype(jnp.float32).reshape(row_count, width)
    normed_in = norm_rows(flat_tokens, gain_first, bias_first).astype(jnp.bfloat16)
    mixed_qkv = jnp.dot(normed_in, full_qkv, preferred_element_type=jnp.float32).astype(
        jnp.bfloat16
    )
    mixed_qkv = mixed_qkv.reshape(images, seq_len, 3, HEADS, head_dim)
    head_qkv = lax.all_to_all(mixed_qkv, "seq", split_axis=3, concat_axis=0, tiled=True)
    queries = head_qkv[:, :, 0]
    key_rows = head_qkv[:, :, 1]
    value_rows = head_qkv[:, :, 2]

    def score_block():
        raw = (
            jnp.einsum("gahd,gbhd->ghab", queries, key_rows, preferred_element_type=jnp.float32)
            * scaling
        )
        return jnp.where(usable, raw, masked_score)

    scores = score_block()
    row_top = jnp.max(scores, axis=-1, keepdims=True)
    shifted = jnp.exp(scores - row_top)
    row_total = jnp.sum(shifted, axis=-1, keepdims=True)
    attn_probs = (shifted / row_total).astype(jnp.bfloat16)
    log_total = row_top + jnp.log(row_total)
    head_out = jnp.einsum(
        "ghab,gbhd->gahd", attn_probs, value_rows, preferred_element_type=jnp.float32
    ).astype(jnp.bfloat16)
    attended = lax.all_to_all(head_out, "seq", split_axis=0, concat_axis=2, tiled=True).reshape(
        row_count, width
    )
    middle = (
        flat_tokens + jnp.dot(attended, full_proj, preferred_element_type=jnp.float32) + bias_proj
    )
    normed_mid = norm_rows(middle, gain_second, bias_second).astype(jnp.bfloat16)
    routing = softmax_rows(jnp.dot(normed_mid, full_router, preferred_element_type=jnp.float32))
    chosen = expert_ids.reshape(row_count, 2)
    flat_ids, slot_pos = expert_slots(chosen, experts)
    gating = jnp.take_along_axis(routing, chosen, axis=1)
    buffer = (
        jnp.zeros((experts, CAP, width), jnp.bfloat16)
        .at[flat_ids, slot_pos]
        .set(jnp.repeat(normed_mid, 2, axis=0))
    )
    pre_act = (
        jnp.einsum("ecd,edf->ecf", buffer, inner_weight, preferred_element_type=jnp.float32)
        + inner_bias[:, None, :]
    )
    activated = exact_gelu(pre_act).astype(jnp.bfloat16)
    expert_out = (
        jnp.einsum("ecf,efd->ecd", activated, outer_weight, preferred_element_type=jnp.float32)
        + outer_bias[:, None, :]
    )
    picked = expert_out[flat_ids, slot_pos].reshape(row_count, 2, width)
    mixture = jnp.sum(gating[:, :, None] * picked, axis=1)
    mixed = (keep_rows * (middle + mixture)).astype(jnp.bfloat16).reshape(images, seq_len, width)
    grad_out = cotangent.astype(jnp.float32).reshape(row_count, width) * keep_rows
    grad_gate = jnp.sum(grad_out[:, None, :] * picked, axis=2)
    grad_picked = (
        (gating[:, :, None] * grad_out[:, None, :])
        .astype(jnp.bfloat16)
        .reshape(2 * row_count, width)
    )
    grad_expert_out = (
        jnp.zeros((experts, CAP, width), jnp.bfloat16).at[flat_ids, slot_pos].set(grad_picked)
    )
    grad_outer_bias = jnp.sum(grad_expert_out, axis=1, dtype=jnp.float32)
    hidden_pre = (
        jnp.einsum("ecd,edf->ecf", buffer, inner_weight, preferred_element_type=jnp.float32)
        + inner_bias[:, None, :]
    )
    hidden_act = exact_gelu(hidden_pre).astype(jnp.bfloat16)
    grad_outer_weight = jnp.einsum(
        "ecf,ecd->efd", hidden_act, grad_expert_out, preferred_element_type=jnp.float32
    )
    grad_act = jnp.einsum(
        "ecd,efd->ecf", grad_expert_out, outer_weight, preferred_element_type=jnp.float32
    )
    gelu_pull = jax.vjp(exact_gelu, hidden_pre)[1]
    grad_pre = gelu_pull(grad_act)[0].astype(jnp.bfloat16)
    grad_inner_bias = jnp.sum(grad_pre, axis=1, dtype=jnp.float32)
    grad_inner_weight = jnp.einsum(
        "ecd,ecf->edf", buffer, grad_pre, preferred_element_type=jnp.float32
    )
    grad_buffer = jnp.einsum(
        "ecf,edf->ecd", grad_pre, inner_weight, preferred_element_type=jnp.float32
    )
    grad_rows = jnp.sum(grad_buffer[flat_ids, slot_pos].reshape(row_count, 2, width), axis=1)
    expert_range = jnp.arange(experts, dtype=jnp.int32)[None, None, :]
    grad_route = jnp.sum(
        grad_gate[:, :, None] * (chosen[:, :, None] == expert_range).astype(jnp.float32), axis=1
    )
    grad_logits = (
        routing * (grad_route - jnp.sum(routing * grad_route, axis=-1, keepdims=True))
    ).astype(jnp.bfloat16)
    grad_router = jnp.einsum(
        "nd,ne->de", normed_mid, grad_logits, preferred_element_type=jnp.float32
    )
    grad_normed_mid = grad_rows + jnp.einsum(
        "ne,de->nd", grad_logits, full_router, preferred_element_type=jnp.float32
    )
    second_pull = jax.vjp(norm_rows, middle, gain_second, bias_second)[1]
    grad_mid_norm, grad_gain_second, grad_bias_second = second_pull(grad_normed_mid)
    grad_middle = grad_out + grad_mid_norm
    grad_proj = grad_middle.astype(jnp.bfloat16)
    grad_bias_proj = jnp.sum(grad_proj, axis=0, dtype=jnp.float32)
    grad_proj_weight = jnp.einsum(
        "nd,ne->de", attended, grad_proj, preferred_element_type=jnp.float32
    )
    grad_attended = jnp.einsum(
        "ne,de->nd", grad_proj, full_proj, preferred_element_type=jnp.float32
    ).astype(jnp.bfloat16)
    grad_head_out = lax.all_to_all(
        grad_attended.reshape(images, seq_len, HEADS, head_dim),
        "seq",
        split_axis=2,
        concat_axis=0,
        tiled=True,
    )
    recomputed = jnp.exp(score_block() - log_total)
    grad_values = jnp.einsum(
        "ghab,gahd->gbhd",
        recomputed.astype(jnp.bfloat16),
        grad_head_out,
        preferred_element_type=jnp.float32,
    )
    grad_probs = jnp.einsum(
        "gahd,gbhd->ghab", grad_head_out, value_rows, preferred_element_type=jnp.float32
    )
    grad_scores = (
        recomputed * (grad_probs - jnp.sum(recomputed * grad_probs, axis=-1, keepdims=True))
    ).astype(jnp.bfloat16)
    grad_queries = (
        jnp.einsum("ghab,gbhd->gahd", grad_scores, key_rows, preferred_element_type=jnp.float32)
        * scaling
    )
    grad_keys = (
        jnp.einsum("ghab,gahd->gbhd", grad_scores, queries, preferred_element_type=jnp.float32)
        * scaling
    )
    grad_head_qkv = jnp.stack([grad_queries, grad_keys, grad_values], axis=2).astype(jnp.bfloat16)
    grad_qkv = lax.all_to_all(
        grad_head_qkv, "seq", split_axis=0, concat_axis=3, tiled=True
    ).reshape(row_count, 3 * width)
    grad_qkv_weight = jnp.einsum(
        "nd,ne->de", normed_in, grad_qkv, preferred_element_type=jnp.float32
    )
    grad_normed_in = jnp.einsum("ne,de->nd", grad_qkv, full_qkv, preferred_element_type=jnp.float32)
    first_pull = jax.vjp(norm_rows, flat_tokens, gain_first, bias_first)[1]
    grad_first, grad_gain_first, grad_bias_first = first_pull(grad_normed_in)
    token_grad = (grad_middle + grad_first).astype(jnp.bfloat16).reshape(images, seq_len, width)
    shares = (
        lax.psum_scatter(grad_gain_first, "fsdp", scatter_dimension=0, tiled=True),
        lax.psum_scatter(grad_bias_first, "fsdp", scatter_dimension=0, tiled=True),
        lax.psum_scatter(grad_qkv_weight, "fsdp", scatter_dimension=0, tiled=True),
        lax.psum_scatter(grad_proj_weight, "fsdp", scatter_dimension=0, tiled=True),
        lax.psum_scatter(grad_bias_proj, "fsdp", scatter_dimension=0, tiled=True),
        lax.psum_scatter(grad_gain_second, "fsdp", scatter_dimension=0, tiled=True),
        lax.psum_scatter(grad_bias_second, "fsdp", scatter_dimension=0, tiled=True),
        lax.psum_scatter(grad_router, "fsdp", scatter_dimension=0, tiled=True),
        lax.psum_scatter(grad_inner_weight, "fsdp", scatter_dimension=1, tiled=True),
        lax.psum_scatter(grad_inner_bias, "fsdp", scatter_dimension=1, tiled=True),
        lax.psum_scatter(grad_outer_weight, "fsdp", scatter_dimension=1, tiled=True),
        lax.psum_scatter(grad_outer_bias, "fsdp", scatter_dimension=1, tiled=True),
    )
    parted = (
        lax.psum_scatter(
            shares[0].astype(jnp.bfloat16), "seq", scatter_dimension=0, tiled=True
        ).astype(jnp.float32),
        lax.psum_scatter(
            shares[1].astype(jnp.bfloat16), "seq", scatter_dimension=0, tiled=True
        ).astype(jnp.float32),
        lax.psum_scatter(
            shares[2].astype(jnp.bfloat16), "seq", scatter_dimension=0, tiled=True
        ).astype(jnp.float32),
        lax.psum_scatter(
            shares[3].astype(jnp.bfloat16), "seq", scatter_dimension=0, tiled=True
        ).astype(jnp.float32),
        lax.psum_scatter(
            shares[4].astype(jnp.bfloat16), "seq", scatter_dimension=0, tiled=True
        ).astype(jnp.float32),
        lax.psum_scatter(
            shares[5].astype(jnp.bfloat16), "seq", scatter_dimension=0, tiled=True
        ).astype(jnp.float32),
        lax.psum_scatter(
            shares[6].astype(jnp.bfloat16), "seq", scatter_dimension=0, tiled=True
        ).astype(jnp.float32),
        lax.psum_scatter(
            shares[7].astype(jnp.bfloat16), "seq", scatter_dimension=0, tiled=True
        ).astype(jnp.float32),
        lax.psum_scatter(
            shares[8].astype(jnp.bfloat16), "seq", scatter_dimension=1, tiled=True
        ).astype(jnp.float32),
        lax.psum_scatter(
            shares[9].astype(jnp.bfloat16), "seq", scatter_dimension=1, tiled=True
        ).astype(jnp.float32),
        lax.psum_scatter(
            shares[10].astype(jnp.bfloat16), "seq", scatter_dimension=1, tiled=True
        ).astype(jnp.float32),
        lax.psum_scatter(
            shares[11].astype(jnp.bfloat16), "seq", scatter_dimension=1, tiled=True
        ).astype(jnp.float32),
    )
    totals = (
        lax.all_gather(parted[0].astype(jnp.bfloat16), "seq", axis=0, tiled=True).astype(
            jnp.float32
        ),
        lax.all_gather(parted[1].astype(jnp.bfloat16), "seq", axis=0, tiled=True).astype(
            jnp.float32
        ),
        lax.all_gather(parted[2].astype(jnp.bfloat16), "seq", axis=0, tiled=True).astype(
            jnp.float32
        ),
        lax.all_gather(parted[3].astype(jnp.bfloat16), "seq", axis=0, tiled=True).astype(
            jnp.float32
        ),
        lax.all_gather(parted[4].astype(jnp.bfloat16), "seq", axis=0, tiled=True).astype(
            jnp.float32
        ),
        lax.all_gather(parted[5].astype(jnp.bfloat16), "seq", axis=0, tiled=True).astype(
            jnp.float32
        ),
        lax.all_gather(parted[6].astype(jnp.bfloat16), "seq", axis=0, tiled=True).astype(
            jnp.float32
        ),
        lax.all_gather(parted[7].astype(jnp.bfloat16), "seq", axis=0, tiled=True).astype(
            jnp.float32
        ),
        lax.all_gather(parted[8].astype(jnp.bfloat16), "seq", axis=1, tiled=True).astype(
            jnp.float32
        ),
        lax.all_gather(parted[9].astype(jnp.bfloat16), "seq", axis=1, tiled=True).astype(
            jnp.float32
        ),
        lax.all_gather(parted[10].astype(jnp.bfloat16), "seq", axis=1, tiled=True).astype(
            jnp.float32
        ),
        lax.all_gather(parted[11].astype(jnp.bfloat16), "seq", axis=1, tiled=True).astype(
            jnp.float32
        ),
    )
    return (
        mixed,
        token_grad,
        totals[0],
        totals[1],
        totals[2],
        totals[3],
        totals[4],
        totals[5],
        totals[6],
        totals[7],
        totals[8],
        totals[9],
        totals[10],
        totals[11],
    )


MESH = pl.DeviceIdType.MESH
NT = (((1,), (1,)), ((), ()))
TN = (((0,), (0,)), ((), ()))


def dot(a, b):
    return jnp.dot(a, b, preferred_element_type=jnp.float32)


class Place:
    def __init__(self, planes):
        self.planes = planes
        s, f = lax.axis_index("seq"), lax.axis_index("fsdp")
        self.y, self.c, self.z, self.x = s // 2, s % 2, f // 2, f % 2

    def at(self, y, c, z, x):
        return (y * 2 + c, z * 2 + x)

    def other_core(self):
        return self.at(self.y, 1 - self.c, self.z, self.x)

    def other_x(self):
        return self.at(self.y, self.c, self.z, 1 - self.x)

    def other_y(self):
        return self.at(1 - self.y, self.c, self.z, self.x)

    def level(self, k):
        return self.at(self.y, self.c, lax.rem(self.z + k + self.planes, self.planes), self.x)


def greet(partners):
    barrier = pltpu.get_barrier_semaphore()
    for partner in partners:
        pl.semaphore_signal(barrier, inc=1, device_id=partner, device_id_type=MESH)
    pl.semaphore_wait(barrier, len(partners))


def nearest(place, i):
    level = 0
    for z in range(place.planes):
        order = sorted(range(place.planes), key=lambda other: (abs(other - z), other))
        for at in range(place.planes):
            level = level + jnp.where((place.z == z) & (i == at), order[at], 0)
    return level


def expert_kernel(
    planes,
    own,
    rows,
    real,
    normed_ref,
    grads_ref,
    inner_ref,
    outer_all_ref,
    bias_all_ref,
    small_ref,
    mix_ref,
    out_ref,
    inner_grad_ref,
    outer_grad_ref,
    bias_grad_ref,
    router_grad_ref,
    outer_ref,
    inner_t_ref,
    outer_t_ref,
    router_ref,
    router_t_ref,
    tokens,
    part,
    from_core,
    from_x,
    from_z,
    hidden,
    hidden_grad,
    logit_grad,
    inner_acc,
    outer_acc,
    outer_sem,
    z_send,
    z_recv,
    x_send,
    x_recv,
    c_send,
    c_recv,
    sum_c_send,
    sum_c_recv,
    sum_x_send,
    sum_x_recv,
    sum_z_send,
    sum_z_recv,
):
    f32, bf16 = jnp.float32, jnp.bfloat16
    place = Place(planes)
    y, c, z, x = place.y, place.c, place.z, place.x
    width = inner_ref.shape[0]
    lanes = inner_ref.shape[1] // own
    first = real % 16

    def remote(src, dst, send, recv, device):
        return pltpu.make_async_remote_copy(
            src_ref=src, dst_ref=dst, send_sem=send, recv_sem=recv, device_id=device, device_id_type=MESH
        )

    def slot(buffer, level, at, count=1):
        return buffer.at[level, pl.ds(at * rows, count * rows)]

    def up_copy(level):
        here = slot(tokens, level, 0)
        return remote(here, here, z_send.at[0, level], z_recv.at[0, level], place.at(y, c, z + 1, x))

    def down_copy(level):
        here = slot(tokens, level, 0)
        return remote(here, here, z_send.at[1, level], z_recv.at[1, level], place.at(y, c, z - 1, x))

    def x_copy(level):
        return remote(
            slot(tokens, level, 0), slot(tokens, level, 2), x_send.at[level], x_recv.at[level], place.other_x()
        )

    def c_copy(level, r):
        return remote(
            slot(tokens, level, 2 * r),
            slot(tokens, level, 2 * r + 1),
            c_send.at[level, r],
            c_recv.at[level, r],
            place.other_core(),
        )

    def sum_c_copy(level, r):
        return remote(
            slot(part, level, 2 * r + 1),
            slot(from_core, level, r),
            sum_c_send.at[level, r],
            sum_c_recv.at[level, r],
            place.other_core(),
        )

    def sum_x_copy(level):
        return remote(
            slot(part, level, 2), from_x.at[level], sum_x_send.at[level], sum_x_recv.at[level], place.other_x()
        )

    def sum_z_copy(level, source):
        return remote(
            slot(part, level, 0),
            from_z.at[source],
            sum_z_send.at[level],
            sum_z_recv.at[source],
            place.at(y, c, level, x),
        )

    partners = [place.other_core(), place.other_x()] + [place.level(k) for k in range(1, planes)]
    greet(partners)
    tokens[z, 0:rows, :] = normed_ref[...]

    @pl.when(z < planes - 1)
    def _():
        up_copy(z).start()

    @pl.when(z > 0)
    def _():
        down_copy(z).start()

    c_copy(z, 0).start()
    x_copy(z).start()
    loads = [
        pltpu.make_async_copy(
            outer_all_ref.at[c * own + i], outer_ref.at[pl.ds(i * lanes, lanes)], outer_sem.at[i]
        )
        for i in range(own)
    ]
    for load in loads:
        load.start()
    inner_t_ref[...] = jnp.transpose(inner_ref[...])
    place_row = lax.broadcasted_iota(jnp.int32, (128, 128), 0)
    place_lane = lax.broadcasted_iota(jnp.int32, (128, 128), 1)
    take = (place_row - (5 + 2 * own) == place_lane - first) & (place_lane >= first)
    take = take & (place_lane < first + 2 * own)
    router = dot(small_ref[...], take.astype(bf16))
    router_ref[...] = router.astype(bf16)
    router_t_ref[...] = jnp.transpose(router).astype(bf16)
    inner_acc[...] = jnp.zeros_like(inner_acc)
    outer_acc[...] = jnp.zeros_like(outer_acc)
    bias_grad_ref[...] = jnp.zeros_like(bias_grad_ref)
    router_grad_ref[...] = jnp.zeros_like(router_grad_ref)
    for load in loads:
        load.wait()
    outer_t_ref[...] = jnp.transpose(outer_ref[...])

    def hop(h):
        @pl.when(z >= h)
        def _():
            up_copy(z - h).wait_recv()

            @pl.when(z < planes - 1)
            def _():
                up_copy(z - h).start()

            x_copy(z - h).start()
            c_copy(z - h, 0).start()

        @pl.when(z + h < planes)
        def _():
            down_copy(z + h).wait_recv()

            @pl.when(z > 0)
            def _():
                down_copy(z + h).start()

            x_copy(z + h).start()
            c_copy(z + h, 0).start()

    def tiles(level, r):
        here = slice(2 * r * rows, 2 * (r + 1) * rows)
        normed, grad_out = tokens[level, here, :], grads_ref[level, here, :]
        select = []
        for t in range(2 * r, 2 * r + 2):
            last = slice(t * rows + real - first, t * rows + real - first + 16)
            chosen = grads_ref[level, last, :256].astype(f32)
            chosen = jnp.concatenate([chosen, jnp.zeros((112, 256), f32)], axis=0)
            select.append(jnp.transpose(chosen)[:rows])
        select = jnp.concatenate(select, axis=0)
        lane = lax.broadcasted_iota(jnp.int32, select.shape, 1)
        named = (lane >= first) & (lane < first + 2 * own)
        select = jnp.where(named, select, 0.0)
        logits = jnp.where(named, dot(normed, router_ref[...]), -1e30)
        routing = jnp.exp(logits - jnp.max(logits, axis=1, keepdims=True))
        routing = routing / jnp.sum(routing, axis=1, keepdims=True)
        gates = routing * select
        gate_grads = jnp.zeros_like(gates)
        all_pre = dot(normed, inner_ref[...])
        all_grad_act = dot(grad_out, outer_t_ref[...])
        for i in range(own):
            mine = lane == first + c * own + i
            units = slice(i * lanes, (i + 1) * lanes)
            gate = jnp.sum(jnp.where(mine, gates, 0.0), axis=1, keepdims=True)
            bias = jnp.where(c == 0, bias_all_ref[i : i + 1, :], bias_all_ref[own + i : own + i + 1, :])
            pre = all_pre[:, units] + bias.astype(f32)
            grad_act = all_grad_act[:, units]
            cdf = 0.5 * (1.0 + lax.erf(pre * (0.5**0.5)))
            act = pre * cdf
            hidden[here, units] = (gate * act).astype(bf16)
            gate_grad = jnp.sum(act * grad_act, axis=1, keepdims=True)
            gate_grads = gate_grads + jnp.where(mine, gate_grad * select, 0.0)
            slope = cdf + pre * jnp.exp(-0.5 * pre * pre) * 0.3989422804014327
            grad_pre = gate * grad_act * slope
            bias_grad_ref[0:1, units] += jnp.sum(grad_pre, axis=0, keepdims=True)
            hidden_grad[here, units] = grad_pre.astype(bf16)
        grad_logits = routing * (gate_grads - jnp.sum(routing * gate_grads, axis=1, keepdims=True))
        logit_grad[here, :] = grad_logits.astype(bf16)
        mix_ref[level, here, :] = dot(hidden[here, :], outer_ref[...]).astype(bf16)
        row_grad = dot(hidden_grad[here, :], inner_t_ref[...])
        row_grad = row_grad + dot(logit_grad[here, :], router_t_ref[...])
        part[level, here, :] = row_grad.astype(bf16)

    def across_sum(level):
        sum_c_copy(level, 1).wait_recv()
        here = slice(2 * rows, 3 * rows)
        total = part[level, here, :].astype(f32) + from_core[level, rows : 2 * rows, :].astype(f32)
        part[level, here, :] = total.astype(bf16)
        sum_x_copy(level).start()

    def level_sum(level):
        sum_c_copy(level, 0).wait_recv()
        sum_x_copy(level).wait_recv()
        total = part[level, 0:rows, :].astype(f32) + from_core[level, 0:rows, :].astype(f32)
        total = total + from_x[level].astype(f32)
        part[level, 0:rows, :] = total.astype(bf16)

    def weight_grads(level):
        for j in range(width // 256):
            some = slice(j * 256, (j + 1) * 256)
            outer_acc[some, :] += lax.dot_general(
                hidden[:, some], grads_ref[level], TN, preferred_element_type=f32
            )
            inner_acc[some, :] += lax.dot_general(
                tokens[level, :, some], hidden_grad[...], TN, preferred_element_type=f32
            )
        router_grad_ref[...] += lax.dot_general(tokens[level], logit_grad[...], TN, preferred_element_type=f32)

    def order(i):
        return nearest(place, jnp.where(i == planes - 1, 1, i + 1))

    def step(i, before, last):
        level = order(i)
        x_copy(level).wait_recv()
        c_copy(level, 1).start()
        c_copy(level, 1).wait_recv()
        tiles(level, 1)
        sum_c_copy(level, 1).start()

        if not last:
            @pl.when(i + 2 < planes)
            def _():
                hop(i + 2)

        level_sum(before)

        @pl.when(before != z)
        def _():
            sum_z_copy(before, z).start()

        across_sum(level)
        c_copy(level, 0).wait_recv()
        tiles(level, 0)
        sum_c_copy(level, 0).start()
        if last:
            level_sum(level)
            sum_z_copy(level, z).start()
        weight_grads(level)

    c_copy(z, 0).wait_recv()
    tiles(z, 0)
    sum_c_copy(z, 0).start()
    hop(1)
    x_copy(z).wait_recv()
    c_copy(z, 1).start()
    c_copy(z, 1).wait_recv()
    tiles(z, 1)
    sum_c_copy(z, 1).start()
    if planes > 2:
        hop(2)
    weight_grads(z)
    across_sum(z)

    def middle(i, carry):
        step(i, jnp.where(i == 1, z, order(i - 1)), False)
        return carry

    lax.fori_loop(1, planes - 1, middle, 0)
    step(planes - 1, order(planes - 2) if planes > 2 else z, True)
    inner_grad_ref[...] = inner_acc[...].astype(bf16)
    outer_grad_ref[...] = outer_acc[...].astype(bf16)
    total = part[z, 0:rows, :].astype(f32)
    for k in range(1, planes):
        source = lax.rem(z + k, planes)
        sum_z_copy(z, source).wait_recv()
        total = total + from_z[source].astype(f32)
    out_ref[...] = total
    for level in range(planes):
        x_copy(level).wait_send()
        c_copy(level, 0).wait_send()
        c_copy(level, 1).wait_send()
        sum_c_copy(level, 0).wait_send()
        sum_c_copy(level, 1).wait_send()
        sum_x_copy(level).wait_send()

        @pl.when(level != z)
        def _():
            sum_z_copy(level, z).wait_send()

        @pl.when((z >= level) & (z < planes - 1))
        def _():
            up_copy(level).wait_send()

        @pl.when((z <= level) & (z > 0))
        def _():
            down_copy(level).wait_send()


def experts_of_the_plane(planes, own, real, normed, grads, inner, outer, bias, small):
    f32, bf16 = jnp.float32, jnp.bfloat16
    rows = normed.shape[0]
    chunk = 4 * rows
    width, units = inner.shape
    shape = jax.ShapeDtypeStruct
    vmem = pl.BlockSpec(memory_space=pltpu.VMEM)
    dma = pltpu.SemaphoreType.DMA
    flops = 12 * planes * chunk * width * units
    return pl.pallas_call(
        functools.partial(expert_kernel, planes, own, rows, real),
        out_shape=[
            shape((planes, chunk, width), bf16),
            shape((rows, width), f32),
            shape((width, units), bf16),
            shape((units, width), bf16),
            shape((8, units), f32),
            shape((width, 128), f32),
        ],
        in_specs=[vmem] * 3 + [pl.BlockSpec(memory_space=pl.ANY)] + [vmem] * 2,
        out_specs=[vmem] * 6,
        scratch_shapes=[
            pltpu.VMEM((units, width), bf16),
            pltpu.VMEM((units, width), bf16),
            pltpu.VMEM((width, units), bf16),
            pltpu.VMEM((width, 128), bf16),
            pltpu.VMEM((128, width), bf16),
            pltpu.VMEM((planes, chunk, width), bf16),
            pltpu.VMEM((planes, chunk, width), bf16),
            pltpu.VMEM((planes, 2 * rows, width), bf16),
            pltpu.VMEM((planes, rows, width), bf16),
            pltpu.VMEM((planes, rows, width), bf16),
            pltpu.VMEM((chunk, units), bf16),
            pltpu.VMEM((chunk, units), bf16),
            pltpu.VMEM((chunk, 128), bf16),
            pltpu.VMEM((width, units), f32),
            pltpu.VMEM((units, width), f32),
            dma((own,)),
        ]
        + [dma((2, planes))] * 2
        + [dma((planes,))] * 2
        + [dma((planes, 2))] * 4
        + [dma((planes,))] * 4,
        compiler_params=pltpu.CompilerParams(
            collective_id=1, has_side_effects=True, vmem_limit_bytes=60 * 2**20
        ),
        cost_estimate=pl.CostEstimate(flops=flops, bytes_accessed=40 * 2**20, transcendentals=0),
        name="experts_of_the_plane",
    )(normed, grads, inner, outer, bias, small)


def front_kernel(
    planes,
    heads,
    real,
    tokens_ref,
    mask_ref,
    ids_ref,
    cotangent_ref,
    *refs,
):
    vector_refs, refs = refs[:5], refs[5:]
    (
        router_part_ref,
        outer_bias_ref,
        qkv_part_ref,
    proj_part_ref,
    inner_part_ref,
    small_all,
    w_qkv_all,
    w_proj_all,
    inner_all,
    normed_in_ref,
    qkv_ref,
    attended_ref,
    middle_ref,
    normed_ref,
    grad_ref,
    grads_all,
    wide_ref,
    select_ref,
    keys_ref,
    keep_ref,
    up_send,
    up_recv,
    down_send,
    down_recv,
    x_send,
    x_recv,
    c_send,
    c_recv,
    over_send,
    over_recv,
    over_c_send,
    over_c_recv,
    g_z_send,
    g_z_recv,
    g_x_send,
    g_x_recv,
    g_c_send,
    g_c_recv,
    spread_send,
    spread_recv,
    own_sem,
    y_send,
    y_recv,
    ) = refs
    f32, bf16 = jnp.float32, jnp.bfloat16
    place = Place(planes)
    rows, width = wide_ref.shape
    depth = qkv_part_ref.shape[0]
    experts = inner_part_ref.shape[0]
    half = depth // 2
    lanes = inner_part_ref.shape[2] // (2 * planes)
    head_dim = width // heads
    y, c, z, x = place.y, place.c, place.z, place.x
    gathered = [small_all, w_qkv_all, w_proj_all]

    def remote(src, dst, send, recv, device):
        return pltpu.make_async_remote_copy(
            src_ref=src, dst_ref=dst, send_sem=send, recv_sem=recv, device_id=device, device_id_type=MESH
        )

    def block(j, level, across, core, plane):
        start = pl.multiple_of((level * 2 + across) * depth + core * half, 16)
        if j == 0:
            return gathered[j].at[pl.ds(start, half)]
        columns = gathered[j].shape[1] // 2
        return gathered[j].at[pl.ds(start, half), pl.ds(pl.multiple_of(plane * columns, 128), columns)]

    def piece(j, level, across):
        return block(j, level, across, c, y)

    def up_copy(j, level):
        here = piece(j, level, x)
        return remote(here, here, up_send.at[j, level], up_recv.at[j, level], place.at(y, c, z + 1, x))

    def down_copy(j, level):
        here = piece(j, level, x)
        return remote(here, here, down_send.at[j, level], down_recv.at[j, level], place.at(y, c, z - 1, x))

    def x_copy(j, level, across):
        here = piece(j, level, across)
        return remote(here, here, x_send.at[j, level], x_recv.at[j, level], place.other_x())

    def c_copy(j, level, across):
        here = piece(j, level, across)
        at = level * 2 + across
        return remote(here, here, c_send.at[j, at], c_recv.at[j, at], place.other_core())

    def over_copy(j, level, across):
        here = piece(j, level, across)
        at = level * 2 + across
        return remote(here, here, over_send.at[j, at], over_recv.at[j, at], place.other_y())

    def over_c_copy(j, level, across):
        here = block(j, level, across, c, 1 - y)
        at = level * 2 + across
        return remote(here, here, over_c_send.at[j, at], over_c_recv.at[j, at], place.other_core())

    def g_slot(level, at):
        return grads_all.at[level, pl.ds(at * rows, rows)]

    def g_up(level):
        here = g_slot(level, 0)
        return remote(here, here, g_z_send.at[0, level], g_z_recv.at[0, level], place.at(y, c, z + 1, x))

    def g_down(level):
        here = g_slot(level, 0)
        return remote(here, here, g_z_send.at[1, level], g_z_recv.at[1, level], place.at(y, c, z - 1, x))

    def g_x(level):
        return remote(g_slot(level, 0), g_slot(level, 2), g_x_send.at[level], g_x_recv.at[level], place.other_x())

    def g_c(level, r):
        return remote(
            g_slot(level, 2 * r), g_slot(level, 2 * r + 1), g_c_send.at[level, r], g_c_recv.at[level, r], place.other_core()
        )

    def columns_of(f):
        return pl.ds(pl.multiple_of(f * lanes, 128), lanes)

    here_rows = pl.ds(pl.multiple_of((z * 2 + x) * depth, 16), depth)
    my_units = pl.ds(pl.multiple_of(y * lanes, 128), lanes)

    def spread_copy(k, r):
        level, across = lax.rem(z + k, planes), (x + r) % 2
        return remote(
            inner_part_ref.at[c * 2 + y, :, columns_of(level * 2 + across)],
            inner_all.at[here_rows, my_units],
            spread_send.at[k, r],
            spread_recv.at[k, r],
            place.at(y, c, level, across),
        )

    own_copy = pltpu.make_async_copy(
        inner_part_ref.at[c * 2 + y, :, columns_of(z * 2 + x)], inner_all.at[here_rows, my_units], own_sem
    )
    y_copy = remote(inner_all.at[:, my_units], inner_all.at[:, my_units], y_send, y_recv, place.other_y())
    their_units = pl.ds(pl.multiple_of((1 - y) * lanes, 128), lanes)
    from_y = remote(inner_all.at[:, their_units], inner_all.at[:, their_units], y_send, y_recv, place.other_y())

    others = [(k, r) for k in range(planes) for r in range(2) if k or r]
    partners = [place.other_core(), place.other_y()]
    partners += [place.at(y, c, lax.rem(z + k, planes), (x + r) % 2) for k, r in others]
    greet(partners)

    w_qkv_all[here_rows, :] = qkv_part_ref[...]

    def share(j, level, across):
        c_copy(j, level, across).start()
        if j:
            over_copy(j, level, across).start()

    def line(flows):
        @pl.when(z < planes - 1)
        def _():
            for j in flows:
                up_copy(j, z).start()

        @pl.when(z > 0)
        def _():
            for j in flows:
                down_copy(j, z).start()

        for j in flows:
            x_copy(j, z, x).start()

    def hops(flows):
        for h in range(1, planes):
            @pl.when(z >= h)
            def _():
                for j in flows:
                    up_copy(j, z - h).wait_recv()

                    @pl.when(z < planes - 1)
                    def _():
                        up_copy(j, z - h).start()

                    x_copy(j, z - h, x).start()
                    share(j, z - h, x)

            @pl.when(z + h < planes)
            def _():
                for j in flows:
                    down_copy(j, z + h).wait_recv()

                    @pl.when(z > 0)
                    def _():
                        down_copy(j, z + h).start()

                    x_copy(j, z + h, x).start()
                    share(j, z + h, x)

    def arrive(flows):
        for i in range(planes):
            level = nearest(place, i)
            for j in flows:
                x_copy(j, level, 1 - x).wait_recv()
                share(j, level, 1 - x)

    def over_arrive(flows):
        for i in range(planes):
            level = nearest(place, i)
            for j in flows:
                if i:
                    over_copy(j, level, x).wait_recv()
                    over_c_copy(j, level, x).start()
                over_copy(j, level, 1 - x).wait_recv()
                over_c_copy(j, level, 1 - x).start()

    def gather_done(flows):
        for level in range(planes):
            for j in flows:
                c_copy(j, level, 1 - x).wait_recv()
                if j:
                    over_c_copy(j, level, 1 - x).wait_recv()

            @pl.when(level != z)
            def _():
                for j in flows:
                    c_copy(j, level, x).wait_recv()
                    if j:
                        over_c_copy(j, level, x).wait_recv()

    def g_hop(h):
        @pl.when(z >= h)
        def _():
            g_up(z - h).wait_recv()

            @pl.when(z < planes - 1)
            def _():
                g_up(z - h).start()

            g_x(z - h).start()
            g_c(z - h, 0).start()

        @pl.when(z + h < planes)
        def _():
            g_down(z + h).wait_recv()

            @pl.when(z > 0)
            def _():
                g_down(z + h).start()

            g_x(z + h).start()
            g_c(z + h, 0).start()

    line([1])
    lined = [ref[...].astype(f32) for ref in vector_refs] + [outer_bias_ref[...].astype(f32)]
    lined = jnp.concatenate(lined, axis=0)
    lined = jnp.concatenate([lined, jnp.zeros((128 - lined.shape[0], depth), f32)], axis=0)
    lined = jnp.concatenate([lined, jnp.zeros((128, 128 - depth), f32)], axis=1)
    routed = jnp.concatenate([router_part_ref[...].astype(f32), jnp.zeros((depth, 128 - experts), f32)], axis=1)
    small = jnp.transpose(lined)[:depth] + pltpu.roll(routed, 5 + experts, 1)
    small_all[here_rows, :] = small.astype(bf16)
    line([0])
    w_proj_all[here_rows, :] = proj_part_ref[...]
    line([2])
    spare = jnp.zeros((rows - real, width), f32)
    values = jnp.concatenate([tokens_ref[...].astype(f32), spare], axis=0)
    wide_ref[...] = values.astype(bf16)
    normal, _ = norm_parts(values)
    mask = mask_ref[pl.ds(y * 2 + c, 1), :].astype(f32)
    keys = jnp.concatenate([mask, jnp.zeros((1, rows - real), f32)], axis=1)
    keys_ref[...] = keys
    keep = lax.broadcasted_iota(jnp.int32, (rows, rows), 0) == lax.broadcasted_iota(jnp.int32, (rows, rows), 1)
    keep = jnp.sum(jnp.where(keep, keys, 0.0), axis=1, keepdims=True)
    keep_ref[...] = keep
    ids = ids_ref[...]
    number = lax.broadcasted_iota(jnp.int32, (real, 128), 1)
    select = ((number == ids[:, 0:1]) | (number == ids[:, 1:2])).astype(f32)
    select = jnp.concatenate([select, jnp.zeros((rows - real, 128), f32)], axis=0)
    select_ref[...] = select.astype(bf16)
    chosen = jnp.transpose(jnp.concatenate([select, jnp.zeros((256 - rows, 128), f32)], axis=0))[:8]
    chosen = jnp.concatenate([chosen, jnp.zeros((8, width - 256), f32)], axis=1)
    if rows - real > 8:
        chosen = jnp.concatenate([chosen, jnp.zeros((rows - real - 8, width), f32)], axis=0)
    grad_out = cotangent_ref[...].astype(f32) * keep[:real]
    grad_out = jnp.concatenate([grad_out, chosen], axis=0).astype(bf16)
    grad_ref[...] = grad_out
    grads_all[z, 0:rows, :] = grad_out
    hops([1, 0])
    arrive([1, 0])
    hops([2])
    own_copy.start()
    for k, r in others:
        spread_copy(k, r).start()

    @pl.when(z < planes - 1)
    def _():
        g_up(z).start()

    @pl.when(z > 0)
    def _():
        g_down(z).start()

    g_x(z).start()
    g_c(z, 0).start()
    arrive([2])
    over_arrive([1])
    gather_done([1, 0])
    vectors = jnp.transpose(small_all[...].astype(f32))
    normed_in = (normal * vectors[0:1] + vectors[1:2]).astype(bf16)
    normed_in_ref[...] = normed_in
    for j in range(3):
        part = slice(j * width, (j + 1) * width)
        qkv_ref[:, part] = dot(normed_in, w_qkv_all[:, part]).astype(bf16)
    g_hop(1)
    over_arrive([2])
    lane = lax.broadcasted_iota(jnp.int32, (rows, 2 * head_dim), 1)
    usable = keys_ref[...] > 0
    for pair in range(heads // 2):
        if pair == heads // 4:
            g_hop(2)
        at = pair * 2 * head_dim
        queries = qkv_ref[:, at : at + 2 * head_dim]
        keys = qkv_ref[:, width + at : width + at + 2 * head_dim]
        held = qkv_ref[:, 2 * width + at : 2 * width + at + 2 * head_dim]
        outs = []
        for side in range(2):
            only = (lane < head_dim) if side == 0 else (lane >= head_dim)
            scores = lax.dot_general(
                jnp.where(only, queries, 0).astype(bf16), keys, NT, preferred_element_type=f32
            )
            scores = jnp.where(usable, scores * head_dim ** (-0.5), masked_score)
            shifted = jnp.exp(scores - jnp.max(scores, axis=1, keepdims=True))
            probs = (shifted / jnp.sum(shifted, axis=1, keepdims=True)).astype(bf16)
            outs.append(dot(probs, held))
        attended_ref[:, at : at + 2 * head_dim] = jnp.where(lane < head_dim, outs[0], outs[1]).astype(bf16)
    for h in range(3, planes):
        g_hop(h)
    own_copy.wait()
    for k, r in others:
        spread_copy(k, r).wait_recv()
    y_copy.start()
    gather_done([2])
    middle = values + dot(attended_ref[...], w_proj_all[...]) + vectors[2:3]
    middle_ref[...] = middle
    normal_mid, _ = norm_parts(middle)
    normed = normal_mid * vectors[3:4] + vectors[4:5]
    row = lax.broadcasted_iota(jnp.int32, normed.shape, 0)
    normed_ref[...] = jnp.where(row < real, normed, 0.0).astype(bf16)
    for i in range(planes):
        level = nearest(place, i)
        g_x(level).wait_recv()
        g_c(level, 1).start()
    from_y.wait_recv()
    for level in range(planes):
        g_c(level, 0).wait_recv()
        g_c(level, 1).wait_recv()
    y_copy.wait_send()
    for k, r in others:
        spread_copy(k, r).wait_send()
    for level in range(planes):
        g_x(level).wait_send()
        g_c(level, 0).wait_send()
        g_c(level, 1).wait_send()

        @pl.when((z >= level) & (z < planes - 1))
        def _():
            g_up(level).wait_send()

        @pl.when((z <= level) & (z > 0))
        def _():
            g_down(level).wait_send()

    def shared(j, level, across):
        c_copy(j, level, across).wait_send()
        if j:
            over_copy(j, level, across).wait_send()
            over_c_copy(j, level, across).wait_send()

    for j in range(3):
        for level in range(planes):
            x_copy(j, level, x).wait_send()
            shared(j, level, 1 - x)

            @pl.when(level != z)
            def _():
                shared(j, level, x)

            @pl.when((z >= level) & (z < planes - 1))
            def _():
                up_copy(j, level).wait_send()

            @pl.when((z <= level) & (z > 0))
            def _():
                down_copy(j, level).wait_send()


def front(planes, rows, tokens, mask, ids, cotangent, vectors, router, outer_bias, w_qkv, w_proj, w_in):
    f32, bf16 = jnp.float32, jnp.bfloat16
    real, width = tokens.shape
    lanes = w_in.shape[2] // (2 * planes)
    shape = jax.ShapeDtypeStruct
    vmem = pl.BlockSpec(memory_space=pltpu.VMEM)
    dma = pltpu.SemaphoreType.DMA
    return pl.pallas_call(
        functools.partial(front_kernel, planes, HEADS, real),
        out_shape=[
            shape((width, 128), bf16),
            shape((width, 3 * width), bf16),
            shape((width, width), bf16),
            shape((width, 2 * lanes), bf16),
            shape((rows, width), bf16),
            shape((rows, 3 * width), bf16),
            shape((rows, width), bf16),
            shape((rows, width), f32),
            shape((rows, width), bf16),
            shape((rows, width), bf16),
            shape((planes, 4 * rows, width), bf16),
            shape((rows, width), bf16),
            shape((rows, 128), bf16),
            shape((1, rows), f32),
            shape((rows, 1), f32),
        ],
        in_specs=[vmem] * (6 + len(vectors)) + [vmem] * 2 + [pl.BlockSpec(memory_space=pl.ANY)],
        out_specs=[vmem] * 15,
        scratch_shapes=[dma((3, planes))] * 6
        + [dma((3, 2 * planes))] * 6
        + [dma((2, planes))] * 2
        + [dma((planes,))] * 2
        + [dma((planes, 2))] * 4
        + [dma] * 3,
        compiler_params=pltpu.CompilerParams(
            collective_id=2, has_side_effects=True, vmem_limit_bytes=60 * 2**20
        ),
        cost_estimate=pl.CostEstimate(flops=2**32, bytes_accessed=40 * 2**20, transcendentals=0),
        name="dense_weights_and_attention",
    )(tokens, mask, ids, cotangent, *vectors, router, outer_bias, w_qkv, w_proj, w_in)


def back_kernel(planes, heads, own, groups, real, *refs):
    (
        row_grad_ref,
        normed_ref,
        grad_ref,
        middle_ref,
        tokens_ref,
        normed_in_ref,
        qkv_ref,
        attended_ref,
        small_ref,
        w_qkv_ref,
        w_proj_ref,
        keys_ref,
        keep_ref,
        select_ref,
        mix_ref,
        inner_ref,
        outer_ref,
        bias_ref,
        router_grad_ref,
    ) = refs[:19]
    mixed_ref, token_grad_ref, qkv_out, proj_out, small_out, inner_out, outer_out, bias_out = refs[19:27]
    refs = refs[27:]
    (
        grad_attended,
        grad_qkv,
        mix_x,
        mix_z,
        mix_from_core,
        mix_from_x,
        mix_from_z,
        inner_from_y,
        inner_sum,
        outer_from_y,
        bias_from_y,
        held,
        held_small,
        from_core,
        from_core_small,
        from_x,
        from_x_small,
        from_z,
        from_z_small,
        plane_sum,
        plane_sum_small,
        from_y,
        from_y_small,
        final,
        final_small,
    ) = refs[:25]
    (
        mix_c_send,
        mix_c_recv,
        mix_x_send,
        mix_x_recv,
        mix_z_send,
        mix_z_recv,
        inner_y_sem,
        spread_send,
        spread_recv,
        inner_back_sem,
        inner_core_sem,
        outer_y_sem,
        outer_c_sem,
        bias_y_sem,
        bias_c_sem,
        own_sem,
        flow_c_sem,
        flow_x_sem,
        flow_z_send,
        flow_z_recv,
        flow_y_sem,
        flow_end_sem,
    ) = refs[25:]
    f32, bf16 = jnp.float32, jnp.bfloat16
    place = Place(planes)
    y, c, z, x = place.y, place.c, place.z, place.x
    rows, width = middle_ref.shape
    depth = width // (2 * planes)
    half = depth // 2
    lanes = inner_ref.shape[1] // own
    head_dim = width // heads
    pair_width = 2 * head_dim
    small_at = groups + 1

    def remote(src, dst, send, recv, device):
        return pltpu.make_async_remote_copy(
            src_ref=src, dst_ref=dst, send_sem=send, recv_sem=recv, device_id=device, device_id_type=MESH
        )

    def swap(src, dst, sem, device):
        return remote(src, dst, sem.at[0], sem.at[1], device)

    def of_flow(j, many, alone):
        return alone if j == small_at else many.at[j]

    mine, theirs = pl.ds(pl.multiple_of(c * half, 16), half), pl.ds(pl.multiple_of((1 - c) * half, 16), half)

    def flow_c(j):
        source = of_flow(j, held, held_small)
        return swap(
            source.at[:, :, theirs], of_flow(j, from_core, from_core_small), flow_c_sem.at[j], place.other_core()
        )

    def flow_x(j):
        source = of_flow(j, held, held_small)
        return swap(source.at[:, 1 - x, mine], of_flow(j, from_x, from_x_small), flow_x_sem.at[j], place.other_x())

    def flow_z(j, k):
        level = lax.rem(z + k, planes)
        source = of_flow(j, held, held_small)
        return remote(
            source.at[level, x, mine],
            of_flow(j, from_z, from_z_small).at[k],
            flow_z_send.at[j, k],
            flow_z_recv.at[j, k],
            place.level(k),
        )

    def flow_y(j):
        return swap(
            of_flow(j, plane_sum, plane_sum_small),
            of_flow(j, from_y, from_y_small),
            flow_y_sem.at[j],
            place.other_y(),
        )

    def flow_end(j):
        here = of_flow(j, final, final_small).at[mine]
        return swap(here, here, flow_end_sem.at[j], place.other_core())

    def flow_core_sum(j):
        flow_c(j).wait_recv()
        kept = of_flow(j, held, held_small)
        total = kept[:, :, mine, :].astype(f32) + of_flow(j, from_core, from_core_small)[...].astype(f32)
        kept[:, :, mine, :] = total.astype(bf16)
        flow_x(j).start()

    def flow_x_sum(j):
        flow_x(j).wait_recv()
        kept = of_flow(j, held, held_small)
        total = kept[:, x, mine, :].astype(f32) + of_flow(j, from_x, from_x_small)[...].astype(f32)
        kept[:, x, mine, :] = total.astype(bf16)
        for k in range(1, planes):
            flow_z(j, k).start()

    def flow_z_sum(j):
        kept = of_flow(j, held, held_small)
        total = kept[z, x, mine, :].astype(f32)
        for k in range(1, planes):
            flow_z(j, k).wait_recv()
            total = total + of_flow(j, from_z, from_z_small)[k].astype(f32)
        of_flow(j, plane_sum, plane_sum_small)[...] = total.astype(bf16)
        flow_y(j).start()

    def flow_y_sum(j):
        flow_y(j).wait_recv()
        total = of_flow(j, plane_sum, plane_sum_small)[...].astype(f32)
        total = total + of_flow(j, from_y, from_y_small)[...].astype(f32)
        of_flow(j, final, final_small)[mine, :] = total.astype(bf16)
        flow_end(j).start()

    def mix_c(r):
        return remote(
            mix_ref.at[:, pl.ds((2 * r + 1) * rows, rows)],
            mix_from_core.at[:, pl.ds(r * rows, rows)],
            mix_c_send.at[r],
            mix_c_recv.at[r],
            place.other_core(),
        )

    def mix_to_x(level):
        return remote(mix_x.at[level], mix_from_x.at[level], mix_x_send.at[level], mix_x_recv.at[level], place.other_x())

    def mix_to_z(level, source):
        return remote(
            mix_z.at[level], mix_from_z.at[source], mix_z_send.at[level], mix_z_recv.at[source], place.at(y, c, level, x)
        )

    def mix_core_sum():
        mix_c(0).wait_recv()
        mix_c(1).wait_recv()
        for k in range(1, planes + 1):
            level = lax.rem(z + k, planes)
            total = mix_ref[level, 2 * rows : 3 * rows, :].astype(f32) + mix_from_core[level, rows:, :].astype(f32)
            mix_x[level] = total.astype(bf16)
            mix_to_x(level).start()
        for level in range(planes):
            total = mix_ref[level, :rows, :].astype(f32) + mix_from_core[level, :rows, :].astype(f32)
            mix_z[level] = total.astype(bf16)

    def mix_x_sum(k):
        level = lax.rem(z + k, planes)
        mix_to_x(level).wait_recv()
        mix_z[level] = (mix_z[level].astype(f32) + mix_from_x[level].astype(f32)).astype(bf16)
        if k < planes:
            mix_to_z(level, z).start()

    my_units = pl.ds(pl.multiple_of(y * lanes, 128), lanes)
    their_units = pl.ds(pl.multiple_of((1 - y) * lanes, 128), lanes)
    my_expert, their_expert = c * 2 + y, c * 2 + 1 - y
    my_columns = pl.ds(pl.multiple_of((z * 2 + x) * lanes, 128), lanes)

    def inner_y():
        return swap(inner_ref.at[:, their_units], inner_from_y, inner_y_sem, place.other_y())

    def shard_rows(f):
        return pl.ds(pl.multiple_of(f * depth, 16), depth)

    def spread(k, r):
        level, across = lax.rem(z + k, planes), (x + r) % 2
        return remote(
            inner_sum.at[shard_rows(level * 2 + across)],
            inner_out.at[my_expert, :, my_columns],
            spread_send.at[k, r],
            spread_recv.at[k, r],
            place.at(y, c, level, across),
        )

    own_copy = pltpu.make_async_copy(
        inner_sum.at[shard_rows(z * 2 + x)], inner_out.at[my_expert, :, my_columns], own_sem
    )

    def inner_back():
        here = inner_out.at[my_expert]
        return swap(here, here, inner_back_sem, place.other_y())

    def inner_core(expert, at):
        here = inner_out.at[expert]
        return swap(here, here, inner_core_sem.at[at], place.other_core())

    def outer_y():
        return swap(outer_ref, outer_from_y, outer_y_sem, place.other_y())

    def outer_c():
        here = outer_out.at[c]
        return swap(here, here, outer_c_sem, place.other_core())

    def bias_y():
        return swap(bias_ref, bias_from_y, bias_y_sem, place.other_y())

    def bias_c():
        here = bias_out.at[c]
        return swap(here, here, bias_c_sem, place.other_core())

    others = [(k, r) for k in range(planes) for r in range(2) if k or r]

    def inner_y_sum():
        inner_y().wait_recv()
        total = inner_ref[:, my_units].astype(f32) + inner_from_y[...].astype(f32)
        inner_sum[...] = total.astype(bf16)
        own_copy.start()
        for k, r in others:
            spread(k, r).start()
        outer_y().start()

    def inner_spread_done():
        own_copy.wait()
        for k, r in others:
            spread(k, r).wait_recv()
        inner_back().start()
        inner_core(my_expert, 0).start()

    def outer_y_sum():
        outer_y().wait_recv()
        total = outer_ref[...].astype(f32) + outer_from_y[...].astype(f32)
        outer_out[c] = total.astype(bf16)
        outer_c().start()
        bias_y().wait_recv()
        bias_out[c] = bias_ref[...] + bias_from_y[...]
        bias_c().start()

    partners = [place.other_core(), place.other_y()]
    partners += [place.at(y, c, lax.rem(z + k, planes), (x + r) % 2) for k, r in others]
    greet(partners)
    inner_y().start()
    bias_y().start()
    mix_c(1).start()
    mix_c(0).start()

    vectors = jnp.transpose(small_ref[...].astype(f32))
    gain_first, gain_second = vectors[0:1], vectors[3:4]
    place_row = lax.broadcasted_iota(jnp.int32, (128, 128), 0)
    place_lane = lax.broadcasted_iota(jnp.int32, (128, 128), 1)

    def lanes_from(first):
        take = (place_row == place_lane + first) & (place_lane < 2 * own)
        return dot(small_ref[...], take.astype(bf16)).astype(bf16)

    outer_bias, router = lanes_from(5), lanes_from(5 + 2 * own)
    normed_mid, grad_out = normed_ref[...], grad_ref[...]
    real_row = lax.broadcasted_iota(jnp.int32, grad_out.shape, 0) < real
    grad_out = jnp.where(real_row, grad_out, 0).astype(bf16)
    select = select_ref[...].astype(f32)
    lane = lax.broadcasted_iota(jnp.int32, select.shape, 1)
    logits = jnp.where(lane < 2 * own, dot(normed_mid, router), -1e30)
    routing = jnp.exp(logits - jnp.max(logits, axis=1, keepdims=True))
    routing = routing / jnp.sum(routing, axis=1, keepdims=True)
    gates = routing * select
    bias_gate = select * dot(grad_out, outer_bias)
    bias_logits = routing * (bias_gate - jnp.sum(routing * bias_gate, axis=1, keepdims=True))
    bias_logits = bias_logits.astype(bf16)
    router_grad = lax.dot_general(normed_mid, bias_logits, TN, preferred_element_type=f32)
    router_grad = pltpu.roll(router_grad, 16, 1) + pltpu.roll(router_grad_ref[...], 16 - real % 16, 1)
    outer_bias_grad = lax.dot_general(gates.astype(bf16), grad_out, TN, preferred_element_type=f32)
    grad_normed_mid = row_grad_ref[...] + lax.dot_general(bias_logits, router, NT, preferred_element_type=f32)
    normal_mid, rstd_mid = norm_parts(middle_ref[...])
    gain_second_grad = jnp.sum(grad_normed_mid * normal_mid, axis=0, keepdims=True)
    bias_second_grad = jnp.sum(grad_normed_mid, axis=0, keepdims=True)
    grad_middle = grad_out.astype(f32) + norm_back(grad_normed_mid, normal_mid, rstd_mid, gain_second)
    grad_proj = grad_middle.astype(bf16)
    proj_bias_grad = jnp.sum(grad_proj.astype(f32), axis=0, keepdims=True)
    mix_core_sum()

    def hold(j, value):
        held[j] = value.astype(bf16).reshape(planes, 2, depth, width)
        flow_c(j).start()

    hold(0, lax.dot_general(attended_ref[...], grad_proj, TN, preferred_element_type=f32))
    grad_attended[...] = lax.dot_general(grad_proj, w_proj_ref[...], NT, preferred_element_type=f32).astype(bf16)
    flow_core_sum(0)

    pair_lane = lax.broadcasted_iota(jnp.int32, (rows, pair_width), 1)
    usable = keys_ref[...] > 0
    scaling = head_dim ** (-0.5)
    group_width = width // groups

    def pair_back(pair):
        at = pair * pair_width
        group, inside = at // group_width, at % group_width
        queries = qkv_ref[:, at : at + pair_width]
        keys = qkv_ref[:, width + at : width + at + pair_width]
        values = qkv_ref[:, 2 * width + at : 2 * width + at + pair_width]
        grads = grad_attended[:, at : at + pair_width]
        found = []
        for side in range(2):
            only = (pair_lane < head_dim) if side == 0 else (pair_lane >= head_dim)
            some_queries = jnp.where(only, queries, 0).astype(bf16)
            some_grads = jnp.where(only, grads, 0).astype(bf16)
            scores = lax.dot_general(some_queries, keys, NT, preferred_element_type=f32)
            scores = jnp.where(usable, scores * scaling, masked_score)
            shifted = jnp.exp(scores - jnp.max(scores, axis=1, keepdims=True))
            probs = shifted / jnp.sum(shifted, axis=1, keepdims=True)
            grad_probs = lax.dot_general(some_grads, values, NT, preferred_element_type=f32)
            grad_scores = probs * (grad_probs - jnp.sum(probs * grad_probs, axis=1, keepdims=True))
            grad_scores = grad_scores.astype(bf16)
            found.append(
                (
                    dot(grad_scores, keys),
                    lax.dot_general(grad_scores, some_queries, TN, preferred_element_type=f32),
                    lax.dot_general(probs.astype(bf16), some_grads, TN, preferred_element_type=f32),
                )
            )
        grad_queries = jnp.where(pair_lane < head_dim, found[0][0], found[1][0]) * scaling
        grad_keys = (found[0][1] + found[1][1]) * scaling
        grad_values = found[0][2] + found[1][2]
        for part, value in enumerate((grad_queries, grad_keys, grad_values)):
            start = part * group_width + inside
            grad_qkv[group, :, start : start + pair_width] = value.astype(bf16)

    def group_back(group):
        per_group = heads // 2 // groups
        for pair in range(group * per_group, (group + 1) * per_group):
            pair_back(pair)
        hold(
            1 + group,
            lax.dot_general(normed_in_ref[...], grad_qkv[group], TN, preferred_element_type=f32),
        )

    group_back(0)
    inner_y_sum()
    flow_core_sum(1)
    mix_x_sum(1)
    for group in range(1, groups):
        group_back(group)
        flow_core_sum(1 + group)
        if group == 1:
            mix_x_sum(2)

    grad_normed_in = jnp.zeros((rows, width), f32)
    for group in range(groups):
        for part in range(3):
            grad_normed_in = grad_normed_in + lax.dot_general(
                grad_qkv[group, :, part * group_width : (part + 1) * group_width],
                w_qkv_ref[:, part * width + group * group_width : part * width + (group + 1) * group_width],
                NT,
                preferred_element_type=f32,
            )
    normal_first, rstd_first = norm_parts(tokens_ref[...].astype(f32))
    gain_first_grad = jnp.sum(grad_normed_in * normal_first, axis=0, keepdims=True)
    bias_first_grad = jnp.sum(grad_normed_in, axis=0, keepdims=True)
    token_grad = grad_middle + norm_back(grad_normed_in, normal_first, rstd_first, gain_first)
    token_grad_ref[...] = token_grad.astype(bf16)[:real]
    vector_rows = jnp.concatenate(
        [
            gain_first_grad,
            bias_first_grad,
            proj_bias_grad,
            gain_second_grad,
            bias_second_grad,
            jnp.zeros((3, width), f32),
            outer_bias_grad[:8],
            jnp.zeros((112, width), f32),
        ],
        axis=0,
    )
    vector_grads = jnp.transpose(vector_rows) + router_grad
    held_small[...] = vector_grads.astype(bf16).reshape(planes, 2, depth, 128)
    flow_c(small_at).start()
    flow_core_sum(small_at)
    for k in range(3, planes):
        mix_x_sum(k)
    inner_spread_done()
    flow_x_sum(0)
    flow_x_sum(1)
    mix_x_sum(planes)
    outer_y_sum()
    for group in range(1, groups):
        flow_x_sum(1 + group)
    flow_z_sum(0)
    flow_x_sum(small_at)
    mixture = mix_z[z].astype(f32) + dot(gates.astype(bf16), jnp.transpose(outer_bias.astype(f32)).astype(bf16))
    for k in range(1, planes):
        source = lax.rem(z + k, planes)
        mix_to_z(z, source).wait_recv()
        mixture = mixture + mix_from_z[source].astype(f32)
    mixed = (keep_ref[...] * (middle_ref[...] + mixture)).astype(bf16)
    mixed_ref[...] = mixed[:real]
    flow_y_sum(0)
    for group in range(groups):
        flow_z_sum(1 + group)
    flow_z_sum(small_at)
    inner_back().wait_recv()
    inner_core(their_expert, 1).start()
    for group in range(groups):
        flow_y_sum(1 + group)
    flow_y_sum(small_at)

    def arrived(j):
        here = of_flow(j, final, final_small).at[theirs]
        swap(here, here, flow_end_sem.at[j], place.other_core()).wait_recv()

    arrived(0)
    proj_out[...] = final[0]
    for group in range(groups):
        arrived(1 + group)
        for part in range(3):
            start = part * width + group * group_width
            qkv_out[:, start : start + group_width] = final[
                1 + group, :, part * group_width : (part + 1) * group_width
            ]
    arrived(small_at)
    small_out[...] = final_small[...].astype(f32)
    outer_theirs = outer_out.at[1 - c]
    swap(outer_theirs, outer_theirs, outer_c_sem, place.other_core()).wait_recv()
    bias_theirs = bias_out.at[1 - c]
    swap(bias_theirs, bias_theirs, bias_c_sem, place.other_core()).wait_recv()
    for at, expert in enumerate(((1 - c) * 2 + y, (1 - c) * 2 + 1 - y)):
        inner_core(expert, at).wait_recv()

    mix_c(0).wait_send()
    mix_c(1).wait_send()
    inner_y().wait_send()
    inner_back().wait_send()
    inner_core(my_expert, 0).wait_send()
    inner_core(their_expert, 1).wait_send()
    outer_y().wait_send()
    outer_c().wait_send()
    bias_y().wait_send()
    bias_c().wait_send()
    for k, r in others:
        spread(k, r).wait_send()
    for k in range(1, planes + 1):
        level = lax.rem(z + k, planes)
        mix_to_x(level).wait_send()
        if k < planes:
            mix_to_z(level, z).wait_send()
    for j in range(groups + 2):
        flow_c(j).wait_send()
        flow_x(j).wait_send()
        for k in range(1, planes):
            flow_z(j, k).wait_send()
        flow_y(j).wait_send()
        flow_end(j).wait_send()


def back(planes, own, real, *args):
    f32, bf16 = jnp.float32, jnp.bfloat16
    (
        row_grad,
        normed_mid,
        grad_out,
        middle,
        tokens,
        normed_in,
        qkv,
        attended,
        small,
        w_qkv,
        w_proj,
        keys,
        keep,
        select,
        mix_parts,
        inner_grad,
        outer_grad,
        bias_grad,
        router_grad,
    ) = args
    rows, width = middle.shape
    depth = width // (2 * planes)
    half = depth // 2
    lanes = inner_grad.shape[1] // own
    tall = outer_grad.shape[0]
    pairs = HEADS // 2
    groups = 3 if pairs % 3 == 0 and (pairs // 3) * 2 * (width // HEADS) % 128 == 0 else 1
    flows = groups + 1
    shape = jax.ShapeDtypeStruct
    vmem = pl.BlockSpec(memory_space=pltpu.VMEM)
    dma = pltpu.SemaphoreType.DMA

    def both(*dims):
        return [pltpu.VMEM((flows, *dims, width), bf16), pltpu.VMEM((*dims, 128), bf16)]

    return pl.pallas_call(
        functools.partial(back_kernel, planes, HEADS, own, groups, real),
        out_shape=[
            shape((real, width), bf16),
            shape((real, width), bf16),
            shape((depth, 3 * width), bf16),
            shape((depth, width), bf16),
            shape((depth, 128), f32),
            shape((2 * own, depth, 2 * planes * lanes), bf16),
            shape((2, tall, width), bf16),
            shape((2, *bias_grad.shape), f32),
        ],
        in_specs=[vmem] * 19,
        out_specs=[vmem] * 8,
        scratch_shapes=[
            pltpu.VMEM((rows, width), bf16),
            pltpu.VMEM((groups, rows, 3 * width // groups), bf16),
            pltpu.VMEM((planes, rows, width), bf16),
            pltpu.VMEM((planes, rows, width), bf16),
            pltpu.VMEM((planes, 2 * rows, width), bf16),
            pltpu.VMEM((planes, rows, width), bf16),
            pltpu.VMEM((planes, rows, width), bf16),
            pltpu.VMEM((width, lanes), bf16),
            pltpu.VMEM((width, lanes), bf16),
            pltpu.VMEM((tall, width), bf16),
            pltpu.VMEM(bias_grad.shape, f32),
        ]
        + both(planes, 2, depth)
        + both(planes, 2, half)
        + both(planes, half)
        + both(planes, half)
        + both(half)
        + both(half)
        + both(depth)
        + [dma((2,))] * 2
        + [dma((planes,))] * 4
        + [dma((2,))]
        + [dma((planes, 2))] * 2
        + [dma((2,)), dma((2, 2)), dma((2,)), dma((2,)), dma((2,)), dma((2,)), dma]
        + [dma((flows + 1, 2))] * 2
        + [dma((flows + 1, planes))] * 2
        + [dma((flows + 1, 2))] * 2,
        compiler_params=pltpu.CompilerParams(
            collective_id=3, has_side_effects=True, vmem_limit_bytes=60 * 2**20
        ),
        cost_estimate=pl.CostEstimate(flops=2**33, bytes_accessed=40 * 2**20, transcendentals=0),
        name="attention_backward_and_sums",
    )(*args)


def norm_parts(values):
    center = values - jnp.mean(values, axis=-1, keepdims=True)
    rstd = lax.rsqrt(jnp.mean(center * center, axis=-1, keepdims=True) + epsilon)
    return center * rstd, rstd


def norm_back(grad, normal, rstd, gain):
    scaled = grad * gain
    return rstd * (
        scaled
        - jnp.mean(scaled, axis=-1, keepdims=True)
        - normal * jnp.mean(scaled * normal, axis=-1, keepdims=True)
    )


def move_tokens_plan(
    tokens,
    key_mask,
    expert_ids,
    cotangent,
    norm1_gain,
    norm1_bias,
    w_qkv,
    w_proj,
    proj_bias,
    norm2_gain,
    norm2_bias,
    w_router,
    w_in,
    b_in,
    w_out,
    b_out,
):
    f32 = jnp.float32
    _, rows, width = tokens.shape
    experts, depth, hidden = w_in.shape
    slice_width = w_out.shape[1]
    planes = hidden // slice_width // 2
    own = experts // 2
    padded = (rows + experts + 15) // 16 * 16
    vectors = [v[None] for v in (norm1_gain, norm1_bias, proj_bias, norm2_gain, norm2_bias)]
    fronts = front(
        planes,
        padded,
        tokens[0],
        key_mask,
        expert_ids[0],
        cotangent[0],
        vectors,
        w_router,
        b_out,
        w_qkv,
        w_proj,
        w_in,
    )
    small, full_qkv, full_proj, inner, normed_in, qkv, attended, middle = fronts[:8]
    normed_mid, grad_out, all_grad_out, wide, select, keys, keep = fronts[8:]
    mix_parts, row_grad, inner_grad, outer_grad, bias_grad, router_grad = experts_of_the_plane(
        planes, own, rows, normed_mid, all_grad_out, inner, w_out, b_in, small
    )
    mixed, token_grad, qkv_grad, proj_grad, vector_grads, inner_grad, outer_grad, bias_grad = back(
        planes,
        own,
        rows,
        row_grad,
        normed_mid,
        grad_out,
        middle,
        wide,
        normed_in,
        qkv,
        attended,
        small,
        full_qkv,
        full_proj,
        keys,
        keep,
        select,
        mix_parts,
        inner_grad,
        outer_grad,
        bias_grad,
        router_grad,
    )
    return (
        mixed[None],
        token_grad[None],
        vector_grads[:, 0],
        vector_grads[:, 1],
        qkv_grad.astype(f32),
        proj_grad.astype(f32),
        vector_grads[:, 2],
        vector_grads[:, 3],
        vector_grads[:, 4],
        vector_grads[:, 16 : 16 + experts],
        inner_grad.astype(f32),
        bias_grad[:, 0].reshape(experts, slice_width),
        outer_grad.reshape(experts, slice_width, width).astype(f32),
        vector_grads[:, 8 : 8 + experts].T,
    )


def solution(mesh):
    n_seq, n_fsdp = mesh.shape["seq"], mesh.shape["fsdp"]

    def per_device(*args):
        tokens, w_in, w_out = args[0], args[12], args[14]
        experts, _, hidden = w_in.shape
        lanes = hidden // n_fsdp
        whole_tiles = lanes % 128 == 0 and tokens.shape[2] % 256 == 0 and w_in.shape[1] % 32 == 0 and 2 * lanes <= tokens.shape[2]
        if n_seq == 4 and experts == n_seq and tokens.shape[0] == 1 and whole_tiles:
            return move_tokens_plan(*args)
        return gather_weights_plan(*args)

    return jax.shard_map(
        per_device,
        mesh=mesh,
        in_specs=(
            P(("fsdp", "seq"), None, None),
            P("fsdp", None),
            P(("fsdp", "seq"), None, None),
            P(("fsdp", "seq"), None, None),
            P("fsdp"),
            P("fsdp"),
            P("fsdp", None),
            P("fsdp", None),
            P("fsdp"),
            P("fsdp"),
            P("fsdp"),
            P("fsdp", None),
            P(None, "fsdp", None),
            P(None, "fsdp"),
            P(None, "fsdp", None),
            P(None, "fsdp"),
        ),
        out_specs=(
            P(("fsdp", "seq"), None, None),
            P(("fsdp", "seq"), None, None),
            P("fsdp"),
            P("fsdp"),
            P("fsdp", None),
            P("fsdp", None),
            P("fsdp"),
            P("fsdp"),
            P("fsdp"),
            P("fsdp", None),
            P(None, "fsdp", None),
            P(None, "fsdp"),
            P(None, "fsdp", None),
            P(None, "fsdp"),
        ),
        check_vma=False,
    )
```

```python
import functools

import jax
import jax.numpy as jnp
from jax import lax
from jax.experimental import pallas as pl
from jax.experimental.pallas import tpu as pltpu
from jax.sharding import PartitionSpec as P

HEADS = 12
CAP = 142


epsilon = 1e-06
masked_score = -1e30


def norm_rows(values, gain, offset):
    center = values - jnp.mean(values, axis=-1, keepdims=True)
    spread = jnp.mean(center * center, axis=-1, keepdims=True)
    return center * lax.rsqrt(spread + epsilon) * gain + offset


def softmax_rows(values):
    shifted = jnp.exp(values - jnp.max(values, axis=-1, keepdims=True))
    return shifted / jnp.sum(shifted, axis=-1, keepdims=True)


def exact_gelu(values):
    return jax.nn.gelu(values, approximate=False)


def expert_slots(chosen, experts):
    flat_ids = chosen.reshape(-1)
    onehot = (flat_ids[:, None] == jnp.arange(experts, dtype=jnp.int32)[None, :]).astype(jnp.int32)
    ranks = jnp.cumsum(onehot, axis=0, dtype=jnp.int32)
    slot_pos = jnp.sum(onehot * ranks, axis=1, dtype=jnp.int32) - 1
    return (flat_ids, slot_pos)


def gather_weights_plan(
    tokens,
    key_mask,
    expert_ids,
    cotangent,
    norm1_gain,
    norm1_bias,
    w_qkv,
    w_proj,
    proj_bias,
    norm2_gain,
    norm2_bias,
    w_router,
    w_in,
    b_in,
    w_out,
    b_out,
):
    images, seq_len, width = tokens.shape
    experts = w_in.shape[0]
    head_dim = width // HEADS
    scaling = head_dim ** (-0.5)
    row_count = images * seq_len
    dense_set = (
        lax.all_gather(norm1_gain, "fsdp", axis=0, tiled=True),
        lax.all_gather(norm1_bias, "fsdp", axis=0, tiled=True),
        lax.all_gather(w_qkv, "fsdp", axis=0, tiled=True),
        lax.all_gather(w_proj, "fsdp", axis=0, tiled=True),
        lax.all_gather(proj_bias, "fsdp", axis=0, tiled=True),
        lax.all_gather(norm2_gain, "fsdp", axis=0, tiled=True),
        lax.all_gather(norm2_bias, "fsdp", axis=0, tiled=True),
        lax.all_gather(w_router, "fsdp", axis=0, tiled=True),
    )
    gain_first = dense_set[0].astype(jnp.float32)
    bias_first = dense_set[1].astype(jnp.float32)
    full_qkv = dense_set[2]
    full_proj = dense_set[3]
    bias_proj = dense_set[4].astype(jnp.float32)
    gain_second = dense_set[5].astype(jnp.float32)
    bias_second = dense_set[6].astype(jnp.float32)
    full_router = dense_set[7]
    expert_set = (
        lax.all_gather(w_in, "fsdp", axis=1, tiled=True),
        lax.all_gather(b_in, "fsdp", axis=1, tiled=True),
        lax.all_gather(w_out, "fsdp", axis=1, tiled=True),
        lax.all_gather(b_out, "fsdp", axis=1, tiled=True),
    )
    inner_weight = expert_set[0]
    inner_bias = expert_set[1].astype(jnp.float32)
    outer_weight = expert_set[2]
    outer_bias = expert_set[3].astype(jnp.float32)
    own_mask = lax.dynamic_slice_in_dim(key_mask, lax.axis_index("seq") * images, images, 0)
    keep_rows = own_mask.reshape(row_count, 1).astype(jnp.float32)
    usable = (key_mask > 0)[:, None, None, :]
    flat_tokens = tokens.astype(jnp.float32).reshape(row_count, width)
    normed_in = norm_rows(flat_tokens, gain_first, bias_first).astype(jnp.bfloat16)
    mixed_qkv = jnp.dot(normed_in, full_qkv, preferred_element_type=jnp.float32).astype(
        jnp.bfloat16
    )
    mixed_qkv = mixed_qkv.reshape(images, seq_len, 3, HEADS, head_dim)
    head_qkv = lax.all_to_all(mixed_qkv, "seq", split_axis=3, concat_axis=0, tiled=True)
    queries = head_qkv[:, :, 0]
    key_rows = head_qkv[:, :, 1]
    value_rows = head_qkv[:, :, 2]

    def score_block():
        raw = (
            jnp.einsum("gahd,gbhd->ghab", queries, key_rows, preferred_element_type=jnp.float32)
            * scaling
        )
        return jnp.where(usable, raw, masked_score)

    scores = score_block()
    row_top = jnp.max(scores, axis=-1, keepdims=True)
    shifted = jnp.exp(scores - row_top)
    row_total = jnp.sum(shifted, axis=-1, keepdims=True)
    attn_probs = (shifted / row_total).astype(jnp.bfloat16)
    log_total = row_top + jnp.log(row_total)
    head_out = jnp.einsum(
        "ghab,gbhd->gahd", attn_probs, value_rows, preferred_element_type=jnp.float32
    ).astype(jnp.bfloat16)
    attended = lax.all_to_all(head_out, "seq", split_axis=0, concat_axis=2, tiled=True).reshape(
        row_count, width
    )
    middle = (
        flat_tokens + jnp.dot(attended, full_proj, preferred_element_type=jnp.float32) + bias_proj
    )
    normed_mid = norm_rows(middle, gain_second, bias_second).astype(jnp.bfloat16)
    routing = softmax_rows(jnp.dot(normed_mid, full_router, preferred_element_type=jnp.float32))
    chosen = expert_ids.reshape(row_count, 2)
    flat_ids, slot_pos = expert_slots(chosen, experts)
    gating = jnp.take_along_axis(routing, chosen, axis=1)
    buffer = (
        jnp.zeros((experts, CAP, width), jnp.bfloat16)
        .at[flat_ids, slot_pos]
        .set(jnp.repeat(normed_mid, 2, axis=0))
    )
    pre_act = (
        jnp.einsum("ecd,edf->ecf", buffer, inner_weight, preferred_element_type=jnp.float32)
        + inner_bias[:, None, :]
    )
    activated = exact_gelu(pre_act).astype(jnp.bfloat16)
    expert_out = (
        jnp.einsum("ecf,efd->ecd", activated, outer_weight, preferred_element_type=jnp.float32)
        + outer_bias[:, None, :]
    )
    picked = expert_out[flat_ids, slot_pos].reshape(row_count, 2, width)
    mixture = jnp.sum(gating[:, :, None] * picked, axis=1)
    mixed = (keep_rows * (middle + mixture)).astype(jnp.bfloat16).reshape(images, seq_len, width)
    grad_out = cotangent.astype(jnp.float32).reshape(row_count, width) * keep_rows
    grad_gate = jnp.sum(grad_out[:, None, :] * picked, axis=2)
    grad_picked = (
        (gating[:, :, None] * grad_out[:, None, :])
        .astype(jnp.bfloat16)
        .reshape(2 * row_count, width)
    )
    grad_expert_out = (
        jnp.zeros((experts, CAP, width), jnp.bfloat16).at[flat_ids, slot_pos].set(grad_picked)
    )
    grad_outer_bias = jnp.sum(grad_expert_out, axis=1, dtype=jnp.float32)
    hidden_pre = (
        jnp.einsum("ecd,edf->ecf", buffer, inner_weight, preferred_element_type=jnp.float32)
        + inner_bias[:, None, :]
    )
    hidden_act = exact_gelu(hidden_pre).astype(jnp.bfloat16)
    grad_outer_weight = jnp.einsum(
        "ecf,ecd->efd", hidden_act, grad_expert_out, preferred_element_type=jnp.float32
    )
    grad_act = jnp.einsum(
        "ecd,efd->ecf", grad_expert_out, outer_weight, preferred_element_type=jnp.float32
    )
    gelu_pull = jax.vjp(exact_gelu, hidden_pre)[1]
    grad_pre = gelu_pull(grad_act)[0].astype(jnp.bfloat16)
    grad_inner_bias = jnp.sum(grad_pre, axis=1, dtype=jnp.float32)
    grad_inner_weight = jnp.einsum(
        "ecd,ecf->edf", buffer, grad_pre, preferred_element_type=jnp.float32
    )
    grad_buffer = jnp.einsum(
        "ecf,edf->ecd", grad_pre, inner_weight, preferred_element_type=jnp.float32
    )
    grad_rows = jnp.sum(grad_buffer[flat_ids, slot_pos].reshape(row_count, 2, width), axis=1)
    expert_range = jnp.arange(experts, dtype=jnp.int32)[None, None, :]
    grad_route = jnp.sum(
        grad_gate[:, :, None] * (chosen[:, :, None] == expert_range).astype(jnp.float32), axis=1
    )
    grad_logits = (
        routing * (grad_route - jnp.sum(routing * grad_route, axis=-1, keepdims=True))
    ).astype(jnp.bfloat16)
    grad_router = jnp.einsum(
        "nd,ne->de", normed_mid, grad_logits, preferred_element_type=jnp.float32
    )
    grad_normed_mid = grad_rows + jnp.einsum(
        "ne,de->nd", grad_logits, full_router, preferred_element_type=jnp.float32
    )
    second_pull = jax.vjp(norm_rows, middle, gain_second, bias_second)[1]
    grad_mid_norm, grad_gain_second, grad_bias_second = second_pull(grad_normed_mid)
    grad_middle = grad_out + grad_mid_norm
    grad_proj = grad_middle.astype(jnp.bfloat16)
    grad_bias_proj = jnp.sum(grad_proj, axis=0, dtype=jnp.float32)
    grad_proj_weight = jnp.einsum(
        "nd,ne->de", attended, grad_proj, preferred_element_type=jnp.float32
    )
    grad_attended = jnp.einsum(
        "ne,de->nd", grad_proj, full_proj, preferred_element_type=jnp.float32
    ).astype(jnp.bfloat16)
    grad_head_out = lax.all_to_all(
        grad_attended.reshape(images, seq_len, HEADS, head_dim),
        "seq",
        split_axis=2,
        concat_axis=0,
        tiled=True,
    )
    recomputed = jnp.exp(score_block() - log_total)
    grad_values = jnp.einsum(
        "ghab,gahd->gbhd",
        recomputed.astype(jnp.bfloat16),
        grad_head_out,
        preferred_element_type=jnp.float32,
    )
    grad_probs = jnp.einsum(
        "gahd,gbhd->ghab", grad_head_out, value_rows, preferred_element_type=jnp.float32
    )
    grad_scores = (
        recomputed * (grad_probs - jnp.sum(recomputed * grad_probs, axis=-1, keepdims=True))
    ).astype(jnp.bfloat16)
    grad_queries = (
        jnp.einsum("ghab,gbhd->gahd", grad_scores, key_rows, preferred_element_type=jnp.float32)
        * scaling
    )
    grad_keys = (
        jnp.einsum("ghab,gahd->gbhd", grad_scores, queries, preferred_element_type=jnp.float32)
        * scaling
    )
    grad_head_qkv = jnp.stack([grad_queries, grad_keys, grad_values], axis=2).astype(jnp.bfloat16)
    grad_qkv = lax.all_to_all(
        grad_head_qkv, "seq", split_axis=0, concat_axis=3, tiled=True
    ).reshape(row_count, 3 * width)
    grad_qkv_weight = jnp.einsum(
        "nd,ne->de", normed_in, grad_qkv, preferred_element_type=jnp.float32
    )
    grad_normed_in = jnp.einsum("ne,de->nd", grad_qkv, full_qkv, preferred_element_type=jnp.float32)
    first_pull = jax.vjp(norm_rows, flat_tokens, gain_first, bias_first)[1]
    grad_first, grad_gain_first, grad_bias_first = first_pull(grad_normed_in)
    token_grad = (grad_middle + grad_first).astype(jnp.bfloat16).reshape(images, seq_len, width)
    shares = (
        lax.psum_scatter(grad_gain_first, "fsdp", scatter_dimension=0, tiled=True),
        lax.psum_scatter(grad_bias_first, "fsdp", scatter_dimension=0, tiled=True),
        lax.psum_scatter(grad_qkv_weight, "fsdp", scatter_dimension=0, tiled=True),
        lax.psum_scatter(grad_proj_weight, "fsdp", scatter_dimension=0, tiled=True),
        lax.psum_scatter(grad_bias_proj, "fsdp", scatter_dimension=0, tiled=True),
        lax.psum_scatter(grad_gain_second, "fsdp", scatter_dimension=0, tiled=True),
        lax.psum_scatter(grad_bias_second, "fsdp", scatter_dimension=0, tiled=True),
        lax.psum_scatter(grad_router, "fsdp", scatter_dimension=0, tiled=True),
        lax.psum_scatter(grad_inner_weight, "fsdp", scatter_dimension=1, tiled=True),
        lax.psum_scatter(grad_inner_bias, "fsdp", scatter_dimension=1, tiled=True),
        lax.psum_scatter(grad_outer_weight, "fsdp", scatter_dimension=1, tiled=True),
        lax.psum_scatter(grad_outer_bias, "fsdp", scatter_dimension=1, tiled=True),
    )
    parted = (
        lax.psum_scatter(
            shares[0].astype(jnp.bfloat16), "seq", scatter_dimension=0, tiled=True
        ).astype(jnp.float32),
        lax.psum_scatter(
            shares[1].astype(jnp.bfloat16), "seq", scatter_dimension=0, tiled=True
        ).astype(jnp.float32),
        lax.psum_scatter(
            shares[2].astype(jnp.bfloat16), "seq", scatter_dimension=0, tiled=True
        ).astype(jnp.float32),
        lax.psum_scatter(
            shares[3].astype(jnp.bfloat16), "seq", scatter_dimension=0, tiled=True
        ).astype(jnp.float32),
        lax.psum_scatter(
            shares[4].astype(jnp.bfloat16), "seq", scatter_dimension=0, tiled=True
        ).astype(jnp.float32),
        lax.psum_scatter(
            shares[5].astype(jnp.bfloat16), "seq", scatter_dimension=0, tiled=True
        ).astype(jnp.float32),
        lax.psum_scatter(
            shares[6].astype(jnp.bfloat16), "seq", scatter_dimension=0, tiled=True
        ).astype(jnp.float32),
        lax.psum_scatter(
            shares[7].astype(jnp.bfloat16), "seq", scatter_dimension=0, tiled=True
        ).astype(jnp.float32),
        lax.psum_scatter(
            shares[8].astype(jnp.bfloat16), "seq", scatter_dimension=1, tiled=True
        ).astype(jnp.float32),
        lax.psum_scatter(
            shares[9].astype(jnp.bfloat16), "seq", scatter_dimension=1, tiled=True
        ).astype(jnp.float32),
        lax.psum_scatter(
            shares[10].astype(jnp.bfloat16), "seq", scatter_dimension=1, tiled=True
        ).astype(jnp.float32),
        lax.psum_scatter(
            shares[11].astype(jnp.bfloat16), "seq", scatter_dimension=1, tiled=True
        ).astype(jnp.float32),
    )
    totals = (
        lax.all_gather(parted[0].astype(jnp.bfloat16), "seq", axis=0, tiled=True).astype(
            jnp.float32
        ),
        lax.all_gather(parted[1].astype(jnp.bfloat16), "seq", axis=0, tiled=True).astype(
            jnp.float32
        ),
        lax.all_gather(parted[2].astype(jnp.bfloat16), "seq", axis=0, tiled=True).astype(
            jnp.float32
        ),
        lax.all_gather(parted[3].astype(jnp.bfloat16), "seq", axis=0, tiled=True).astype(
            jnp.float32
        ),
        lax.all_gather(parted[4].astype(jnp.bfloat16), "seq", axis=0, tiled=True).astype(
            jnp.float32
        ),
        lax.all_gather(parted[5].astype(jnp.bfloat16), "seq", axis=0, tiled=True).astype(
            jnp.float32
        ),
        lax.all_gather(parted[6].astype(jnp.bfloat16), "seq", axis=0, tiled=True).astype(
            jnp.float32
        ),
        lax.all_gather(parted[7].astype(jnp.bfloat16), "seq", axis=0, tiled=True).astype(
            jnp.float32
        ),
        lax.all_gather(parted[8].astype(jnp.bfloat16), "seq", axis=1, tiled=True).astype(
            jnp.float32
        ),
        lax.all_gather(parted[9].astype(jnp.bfloat16), "seq", axis=1, tiled=True).astype(
            jnp.float32
        ),
        lax.all_gather(parted[10].astype(jnp.bfloat16), "seq", axis=1, tiled=True).astype(
            jnp.float32
        ),
        lax.all_gather(parted[11].astype(jnp.bfloat16), "seq", axis=1, tiled=True).astype(
            jnp.float32
        ),
    )
    return (
        mixed,
        token_grad,
        totals[0],
        totals[1],
        totals[2],
        totals[3],
        totals[4],
        totals[5],
        totals[6],
        totals[7],
        totals[8],
        totals[9],
        totals[10],
        totals[11],
    )


MESH = pl.DeviceIdType.MESH
NT = (((1,), (1,)), ((), ()))
TN = (((0,), (0,)), ((), ()))


def dot(a, b):
    return jnp.dot(a, b, preferred_element_type=jnp.float32)


class Place:
    def __init__(self, planes):
        self.planes = planes
        s, f = lax.axis_index("seq"), lax.axis_index("fsdp")
        self.y, self.c, self.z, self.x = s // 2, s % 2, f // 2, f % 2

    def at(self, y, c, z, x):
        return (y * 2 + c, z * 2 + x)

    def other_core(self):
        return self.at(self.y, 1 - self.c, self.z, self.x)

    def other_x(self):
        return self.at(self.y, self.c, self.z, 1 - self.x)

    def other_y(self):
        return self.at(1 - self.y, self.c, self.z, self.x)

    def level(self, k):
        return self.at(self.y, self.c, lax.rem(self.z + k + self.planes, self.planes), self.x)


def greet(partners):
    barrier = pltpu.get_barrier_semaphore()
    for partner in partners:
        pl.semaphore_signal(barrier, inc=1, device_id=partner, device_id_type=MESH)
    pl.semaphore_wait(barrier, len(partners))


def nearest(place, i):
    level = 0
    for z in range(place.planes):
        order = sorted(range(place.planes), key=lambda other: (abs(other - z), other))
        for at in range(place.planes):
            level = level + jnp.where((place.z == z) & (i == at), order[at], 0)
    return level


def expert_kernel(
    planes,
    own,
    rows,
    real,
    normed_ref,
    grads_all_ref,
    inner_ref,
    outer_all_ref,
    bias_all_ref,
    small_ref,
    mix_out_ref,
    out_ref,
    inner_grad_ref,
    outer_grad_ref,
    bias_grad_ref,
    router_grad_ref,
    grads_ref,
    mix_ref,
    outer_ref,
    inner_t_ref,
    outer_t_ref,
    router_ref,
    router_t_ref,
    tokens,
    part,
    from_core,
    from_x,
    from_z,
    hidden,
    hidden_grad,
    logit_grad,
    inner_acc,
    outer_acc,
    outer_sem,
    grads_sem,
    mix_sem,
    z_send,
    z_recv,
    x_send,
    x_recv,
    c_send,
    c_recv,
    sum_c_send,
    sum_c_recv,
    sum_x_send,
    sum_x_recv,
    sum_z_send,
    sum_z_recv,
):
    f32, bf16 = jnp.float32, jnp.bfloat16
    place = Place(planes)
    y, c, z, x = place.y, place.c, place.z, place.x
    width = inner_ref.shape[0]
    lanes = inner_ref.shape[1] // own
    first = real % 16

    def remote(src, dst, send, recv, device):
        return pltpu.make_async_remote_copy(
            src_ref=src, dst_ref=dst, send_sem=send, recv_sem=recv, device_id=device, device_id_type=MESH
        )

    def slot(buffer, level, at, count=1):
        return buffer.at[level, pl.ds(at * rows, count * rows)]

    def up_copy(level):
        here = slot(tokens, level, 0)
        return remote(here, here, z_send.at[0, level], z_recv.at[0, level], place.at(y, c, z + 1, x))

    def down_copy(level):
        here = slot(tokens, level, 0)
        return remote(here, here, z_send.at[1, level], z_recv.at[1, level], place.at(y, c, z - 1, x))

    def x_copy(level):
        return remote(
            slot(tokens, level, 0), slot(tokens, level, 2), x_send.at[level], x_recv.at[level], place.other_x()
        )

    def c_copy(level, r):
        return remote(
            slot(tokens, level, 2 * r),
            slot(tokens, level, 2 * r + 1),
            c_send.at[level, r],
            c_recv.at[level, r],
            place.other_core(),
        )

    def sum_c_copy(level, r):
        return remote(
            slot(part, level, 2 * r + 1),
            slot(from_core, level, r),
            sum_c_send.at[level, r],
            sum_c_recv.at[level, r],
            place.other_core(),
        )

    def sum_x_copy(level):
        return remote(
            slot(part, level, 2), from_x.at[level], sum_x_send.at[level], sum_x_recv.at[level], place.other_x()
        )

    def sum_z_copy(level, source):
        return remote(
            slot(part, level, 0),
            from_z.at[source],
            sum_z_send.at[level],
            sum_z_recv.at[source],
            place.at(y, c, level, x),
        )

    partners = [place.other_core(), place.other_x()] + [place.level(k) for k in range(1, planes)]
    greet(partners)
    tokens[z, 0:rows, :] = normed_ref[...]

    @pl.when(z < planes - 1)
    def _():
        up_copy(z).start()

    @pl.when(z > 0)
    def _():
        down_copy(z).start()

    c_copy(z, 0).start()
    x_copy(z).start()
    def grads_load(level):
        return pltpu.make_async_copy(grads_all_ref.at[level], grads_ref.at[level], grads_sem.at[level])

    def mix_store(level, r):
        here = pl.ds(pl.multiple_of(2 * r * rows, 16), 2 * rows)
        return pltpu.make_async_copy(mix_ref.at[level, here], mix_out_ref.at[level, here], mix_sem.at[level, r])

    for i in range(planes):
        grads_load(nearest(place, i)).start()
    loads = [
        pltpu.make_async_copy(
            outer_all_ref.at[c * own + i], outer_ref.at[pl.ds(i * lanes, lanes)], outer_sem.at[i]
        )
        for i in range(own)
    ]
    for load in loads:
        load.start()
    inner_t_ref[...] = jnp.transpose(inner_ref[...])
    place_row = lax.broadcasted_iota(jnp.int32, (128, 128), 0)
    place_lane = lax.broadcasted_iota(jnp.int32, (128, 128), 1)
    take = (place_row - (5 + 2 * own) == place_lane - first) & (place_lane >= first)
    take = take & (place_lane < first + 2 * own)
    router = dot(small_ref[...], take.astype(bf16))
    router_ref[...] = router.astype(bf16)
    router_t_ref[...] = jnp.transpose(router).astype(bf16)
    inner_acc[...] = jnp.zeros_like(inner_acc)
    outer_acc[...] = jnp.zeros_like(outer_acc)
    bias_grad_ref[...] = jnp.zeros_like(bias_grad_ref)
    router_grad_ref[...] = jnp.zeros_like(router_grad_ref)
    for load in loads:
        load.wait()
    outer_t_ref[...] = jnp.transpose(outer_ref[...])

    def hop(h):
        @pl.when(z >= h)
        def _():
            up_copy(z - h).wait_recv()

            @pl.when(z < planes - 1)
            def _():
                up_copy(z - h).start()

            x_copy(z - h).start()
            c_copy(z - h, 0).start()

        @pl.when(z + h < planes)
        def _():
            down_copy(z + h).wait_recv()

            @pl.when(z > 0)
            def _():
                down_copy(z + h).start()

            x_copy(z + h).start()
            c_copy(z + h, 0).start()

    def tiles(level, r):
        here = pl.ds(pl.multiple_of(2 * r * rows, 16), 2 * rows)
        normed, grad_out = tokens[level, here, :], grads_ref[level, here, :]
        select = []
        for t in range(2):
            last = pl.ds(pl.multiple_of((2 * r + t) * rows + real - first, 16), 16)
            chosen = grads_ref[level, last, :256].astype(f32)
            chosen = jnp.concatenate([chosen, jnp.zeros((112, 256), f32)], axis=0)
            select.append(jnp.transpose(chosen)[:rows])
        select = jnp.concatenate(select, axis=0)
        lane = lax.broadcasted_iota(jnp.int32, select.shape, 1)
        named = (lane >= first) & (lane < first + 2 * own)
        select = jnp.where(named, select, 0.0)
        logits = jnp.where(named, dot(normed, router_ref[...]), -1e30)
        routing = jnp.exp(logits - jnp.max(logits, axis=1, keepdims=True))
        routing = routing / jnp.sum(routing, axis=1, keepdims=True)
        gates = routing * select
        gate_grads = jnp.zeros_like(gates)
        all_pre = dot(normed, inner_ref[...])
        all_grad_act = dot(grad_out, outer_t_ref[...])
        for i in range(own):
            mine = lane == first + c * own + i
            units = slice(i * lanes, (i + 1) * lanes)
            gate = jnp.sum(jnp.where(mine, gates, 0.0), axis=1, keepdims=True)
            bias = jnp.where(c == 0, bias_all_ref[i : i + 1, :], bias_all_ref[own + i : own + i + 1, :])
            pre = all_pre[:, units] + bias.astype(f32)
            grad_act = all_grad_act[:, units]
            cdf = 0.5 * (1.0 + lax.erf(pre * (0.5**0.5)))
            act = pre * cdf
            hidden[here, units] = (gate * act).astype(bf16)
            gate_grad = jnp.sum(act * grad_act, axis=1, keepdims=True)
            gate_grads = gate_grads + jnp.where(mine, gate_grad * select, 0.0)
            slope = cdf + pre * jnp.exp(-0.5 * pre * pre) * 0.3989422804014327
            grad_pre = gate * grad_act * slope
            bias_grad_ref[0:1, units] += jnp.sum(grad_pre, axis=0, keepdims=True)
            hidden_grad[here, units] = grad_pre.astype(bf16)
        grad_logits = routing * (gate_grads - jnp.sum(routing * gate_grads, axis=1, keepdims=True))
        logit_grad[here, :] = grad_logits.astype(bf16)
        mix_ref[level, here, :] = dot(hidden[here, :], outer_ref[...]).astype(bf16)
        row_grad = dot(hidden_grad[here, :], inner_t_ref[...])
        row_grad = row_grad + dot(logit_grad[here, :], router_t_ref[...])
        part[level, here, :] = row_grad.astype(bf16)

    def across_sum(level):
        sum_c_copy(level, 1).wait_recv()
        here = slice(2 * rows, 3 * rows)
        total = part[level, here, :].astype(f32) + from_core[level, rows : 2 * rows, :].astype(f32)
        part[level, here, :] = total.astype(bf16)
        sum_x_copy(level).start()

    def level_sum(level):
        sum_c_copy(level, 0).wait_recv()
        sum_x_copy(level).wait_recv()
        total = part[level, 0:rows, :].astype(f32) + from_core[level, 0:rows, :].astype(f32)
        total = total + from_x[level].astype(f32)
        part[level, 0:rows, :] = total.astype(bf16)

    def weight_grads(level):
        for j in range(width // 256):
            some = slice(j * 256, (j + 1) * 256)
            outer_acc[some, :] += lax.dot_general(
                hidden[:, some], grads_ref[level], TN, preferred_element_type=f32
            )
            inner_acc[some, :] += lax.dot_general(
                tokens[level, :, some], hidden_grad[...], TN, preferred_element_type=f32
            )
        router_grad_ref[...] += lax.dot_general(tokens[level], logit_grad[...], TN, preferred_element_type=f32)

    def order(i):
        return nearest(place, jnp.where(i == 0, 0, jnp.where(i == planes - 1, 1, i + 1)))

    def step(i, carry):
        level, before = order(i), order(i - 1)

        def half(s, carry):
            r = jnp.where(i == 0, s, 1 - s)

            @pl.when((i == 0) & (s == 0))
            def _():
                grads_load(z).wait()
                c_copy(z, 0).wait_recv()

            @pl.when((i == 0) & (s == 1))
            def _():
                hop(1)

            @pl.when((i == 0) == (s == 1))
            def _():
                x_copy(level).wait_recv()
                c_copy(level, 1).start()
                c_copy(level, 1).wait_recv()

            @pl.when((i > 0) & (s == 0))
            def _():
                grads_load(level).wait()

            @pl.when((i > 0) & (s == 1))
            def _():
                @pl.when(i + 2 < planes)
                def _():
                    hop(i + 2)

                level_sum(before)

                @pl.when(before != z)
                def _():
                    sum_z_copy(before, z).start()

                across_sum(level)
                c_copy(level, 0).wait_recv()

            tiles(level, r)
            sum_c_copy(level, r).start()
            mix_store(level, r).start()
            return carry

        lax.fori_loop(0, 2, half, 0)

        @pl.when((i == 0) & (i + 2 < planes))
        def _():
            hop(2)

        @pl.when(i == planes - 1)
        def _():
            level_sum(level)
            sum_z_copy(level, z).start()

        weight_grads(level)

        @pl.when(i == 0)
        def _():
            across_sum(z)

        return carry

    lax.fori_loop(0, planes, step, 0)
    inner_grad_ref[...] = inner_acc[...].astype(bf16)
    outer_grad_ref[...] = outer_acc[...].astype(bf16)
    total = part[z, 0:rows, :].astype(f32)
    for k in range(1, planes):
        source = lax.rem(z + k, planes)
        sum_z_copy(z, source).wait_recv()
        total = total + from_z[source].astype(f32)
    out_ref[...] = total
    for level in range(planes):
        mix_store(level, 0).wait()
        mix_store(level, 1).wait()
        x_copy(level).wait_send()
        c_copy(level, 0).wait_send()
        c_copy(level, 1).wait_send()
        sum_c_copy(level, 0).wait_send()
        sum_c_copy(level, 1).wait_send()
        sum_x_copy(level).wait_send()

        @pl.when(level != z)
        def _():
            sum_z_copy(level, z).wait_send()

        @pl.when((z >= level) & (z < planes - 1))
        def _():
            up_copy(level).wait_send()

        @pl.when((z <= level) & (z > 0))
        def _():
            down_copy(level).wait_send()


def experts_of_the_plane(planes, own, real, normed, grads, inner, outer, bias, small):
    f32, bf16 = jnp.float32, jnp.bfloat16
    rows = normed.shape[0]
    chunk = 4 * rows
    width, units = inner.shape
    shape = jax.ShapeDtypeStruct
    vmem = pl.BlockSpec(memory_space=pltpu.VMEM)
    anywhere = pl.BlockSpec(memory_space=pl.ANY)
    dma = pltpu.SemaphoreType.DMA
    flops = 12 * planes * chunk * width * units
    return pl.pallas_call(
        functools.partial(expert_kernel, planes, own, rows, real),
        out_shape=[
            shape((planes, chunk, width), bf16),
            shape((rows, width), f32),
            shape((width, units), bf16),
            shape((units, width), bf16),
            shape((8, units), f32),
            shape((width, 128), f32),
        ],
        in_specs=[vmem, anywhere, vmem, anywhere, vmem, vmem],
        out_specs=[anywhere] + [vmem] * 5,
        scratch_shapes=[
            pltpu.VMEM((planes, chunk, width), bf16),
            pltpu.VMEM((planes, chunk, width), bf16),
            pltpu.VMEM((units, width), bf16),
            pltpu.VMEM((units, width), bf16),
            pltpu.VMEM((width, units), bf16),
            pltpu.VMEM((width, 128), bf16),
            pltpu.VMEM((128, width), bf16),
            pltpu.VMEM((planes, chunk, width), bf16),
            pltpu.VMEM((planes, chunk, width), bf16),
            pltpu.VMEM((planes, 2 * rows, width), bf16),
            pltpu.VMEM((planes, rows, width), bf16),
            pltpu.VMEM((planes, rows, width), bf16),
            pltpu.VMEM((chunk, units), bf16),
            pltpu.VMEM((chunk, units), bf16),
            pltpu.VMEM((chunk, 128), bf16),
            pltpu.VMEM((width, units), f32),
            pltpu.VMEM((units, width), f32),
            dma((own,)),
            dma((planes,)),
            dma((planes, 2)),
        ]
        + [dma((2, planes))] * 2
        + [dma((planes,))] * 2
        + [dma((planes, 2))] * 4
        + [dma((planes,))] * 4,
        compiler_params=pltpu.CompilerParams(
            collective_id=1, has_side_effects=True, vmem_limit_bytes=60 * 2**20
        ),
        cost_estimate=pl.CostEstimate(flops=flops, bytes_accessed=40 * 2**20, transcendentals=0),
        name="experts_of_the_plane",
    )(normed, grads, inner, outer, bias, small)


def front_kernel(
    planes,
    heads,
    real,
    tokens_ref,
    mask_ref,
    ids_ref,
    cotangent_ref,
    *refs,
):
    vector_refs, refs = refs[:5], refs[5:]
    (
        router_part_ref,
        outer_bias_ref,
        qkv_part_ref,
    proj_part_ref,
    inner_part_ref,
    small_all,
    w_qkv_out,
    w_proj_out,
    inner_all,
    normed_in_ref,
    qkv_ref,
    attended_ref,
    middle_ref,
    normed_ref,
    grad_ref,
    grads_all,
    wide_ref,
    select_ref,
    keys_ref,
    keep_ref,
    w_qkv_all,
    w_proj_all,
    out_sem,
    up_send,
    up_recv,
    down_send,
    down_recv,
    x_send,
    x_recv,
    c_send,
    c_recv,
    over_send,
    over_recv,
    over_c_send,
    over_c_recv,
    g_z_send,
    g_z_recv,
    g_x_send,
    g_x_recv,
    g_c_send,
    g_c_recv,
    spread_send,
    spread_recv,
    own_sem,
    y_send,
    y_recv,
    ) = refs
    f32, bf16 = jnp.float32, jnp.bfloat16
    place = Place(planes)
    rows, width = wide_ref.shape
    depth = qkv_part_ref.shape[0]
    experts = inner_part_ref.shape[0]
    half = depth // 2
    lanes = inner_part_ref.shape[2] // (2 * planes)
    head_dim = width // heads
    y, c, z, x = place.y, place.c, place.z, place.x
    gathered = [small_all, w_qkv_all, w_proj_all]

    def remote(src, dst, send, recv, device):
        return pltpu.make_async_remote_copy(
            src_ref=src, dst_ref=dst, send_sem=send, recv_sem=recv, device_id=device, device_id_type=MESH
        )

    def block(j, level, across, core, plane):
        start = pl.multiple_of((level * 2 + across) * depth + core * half, 16)
        if j == 0:
            return gathered[j].at[pl.ds(start, half)]
        columns = gathered[j].shape[1] // 2
        return gathered[j].at[pl.ds(start, half), pl.ds(pl.multiple_of(plane * columns, 128), columns)]

    def piece(j, level, across):
        return block(j, level, across, c, y)

    def up_copy(j, level):
        here = piece(j, level, x)
        return remote(here, here, up_send.at[j, level], up_recv.at[j, level], place.at(y, c, z + 1, x))

    def down_copy(j, level):
        here = piece(j, level, x)
        return remote(here, here, down_send.at[j, level], down_recv.at[j, level], place.at(y, c, z - 1, x))

    def x_copy(j, level, across):
        here = piece(j, level, across)
        return remote(here, here, x_send.at[j, level], x_recv.at[j, level], place.other_x())

    def c_copy(j, level, across):
        here = piece(j, level, across)
        at = level * 2 + across
        return remote(here, here, c_send.at[j, at], c_recv.at[j, at], place.other_core())

    def over_copy(j, level, across):
        here = piece(j, level, across)
        at = level * 2 + across
        return remote(here, here, over_send.at[j, at], over_recv.at[j, at], place.other_y())

    def over_c_copy(j, level, across):
        here = block(j, level, across, c, 1 - y)
        at = level * 2 + across
        return remote(here, here, over_c_send.at[j, at], over_c_recv.at[j, at], place.other_core())

    def g_slot(level, at):
        return grads_all.at[level, pl.ds(at * rows, rows)]

    def g_up(level):
        here = g_slot(level, 0)
        return remote(here, here, g_z_send.at[0, level], g_z_recv.at[0, level], place.at(y, c, z + 1, x))

    def g_down(level):
        here = g_slot(level, 0)
        return remote(here, here, g_z_send.at[1, level], g_z_recv.at[1, level], place.at(y, c, z - 1, x))

    def g_x(level):
        return remote(g_slot(level, 0), g_slot(level, 2), g_x_send.at[level], g_x_recv.at[level], place.other_x())

    def g_c(level, r):
        return remote(
            g_slot(level, 2 * r), g_slot(level, 2 * r + 1), g_c_send.at[level, r], g_c_recv.at[level, r], place.other_core()
        )

    def columns_of(f):
        return pl.ds(pl.multiple_of(f * lanes, 128), lanes)

    here_rows = pl.ds(pl.multiple_of((z * 2 + x) * depth, 16), depth)
    my_units = pl.ds(pl.multiple_of(y * lanes, 128), lanes)

    def spread_copy(k, r):
        level, across = lax.rem(z + k, planes), (x + r) % 2
        return remote(
            inner_part_ref.at[c * 2 + y, :, columns_of(level * 2 + across)],
            inner_all.at[here_rows, my_units],
            spread_send.at[k, r],
            spread_recv.at[k, r],
            place.at(y, c, level, across),
        )

    own_copy = pltpu.make_async_copy(
        inner_part_ref.at[c * 2 + y, :, columns_of(z * 2 + x)], inner_all.at[here_rows, my_units], own_sem
    )
    y_copy = remote(inner_all.at[:, my_units], inner_all.at[:, my_units], y_send, y_recv, place.other_y())
    their_units = pl.ds(pl.multiple_of((1 - y) * lanes, 128), lanes)
    from_y = remote(inner_all.at[:, their_units], inner_all.at[:, their_units], y_send, y_recv, place.other_y())

    others = [(k, r) for k in range(planes) for r in range(2) if k or r]
    partners = [place.other_core(), place.other_y()]
    partners += [place.at(y, c, lax.rem(z + k, planes), (x + r) % 2) for k, r in others]
    greet(partners)

    w_qkv_all[here_rows, :] = qkv_part_ref[...]

    def share(j, level, across):
        c_copy(j, level, across).start()
        if j:
            over_copy(j, level, across).start()

    def line(flows):
        @pl.when(z < planes - 1)
        def _():
            for j in flows:
                up_copy(j, z).start()

        @pl.when(z > 0)
        def _():
            for j in flows:
                down_copy(j, z).start()

        for j in flows:
            x_copy(j, z, x).start()

    def hops(flows):
        for h in range(1, planes):
            @pl.when(z >= h)
            def _():
                for j in flows:
                    up_copy(j, z - h).wait_recv()

                    @pl.when(z < planes - 1)
                    def _():
                        up_copy(j, z - h).start()

                    x_copy(j, z - h, x).start()
                    share(j, z - h, x)

            @pl.when(z + h < planes)
            def _():
                for j in flows:
                    down_copy(j, z + h).wait_recv()

                    @pl.when(z > 0)
                    def _():
                        down_copy(j, z + h).start()

                    x_copy(j, z + h, x).start()
                    share(j, z + h, x)

    def arrive(flows):
        for i in range(planes):
            level = nearest(place, i)
            for j in flows:
                x_copy(j, level, 1 - x).wait_recv()
                share(j, level, 1 - x)

    def over_arrive(flows):
        for i in range(planes):
            level = nearest(place, i)
            for j in flows:
                if i:
                    over_copy(j, level, x).wait_recv()
                    over_c_copy(j, level, x).start()
                over_copy(j, level, 1 - x).wait_recv()
                over_c_copy(j, level, 1 - x).start()

    def gather_done(flows):
        for level in range(planes):
            for j in flows:
                c_copy(j, level, 1 - x).wait_recv()
                if j:
                    over_c_copy(j, level, 1 - x).wait_recv()

            @pl.when(level != z)
            def _():
                for j in flows:
                    c_copy(j, level, x).wait_recv()
                    if j:
                        over_c_copy(j, level, x).wait_recv()

    def g_hop(h):
        @pl.when(z >= h)
        def _():
            g_up(z - h).wait_recv()

            @pl.when(z < planes - 1)
            def _():
                g_up(z - h).start()

            g_x(z - h).start()
            g_c(z - h, 0).start()

        @pl.when(z + h < planes)
        def _():
            g_down(z + h).wait_recv()

            @pl.when(z > 0)
            def _():
                g_down(z + h).start()

            g_x(z + h).start()
            g_c(z + h, 0).start()

    line([1])
    lined = [ref[...].astype(f32) for ref in vector_refs] + [outer_bias_ref[...].astype(f32)]
    lined = jnp.concatenate(lined, axis=0)
    lined = jnp.concatenate([lined, jnp.zeros((128 - lined.shape[0], depth), f32)], axis=0)
    lined = jnp.concatenate([lined, jnp.zeros((128, 128 - depth), f32)], axis=1)
    routed = jnp.concatenate([router_part_ref[...].astype(f32), jnp.zeros((depth, 128 - experts), f32)], axis=1)
    small = jnp.transpose(lined)[:depth] + pltpu.roll(routed, 5 + experts, 1)
    small_all[here_rows, :] = small.astype(bf16)
    line([0])
    w_proj_all[here_rows, :] = proj_part_ref[...]
    line([2])
    spare = jnp.zeros((rows - real, width), f32)
    values = jnp.concatenate([tokens_ref[...].astype(f32), spare], axis=0)
    wide_ref[...] = values.astype(bf16)
    normal, _ = norm_parts(values)
    mask = mask_ref[pl.ds(y * 2 + c, 1), :].astype(f32)
    keys = jnp.concatenate([mask, jnp.zeros((1, rows - real), f32)], axis=1)
    keys_ref[...] = keys
    keep = lax.broadcasted_iota(jnp.int32, (rows, rows), 0) == lax.broadcasted_iota(jnp.int32, (rows, rows), 1)
    keep = jnp.sum(jnp.where(keep, keys, 0.0), axis=1, keepdims=True)
    keep_ref[...] = keep
    ids = ids_ref[...]
    number = lax.broadcasted_iota(jnp.int32, (real, 128), 1)
    select = ((number == ids[:, 0:1]) | (number == ids[:, 1:2])).astype(f32)
    select = jnp.concatenate([select, jnp.zeros((rows - real, 128), f32)], axis=0)
    select_ref[...] = select.astype(bf16)
    chosen = jnp.transpose(jnp.concatenate([select, jnp.zeros((256 - rows, 128), f32)], axis=0))[:8]
    chosen = jnp.concatenate([chosen, jnp.zeros((8, width - 256), f32)], axis=1)
    if rows - real > 8:
        chosen = jnp.concatenate([chosen, jnp.zeros((rows - real - 8, width), f32)], axis=0)
    grad_out = cotangent_ref[...].astype(f32) * keep[:real]
    grad_out = jnp.concatenate([grad_out, chosen], axis=0).astype(bf16)
    grad_ref[...] = grad_out
    grads_own = pltpu.make_async_copy(grad_ref, g_slot(z, 0), out_sem.at[2])
    grads_own.start()
    hops([1, 0])
    arrive([1, 0])
    hops([2])
    own_copy.start()
    for k, r in others:
        spread_copy(k, r).start()

    grads_own.wait()

    @pl.when(z < planes - 1)
    def _():
        g_up(z).start()

    @pl.when(z > 0)
    def _():
        g_down(z).start()

    g_x(z).start()
    g_c(z, 0).start()
    arrive([2])
    over_arrive([1])
    gather_done([1, 0])
    qkv_out_copy = pltpu.make_async_copy(w_qkv_all, w_qkv_out, out_sem.at[0])
    qkv_out_copy.start()
    vectors = jnp.transpose(small_all[...].astype(f32))
    normed_in = (normal * vectors[0:1] + vectors[1:2]).astype(bf16)
    normed_in_ref[...] = normed_in
    for j in range(3):
        part = slice(j * width, (j + 1) * width)
        qkv_ref[:, part] = dot(normed_in, w_qkv_all[:, part]).astype(bf16)
    g_hop(1)
    over_arrive([2])
    lane = lax.broadcasted_iota(jnp.int32, (rows, 2 * head_dim), 1)
    usable = keys_ref[...] > 0
    for pair in range(heads // 2):
        if pair == heads // 4:
            g_hop(2)
        at = pair * 2 * head_dim
        queries = qkv_ref[:, at : at + 2 * head_dim]
        keys = qkv_ref[:, width + at : width + at + 2 * head_dim]
        held = qkv_ref[:, 2 * width + at : 2 * width + at + 2 * head_dim]
        outs = []
        for side in range(2):
            only = (lane < head_dim) if side == 0 else (lane >= head_dim)
            scores = lax.dot_general(
                jnp.where(only, queries, 0).astype(bf16), keys, NT, preferred_element_type=f32
            )
            scores = jnp.where(usable, scores * head_dim ** (-0.5), masked_score)
            shifted = jnp.exp(scores - jnp.max(scores, axis=1, keepdims=True))
            probs = (shifted / jnp.sum(shifted, axis=1, keepdims=True)).astype(bf16)
            outs.append(dot(probs, held))
        attended_ref[:, at : at + 2 * head_dim] = jnp.where(lane < head_dim, outs[0], outs[1]).astype(bf16)
    for h in range(3, planes):
        g_hop(h)
    own_copy.wait()
    for k, r in others:
        spread_copy(k, r).wait_recv()
    y_copy.start()
    gather_done([2])
    proj_out_copy = pltpu.make_async_copy(w_proj_all, w_proj_out, out_sem.at[1])
    proj_out_copy.start()
    middle = values + dot(attended_ref[...], w_proj_all[...]) + vectors[2:3]
    middle_ref[...] = middle
    normal_mid, _ = norm_parts(middle)
    normed = normal_mid * vectors[3:4] + vectors[4:5]
    row = lax.broadcasted_iota(jnp.int32, normed.shape, 0)
    normed_ref[...] = jnp.where(row < real, normed, 0.0).astype(bf16)
    for i in range(planes):
        level = nearest(place, i)
        g_x(level).wait_recv()
        g_c(level, 1).start()
    from_y.wait_recv()
    qkv_out_copy.wait()
    proj_out_copy.wait()
    for level in range(planes):
        g_c(level, 0).wait_recv()
        g_c(level, 1).wait_recv()
    y_copy.wait_send()
    for k, r in others:
        spread_copy(k, r).wait_send()
    for level in range(planes):
        g_x(level).wait_send()
        g_c(level, 0).wait_send()
        g_c(level, 1).wait_send()

        @pl.when((z >= level) & (z < planes - 1))
        def _():
            g_up(level).wait_send()

        @pl.when((z <= level) & (z > 0))
        def _():
            g_down(level).wait_send()

    def shared(j, level, across):
        c_copy(j, level, across).wait_send()
        if j:
            over_copy(j, level, across).wait_send()
            over_c_copy(j, level, across).wait_send()

    for j in range(3):
        for level in range(planes):
            x_copy(j, level, x).wait_send()
            shared(j, level, 1 - x)

            @pl.when(level != z)
            def _():
                shared(j, level, x)

            @pl.when((z >= level) & (z < planes - 1))
            def _():
                up_copy(j, level).wait_send()

            @pl.when((z <= level) & (z > 0))
            def _():
                down_copy(j, level).wait_send()


def front(planes, rows, tokens, mask, ids, cotangent, vectors, router, outer_bias, w_qkv, w_proj, w_in):
    f32, bf16 = jnp.float32, jnp.bfloat16
    real, width = tokens.shape
    lanes = w_in.shape[2] // (2 * planes)
    shape = jax.ShapeDtypeStruct
    vmem = pl.BlockSpec(memory_space=pltpu.VMEM)
    anywhere = pl.BlockSpec(memory_space=pl.ANY)
    dma = pltpu.SemaphoreType.DMA
    return pl.pallas_call(
        functools.partial(front_kernel, planes, HEADS, real),
        out_shape=[
            shape((width, 128), bf16),
            shape((width, 3 * width), bf16),
            shape((width, width), bf16),
            shape((width, 2 * lanes), bf16),
            shape((rows, width), bf16),
            shape((rows, 3 * width), bf16),
            shape((rows, width), bf16),
            shape((rows, width), f32),
            shape((rows, width), bf16),
            shape((rows, width), bf16),
            shape((planes, 4 * rows, width), bf16),
            shape((rows, width), bf16),
            shape((rows, 128), bf16),
            shape((1, rows), f32),
            shape((rows, 1), f32),
        ],
        in_specs=[vmem] * (6 + len(vectors)) + [vmem] * 2 + [anywhere],
        out_specs=[vmem] + [anywhere] * 3 + [vmem] * 6 + [anywhere] + [vmem] * 4,
        scratch_shapes=[pltpu.VMEM((width, 3 * width), bf16), pltpu.VMEM((width, width), bf16), dma((3,))]
        + [dma((3, planes))] * 6
        + [dma((3, 2 * planes))] * 6
        + [dma((2, planes))] * 2
        + [dma((planes,))] * 2
        + [dma((planes, 2))] * 4
        + [dma] * 3,
        compiler_params=pltpu.CompilerParams(
            collective_id=2, has_side_effects=True, vmem_limit_bytes=60 * 2**20
        ),
        cost_estimate=pl.CostEstimate(flops=2**32, bytes_accessed=40 * 2**20, transcendentals=0),
        name="dense_weights_and_attention",
    )(tokens, mask, ids, cotangent, *vectors, router, outer_bias, w_qkv, w_proj, w_in)


def back_kernel(planes, heads, own, groups, real, *refs):
    (
        row_grad_ref,
        normed_ref,
        grad_ref,
        middle_ref,
        tokens_ref,
        normed_in_ref,
        qkv_ref,
        attended_ref,
        small_ref,
        w_qkv_all_ref,
        w_proj_ref,
        keys_ref,
        keep_ref,
        select_ref,
        mix_ref,
        inner_ref,
        outer_ref,
        bias_ref,
        router_grad_ref,
    ) = refs[:19]
    mixed_ref, token_grad_ref, qkv_out, proj_out, small_out, inner_out, outer_out, bias_out = refs[19:27]
    refs = refs[27:]
    (
        w_qkv_ref,
        outer_sum,
        grad_attended,
        grad_qkv,
        mix_x,
        mix_z,
        mix_from_core,
        mix_from_x,
        mix_from_z,
        inner_from_y,
        inner_sum,
        outer_from_y,
        bias_from_y,
        held,
        held_small,
        from_core,
        from_core_small,
        from_x,
        from_x_small,
        from_z,
        from_z_small,
        plane_sum,
        plane_sum_small,
        from_y,
        from_y_small,
        final,
        final_small,
    ) = refs[:27]
    (
        load_sem,
        outer_own_sem,
        mix_c_send,
        mix_c_recv,
        mix_x_send,
        mix_x_recv,
        mix_z_send,
        mix_z_recv,
        inner_y_sem,
        spread_send,
        spread_recv,
        inner_back_sem,
        inner_core_sem,
        outer_y_sem,
        outer_c_sem,
        bias_y_sem,
        bias_c_sem,
        own_sem,
        flow_c_sem,
        flow_x_sem,
        flow_z_send,
        flow_z_recv,
        flow_y_sem,
        flow_end_sem,
    ) = refs[27:]
    f32, bf16 = jnp.float32, jnp.bfloat16
    place = Place(planes)
    y, c, z, x = place.y, place.c, place.z, place.x
    rows, width = middle_ref.shape
    depth = width // (2 * planes)
    half = depth // 2
    lanes = inner_ref.shape[1] // own
    head_dim = width // heads
    pair_width = 2 * head_dim
    small_at = groups + 1

    def remote(src, dst, send, recv, device):
        return pltpu.make_async_remote_copy(
            src_ref=src, dst_ref=dst, send_sem=send, recv_sem=recv, device_id=device, device_id_type=MESH
        )

    def swap(src, dst, sem, device):
        return remote(src, dst, sem.at[0], sem.at[1], device)

    def of_flow(j, many, alone):
        return alone if j == small_at else many.at[j]

    mine, theirs = pl.ds(pl.multiple_of(c * half, 16), half), pl.ds(pl.multiple_of((1 - c) * half, 16), half)

    def flow_c(j):
        source = of_flow(j, held, held_small)
        return swap(
            source.at[:, :, theirs], of_flow(j, from_core, from_core_small), flow_c_sem.at[j], place.other_core()
        )

    def flow_x(j):
        source = of_flow(j, held, held_small)
        return swap(source.at[:, 1 - x, mine], of_flow(j, from_x, from_x_small), flow_x_sem.at[j], place.other_x())

    def flow_z(j, k):
        level = lax.rem(z + k, planes)
        source = of_flow(j, held, held_small)
        return remote(
            source.at[level, x, mine],
            of_flow(j, from_z, from_z_small).at[k],
            flow_z_send.at[j, k],
            flow_z_recv.at[j, k],
            place.level(k),
        )

    def flow_y(j):
        return swap(
            of_flow(j, plane_sum, plane_sum_small),
            of_flow(j, from_y, from_y_small),
            flow_y_sem.at[j],
            place.other_y(),
        )

    def flow_end(j):
        here = of_flow(j, final, final_small).at[mine]
        return swap(here, here, flow_end_sem.at[j], place.other_core())

    def flow_core_sum(j):
        flow_c(j).wait_recv()
        kept = of_flow(j, held, held_small)
        total = kept[:, :, mine, :].astype(f32) + of_flow(j, from_core, from_core_small)[...].astype(f32)
        kept[:, :, mine, :] = total.astype(bf16)
        flow_x(j).start()

    def flow_x_sum(j):
        flow_x(j).wait_recv()
        kept = of_flow(j, held, held_small)
        total = kept[:, x, mine, :].astype(f32) + of_flow(j, from_x, from_x_small)[...].astype(f32)
        kept[:, x, mine, :] = total.astype(bf16)
        for k in range(1, planes):
            flow_z(j, k).start()

    def flow_z_sum(j):
        kept = of_flow(j, held, held_small)
        total = kept[z, x, mine, :].astype(f32)
        for k in range(1, planes):
            flow_z(j, k).wait_recv()
            total = total + of_flow(j, from_z, from_z_small)[k].astype(f32)
        of_flow(j, plane_sum, plane_sum_small)[...] = total.astype(bf16)
        flow_y(j).start()

    def flow_y_sum(j):
        flow_y(j).wait_recv()
        total = of_flow(j, plane_sum, plane_sum_small)[...].astype(f32)
        total = total + of_flow(j, from_y, from_y_small)[...].astype(f32)
        of_flow(j, final, final_small)[mine, :] = total.astype(bf16)
        flow_end(j).start()

    loads = [
        pltpu.make_async_copy(mix_ref.at[:, pl.ds(2 * rows, rows)], mix_x, load_sem.at[0]),
        pltpu.make_async_copy(mix_ref.at[:, pl.ds(0, rows)], mix_z, load_sem.at[1]),
        pltpu.make_async_copy(w_qkv_all_ref, w_qkv_ref, load_sem.at[2]),
    ]

    def mix_c(r):
        return remote(
            mix_ref.at[:, pl.ds((2 * r + 1) * rows, rows)],
            mix_from_core.at[:, pl.ds(r * rows, rows)],
            mix_c_send.at[r],
            mix_c_recv.at[r],
            place.other_core(),
        )

    def mix_to_x(level):
        return remote(mix_x.at[level], mix_from_x.at[level], mix_x_send.at[level], mix_x_recv.at[level], place.other_x())

    def mix_to_z(level, source):
        return remote(
            mix_z.at[level], mix_from_z.at[source], mix_z_send.at[level], mix_z_recv.at[source], place.at(y, c, level, x)
        )

    def mix_core_sum():
        for load in loads[:2]:
            load.wait()
        mix_c(0).wait_recv()
        mix_c(1).wait_recv()
        for k in range(1, planes + 1):
            level = lax.rem(z + k, planes)
            total = mix_x[level].astype(f32) + mix_from_core[level, rows:, :].astype(f32)
            mix_x[level] = total.astype(bf16)
            mix_to_x(level).start()
        for level in range(planes):
            total = mix_z[level].astype(f32) + mix_from_core[level, :rows, :].astype(f32)
            mix_z[level] = total.astype(bf16)

    def mix_x_sum(k):
        level = lax.rem(z + k, planes)
        mix_to_x(level).wait_recv()
        mix_z[level] = (mix_z[level].astype(f32) + mix_from_x[level].astype(f32)).astype(bf16)
        if k < planes:
            mix_to_z(level, z).start()

    my_units = pl.ds(pl.multiple_of(y * lanes, 128), lanes)
    their_units = pl.ds(pl.multiple_of((1 - y) * lanes, 128), lanes)
    my_expert, their_expert = c * 2 + y, c * 2 + 1 - y
    my_columns = pl.ds(pl.multiple_of((z * 2 + x) * lanes, 128), lanes)

    def inner_y():
        return swap(inner_ref.at[:, their_units], inner_from_y, inner_y_sem, place.other_y())

    def shard_rows(f):
        return pl.ds(pl.multiple_of(f * depth, 16), depth)

    def spread(k, r):
        level, across = lax.rem(z + k, planes), (x + r) % 2
        return remote(
            inner_sum.at[shard_rows(level * 2 + across)],
            inner_out.at[my_expert, :, my_columns],
            spread_send.at[k, r],
            spread_recv.at[k, r],
            place.at(y, c, level, across),
        )

    own_copy = pltpu.make_async_copy(
        inner_sum.at[shard_rows(z * 2 + x)], inner_out.at[my_expert, :, my_columns], own_sem
    )

    def inner_back():
        here = inner_out.at[my_expert]
        return swap(here, here, inner_back_sem, place.other_y())

    def inner_core(expert, at):
        here = inner_out.at[expert]
        return swap(here, here, inner_core_sem.at[at], place.other_core())

    def outer_y():
        return swap(outer_ref, outer_from_y, outer_y_sem, place.other_y())

    def outer_c():
        return swap(outer_sum, outer_out.at[c], outer_c_sem, place.other_core())

    outer_own = pltpu.make_async_copy(outer_sum, outer_out.at[c], outer_own_sem)

    def bias_y():
        return swap(bias_ref, bias_from_y, bias_y_sem, place.other_y())

    def bias_c():
        here = bias_out.at[c]
        return swap(here, here, bias_c_sem, place.other_core())

    others = [(k, r) for k in range(planes) for r in range(2) if k or r]

    def inner_y_sum():
        inner_y().wait_recv()
        total = inner_ref[:, my_units].astype(f32) + inner_from_y[...].astype(f32)
        inner_sum[...] = total.astype(bf16)
        own_copy.start()
        for k, r in others:
            spread(k, r).start()
        outer_y().start()

    def inner_spread_done():
        own_copy.wait()
        for k, r in others:
            spread(k, r).wait_recv()
        inner_back().start()
        inner_core(my_expert, 0).start()

    def outer_y_sum():
        outer_y().wait_recv()
        total = outer_ref[...].astype(f32) + outer_from_y[...].astype(f32)
        outer_sum[...] = total.astype(bf16)
        outer_own.start()
        outer_c().start()
        bias_y().wait_recv()
        bias_out[c] = bias_ref[...] + bias_from_y[...]
        bias_c().start()

    partners = [place.other_core(), place.other_y()]
    partners += [place.at(y, c, lax.rem(z + k, planes), (x + r) % 2) for k, r in others]
    greet(partners)
    inner_y().start()
    bias_y().start()
    mix_c(1).start()
    mix_c(0).start()
    for load in loads:
        load.start()

    vectors = jnp.transpose(small_ref[...].astype(f32))
    gain_first, gain_second = vectors[0:1], vectors[3:4]
    place_row = lax.broadcasted_iota(jnp.int32, (128, 128), 0)
    place_lane = lax.broadcasted_iota(jnp.int32, (128, 128), 1)

    def lanes_from(first):
        take = (place_row == place_lane + first) & (place_lane < 2 * own)
        return dot(small_ref[...], take.astype(bf16)).astype(bf16)

    outer_bias, router = lanes_from(5), lanes_from(5 + 2 * own)
    normed_mid, grad_out = normed_ref[...], grad_ref[...]
    real_row = lax.broadcasted_iota(jnp.int32, grad_out.shape, 0) < real
    grad_out = jnp.where(real_row, grad_out, 0).astype(bf16)
    select = select_ref[...].astype(f32)
    lane = lax.broadcasted_iota(jnp.int32, select.shape, 1)
    logits = jnp.where(lane < 2 * own, dot(normed_mid, router), -1e30)
    routing = jnp.exp(logits - jnp.max(logits, axis=1, keepdims=True))
    routing = routing / jnp.sum(routing, axis=1, keepdims=True)
    gates = routing * select
    bias_gate = select * dot(grad_out, outer_bias)
    bias_logits = routing * (bias_gate - jnp.sum(routing * bias_gate, axis=1, keepdims=True))
    bias_logits = bias_logits.astype(bf16)
    router_grad = lax.dot_general(normed_mid, bias_logits, TN, preferred_element_type=f32)
    router_grad = pltpu.roll(router_grad, 16, 1) + pltpu.roll(router_grad_ref[...], 16 - real % 16, 1)
    outer_bias_grad = lax.dot_general(gates.astype(bf16), grad_out, TN, preferred_element_type=f32)
    grad_normed_mid = row_grad_ref[...] + lax.dot_general(bias_logits, router, NT, preferred_element_type=f32)
    normal_mid, rstd_mid = norm_parts(middle_ref[...])
    gain_second_grad = jnp.sum(grad_normed_mid * normal_mid, axis=0, keepdims=True)
    bias_second_grad = jnp.sum(grad_normed_mid, axis=0, keepdims=True)
    grad_middle = grad_out.astype(f32) + norm_back(grad_normed_mid, normal_mid, rstd_mid, gain_second)
    grad_proj = grad_middle.astype(bf16)
    proj_bias_grad = jnp.sum(grad_proj.astype(f32), axis=0, keepdims=True)
    mix_core_sum()

    def hold(j, value):
        held[j] = value.astype(bf16).reshape(planes, 2, depth, width)
        flow_c(j).start()

    hold(0, lax.dot_general(attended_ref[...], grad_proj, TN, preferred_element_type=f32))
    grad_attended[...] = lax.dot_general(grad_proj, w_proj_ref[...], NT, preferred_element_type=f32).astype(bf16)
    flow_core_sum(0)

    pair_lane = lax.broadcasted_iota(jnp.int32, (rows, pair_width), 1)
    usable = keys_ref[...] > 0
    scaling = head_dim ** (-0.5)
    group_width = width // groups

    def pair_back(pair):
        at = pair * pair_width
        group, inside = at // group_width, at % group_width
        queries = qkv_ref[:, at : at + pair_width]
        keys = qkv_ref[:, width + at : width + at + pair_width]
        values = qkv_ref[:, 2 * width + at : 2 * width + at + pair_width]
        grads = grad_attended[:, at : at + pair_width]
        found = []
        for side in range(2):
            only = (pair_lane < head_dim) if side == 0 else (pair_lane >= head_dim)
            some_queries = jnp.where(only, queries, 0).astype(bf16)
            some_grads = jnp.where(only, grads, 0).astype(bf16)
            scores = lax.dot_general(some_queries, keys, NT, preferred_element_type=f32)
            scores = jnp.where(usable, scores * scaling, masked_score)
            shifted = jnp.exp(scores - jnp.max(scores, axis=1, keepdims=True))
            probs = shifted / jnp.sum(shifted, axis=1, keepdims=True)
            grad_probs = lax.dot_general(some_grads, values, NT, preferred_element_type=f32)
            grad_scores = probs * (grad_probs - jnp.sum(probs * grad_probs, axis=1, keepdims=True))
            grad_scores = grad_scores.astype(bf16)
            found.append(
                (
                    dot(grad_scores, keys),
                    lax.dot_general(grad_scores, some_queries, TN, preferred_element_type=f32),
                    lax.dot_general(probs.astype(bf16), some_grads, TN, preferred_element_type=f32),
                )
            )
        grad_queries = jnp.where(pair_lane < head_dim, found[0][0], found[1][0]) * scaling
        grad_keys = (found[0][1] + found[1][1]) * scaling
        grad_values = found[0][2] + found[1][2]
        for part, value in enumerate((grad_queries, grad_keys, grad_values)):
            start = part * group_width + inside
            grad_qkv[group, :, start : start + pair_width] = value.astype(bf16)

    def group_back(group):
        per_group = heads // 2 // groups
        for pair in range(group * per_group, (group + 1) * per_group):
            pair_back(pair)
        hold(
            1 + group,
            lax.dot_general(normed_in_ref[...], grad_qkv[group], TN, preferred_element_type=f32),
        )

    group_back(0)
    inner_y_sum()
    flow_core_sum(1)
    mix_x_sum(1)
    for group in range(1, groups):
        group_back(group)
        flow_core_sum(1 + group)
        if group == 1:
            mix_x_sum(2)

    loads[2].wait()
    grad_normed_in = jnp.zeros((rows, width), f32)
    for group in range(groups):
        for part in range(3):
            grad_normed_in = grad_normed_in + lax.dot_general(
                grad_qkv[group, :, part * group_width : (part + 1) * group_width],
                w_qkv_ref[:, part * width + group * group_width : part * width + (group + 1) * group_width],
                NT,
                preferred_element_type=f32,
            )
    normal_first, rstd_first = norm_parts(tokens_ref[...].astype(f32))
    gain_first_grad = jnp.sum(grad_normed_in * normal_first, axis=0, keepdims=True)
    bias_first_grad = jnp.sum(grad_normed_in, axis=0, keepdims=True)
    token_grad = grad_middle + norm_back(grad_normed_in, normal_first, rstd_first, gain_first)
    token_grad_ref[...] = token_grad.astype(bf16)[:real]
    vector_rows = jnp.concatenate(
        [
            gain_first_grad,
            bias_first_grad,
            proj_bias_grad,
            gain_second_grad,
            bias_second_grad,
            jnp.zeros((3, width), f32),
            outer_bias_grad[:8],
            jnp.zeros((112, width), f32),
        ],
        axis=0,
    )
    vector_grads = jnp.transpose(vector_rows) + router_grad
    held_small[...] = vector_grads.astype(bf16).reshape(planes, 2, depth, 128)
    flow_c(small_at).start()
    flow_core_sum(small_at)
    for k in range(3, planes):
        mix_x_sum(k)
    inner_spread_done()
    flow_x_sum(0)
    flow_x_sum(1)
    mix_x_sum(planes)
    outer_y_sum()
    for group in range(1, groups):
        flow_x_sum(1 + group)
    flow_z_sum(0)
    flow_x_sum(small_at)
    mixture = mix_z[z].astype(f32) + dot(gates.astype(bf16), jnp.transpose(outer_bias.astype(f32)).astype(bf16))
    for k in range(1, planes):
        source = lax.rem(z + k, planes)
        mix_to_z(z, source).wait_recv()
        mixture = mixture + mix_from_z[source].astype(f32)
    mixed = (keep_ref[...] * (middle_ref[...] + mixture)).astype(bf16)
    mixed_ref[...] = mixed[:real]
    flow_y_sum(0)
    for group in range(groups):
        flow_z_sum(1 + group)
    flow_z_sum(small_at)
    inner_back().wait_recv()
    inner_core(their_expert, 1).start()
    for group in range(groups):
        flow_y_sum(1 + group)
    flow_y_sum(small_at)

    def arrived(j):
        here = of_flow(j, final, final_small).at[theirs]
        swap(here, here, flow_end_sem.at[j], place.other_core()).wait_recv()

    arrived(0)
    proj_out[...] = final[0]
    for group in range(groups):
        arrived(1 + group)
        for part in range(3):
            start = part * width + group * group_width
            qkv_out[:, start : start + group_width] = final[
                1 + group, :, part * group_width : (part + 1) * group_width
            ]
    arrived(small_at)
    small_out[...] = final_small[...].astype(f32)
    outer_own.wait()
    outer_c().wait_recv()
    bias_theirs = bias_out.at[1 - c]
    swap(bias_theirs, bias_theirs, bias_c_sem, place.other_core()).wait_recv()
    for at, expert in enumerate(((1 - c) * 2 + y, (1 - c) * 2 + 1 - y)):
        inner_core(expert, at).wait_recv()

    mix_c(0).wait_send()
    mix_c(1).wait_send()
    inner_y().wait_send()
    inner_back().wait_send()
    inner_core(my_expert, 0).wait_send()
    inner_core(their_expert, 1).wait_send()
    outer_y().wait_send()
    outer_c().wait_send()
    bias_y().wait_send()
    bias_c().wait_send()
    for k, r in others:
        spread(k, r).wait_send()
    for k in range(1, planes + 1):
        level = lax.rem(z + k, planes)
        mix_to_x(level).wait_send()
        if k < planes:
            mix_to_z(level, z).wait_send()
    for j in range(groups + 2):
        flow_c(j).wait_send()
        flow_x(j).wait_send()
        for k in range(1, planes):
            flow_z(j, k).wait_send()
        flow_y(j).wait_send()
        flow_end(j).wait_send()


def back(planes, own, real, *args):
    f32, bf16 = jnp.float32, jnp.bfloat16
    (
        row_grad,
        normed_mid,
        grad_out,
        middle,
        tokens,
        normed_in,
        qkv,
        attended,
        small,
        w_qkv,
        w_proj,
        keys,
        keep,
        select,
        mix_parts,
        inner_grad,
        outer_grad,
        bias_grad,
        router_grad,
    ) = args
    rows, width = middle.shape
    depth = width // (2 * planes)
    half = depth // 2
    lanes = inner_grad.shape[1] // own
    tall = outer_grad.shape[0]
    pairs = HEADS // 2
    groups = 3 if pairs % 3 == 0 and (pairs // 3) * 2 * (width // HEADS) % 128 == 0 else 1
    flows = groups + 1
    shape = jax.ShapeDtypeStruct
    vmem = pl.BlockSpec(memory_space=pltpu.VMEM)
    anywhere = pl.BlockSpec(memory_space=pl.ANY)
    dma = pltpu.SemaphoreType.DMA

    def both(*dims):
        return [pltpu.VMEM((flows, *dims, width), bf16), pltpu.VMEM((*dims, 128), bf16)]

    return pl.pallas_call(
        functools.partial(back_kernel, planes, HEADS, own, groups, real),
        out_shape=[
            shape((real, width), bf16),
            shape((real, width), bf16),
            shape((depth, 3 * width), bf16),
            shape((depth, width), bf16),
            shape((depth, 128), f32),
            shape((2 * own, depth, 2 * planes * lanes), bf16),
            shape((2, tall, width), bf16),
            shape((2, *bias_grad.shape), f32),
        ],
        in_specs=[vmem] * 9 + [anywhere] + [vmem] * 4 + [anywhere] + [vmem] * 4,
        out_specs=[vmem] * 5 + [anywhere] * 2 + [vmem],
        scratch_shapes=[
            pltpu.VMEM((width, 3 * width), bf16),
            pltpu.VMEM((tall, width), bf16),
            pltpu.VMEM((rows, width), bf16),
            pltpu.VMEM((groups, rows, 3 * width // groups), bf16),
            pltpu.VMEM((planes, rows, width), bf16),
            pltpu.VMEM((planes, rows, width), bf16),
            pltpu.VMEM((planes, 2 * rows, width), bf16),
            pltpu.VMEM((planes, rows, width), bf16),
            pltpu.VMEM((planes, rows, width), bf16),
            pltpu.VMEM((width, lanes), bf16),
            pltpu.VMEM((width, lanes), bf16),
            pltpu.VMEM((tall, width), bf16),
            pltpu.VMEM(bias_grad.shape, f32),
        ]
        + both(planes, 2, depth)
        + both(planes, 2, half)
        + both(planes, half)
        + both(planes, half)
        + both(half)
        + both(half)
        + both(depth)
        + [dma((3,)), dma]
        + [dma((2,))] * 2
        + [dma((planes,))] * 4
        + [dma((2,))]
        + [dma((planes, 2))] * 2
        + [dma((2,)), dma((2, 2)), dma((2,)), dma((2,)), dma((2,)), dma((2,)), dma]
        + [dma((flows + 1, 2))] * 2
        + [dma((flows + 1, planes))] * 2
        + [dma((flows + 1, 2))] * 2,
        compiler_params=pltpu.CompilerParams(
            collective_id=3, has_side_effects=True, vmem_limit_bytes=60 * 2**20
        ),
        cost_estimate=pl.CostEstimate(flops=2**33, bytes_accessed=40 * 2**20, transcendentals=0),
        name="attention_backward_and_sums",
    )(*args)


def norm_parts(values):
    center = values - jnp.mean(values, axis=-1, keepdims=True)
    rstd = lax.rsqrt(jnp.mean(center * center, axis=-1, keepdims=True) + epsilon)
    return center * rstd, rstd


def norm_back(grad, normal, rstd, gain):
    scaled = grad * gain
    return rstd * (
        scaled
        - jnp.mean(scaled, axis=-1, keepdims=True)
        - normal * jnp.mean(scaled * normal, axis=-1, keepdims=True)
    )


def move_tokens_plan(
    tokens,
    key_mask,
    expert_ids,
    cotangent,
    norm1_gain,
    norm1_bias,
    w_qkv,
    w_proj,
    proj_bias,
    norm2_gain,
    norm2_bias,
    w_router,
    w_in,
    b_in,
    w_out,
    b_out,
):
    f32 = jnp.float32
    _, rows, width = tokens.shape
    experts, depth, hidden = w_in.shape
    slice_width = w_out.shape[1]
    planes = hidden // slice_width // 2
    own = experts // 2
    padded = (rows + experts + 15) // 16 * 16
    vectors = [v[None] for v in (norm1_gain, norm1_bias, proj_bias, norm2_gain, norm2_bias)]
    fronts = front(
        planes,
        padded,
        tokens[0],
        key_mask,
        expert_ids[0],
        cotangent[0],
        vectors,
        w_router,
        b_out,
        w_qkv,
        w_proj,
        w_in,
    )
    small, full_qkv, full_proj, inner, normed_in, qkv, attended, middle = fronts[:8]
    normed_mid, grad_out, all_grad_out, wide, select, keys, keep = fronts[8:]
    mix_parts, row_grad, inner_grad, outer_grad, bias_grad, router_grad = experts_of_the_plane(
        planes, own, rows, normed_mid, all_grad_out, inner, w_out, b_in, small
    )
    mixed, token_grad, qkv_grad, proj_grad, vector_grads, inner_grad, outer_grad, bias_grad = back(
        planes,
        own,
        rows,
        row_grad,
        normed_mid,
        grad_out,
        middle,
        wide,
        normed_in,
        qkv,
        attended,
        small,
        full_qkv,
        full_proj,
        keys,
        keep,
        select,
        mix_parts,
        inner_grad,
        outer_grad,
        bias_grad,
        router_grad,
    )
    return (
        mixed[None],
        token_grad[None],
        vector_grads[:, 0],
        vector_grads[:, 1],
        qkv_grad.astype(f32),
        proj_grad.astype(f32),
        vector_grads[:, 2],
        vector_grads[:, 3],
        vector_grads[:, 4],
        vector_grads[:, 16 : 16 + experts],
        inner_grad.astype(f32),
        bias_grad[:, 0].reshape(experts, slice_width),
        outer_grad.reshape(experts, slice_width, width).astype(f32),
        vector_grads[:, 8 : 8 + experts].T,
    )


def solution(mesh):
    n_seq, n_fsdp = mesh.shape["seq"], mesh.shape["fsdp"]

    def per_device(*args):
        tokens, w_in, w_out = args[0], args[12], args[14]
        experts, _, hidden = w_in.shape
        lanes = hidden // n_fsdp
        whole_tiles = lanes % 128 == 0 and tokens.shape[2] % 256 == 0 and w_in.shape[1] % 32 == 0 and 2 * lanes <= tokens.shape[2]
        if n_seq == 4 and experts == n_seq and tokens.shape[0] == 1 and whole_tiles:
            return move_tokens_plan(*args)
        return gather_weights_plan(*args)

    return jax.shard_map(
        per_device,
        mesh=mesh,
        in_specs=(
            P(("fsdp", "seq"), None, None),
            P("fsdp", None),
            P(("fsdp", "seq"), None, None),
            P(("fsdp", "seq"), None, None),
            P("fsdp"),
            P("fsdp"),
            P("fsdp", None),
            P("fsdp", None),
            P("fsdp"),
            P("fsdp"),
            P("fsdp"),
            P("fsdp", None),
            P(None, "fsdp", None),
            P(None, "fsdp"),
            P(None, "fsdp", None),
            P(None, "fsdp"),
        ),
        out_specs=(
            P(("fsdp", "seq"), None, None),
            P(("fsdp", "seq"), None, None),
            P("fsdp"),
            P("fsdp"),
            P("fsdp", None),
            P("fsdp", None),
            P("fsdp"),
            P("fsdp"),
            P("fsdp"),
            P("fsdp", None),
            P(None, "fsdp", None),
            P(None, "fsdp"),
            P(None, "fsdp", None),
            P(None, "fsdp"),
        ),
        check_vma=False,
    )
```

```python
import functools

import jax
import jax.numpy as jnp
from jax import lax
from jax.experimental import pallas as pl
from jax.experimental.pallas import tpu as pltpu
from jax.sharding import PartitionSpec as P

HEADS = 12
CAP = 142


epsilon = 1e-06
masked_score = -1e30


def norm_rows(values, gain, offset):
    center = values - jnp.mean(values, axis=-1, keepdims=True)
    spread = jnp.mean(center * center, axis=-1, keepdims=True)
    return center * lax.rsqrt(spread + epsilon) * gain + offset


def softmax_rows(values):
    shifted = jnp.exp(values - jnp.max(values, axis=-1, keepdims=True))
    return shifted / jnp.sum(shifted, axis=-1, keepdims=True)


def exact_gelu(values):
    return jax.nn.gelu(values, approximate=False)


def expert_slots(chosen, experts):
    flat_ids = chosen.reshape(-1)
    onehot = (flat_ids[:, None] == jnp.arange(experts, dtype=jnp.int32)[None, :]).astype(jnp.int32)
    ranks = jnp.cumsum(onehot, axis=0, dtype=jnp.int32)
    slot_pos = jnp.sum(onehot * ranks, axis=1, dtype=jnp.int32) - 1
    return (flat_ids, slot_pos)


def gather_weights_plan(
    tokens,
    key_mask,
    expert_ids,
    cotangent,
    norm1_gain,
    norm1_bias,
    w_qkv,
    w_proj,
    proj_bias,
    norm2_gain,
    norm2_bias,
    w_router,
    w_in,
    b_in,
    w_out,
    b_out,
):
    images, seq_len, width = tokens.shape
    experts = w_in.shape[0]
    head_dim = width // HEADS
    scaling = head_dim ** (-0.5)
    row_count = images * seq_len
    dense_set = (
        lax.all_gather(norm1_gain, "fsdp", axis=0, tiled=True),
        lax.all_gather(norm1_bias, "fsdp", axis=0, tiled=True),
        lax.all_gather(w_qkv, "fsdp", axis=0, tiled=True),
        lax.all_gather(w_proj, "fsdp", axis=0, tiled=True),
        lax.all_gather(proj_bias, "fsdp", axis=0, tiled=True),
        lax.all_gather(norm2_gain, "fsdp", axis=0, tiled=True),
        lax.all_gather(norm2_bias, "fsdp", axis=0, tiled=True),
        lax.all_gather(w_router, "fsdp", axis=0, tiled=True),
    )
    gain_first = dense_set[0].astype(jnp.float32)
    bias_first = dense_set[1].astype(jnp.float32)
    full_qkv = dense_set[2]
    full_proj = dense_set[3]
    bias_proj = dense_set[4].astype(jnp.float32)
    gain_second = dense_set[5].astype(jnp.float32)
    bias_second = dense_set[6].astype(jnp.float32)
    full_router = dense_set[7]
    expert_set = (
        lax.all_gather(w_in, "fsdp", axis=1, tiled=True),
        lax.all_gather(b_in, "fsdp", axis=1, tiled=True),
        lax.all_gather(w_out, "fsdp", axis=1, tiled=True),
        lax.all_gather(b_out, "fsdp", axis=1, tiled=True),
    )
    inner_weight = expert_set[0]
    inner_bias = expert_set[1].astype(jnp.float32)
    outer_weight = expert_set[2]
    outer_bias = expert_set[3].astype(jnp.float32)
    own_mask = lax.dynamic_slice_in_dim(key_mask, lax.axis_index("seq") * images, images, 0)
    keep_rows = own_mask.reshape(row_count, 1).astype(jnp.float32)
    usable = (key_mask > 0)[:, None, None, :]
    flat_tokens = tokens.astype(jnp.float32).reshape(row_count, width)
    normed_in = norm_rows(flat_tokens, gain_first, bias_first).astype(jnp.bfloat16)
    mixed_qkv = jnp.dot(normed_in, full_qkv, preferred_element_type=jnp.float32).astype(
        jnp.bfloat16
    )
    mixed_qkv = mixed_qkv.reshape(images, seq_len, 3, HEADS, head_dim)
    head_qkv = lax.all_to_all(mixed_qkv, "seq", split_axis=3, concat_axis=0, tiled=True)
    queries = head_qkv[:, :, 0]
    key_rows = head_qkv[:, :, 1]
    value_rows = head_qkv[:, :, 2]

    def score_block():
        raw = (
            jnp.einsum("gahd,gbhd->ghab", queries, key_rows, preferred_element_type=jnp.float32)
            * scaling
        )
        return jnp.where(usable, raw, masked_score)

    scores = score_block()
    row_top = jnp.max(scores, axis=-1, keepdims=True)
    shifted = jnp.exp(scores - row_top)
    row_total = jnp.sum(shifted, axis=-1, keepdims=True)
    attn_probs = (shifted / row_total).astype(jnp.bfloat16)
    log_total = row_top + jnp.log(row_total)
    head_out = jnp.einsum(
        "ghab,gbhd->gahd", attn_probs, value_rows, preferred_element_type=jnp.float32
    ).astype(jnp.bfloat16)
    attended = lax.all_to_all(head_out, "seq", split_axis=0, concat_axis=2, tiled=True).reshape(
        row_count, width
    )
    middle = (
        flat_tokens + jnp.dot(attended, full_proj, preferred_element_type=jnp.float32) + bias_proj
    )
    normed_mid = norm_rows(middle, gain_second, bias_second).astype(jnp.bfloat16)
    routing = softmax_rows(jnp.dot(normed_mid, full_router, preferred_element_type=jnp.float32))
    chosen = expert_ids.reshape(row_count, 2)
    flat_ids, slot_pos = expert_slots(chosen, experts)
    gating = jnp.take_along_axis(routing, chosen, axis=1)
    buffer = (
        jnp.zeros((experts, CAP, width), jnp.bfloat16)
        .at[flat_ids, slot_pos]
        .set(jnp.repeat(normed_mid, 2, axis=0))
    )
    pre_act = (
        jnp.einsum("ecd,edf->ecf", buffer, inner_weight, preferred_element_type=jnp.float32)
        + inner_bias[:, None, :]
    )
    activated = exact_gelu(pre_act).astype(jnp.bfloat16)
    expert_out = (
        jnp.einsum("ecf,efd->ecd", activated, outer_weight, preferred_element_type=jnp.float32)
        + outer_bias[:, None, :]
    )
    picked = expert_out[flat_ids, slot_pos].reshape(row_count, 2, width)
    mixture = jnp.sum(gating[:, :, None] * picked, axis=1)
    mixed = (keep_rows * (middle + mixture)).astype(jnp.bfloat16).reshape(images, seq_len, width)
    grad_out = cotangent.astype(jnp.float32).reshape(row_count, width) * keep_rows
    grad_gate = jnp.sum(grad_out[:, None, :] * picked, axis=2)
    grad_picked = (
        (gating[:, :, None] * grad_out[:, None, :])
        .astype(jnp.bfloat16)
        .reshape(2 * row_count, width)
    )
    grad_expert_out = (
        jnp.zeros((experts, CAP, width), jnp.bfloat16).at[flat_ids, slot_pos].set(grad_picked)
    )
    grad_outer_bias = jnp.sum(grad_expert_out, axis=1, dtype=jnp.float32)
    hidden_pre = (
        jnp.einsum("ecd,edf->ecf", buffer, inner_weight, preferred_element_type=jnp.float32)
        + inner_bias[:, None, :]
    )
    hidden_act = exact_gelu(hidden_pre).astype(jnp.bfloat16)
    grad_outer_weight = jnp.einsum(
        "ecf,ecd->efd", hidden_act, grad_expert_out, preferred_element_type=jnp.float32
    )
    grad_act = jnp.einsum(
        "ecd,efd->ecf", grad_expert_out, outer_weight, preferred_element_type=jnp.float32
    )
    gelu_pull = jax.vjp(exact_gelu, hidden_pre)[1]
    grad_pre = gelu_pull(grad_act)[0].astype(jnp.bfloat16)
    grad_inner_bias = jnp.sum(grad_pre, axis=1, dtype=jnp.float32)
    grad_inner_weight = jnp.einsum(
        "ecd,ecf->edf", buffer, grad_pre, preferred_element_type=jnp.float32
    )
    grad_buffer = jnp.einsum(
        "ecf,edf->ecd", grad_pre, inner_weight, preferred_element_type=jnp.float32
    )
    grad_rows = jnp.sum(grad_buffer[flat_ids, slot_pos].reshape(row_count, 2, width), axis=1)
    expert_range = jnp.arange(experts, dtype=jnp.int32)[None, None, :]
    grad_route = jnp.sum(
        grad_gate[:, :, None] * (chosen[:, :, None] == expert_range).astype(jnp.float32), axis=1
    )
    grad_logits = (
        routing * (grad_route - jnp.sum(routing * grad_route, axis=-1, keepdims=True))
    ).astype(jnp.bfloat16)
    grad_router = jnp.einsum(
        "nd,ne->de", normed_mid, grad_logits, preferred_element_type=jnp.float32
    )
    grad_normed_mid = grad_rows + jnp.einsum(
        "ne,de->nd", grad_logits, full_router, preferred_element_type=jnp.float32
    )
    second_pull = jax.vjp(norm_rows, middle, gain_second, bias_second)[1]
    grad_mid_norm, grad_gain_second, grad_bias_second = second_pull(grad_normed_mid)
    grad_middle = grad_out + grad_mid_norm
    grad_proj = grad_middle.astype(jnp.bfloat16)
    grad_bias_proj = jnp.sum(grad_proj, axis=0, dtype=jnp.float32)
    grad_proj_weight = jnp.einsum(
        "nd,ne->de", attended, grad_proj, preferred_element_type=jnp.float32
    )
    grad_attended = jnp.einsum(
        "ne,de->nd", grad_proj, full_proj, preferred_element_type=jnp.float32
    ).astype(jnp.bfloat16)
    grad_head_out = lax.all_to_all(
        grad_attended.reshape(images, seq_len, HEADS, head_dim),
        "seq",
        split_axis=2,
        concat_axis=0,
        tiled=True,
    )
    recomputed = jnp.exp(score_block() - log_total)
    grad_values = jnp.einsum(
        "ghab,gahd->gbhd",
        recomputed.astype(jnp.bfloat16),
        grad_head_out,
        preferred_element_type=jnp.float32,
    )
    grad_probs = jnp.einsum(
        "gahd,gbhd->ghab", grad_head_out, value_rows, preferred_element_type=jnp.float32
    )
    grad_scores = (
        recomputed * (grad_probs - jnp.sum(recomputed * grad_probs, axis=-1, keepdims=True))
    ).astype(jnp.bfloat16)
    grad_queries = (
        jnp.einsum("ghab,gbhd->gahd", grad_scores, key_rows, preferred_element_type=jnp.float32)
        * scaling
    )
    grad_keys = (
        jnp.einsum("ghab,gahd->gbhd", grad_scores, queries, preferred_element_type=jnp.float32)
        * scaling
    )
    grad_head_qkv = jnp.stack([grad_queries, grad_keys, grad_values], axis=2).astype(jnp.bfloat16)
    grad_qkv = lax.all_to_all(
        grad_head_qkv, "seq", split_axis=0, concat_axis=3, tiled=True
    ).reshape(row_count, 3 * width)
    grad_qkv_weight = jnp.einsum(
        "nd,ne->de", normed_in, grad_qkv, preferred_element_type=jnp.float32
    )
    grad_normed_in = jnp.einsum("ne,de->nd", grad_qkv, full_qkv, preferred_element_type=jnp.float32)
    first_pull = jax.vjp(norm_rows, flat_tokens, gain_first, bias_first)[1]
    grad_first, grad_gain_first, grad_bias_first = first_pull(grad_normed_in)
    token_grad = (grad_middle + grad_first).astype(jnp.bfloat16).reshape(images, seq_len, width)
    shares = (
        lax.psum_scatter(grad_gain_first, "fsdp", scatter_dimension=0, tiled=True),
        lax.psum_scatter(grad_bias_first, "fsdp", scatter_dimension=0, tiled=True),
        lax.psum_scatter(grad_qkv_weight, "fsdp", scatter_dimension=0, tiled=True),
        lax.psum_scatter(grad_proj_weight, "fsdp", scatter_dimension=0, tiled=True),
        lax.psum_scatter(grad_bias_proj, "fsdp", scatter_dimension=0, tiled=True),
        lax.psum_scatter(grad_gain_second, "fsdp", scatter_dimension=0, tiled=True),
        lax.psum_scatter(grad_bias_second, "fsdp", scatter_dimension=0, tiled=True),
        lax.psum_scatter(grad_router, "fsdp", scatter_dimension=0, tiled=True),
        lax.psum_scatter(grad_inner_weight, "fsdp", scatter_dimension=1, tiled=True),
        lax.psum_scatter(grad_inner_bias, "fsdp", scatter_dimension=1, tiled=True),
        lax.psum_scatter(grad_outer_weight, "fsdp", scatter_dimension=1, tiled=True),
        lax.psum_scatter(grad_outer_bias, "fsdp", scatter_dimension=1, tiled=True),
    )
    parted = (
        lax.psum_scatter(
            shares[0].astype(jnp.bfloat16), "seq", scatter_dimension=0, tiled=True
        ).astype(jnp.float32),
        lax.psum_scatter(
            shares[1].astype(jnp.bfloat16), "seq", scatter_dimension=0, tiled=True
        ).astype(jnp.float32),
        lax.psum_scatter(
            shares[2].astype(jnp.bfloat16), "seq", scatter_dimension=0, tiled=True
        ).astype(jnp.float32),
        lax.psum_scatter(
            shares[3].astype(jnp.bfloat16), "seq", scatter_dimension=0, tiled=True
        ).astype(jnp.float32),
        lax.psum_scatter(
            shares[4].astype(jnp.bfloat16), "seq", scatter_dimension=0, tiled=True
        ).astype(jnp.float32),
        lax.psum_scatter(
            shares[5].astype(jnp.bfloat16), "seq", scatter_dimension=0, tiled=True
        ).astype(jnp.float32),
        lax.psum_scatter(
            shares[6].astype(jnp.bfloat16), "seq", scatter_dimension=0, tiled=True
        ).astype(jnp.float32),
        lax.psum_scatter(
            shares[7].astype(jnp.bfloat16), "seq", scatter_dimension=0, tiled=True
        ).astype(jnp.float32),
        lax.psum_scatter(
            shares[8].astype(jnp.bfloat16), "seq", scatter_dimension=1, tiled=True
        ).astype(jnp.float32),
        lax.psum_scatter(
            shares[9].astype(jnp.bfloat16), "seq", scatter_dimension=1, tiled=True
        ).astype(jnp.float32),
        lax.psum_scatter(
            shares[10].astype(jnp.bfloat16), "seq", scatter_dimension=1, tiled=True
        ).astype(jnp.float32),
        lax.psum_scatter(
            shares[11].astype(jnp.bfloat16), "seq", scatter_dimension=1, tiled=True
        ).astype(jnp.float32),
    )
    totals = (
        lax.all_gather(parted[0].astype(jnp.bfloat16), "seq", axis=0, tiled=True).astype(
            jnp.float32
        ),
        lax.all_gather(parted[1].astype(jnp.bfloat16), "seq", axis=0, tiled=True).astype(
            jnp.float32
        ),
        lax.all_gather(parted[2].astype(jnp.bfloat16), "seq", axis=0, tiled=True).astype(
            jnp.float32
        ),
        lax.all_gather(parted[3].astype(jnp.bfloat16), "seq", axis=0, tiled=True).astype(
            jnp.float32
        ),
        lax.all_gather(parted[4].astype(jnp.bfloat16), "seq", axis=0, tiled=True).astype(
            jnp.float32
        ),
        lax.all_gather(parted[5].astype(jnp.bfloat16), "seq", axis=0, tiled=True).astype(
            jnp.float32
        ),
        lax.all_gather(parted[6].astype(jnp.bfloat16), "seq", axis=0, tiled=True).astype(
            jnp.float32
        ),
        lax.all_gather(parted[7].astype(jnp.bfloat16), "seq", axis=0, tiled=True).astype(
            jnp.float32
        ),
        lax.all_gather(parted[8].astype(jnp.bfloat16), "seq", axis=1, tiled=True).astype(
            jnp.float32
        ),
        lax.all_gather(parted[9].astype(jnp.bfloat16), "seq", axis=1, tiled=True).astype(
            jnp.float32
        ),
        lax.all_gather(parted[10].astype(jnp.bfloat16), "seq", axis=1, tiled=True).astype(
            jnp.float32
        ),
        lax.all_gather(parted[11].astype(jnp.bfloat16), "seq", axis=1, tiled=True).astype(
            jnp.float32
        ),
    )
    return (
        mixed,
        token_grad,
        totals[0],
        totals[1],
        totals[2],
        totals[3],
        totals[4],
        totals[5],
        totals[6],
        totals[7],
        totals[8],
        totals[9],
        totals[10],
        totals[11],
    )


MESH = pl.DeviceIdType.MESH
NT = (((1,), (1,)), ((), ()))
TN = (((0,), (0,)), ((), ()))


def dot(a, b):
    return jnp.dot(a, b, preferred_element_type=jnp.float32)


class Place:
    def __init__(self, planes):
        self.planes = planes
        s, f = lax.axis_index("seq"), lax.axis_index("fsdp")
        self.y, self.c, self.z, self.x = s // 2, s % 2, f // 2, f % 2

    def at(self, y, c, z, x):
        return (y * 2 + c, z * 2 + x)

    def other_core(self):
        return self.at(self.y, 1 - self.c, self.z, self.x)

    def other_x(self):
        return self.at(self.y, self.c, self.z, 1 - self.x)

    def other_y(self):
        return self.at(1 - self.y, self.c, self.z, self.x)

    def level(self, k):
        return self.at(self.y, self.c, lax.rem(self.z + k + self.planes, self.planes), self.x)


def greet(partners):
    barrier = pltpu.get_barrier_semaphore()
    for partner in partners:
        pl.semaphore_signal(barrier, inc=1, device_id=partner, device_id_type=MESH)
    pl.semaphore_wait(barrier, len(partners))


def nearest(place, i):
    level = 0
    for z in range(place.planes):
        order = sorted(range(place.planes), key=lambda other: (abs(other - z), other))
        for at in range(place.planes):
            level = level + jnp.where((place.z == z) & (i == at), order[at], 0)
    return level


def expert_kernel(
    planes,
    own,
    rows,
    real,
    normed_ref,
    grads_all_ref,
    inner_ref,
    outer_all_ref,
    bias_all_ref,
    small_ref,
    mix_out_ref,
    out_ref,
    inner_grad_ref,
    outer_grad_ref,
    bias_grad_ref,
    router_grad_ref,
    grads_ref,
    mix_ref,
    outer_ref,
    inner_t_ref,
    outer_t_ref,
    router_ref,
    router_t_ref,
    tokens,
    part,
    from_core,
    from_x,
    from_z,
    hidden,
    hidden_grad,
    logit_grad,
    inner_acc,
    outer_acc,
    outer_sem,
    grads_sem,
    mix_sem,
    z_send,
    z_recv,
    x_send,
    x_recv,
    c_send,
    c_recv,
    sum_c_send,
    sum_c_recv,
    sum_x_send,
    sum_x_recv,
    sum_z_send,
    sum_z_recv,
):
    f32, bf16 = jnp.float32, jnp.bfloat16
    place = Place(planes)
    y, c, z, x = place.y, place.c, place.z, place.x
    width = inner_ref.shape[0]
    lanes = inner_ref.shape[1] // own
    first = real % 16

    def remote(src, dst, send, recv, device):
        return pltpu.make_async_remote_copy(
            src_ref=src, dst_ref=dst, send_sem=send, recv_sem=recv, device_id=device, device_id_type=MESH
        )

    def slot(buffer, level, at, count=1):
        return buffer.at[level, pl.ds(at * rows, count * rows)]

    def up_copy(level):
        here = slot(tokens, level, 0)
        return remote(here, here, z_send.at[0, level], z_recv.at[0, level], place.at(y, c, z + 1, x))

    def down_copy(level):
        here = slot(tokens, level, 0)
        return remote(here, here, z_send.at[1, level], z_recv.at[1, level], place.at(y, c, z - 1, x))

    def x_copy(level):
        return remote(
            slot(tokens, level, 0), slot(tokens, level, 2), x_send.at[level], x_recv.at[level], place.other_x()
        )

    def c_copy(level, r):
        return remote(
            slot(tokens, level, 2 * r),
            slot(tokens, level, 2 * r + 1),
            c_send.at[level, r],
            c_recv.at[level, r],
            place.other_core(),
        )

    def sum_c_copy(level, r):
        return remote(
            slot(part, level, 2 * r + 1),
            slot(from_core, level, r),
            sum_c_send.at[level, r],
            sum_c_recv.at[level, r],
            place.other_core(),
        )

    def sum_x_copy(level):
        return remote(
            slot(part, level, 2), from_x.at[level], sum_x_send.at[level], sum_x_recv.at[level], place.other_x()
        )

    def sum_z_copy(level, source):
        return remote(
            slot(part, level, 0),
            from_z.at[source],
            sum_z_send.at[level],
            sum_z_recv.at[source],
            place.at(y, c, level, x),
        )

    partners = [place.other_core(), place.other_x()] + [place.level(k) for k in range(1, planes)]
    greet(partners)
    tokens[z, 0:rows, :] = normed_ref[...]

    @pl.when(z < planes - 1)
    def _():
        up_copy(z).start()

    @pl.when(z > 0)
    def _():
        down_copy(z).start()

    c_copy(z, 0).start()
    x_copy(z).start()
    def grads_load(level):
        return pltpu.make_async_copy(grads_all_ref.at[level], grads_ref.at[level], grads_sem.at[level])

    def mix_store(level, r):
        here = pl.ds(pl.multiple_of(2 * r * rows, 16), 2 * rows)
        return pltpu.make_async_copy(mix_ref.at[level, here], mix_out_ref.at[level, here], mix_sem.at[level, r])

    for i in range(planes):
        grads_load(nearest(place, i)).start()
    loads = [
        pltpu.make_async_copy(
            outer_all_ref.at[c * own + i], outer_ref.at[pl.ds(i * lanes, lanes)], outer_sem.at[i]
        )
        for i in range(own)
    ]
    for load in loads:
        load.start()
    inner_t_ref[...] = jnp.transpose(inner_ref[...])
    place_row = lax.broadcasted_iota(jnp.int32, (128, 128), 0)
    place_lane = lax.broadcasted_iota(jnp.int32, (128, 128), 1)
    take = (place_row - (5 + 2 * own) == place_lane - first) & (place_lane >= first)
    take = take & (place_lane < first + 2 * own)
    router = dot(small_ref[...], take.astype(bf16))
    router_ref[...] = router.astype(bf16)
    router_t_ref[...] = jnp.transpose(router).astype(bf16)
    inner_acc[...] = jnp.zeros_like(inner_acc)
    outer_acc[...] = jnp.zeros_like(outer_acc)
    bias_grad_ref[...] = jnp.zeros_like(bias_grad_ref)
    router_grad_ref[...] = jnp.zeros_like(router_grad_ref)
    for load in loads:
        load.wait()
    outer_t_ref[...] = jnp.transpose(outer_ref[...])

    def hop(h):
        @pl.when(z >= h)
        def _():
            up_copy(z - h).wait_recv()

            @pl.when(z < planes - 1)
            def _():
                up_copy(z - h).start()

            x_copy(z - h).start()
            c_copy(z - h, 0).start()

        @pl.when(z + h < planes)
        def _():
            down_copy(z + h).wait_recv()

            @pl.when(z > 0)
            def _():
                down_copy(z + h).start()

            x_copy(z + h).start()
            c_copy(z + h, 0).start()

    def tiles(level, r):
        here = pl.ds(pl.multiple_of(2 * r * rows, 16), 2 * rows)
        normed, grad_out = tokens[level, here, :], grads_ref[level, here, :]
        select = []
        for t in range(2):
            last = pl.ds(pl.multiple_of((2 * r + t) * rows + real - first, 16), 16)
            chosen = grads_ref[level, last, :256].astype(f32)
            chosen = jnp.concatenate([chosen, jnp.zeros((112, 256), f32)], axis=0)
            select.append(jnp.transpose(chosen)[:rows])
        select = jnp.concatenate(select, axis=0)
        lane = lax.broadcasted_iota(jnp.int32, select.shape, 1)
        named = (lane >= first) & (lane < first + 2 * own)
        select = jnp.where(named, select, 0.0)
        logits = jnp.where(named, dot(normed, router_ref[...]), -1e30)
        routing = jnp.exp(logits - jnp.max(logits, axis=1, keepdims=True))
        routing = routing / jnp.sum(routing, axis=1, keepdims=True)
        gates = routing * select
        gate_grads = jnp.zeros_like(gates)
        all_pre = dot(normed, inner_ref[...])
        all_grad_act = dot(grad_out, outer_t_ref[...])
        for i in range(own):
            mine = lane == first + c * own + i
            units = slice(i * lanes, (i + 1) * lanes)
            gate = jnp.sum(jnp.where(mine, gates, 0.0), axis=1, keepdims=True)
            bias = jnp.where(c == 0, bias_all_ref[i : i + 1, :], bias_all_ref[own + i : own + i + 1, :])
            pre = all_pre[:, units] + bias.astype(f32)
            grad_act = all_grad_act[:, units]
            cdf = 0.5 * (1.0 + lax.erf(pre * (0.5**0.5)))
            act = pre * cdf
            hidden[here, units] = (gate * act).astype(bf16)
            gate_grad = jnp.sum(act * grad_act, axis=1, keepdims=True)
            gate_grads = gate_grads + jnp.where(mine, gate_grad * select, 0.0)
            slope = cdf + pre * jnp.exp(-0.5 * pre * pre) * 0.3989422804014327
            grad_pre = gate * grad_act * slope
            bias_grad_ref[0:1, units] += jnp.sum(grad_pre, axis=0, keepdims=True)
            hidden_grad[here, units] = grad_pre.astype(bf16)
        grad_logits = routing * (gate_grads - jnp.sum(routing * gate_grads, axis=1, keepdims=True))
        logit_grad[here, :] = grad_logits.astype(bf16)
        mix_ref[level, here, :] = dot(hidden[here, :], outer_ref[...]).astype(bf16)
        row_grad = dot(hidden_grad[here, :], inner_t_ref[...])
        row_grad = row_grad + dot(logit_grad[here, :], router_t_ref[...])
        part[level, here, :] = row_grad.astype(bf16)

    def across_sum(level):
        sum_c_copy(level, 1).wait_recv()
        here = slice(2 * rows, 3 * rows)
        total = part[level, here, :].astype(f32) + from_core[level, rows : 2 * rows, :].astype(f32)
        part[level, here, :] = total.astype(bf16)
        sum_x_copy(level).start()

    def level_sum(level):
        sum_c_copy(level, 0).wait_recv()
        sum_x_copy(level).wait_recv()
        total = part[level, 0:rows, :].astype(f32) + from_core[level, 0:rows, :].astype(f32)
        total = total + from_x[level].astype(f32)
        part[level, 0:rows, :] = total.astype(bf16)

    def weight_grads(level):
        for j in range(width // 256):
            some = slice(j * 256, (j + 1) * 256)
            outer_acc[some, :] += lax.dot_general(
                hidden[:, some], grads_ref[level], TN, preferred_element_type=f32
            )
            inner_acc[some, :] += lax.dot_general(
                tokens[level, :, some], hidden_grad[...], TN, preferred_element_type=f32
            )
        router_grad_ref[...] += lax.dot_general(tokens[level], logit_grad[...], TN, preferred_element_type=f32)

    def order(i):
        return nearest(place, jnp.where(i == 0, 0, jnp.where(i == planes - 1, 1, i + 1)))

    def step(i, carry):
        level, before = order(i), order(i - 1)

        def half(s, carry):
            r = jnp.where(i == 0, s, 1 - s)

            @pl.when((i == 0) & (s == 0))
            def _():
                grads_load(z).wait()
                c_copy(z, 0).wait_recv()

            @pl.when((i == 0) & (s == 1))
            def _():
                hop(1)

            @pl.when((i == 0) == (s == 1))
            def _():
                x_copy(level).wait_recv()
                c_copy(level, 1).start()
                c_copy(level, 1).wait_recv()

            @pl.when((i > 0) & (s == 0))
            def _():
                grads_load(level).wait()

            @pl.when((i > 0) & (s == 1))
            def _():
                @pl.when(i + 2 < planes)
                def _():
                    hop(i + 2)

                level_sum(before)

                @pl.when(before != z)
                def _():
                    sum_z_copy(before, z).start()

                across_sum(level)
                c_copy(level, 0).wait_recv()

            tiles(level, r)
            sum_c_copy(level, r).start()
            mix_store(level, r).start()
            return carry

        lax.fori_loop(0, 2, half, 0)

        @pl.when((i == 0) & (i + 2 < planes))
        def _():
            hop(2)

        @pl.when(i == planes - 1)
        def _():
            level_sum(level)
            sum_z_copy(level, z).start()

        weight_grads(level)

        @pl.when(i == 0)
        def _():
            across_sum(z)

        return carry

    lax.fori_loop(0, planes, step, 0)
    inner_grad_ref[...] = inner_acc[...].astype(bf16)
    outer_grad_ref[...] = outer_acc[...].astype(bf16)
    total = part[z, 0:rows, :].astype(f32)
    for k in range(1, planes):
        source = lax.rem(z + k, planes)
        sum_z_copy(z, source).wait_recv()
        total = total + from_z[source].astype(f32)
    out_ref[...] = total
    for level in range(planes):
        mix_store(level, 0).wait()
        mix_store(level, 1).wait()
        x_copy(level).wait_send()
        c_copy(level, 0).wait_send()
        c_copy(level, 1).wait_send()
        sum_c_copy(level, 0).wait_send()
        sum_c_copy(level, 1).wait_send()
        sum_x_copy(level).wait_send()

        @pl.when(level != z)
        def _():
            sum_z_copy(level, z).wait_send()

        @pl.when((z >= level) & (z < planes - 1))
        def _():
            up_copy(level).wait_send()

        @pl.when((z <= level) & (z > 0))
        def _():
            down_copy(level).wait_send()


def experts_of_the_plane(planes, own, real, normed, grads, inner, outer, bias, small):
    f32, bf16 = jnp.float32, jnp.bfloat16
    rows = normed.shape[0]
    chunk = 4 * rows
    width, units = inner.shape
    shape = jax.ShapeDtypeStruct
    vmem = pl.BlockSpec(memory_space=pltpu.VMEM)
    anywhere = pl.BlockSpec(memory_space=pl.ANY)
    dma = pltpu.SemaphoreType.DMA
    flops = 12 * planes * chunk * width * units
    return pl.pallas_call(
        functools.partial(expert_kernel, planes, own, rows, real),
        out_shape=[
            shape((planes, chunk, width), bf16),
            shape((rows, width), f32),
            shape((width, units), bf16),
            shape((units, width), bf16),
            shape((8, units), f32),
            shape((width, 128), f32),
        ],
        in_specs=[vmem, anywhere, vmem, anywhere, vmem, vmem],
        out_specs=[anywhere] + [vmem] * 5,
        scratch_shapes=[
            pltpu.VMEM((planes, chunk, width), bf16),
            pltpu.VMEM((planes, chunk, width), bf16),
            pltpu.VMEM((units, width), bf16),
            pltpu.VMEM((units, width), bf16),
            pltpu.VMEM((width, units), bf16),
            pltpu.VMEM((width, 128), bf16),
            pltpu.VMEM((128, width), bf16),
            pltpu.VMEM((planes, chunk, width), bf16),
            pltpu.VMEM((planes, chunk, width), bf16),
            pltpu.VMEM((planes, 2 * rows, width), bf16),
            pltpu.VMEM((planes, rows, width), bf16),
            pltpu.VMEM((planes, rows, width), bf16),
            pltpu.VMEM((chunk, units), bf16),
            pltpu.VMEM((chunk, units), bf16),
            pltpu.VMEM((chunk, 128), bf16),
            pltpu.VMEM((width, units), f32),
            pltpu.VMEM((units, width), f32),
            dma((own,)),
            dma((planes,)),
            dma((planes, 2)),
        ]
        + [dma((2, planes))] * 2
        + [dma((planes,))] * 2
        + [dma((planes, 2))] * 4
        + [dma((planes,))] * 4,
        compiler_params=pltpu.CompilerParams(
            collective_id=1, has_side_effects=True, vmem_limit_bytes=60 * 2**20
        ),
        cost_estimate=pl.CostEstimate(flops=flops, bytes_accessed=40 * 2**20, transcendentals=0),
        name="experts_of_the_plane",
    )(normed, grads, inner, outer, bias, small)


def front_kernel(
    planes,
    heads,
    real,
    tokens_ref,
    mask_ref,
    ids_ref,
    cotangent_ref,
    *refs,
):
    vector_refs, refs = refs[:5], refs[5:]
    (
        router_part_ref,
        outer_bias_ref,
        qkv_part_ref,
    proj_part_ref,
    inner_part_ref,
    small_all,
    w_qkv_out,
    w_proj_out,
    inner_all,
    normed_in_ref,
    qkv_ref,
    attended_ref,
    middle_ref,
    normed_ref,
    grad_ref,
    grads_all,
    wide_ref,
    select_ref,
    keys_ref,
    keep_ref,
    w_qkv_all,
    w_proj_all,
    out_sem,
    up_send,
    up_recv,
    down_send,
    down_recv,
    x_send,
    x_recv,
    c_send,
    c_recv,
    over_send,
    over_recv,
    over_c_send,
    over_c_recv,
    g_z_send,
    g_z_recv,
    g_x_send,
    g_x_recv,
    g_c_send,
    g_c_recv,
    spread_send,
    spread_recv,
    own_sem,
    y_send,
    y_recv,
    ) = refs
    f32, bf16 = jnp.float32, jnp.bfloat16
    place = Place(planes)
    rows, width = wide_ref.shape
    depth = qkv_part_ref.shape[0]
    experts = inner_part_ref.shape[0]
    half = depth // 2
    lanes = inner_part_ref.shape[2] // (2 * planes)
    head_dim = width // heads
    y, c, z, x = place.y, place.c, place.z, place.x
    gathered = [small_all, w_qkv_all, w_proj_all]

    def remote(src, dst, send, recv, device):
        return pltpu.make_async_remote_copy(
            src_ref=src, dst_ref=dst, send_sem=send, recv_sem=recv, device_id=device, device_id_type=MESH
        )

    def block(j, level, across, core, plane):
        start = pl.multiple_of((level * 2 + across) * depth + core * half, 16)
        if j == 0:
            return gathered[j].at[pl.ds(start, half)]
        columns = gathered[j].shape[1] // 2
        return gathered[j].at[pl.ds(start, half), pl.ds(pl.multiple_of(plane * columns, 128), columns)]

    def piece(j, level, across):
        return block(j, level, across, c, y)

    def up_copy(j, level):
        here = piece(j, level, x)
        return remote(here, here, up_send.at[j, level], up_recv.at[j, level], place.at(y, c, z + 1, x))

    def down_copy(j, level):
        here = piece(j, level, x)
        return remote(here, here, down_send.at[j, level], down_recv.at[j, level], place.at(y, c, z - 1, x))

    def x_copy(j, level, across):
        here = piece(j, level, across)
        return remote(here, here, x_send.at[j, level], x_recv.at[j, level], place.other_x())

    def c_copy(j, level, across):
        here = piece(j, level, across)
        at = level * 2 + across
        return remote(here, here, c_send.at[j, at], c_recv.at[j, at], place.other_core())

    def over_copy(j, level, across):
        here = piece(j, level, across)
        at = level * 2 + across
        return remote(here, here, over_send.at[j, at], over_recv.at[j, at], place.other_y())

    def over_c_copy(j, level, across):
        here = block(j, level, across, c, 1 - y)
        at = level * 2 + across
        return remote(here, here, over_c_send.at[j, at], over_c_recv.at[j, at], place.other_core())

    def g_slot(level, at):
        return grads_all.at[level, pl.ds(at * rows, rows)]

    def g_up(level):
        here = g_slot(level, 0)
        return remote(here, here, g_z_send.at[0, level], g_z_recv.at[0, level], place.at(y, c, z + 1, x))

    def g_down(level):
        here = g_slot(level, 0)
        return remote(here, here, g_z_send.at[1, level], g_z_recv.at[1, level], place.at(y, c, z - 1, x))

    def g_x(level):
        return remote(g_slot(level, 0), g_slot(level, 2), g_x_send.at[level], g_x_recv.at[level], place.other_x())

    def g_c(level, r):
        return remote(
            g_slot(level, 2 * r), g_slot(level, 2 * r + 1), g_c_send.at[level, r], g_c_recv.at[level, r], place.other_core()
        )

    def columns_of(f):
        return pl.ds(pl.multiple_of(f * lanes, 128), lanes)

    here_rows = pl.ds(pl.multiple_of((z * 2 + x) * depth, 16), depth)
    my_units = pl.ds(pl.multiple_of(y * lanes, 128), lanes)

    def spread_copy(k, r):
        level, across = lax.rem(z + k, planes), (x + r) % 2
        return remote(
            inner_part_ref.at[c * 2 + y, :, columns_of(level * 2 + across)],
            inner_all.at[here_rows, my_units],
            spread_send.at[k, r],
            spread_recv.at[k, r],
            place.at(y, c, level, across),
        )

    own_copy = pltpu.make_async_copy(
        inner_part_ref.at[c * 2 + y, :, columns_of(z * 2 + x)], inner_all.at[here_rows, my_units], own_sem
    )
    y_copy = remote(inner_all.at[:, my_units], inner_all.at[:, my_units], y_send, y_recv, place.other_y())
    their_units = pl.ds(pl.multiple_of((1 - y) * lanes, 128), lanes)
    from_y = remote(inner_all.at[:, their_units], inner_all.at[:, their_units], y_send, y_recv, place.other_y())

    others = [(k, r) for k in range(planes) for r in range(2) if k or r]
    partners = [place.other_core(), place.other_y()]
    partners += [place.at(y, c, lax.rem(z + k, planes), (x + r) % 2) for k, r in others]
    greet(partners)

    w_qkv_all[here_rows, :] = qkv_part_ref[...]

    def share(j, level, across):
        c_copy(j, level, across).start()
        if j:
            over_copy(j, level, across).start()

    def line(flows):
        @pl.when(z < planes - 1)
        def _():
            for j in flows:
                up_copy(j, z).start()

        @pl.when(z > 0)
        def _():
            for j in flows:
                down_copy(j, z).start()

        for j in flows:
            x_copy(j, z, x).start()

    def hops(flows):
        for h in range(1, planes):
            @pl.when(z >= h)
            def _():
                for j in flows:
                    up_copy(j, z - h).wait_recv()

                    @pl.when(z < planes - 1)
                    def _():
                        up_copy(j, z - h).start()

                    x_copy(j, z - h, x).start()
                    share(j, z - h, x)

            @pl.when(z + h < planes)
            def _():
                for j in flows:
                    down_copy(j, z + h).wait_recv()

                    @pl.when(z > 0)
                    def _():
                        down_copy(j, z + h).start()

                    x_copy(j, z + h, x).start()
                    share(j, z + h, x)

    def arrive(flows):
        for i in range(planes):
            level = nearest(place, i)
            for j in flows:
                x_copy(j, level, 1 - x).wait_recv()
                share(j, level, 1 - x)

    def over_arrive(flows):
        for i in range(planes):
            level = nearest(place, i)
            for j in flows:
                if i:
                    over_copy(j, level, x).wait_recv()
                    over_c_copy(j, level, x).start()
                over_copy(j, level, 1 - x).wait_recv()
                over_c_copy(j, level, 1 - x).start()

    def gather_done(flows):
        for level in range(planes):
            for j in flows:
                c_copy(j, level, 1 - x).wait_recv()
                if j:
                    over_c_copy(j, level, 1 - x).wait_recv()

            @pl.when(level != z)
            def _():
                for j in flows:
                    c_copy(j, level, x).wait_recv()
                    if j:
                        over_c_copy(j, level, x).wait_recv()

    def g_hop(h):
        @pl.when(z >= h)
        def _():
            g_up(z - h).wait_recv()

            @pl.when(z < planes - 1)
            def _():
                g_up(z - h).start()

            g_x(z - h).start()
            g_c(z - h, 0).start()

        @pl.when(z + h < planes)
        def _():
            g_down(z + h).wait_recv()

            @pl.when(z > 0)
            def _():
                g_down(z + h).start()

            g_x(z + h).start()
            g_c(z + h, 0).start()

    line([1])
    lined = [ref[...].astype(f32) for ref in (*vector_refs, outer_bias_ref, router_part_ref)]
    lined = jnp.concatenate(lined, axis=0)
    lined = jnp.concatenate([lined, jnp.zeros((128 - lined.shape[0], depth), f32)], axis=0)
    lined = jnp.concatenate([lined, jnp.zeros((128, 128 - depth), f32)], axis=1)
    small = jnp.transpose(lined)[:depth]
    small_all[here_rows, :] = small.astype(bf16)
    line([0])
    w_proj_all[here_rows, :] = proj_part_ref[...]
    line([2])
    spare = jnp.zeros((rows - real, width), f32)
    values = jnp.concatenate([tokens_ref[...].astype(f32), spare], axis=0)
    wide_ref[...] = values.astype(bf16)
    normal, _ = norm_parts(values)
    mask = mask_ref[pl.ds(y * 2 + c, 1), :].astype(f32)
    keys = jnp.concatenate([mask, jnp.zeros((1, rows - real), f32)], axis=1)
    keys_ref[...] = keys
    keep = lax.broadcasted_iota(jnp.int32, (rows, rows), 0) == lax.broadcasted_iota(jnp.int32, (rows, rows), 1)
    keep = jnp.sum(jnp.where(keep, keys, 0.0), axis=1, keepdims=True)
    keep_ref[...] = keep
    ids = ids_ref[...]
    number = lax.broadcasted_iota(jnp.int32, (8, real), 0)
    chosen = ((number == ids[0:1]) | (number == ids[1:2])).astype(f32)
    chosen = jnp.concatenate([chosen, jnp.zeros((8, width - real), f32)], axis=1)
    select = jnp.concatenate([chosen[:, :256], jnp.zeros((120, 256), f32)], axis=0)
    select_ref[...] = jnp.transpose(select)[:rows].astype(bf16)
    if rows - real > 8:
        chosen = jnp.concatenate([chosen, jnp.zeros((rows - real - 8, width), f32)], axis=0)
    grad_out = cotangent_ref[...].astype(f32) * keep[:real]
    grad_out = jnp.concatenate([grad_out, chosen], axis=0).astype(bf16)
    grad_ref[...] = grad_out
    grads_own = pltpu.make_async_copy(grad_ref, g_slot(z, 0), out_sem.at[2])
    grads_own.start()
    hops([1, 0])
    arrive([1, 0])
    hops([2])
    own_copy.start()
    for k, r in others:
        spread_copy(k, r).start()

    grads_own.wait()

    @pl.when(z < planes - 1)
    def _():
        g_up(z).start()

    @pl.when(z > 0)
    def _():
        g_down(z).start()

    g_x(z).start()
    g_c(z, 0).start()
    arrive([2])
    over_arrive([1])
    gather_done([1, 0])
    qkv_out_copy = pltpu.make_async_copy(w_qkv_all, w_qkv_out, out_sem.at[0])
    qkv_out_copy.start()
    vectors = jnp.transpose(small_all[...].astype(f32))
    normed_in = (normal * vectors[0:1] + vectors[1:2]).astype(bf16)
    normed_in_ref[...] = normed_in
    for j in range(3):
        part = slice(j * width, (j + 1) * width)
        qkv_ref[:, part] = dot(normed_in, w_qkv_all[:, part]).astype(bf16)
    g_hop(1)
    over_arrive([2])
    lane = lax.broadcasted_iota(jnp.int32, (rows, 2 * head_dim), 1)
    usable = keys_ref[...] > 0
    for pair in range(heads // 2):
        if pair == heads // 4:
            g_hop(2)
        at = pair * 2 * head_dim
        queries = qkv_ref[:, at : at + 2 * head_dim]
        keys = qkv_ref[:, width + at : width + at + 2 * head_dim]
        held = qkv_ref[:, 2 * width + at : 2 * width + at + 2 * head_dim]
        outs = []
        for side in range(2):
            only = (lane < head_dim) if side == 0 else (lane >= head_dim)
            scores = lax.dot_general(
                jnp.where(only, queries, 0).astype(bf16), keys, NT, preferred_element_type=f32
            )
            scores = jnp.where(usable, scores * head_dim ** (-0.5), masked_score)
            shifted = jnp.exp(scores - jnp.max(scores, axis=1, keepdims=True))
            probs = (shifted / jnp.sum(shifted, axis=1, keepdims=True)).astype(bf16)
            outs.append(dot(probs, held))
        attended_ref[:, at : at + 2 * head_dim] = jnp.where(lane < head_dim, outs[0], outs[1]).astype(bf16)
    for h in range(3, planes):
        g_hop(h)
    own_copy.wait()
    for k, r in others:
        spread_copy(k, r).wait_recv()
    y_copy.start()
    gather_done([2])
    proj_out_copy = pltpu.make_async_copy(w_proj_all, w_proj_out, out_sem.at[1])
    proj_out_copy.start()
    middle = values + dot(attended_ref[...], w_proj_all[...]) + vectors[2:3]
    middle_ref[...] = middle
    normal_mid, _ = norm_parts(middle)
    normed = normal_mid * vectors[3:4] + vectors[4:5]
    row = lax.broadcasted_iota(jnp.int32, normed.shape, 0)
    normed_ref[...] = jnp.where(row < real, normed, 0.0).astype(bf16)
    for i in range(planes):
        level = nearest(place, i)
        g_x(level).wait_recv()
        g_c(level, 1).start()
    from_y.wait_recv()
    qkv_out_copy.wait()
    proj_out_copy.wait()
    for level in range(planes):
        g_c(level, 0).wait_recv()
        g_c(level, 1).wait_recv()
    y_copy.wait_send()
    for k, r in others:
        spread_copy(k, r).wait_send()
    for level in range(planes):
        g_x(level).wait_send()
        g_c(level, 0).wait_send()
        g_c(level, 1).wait_send()

        @pl.when((z >= level) & (z < planes - 1))
        def _():
            g_up(level).wait_send()

        @pl.when((z <= level) & (z > 0))
        def _():
            g_down(level).wait_send()

    def shared(j, level, across):
        c_copy(j, level, across).wait_send()
        if j:
            over_copy(j, level, across).wait_send()
            over_c_copy(j, level, across).wait_send()

    for j in range(3):
        for level in range(planes):
            x_copy(j, level, x).wait_send()
            shared(j, level, 1 - x)

            @pl.when(level != z)
            def _():
                shared(j, level, x)

            @pl.when((z >= level) & (z < planes - 1))
            def _():
                up_copy(j, level).wait_send()

            @pl.when((z <= level) & (z > 0))
            def _():
                down_copy(j, level).wait_send()


def front(planes, rows, tokens, mask, ids, cotangent, vectors, router, outer_bias, w_qkv, w_proj, w_in):
    f32, bf16 = jnp.float32, jnp.bfloat16
    real, width = tokens.shape
    lanes = w_in.shape[2] // (2 * planes)
    shape = jax.ShapeDtypeStruct
    vmem = pl.BlockSpec(memory_space=pltpu.VMEM)
    anywhere = pl.BlockSpec(memory_space=pl.ANY)
    dma = pltpu.SemaphoreType.DMA
    return pl.pallas_call(
        functools.partial(front_kernel, planes, HEADS, real),
        out_shape=[
            shape((width, 128), bf16),
            shape((width, 3 * width), bf16),
            shape((width, width), bf16),
            shape((width, 2 * lanes), bf16),
            shape((rows, width), bf16),
            shape((rows, 3 * width), bf16),
            shape((rows, width), bf16),
            shape((rows, width), f32),
            shape((rows, width), bf16),
            shape((rows, width), bf16),
            shape((planes, 4 * rows, width), bf16),
            shape((rows, width), bf16),
            shape((rows, 128), bf16),
            shape((1, rows), f32),
            shape((rows, 1), f32),
        ],
        in_specs=[vmem] * (6 + len(vectors)) + [vmem] * 2 + [anywhere],
        out_specs=[vmem] + [anywhere] * 3 + [vmem] * 6 + [anywhere] + [vmem] * 4,
        scratch_shapes=[pltpu.VMEM((width, 3 * width), bf16), pltpu.VMEM((width, width), bf16), dma((3,))]
        + [dma((3, planes))] * 6
        + [dma((3, 2 * planes))] * 6
        + [dma((2, planes))] * 2
        + [dma((planes,))] * 2
        + [dma((planes, 2))] * 4
        + [dma] * 3,
        compiler_params=pltpu.CompilerParams(
            collective_id=2, has_side_effects=True, vmem_limit_bytes=60 * 2**20
        ),
        cost_estimate=pl.CostEstimate(flops=2**32, bytes_accessed=40 * 2**20, transcendentals=0),
        name="dense_weights_and_attention",
    )(tokens, mask, ids, cotangent, *vectors, router, outer_bias, w_qkv, w_proj, w_in)


def back_kernel(planes, heads, own, groups, real, *refs):
    (
        row_grad_ref,
        normed_ref,
        grad_ref,
        middle_ref,
        tokens_ref,
        normed_in_ref,
        qkv_ref,
        attended_ref,
        small_ref,
        w_qkv_all_ref,
        w_proj_ref,
        keys_ref,
        keep_ref,
        select_ref,
        mix_ref,
        inner_ref,
        outer_ref,
        bias_ref,
        router_grad_ref,
    ) = refs[:19]
    mixed_ref, token_grad_ref, qkv_out, proj_out, small_out, inner_out, outer_out, bias_out = refs[19:27]
    refs = refs[27:]
    (
        w_qkv_ref,
        outer_sum,
        grad_attended,
        grad_qkv,
        mix_x,
        mix_z,
        mix_from_core,
        mix_from_x,
        mix_from_z,
        inner_from_y,
        inner_sum,
        outer_from_y,
        bias_from_y,
        held,
        held_small,
        from_core,
        from_core_small,
        from_x,
        from_x_small,
        from_z,
        from_z_small,
        plane_sum,
        plane_sum_small,
        from_y,
        from_y_small,
        final,
        final_small,
    ) = refs[:27]
    (
        load_sem,
        outer_own_sem,
        mix_c_send,
        mix_c_recv,
        mix_x_send,
        mix_x_recv,
        mix_z_send,
        mix_z_recv,
        inner_y_sem,
        spread_send,
        spread_recv,
        inner_back_sem,
        inner_core_sem,
        outer_y_sem,
        outer_c_sem,
        bias_y_sem,
        bias_c_sem,
        own_sem,
        flow_c_sem,
        flow_x_sem,
        flow_z_send,
        flow_z_recv,
        flow_y_sem,
        flow_end_sem,
    ) = refs[27:]
    f32, bf16 = jnp.float32, jnp.bfloat16
    place = Place(planes)
    y, c, z, x = place.y, place.c, place.z, place.x
    rows, width = middle_ref.shape
    depth = width // (2 * planes)
    half = depth // 2
    lanes = inner_ref.shape[1] // own
    head_dim = width // heads
    pair_width = 2 * head_dim
    small_at = groups + 1

    def remote(src, dst, send, recv, device):
        return pltpu.make_async_remote_copy(
            src_ref=src, dst_ref=dst, send_sem=send, recv_sem=recv, device_id=device, device_id_type=MESH
        )

    def swap(src, dst, sem, device):
        return remote(src, dst, sem.at[0], sem.at[1], device)

    def of_flow(j, many, alone):
        return alone if j == small_at else many.at[j]

    mine, theirs = pl.ds(pl.multiple_of(c * half, 16), half), pl.ds(pl.multiple_of((1 - c) * half, 16), half)

    def flow_c(j):
        source = of_flow(j, held, held_small)
        return swap(
            source.at[:, :, theirs], of_flow(j, from_core, from_core_small), flow_c_sem.at[j], place.other_core()
        )

    def flow_x(j):
        source = of_flow(j, held, held_small)
        return swap(source.at[:, 1 - x, mine], of_flow(j, from_x, from_x_small), flow_x_sem.at[j], place.other_x())

    def flow_z(j, k):
        level = lax.rem(z + k, planes)
        source = of_flow(j, held, held_small)
        return remote(
            source.at[level, x, mine],
            of_flow(j, from_z, from_z_small).at[k],
            flow_z_send.at[j, k],
            flow_z_recv.at[j, k],
            place.level(k),
        )

    def flow_y(j):
        return swap(
            of_flow(j, plane_sum, plane_sum_small),
            of_flow(j, from_y, from_y_small),
            flow_y_sem.at[j],
            place.other_y(),
        )

    def flow_end(j):
        here = of_flow(j, final, final_small).at[mine]
        return swap(here, here, flow_end_sem.at[j], place.other_core())

    def flow_core_sum(j):
        flow_c(j).wait_recv()
        kept = of_flow(j, held, held_small)
        total = kept[:, :, mine, :].astype(f32) + of_flow(j, from_core, from_core_small)[...].astype(f32)
        kept[:, :, mine, :] = total.astype(bf16)
        flow_x(j).start()

    def flow_x_sum(j):
        flow_x(j).wait_recv()
        kept = of_flow(j, held, held_small)
        total = kept[:, x, mine, :].astype(f32) + of_flow(j, from_x, from_x_small)[...].astype(f32)
        kept[:, x, mine, :] = total.astype(bf16)
        for k in range(1, planes):
            flow_z(j, k).start()

    def flow_z_sum(j):
        kept = of_flow(j, held, held_small)
        total = kept[z, x, mine, :].astype(f32)
        for k in range(1, planes):
            flow_z(j, k).wait_recv()
            total = total + of_flow(j, from_z, from_z_small)[k].astype(f32)
        of_flow(j, plane_sum, plane_sum_small)[...] = total.astype(bf16)
        flow_y(j).start()

    def flow_y_sum(j):
        flow_y(j).wait_recv()
        total = of_flow(j, plane_sum, plane_sum_small)[...].astype(f32)
        total = total + of_flow(j, from_y, from_y_small)[...].astype(f32)
        of_flow(j, final, final_small)[mine, :] = total.astype(bf16)
        flow_end(j).start()

    loads = [
        pltpu.make_async_copy(mix_ref.at[:, pl.ds(2 * rows, rows)], mix_x, load_sem.at[0]),
        pltpu.make_async_copy(mix_ref.at[:, pl.ds(0, rows)], mix_z, load_sem.at[1]),
        pltpu.make_async_copy(w_qkv_all_ref, w_qkv_ref, load_sem.at[2]),
    ]

    def mix_c(r):
        return remote(
            mix_ref.at[:, pl.ds((2 * r + 1) * rows, rows)],
            mix_from_core.at[:, pl.ds(r * rows, rows)],
            mix_c_send.at[r],
            mix_c_recv.at[r],
            place.other_core(),
        )

    def mix_to_x(level):
        return remote(mix_x.at[level], mix_from_x.at[level], mix_x_send.at[level], mix_x_recv.at[level], place.other_x())

    def mix_to_z(level, source):
        return remote(
            mix_z.at[level], mix_from_z.at[source], mix_z_send.at[level], mix_z_recv.at[source], place.at(y, c, level, x)
        )

    def mix_core_sum():
        for load in loads[:2]:
            load.wait()
        mix_c(0).wait_recv()
        mix_c(1).wait_recv()
        for k in range(1, planes + 1):
            level = lax.rem(z + k, planes)
            total = mix_x[level].astype(f32) + mix_from_core[level, rows:, :].astype(f32)
            mix_x[level] = total.astype(bf16)
            mix_to_x(level).start()
        for level in range(planes):
            total = mix_z[level].astype(f32) + mix_from_core[level, :rows, :].astype(f32)
            mix_z[level] = total.astype(bf16)

    def mix_x_sum(k):
        level = lax.rem(z + k, planes)
        mix_to_x(level).wait_recv()
        mix_z[level] = (mix_z[level].astype(f32) + mix_from_x[level].astype(f32)).astype(bf16)
        if k < planes:
            mix_to_z(level, z).start()

    my_units = pl.ds(pl.multiple_of(y * lanes, 128), lanes)
    their_units = pl.ds(pl.multiple_of((1 - y) * lanes, 128), lanes)
    my_expert, their_expert = c * 2 + y, c * 2 + 1 - y
    my_columns = pl.ds(pl.multiple_of((z * 2 + x) * lanes, 128), lanes)

    def inner_y():
        return swap(inner_ref.at[:, their_units], inner_from_y, inner_y_sem, place.other_y())

    def shard_rows(f):
        return pl.ds(pl.multiple_of(f * depth, 16), depth)

    def spread(k, r):
        level, across = lax.rem(z + k, planes), (x + r) % 2
        return remote(
            inner_sum.at[shard_rows(level * 2 + across)],
            inner_out.at[my_expert, :, my_columns],
            spread_send.at[k, r],
            spread_recv.at[k, r],
            place.at(y, c, level, across),
        )

    own_copy = pltpu.make_async_copy(
        inner_sum.at[shard_rows(z * 2 + x)], inner_out.at[my_expert, :, my_columns], own_sem
    )

    def inner_back():
        here = inner_out.at[my_expert]
        return swap(here, here, inner_back_sem, place.other_y())

    def inner_core(expert, at):
        here = inner_out.at[expert]
        return swap(here, here, inner_core_sem.at[at], place.other_core())

    def outer_y():
        return swap(outer_ref, outer_from_y, outer_y_sem, place.other_y())

    def outer_c():
        return swap(outer_sum, outer_out.at[c], outer_c_sem, place.other_core())

    outer_own = pltpu.make_async_copy(outer_sum, outer_out.at[c], outer_own_sem)

    def bias_y():
        return swap(bias_ref, bias_from_y, bias_y_sem, place.other_y())

    def bias_c():
        here = bias_out.at[c]
        return swap(here, here, bias_c_sem, place.other_core())

    others = [(k, r) for k in range(planes) for r in range(2) if k or r]

    def inner_y_sum():
        inner_y().wait_recv()
        total = inner_ref[:, my_units].astype(f32) + inner_from_y[...].astype(f32)
        inner_sum[...] = total.astype(bf16)
        own_copy.start()
        for k, r in others:
            spread(k, r).start()
        outer_y().start()

    def inner_spread_done():
        own_copy.wait()
        for k, r in others:
            spread(k, r).wait_recv()
        inner_back().start()
        inner_core(my_expert, 0).start()

    def outer_y_sum():
        outer_y().wait_recv()
        total = outer_ref[...].astype(f32) + outer_from_y[...].astype(f32)
        outer_sum[...] = total.astype(bf16)
        outer_own.start()
        outer_c().start()
        bias_y().wait_recv()
        bias_out[c] = bias_ref[...] + bias_from_y[...]
        bias_c().start()

    partners = [place.other_core(), place.other_y()]
    partners += [place.at(y, c, lax.rem(z + k, planes), (x + r) % 2) for k, r in others]
    greet(partners)
    inner_y().start()
    bias_y().start()
    mix_c(1).start()
    mix_c(0).start()
    for load in loads:
        load.start()

    vectors = jnp.transpose(small_ref[...].astype(f32))
    gain_first, gain_second = vectors[0:1], vectors[3:4]
    place_row = lax.broadcasted_iota(jnp.int32, (128, 128), 0)
    place_lane = lax.broadcasted_iota(jnp.int32, (128, 128), 1)

    def lanes_from(first):
        take = (place_row == place_lane + first) & (place_lane < 2 * own)
        return dot(small_ref[...], take.astype(bf16)).astype(bf16)

    outer_bias, router = lanes_from(5), lanes_from(5 + 2 * own)
    normed_mid, grad_out = normed_ref[...], grad_ref[...]
    real_row = lax.broadcasted_iota(jnp.int32, grad_out.shape, 0) < real
    grad_out = jnp.where(real_row, grad_out, 0).astype(bf16)
    select = select_ref[...].astype(f32)
    lane = lax.broadcasted_iota(jnp.int32, select.shape, 1)
    logits = jnp.where(lane < 2 * own, dot(normed_mid, router), -1e30)
    routing = jnp.exp(logits - jnp.max(logits, axis=1, keepdims=True))
    routing = routing / jnp.sum(routing, axis=1, keepdims=True)
    gates = routing * select
    bias_gate = select * dot(grad_out, outer_bias)
    bias_logits = routing * (bias_gate - jnp.sum(routing * bias_gate, axis=1, keepdims=True))
    bias_logits = bias_logits.astype(bf16)
    router_grad = lax.dot_general(normed_mid, bias_logits, TN, preferred_element_type=f32)
    router_grad = pltpu.roll(router_grad, 16, 1) + pltpu.roll(router_grad_ref[...], 16 - real % 16, 1)
    outer_bias_grad = lax.dot_general(gates.astype(bf16), grad_out, TN, preferred_element_type=f32)
    grad_normed_mid = row_grad_ref[...] + lax.dot_general(bias_logits, router, NT, preferred_element_type=f32)
    normal_mid, rstd_mid = norm_parts(middle_ref[...])
    gain_second_grad = jnp.sum(grad_normed_mid * normal_mid, axis=0, keepdims=True)
    bias_second_grad = jnp.sum(grad_normed_mid, axis=0, keepdims=True)
    grad_middle = grad_out.astype(f32) + norm_back(grad_normed_mid, normal_mid, rstd_mid, gain_second)
    grad_proj = grad_middle.astype(bf16)
    proj_bias_grad = jnp.sum(grad_proj.astype(f32), axis=0, keepdims=True)
    mix_core_sum()

    def hold(j, value):
        held[j] = value.astype(bf16).reshape(planes, 2, depth, width)
        flow_c(j).start()

    hold(0, lax.dot_general(attended_ref[...], grad_proj, TN, preferred_element_type=f32))
    grad_attended[...] = lax.dot_general(grad_proj, w_proj_ref[...], NT, preferred_element_type=f32).astype(bf16)
    flow_core_sum(0)

    pair_lane = lax.broadcasted_iota(jnp.int32, (rows, pair_width), 1)
    usable = keys_ref[...] > 0
    scaling = head_dim ** (-0.5)
    group_width = width // groups

    def pair_back(pair):
        at = pair * pair_width
        group, inside = at // group_width, at % group_width
        queries = qkv_ref[:, at : at + pair_width]
        keys = qkv_ref[:, width + at : width + at + pair_width]
        values = qkv_ref[:, 2 * width + at : 2 * width + at + pair_width]
        grads = grad_attended[:, at : at + pair_width]
        found = []
        for side in range(2):
            only = (pair_lane < head_dim) if side == 0 else (pair_lane >= head_dim)
            some_queries = jnp.where(only, queries, 0).astype(bf16)
            some_grads = jnp.where(only, grads, 0).astype(bf16)
            scores = lax.dot_general(some_queries, keys, NT, preferred_element_type=f32)
            scores = jnp.where(usable, scores * scaling, masked_score)
            shifted = jnp.exp(scores - jnp.max(scores, axis=1, keepdims=True))
            probs = shifted / jnp.sum(shifted, axis=1, keepdims=True)
            grad_probs = lax.dot_general(some_grads, values, NT, preferred_element_type=f32)
            grad_scores = probs * (grad_probs - jnp.sum(probs * grad_probs, axis=1, keepdims=True))
            grad_scores = grad_scores.astype(bf16)
            found.append(
                (
                    dot(grad_scores, keys),
                    lax.dot_general(grad_scores, some_queries, TN, preferred_element_type=f32),
                    lax.dot_general(probs.astype(bf16), some_grads, TN, preferred_element_type=f32),
                )
            )
        grad_queries = jnp.where(pair_lane < head_dim, found[0][0], found[1][0]) * scaling
        grad_keys = (found[0][1] + found[1][1]) * scaling
        grad_values = found[0][2] + found[1][2]
        for part, value in enumerate((grad_queries, grad_keys, grad_values)):
            start = part * group_width + inside
            grad_qkv[group, :, start : start + pair_width] = value.astype(bf16)

    def group_back(group):
        per_group = heads // 2 // groups
        for pair in range(group * per_group, (group + 1) * per_group):
            pair_back(pair)
        hold(
            1 + group,
            lax.dot_general(normed_in_ref[...], grad_qkv[group], TN, preferred_element_type=f32),
        )

    group_back(0)
    inner_y_sum()
    flow_core_sum(1)
    mix_x_sum(1)
    for group in range(1, groups):
        group_back(group)
        flow_core_sum(1 + group)
        if group == 1:
            mix_x_sum(2)

    loads[2].wait()
    grad_normed_in = jnp.zeros((rows, width), f32)
    for group in range(groups):
        for part in range(3):
            grad_normed_in = grad_normed_in + lax.dot_general(
                grad_qkv[group, :, part * group_width : (part + 1) * group_width],
                w_qkv_ref[:, part * width + group * group_width : part * width + (group + 1) * group_width],
                NT,
                preferred_element_type=f32,
            )
    normal_first, rstd_first = norm_parts(tokens_ref[...].astype(f32))
    gain_first_grad = jnp.sum(grad_normed_in * normal_first, axis=0, keepdims=True)
    bias_first_grad = jnp.sum(grad_normed_in, axis=0, keepdims=True)
    token_grad = grad_middle + norm_back(grad_normed_in, normal_first, rstd_first, gain_first)
    token_grad_ref[...] = token_grad.astype(bf16)[:real]
    vector_rows = jnp.concatenate(
        [
            gain_first_grad,
            bias_first_grad,
            proj_bias_grad,
            gain_second_grad,
            bias_second_grad,
            jnp.zeros((3, width), f32),
            outer_bias_grad[:8],
            jnp.zeros((112, width), f32),
        ],
        axis=0,
    )
    vector_grads = jnp.transpose(vector_rows) + router_grad
    held_small[...] = vector_grads.astype(bf16).reshape(planes, 2, depth, 128)
    flow_c(small_at).start()
    flow_core_sum(small_at)
    for k in range(3, planes):
        mix_x_sum(k)
    inner_spread_done()
    flow_x_sum(0)
    flow_x_sum(1)
    mix_x_sum(planes)
    outer_y_sum()
    for group in range(1, groups):
        flow_x_sum(1 + group)
    flow_z_sum(0)
    flow_x_sum(small_at)
    mixture = mix_z[z].astype(f32) + dot(gates.astype(bf16), jnp.transpose(outer_bias.astype(f32)).astype(bf16))
    for k in range(1, planes):
        source = lax.rem(z + k, planes)
        mix_to_z(z, source).wait_recv()
        mixture = mixture + mix_from_z[source].astype(f32)
    mixed = (keep_ref[...] * (middle_ref[...] + mixture)).astype(bf16)
    mixed_ref[...] = mixed[:real]
    flow_y_sum(0)
    for group in range(groups):
        flow_z_sum(1 + group)
    flow_z_sum(small_at)
    inner_back().wait_recv()
    inner_core(their_expert, 1).start()
    for group in range(groups):
        flow_y_sum(1 + group)
    flow_y_sum(small_at)

    def arrived(j):
        here = of_flow(j, final, final_small).at[theirs]
        swap(here, here, flow_end_sem.at[j], place.other_core()).wait_recv()

    arrived(0)
    proj_out[...] = final[0]
    for group in range(groups):
        arrived(1 + group)
        for part in range(3):
            start = part * width + group * group_width
            qkv_out[:, start : start + group_width] = final[
                1 + group, :, part * group_width : (part + 1) * group_width
            ]
    arrived(small_at)
    small_out[...] = jnp.transpose(
        jnp.concatenate([final_small[...].astype(f32), jnp.zeros((128 - depth, 128), f32)], axis=0)
    )
    outer_own.wait()
    outer_c().wait_recv()
    bias_theirs = bias_out.at[1 - c]
    swap(bias_theirs, bias_theirs, bias_c_sem, place.other_core()).wait_recv()
    for at, expert in enumerate(((1 - c) * 2 + y, (1 - c) * 2 + 1 - y)):
        inner_core(expert, at).wait_recv()

    mix_c(0).wait_send()
    mix_c(1).wait_send()
    inner_y().wait_send()
    inner_back().wait_send()
    inner_core(my_expert, 0).wait_send()
    inner_core(their_expert, 1).wait_send()
    outer_y().wait_send()
    outer_c().wait_send()
    bias_y().wait_send()
    bias_c().wait_send()
    for k, r in others:
        spread(k, r).wait_send()
    for k in range(1, planes + 1):
        level = lax.rem(z + k, planes)
        mix_to_x(level).wait_send()
        if k < planes:
            mix_to_z(level, z).wait_send()
    for j in range(groups + 2):
        flow_c(j).wait_send()
        flow_x(j).wait_send()
        for k in range(1, planes):
            flow_z(j, k).wait_send()
        flow_y(j).wait_send()
        flow_end(j).wait_send()


def back(planes, own, real, *args):
    f32, bf16 = jnp.float32, jnp.bfloat16
    (
        row_grad,
        normed_mid,
        grad_out,
        middle,
        tokens,
        normed_in,
        qkv,
        attended,
        small,
        w_qkv,
        w_proj,
        keys,
        keep,
        select,
        mix_parts,
        inner_grad,
        outer_grad,
        bias_grad,
        router_grad,
    ) = args
    rows, width = middle.shape
    depth = width // (2 * planes)
    half = depth // 2
    lanes = inner_grad.shape[1] // own
    tall = outer_grad.shape[0]
    pairs = HEADS // 2
    groups = 3 if pairs % 3 == 0 and (pairs // 3) * 2 * (width // HEADS) % 128 == 0 else 1
    flows = groups + 1
    shape = jax.ShapeDtypeStruct
    vmem = pl.BlockSpec(memory_space=pltpu.VMEM)
    anywhere = pl.BlockSpec(memory_space=pl.ANY)
    dma = pltpu.SemaphoreType.DMA

    def both(*dims):
        return [pltpu.VMEM((flows, *dims, width), bf16), pltpu.VMEM((*dims, 128), bf16)]

    return pl.pallas_call(
        functools.partial(back_kernel, planes, HEADS, own, groups, real),
        out_shape=[
            shape((real, width), bf16),
            shape((real, width), bf16),
            shape((depth, 3 * width), bf16),
            shape((depth, width), bf16),
            shape((128, 128), f32),
            shape((2 * own, depth, 2 * planes * lanes), bf16),
            shape((2, tall, width), bf16),
            shape((2, *bias_grad.shape), f32),
        ],
        in_specs=[vmem] * 9 + [anywhere] + [vmem] * 4 + [anywhere] + [vmem] * 4,
        out_specs=[vmem] * 5 + [anywhere] * 2 + [vmem],
        scratch_shapes=[
            pltpu.VMEM((width, 3 * width), bf16),
            pltpu.VMEM((tall, width), bf16),
            pltpu.VMEM((rows, width), bf16),
            pltpu.VMEM((groups, rows, 3 * width // groups), bf16),
            pltpu.VMEM((planes, rows, width), bf16),
            pltpu.VMEM((planes, rows, width), bf16),
            pltpu.VMEM((planes, 2 * rows, width), bf16),
            pltpu.VMEM((planes, rows, width), bf16),
            pltpu.VMEM((planes, rows, width), bf16),
            pltpu.VMEM((width, lanes), bf16),
            pltpu.VMEM((width, lanes), bf16),
            pltpu.VMEM((tall, width), bf16),
            pltpu.VMEM(bias_grad.shape, f32),
        ]
        + both(planes, 2, depth)
        + both(planes, 2, half)
        + both(planes, half)
        + both(planes, half)
        + both(half)
        + both(half)
        + both(depth)
        + [dma((3,)), dma]
        + [dma((2,))] * 2
        + [dma((planes,))] * 4
        + [dma((2,))]
        + [dma((planes, 2))] * 2
        + [dma((2,)), dma((2, 2)), dma((2,)), dma((2,)), dma((2,)), dma((2,)), dma]
        + [dma((flows + 1, 2))] * 2
        + [dma((flows + 1, planes))] * 2
        + [dma((flows + 1, 2))] * 2,
        compiler_params=pltpu.CompilerParams(
            collective_id=3, has_side_effects=True, vmem_limit_bytes=60 * 2**20
        ),
        cost_estimate=pl.CostEstimate(flops=2**33, bytes_accessed=40 * 2**20, transcendentals=0),
        name="attention_backward_and_sums",
    )(*args)


def finish_kernel(
    depth,
    experts,
    qkv_ref,
    proj_ref,
    rows_ref,
    inner_ref,
    outer_ref,
    mixed_ref,
    token_grad_ref,
    qkv_out,
    proj_out,
    inner_out,
    outer_out,
    mixed_out,
    token_grad_out,
    router_out,
    outer_bias_out,
    *vector_outs,
):
    f32 = jnp.float32

    @pl.when(pl.program_id(0) == 0)
    def _():
        for i, out in enumerate(vector_outs):
            out[...] = rows_ref[i : i + 1, :depth]
        outer_bias_out[...] = rows_ref[8 : 8 + experts, :depth]
        router_out[...] = rows_ref[16 : 16 + experts, :depth]
        qkv_out[...] = qkv_ref[...].astype(f32)
        proj_out[...] = proj_ref[...].astype(f32)
        mixed_out[...] = mixed_ref[...]
        token_grad_out[...] = token_grad_ref[...]

    inner_out[...] = inner_ref[...].astype(f32)
    outer_out[...] = outer_ref[...].astype(f32)


def finish(qkv, proj, vectors, inner, outer, mixed, token_grad):
    f32 = jnp.float32
    experts, depth, _ = inner.shape
    shape = jax.ShapeDtypeStruct

    def whole(array):
        return pl.BlockSpec(array.shape, lambda i, rank=len(array.shape): (0,) * rank)

    def one(array):
        return pl.BlockSpec((1, *array.shape[1:]), lambda i: (i, 0, 0))

    outs = [
        shape(qkv.shape, f32),
        shape(proj.shape, f32),
        shape(inner.shape, f32),
        shape(outer.shape, f32),
        shape(mixed.shape, mixed.dtype),
        shape(token_grad.shape, token_grad.dtype),
        shape((experts, depth), f32),
        shape((experts, depth), f32),
    ] + [shape((1, depth), f32)] * 5
    return pl.pallas_call(
        functools.partial(finish_kernel, depth, experts),
        out_shape=outs,
        grid=(experts,),
        in_specs=[whole(qkv), whole(proj), whole(vectors), one(inner), one(outer), whole(mixed), whole(token_grad)],
        out_specs=[whole(outs[0]), whole(outs[1]), one(outs[2]), one(outs[3])] + [whole(out) for out in outs[4:]],
        compiler_params=pltpu.CompilerParams(vmem_limit_bytes=62 * 2**20),
        name="results_in_float32",
    )(qkv, proj, vectors, inner, outer, mixed, token_grad)


def norm_parts(values):
    center = values - jnp.mean(values, axis=-1, keepdims=True)
    rstd = lax.rsqrt(jnp.mean(center * center, axis=-1, keepdims=True) + epsilon)
    return center * rstd, rstd


def norm_back(grad, normal, rstd, gain):
    scaled = grad * gain
    return rstd * (
        scaled
        - jnp.mean(scaled, axis=-1, keepdims=True)
        - normal * jnp.mean(scaled * normal, axis=-1, keepdims=True)
    )


def move_tokens_plan(
    tokens,
    key_mask,
    expert_ids,
    cotangent,
    norm1_gain,
    norm1_bias,
    w_qkv,
    w_proj,
    proj_bias,
    norm2_gain,
    norm2_bias,
    w_router,
    w_in,
    b_in,
    w_out,
    b_out,
):
    f32 = jnp.float32
    _, rows, width = tokens.shape
    experts, depth, hidden = w_in.shape
    slice_width = w_out.shape[1]
    planes = hidden // slice_width // 2
    own = experts // 2
    padded = (rows + experts + 15) // 16 * 16
    vectors = [v[None] for v in (norm1_gain, norm1_bias, proj_bias, norm2_gain, norm2_bias)]
    fronts = front(
        planes,
        padded,
        tokens[0],
        key_mask,
        expert_ids[0].T,
        cotangent[0],
        vectors,
        w_router.T,
        b_out,
        w_qkv,
        w_proj,
        w_in,
    )
    small, full_qkv, full_proj, inner, normed_in, qkv, attended, middle = fronts[:8]
    normed_mid, grad_out, all_grad_out, wide, select, keys, keep = fronts[8:]
    mix_parts, row_grad, inner_grad, outer_grad, bias_grad, router_grad = experts_of_the_plane(
        planes, own, rows, normed_mid, all_grad_out, inner, w_out, b_in, small
    )
    mixed, token_grad, qkv_grad, proj_grad, vector_grads, inner_grad, outer_grad, bias_grad = back(
        planes,
        own,
        rows,
        row_grad,
        normed_mid,
        grad_out,
        middle,
        wide,
        normed_in,
        qkv,
        attended,
        small,
        full_qkv,
        full_proj,
        keys,
        keep,
        select,
        mix_parts,
        inner_grad,
        outer_grad,
        bias_grad,
        router_grad,
    )
    outer_grad = outer_grad.reshape(experts, slice_width, width)
    finished = finish(qkv_grad, proj_grad, vector_grads, inner_grad, outer_grad, mixed, token_grad)
    qkv_grad, proj_grad, inner_grad, outer_grad, mixed, token_grad, router_grad, outer_bias_grad = finished[:8]
    vector_grads = [row.reshape(depth) for row in finished[8:]]
    return (
        mixed[None],
        token_grad[None],
        vector_grads[0],
        vector_grads[1],
        qkv_grad,
        proj_grad,
        vector_grads[2],
        vector_grads[3],
        vector_grads[4],
        router_grad.T,
        inner_grad,
        bias_grad[:, 0].reshape(experts, slice_width),
        outer_grad,
        outer_bias_grad,
    )


def solution(mesh):
    n_seq, n_fsdp = mesh.shape["seq"], mesh.shape["fsdp"]

    def per_device(*args):
        tokens, w_in, w_out = args[0], args[12], args[14]
        experts, _, hidden = w_in.shape
        lanes = hidden // n_fsdp
        whole_tiles = lanes % 128 == 0 and tokens.shape[2] % 256 == 0 and w_in.shape[1] % 32 == 0 and 2 * lanes <= tokens.shape[2]
        if n_seq == 4 and experts == n_seq and tokens.shape[0] == 1 and whole_tiles:
            return move_tokens_plan(*args)
        return gather_weights_plan(*args)

    return jax.shard_map(
        per_device,
        mesh=mesh,
        in_specs=(
            P(("fsdp", "seq"), None, None),
            P("fsdp", None),
            P(("fsdp", "seq"), None, None),
            P(("fsdp", "seq"), None, None),
            P("fsdp"),
            P("fsdp"),
            P("fsdp", None),
            P("fsdp", None),
            P("fsdp"),
            P("fsdp"),
            P("fsdp"),
            P("fsdp", None),
            P(None, "fsdp", None),
            P(None, "fsdp"),
            P(None, "fsdp", None),
            P(None, "fsdp"),
        ),
        out_specs=(
            P(("fsdp", "seq"), None, None),
            P(("fsdp", "seq"), None, None),
            P("fsdp"),
            P("fsdp"),
            P("fsdp", None),
            P("fsdp", None),
            P("fsdp"),
            P("fsdp"),
            P("fsdp"),
            P("fsdp", None),
            P(None, "fsdp", None),
            P(None, "fsdp"),
            P(None, "fsdp", None),
            P(None, "fsdp"),
        ),
        check_vma=False,
    )
```

```python
import functools

import jax
import jax.numpy as jnp
from jax import lax
from jax.experimental import pallas as pl
from jax.experimental.pallas import tpu as pltpu
from jax.sharding import PartitionSpec as P

HEADS = 12
CAP = 142


epsilon = 1e-06
masked_score = -1e30


def norm_rows(values, gain, offset):
    center = values - jnp.mean(values, axis=-1, keepdims=True)
    spread = jnp.mean(center * center, axis=-1, keepdims=True)
    return center * lax.rsqrt(spread + epsilon) * gain + offset


def softmax_rows(values):
    shifted = jnp.exp(values - jnp.max(values, axis=-1, keepdims=True))
    return shifted / jnp.sum(shifted, axis=-1, keepdims=True)


def exact_gelu(values):
    return jax.nn.gelu(values, approximate=False)


def expert_slots(chosen, experts):
    flat_ids = chosen.reshape(-1)
    onehot = (flat_ids[:, None] == jnp.arange(experts, dtype=jnp.int32)[None, :]).astype(jnp.int32)
    ranks = jnp.cumsum(onehot, axis=0, dtype=jnp.int32)
    slot_pos = jnp.sum(onehot * ranks, axis=1, dtype=jnp.int32) - 1
    return (flat_ids, slot_pos)


def gather_weights_plan(
    tokens,
    key_mask,
    expert_ids,
    cotangent,
    norm1_gain,
    norm1_bias,
    w_qkv,
    w_proj,
    proj_bias,
    norm2_gain,
    norm2_bias,
    w_router,
    w_in,
    b_in,
    w_out,
    b_out,
):
    images, seq_len, width = tokens.shape
    experts = w_in.shape[0]
    head_dim = width // HEADS
    scaling = head_dim ** (-0.5)
    row_count = images * seq_len
    dense_set = (
        lax.all_gather(norm1_gain, "fsdp", axis=0, tiled=True),
        lax.all_gather(norm1_bias, "fsdp", axis=0, tiled=True),
        lax.all_gather(w_qkv, "fsdp", axis=0, tiled=True),
        lax.all_gather(w_proj, "fsdp", axis=0, tiled=True),
        lax.all_gather(proj_bias, "fsdp", axis=0, tiled=True),
        lax.all_gather(norm2_gain, "fsdp", axis=0, tiled=True),
        lax.all_gather(norm2_bias, "fsdp", axis=0, tiled=True),
        lax.all_gather(w_router, "fsdp", axis=0, tiled=True),
    )
    gain_first = dense_set[0].astype(jnp.float32)
    bias_first = dense_set[1].astype(jnp.float32)
    full_qkv = dense_set[2]
    full_proj = dense_set[3]
    bias_proj = dense_set[4].astype(jnp.float32)
    gain_second = dense_set[5].astype(jnp.float32)
    bias_second = dense_set[6].astype(jnp.float32)
    full_router = dense_set[7]
    expert_set = (
        lax.all_gather(w_in, "fsdp", axis=1, tiled=True),
        lax.all_gather(b_in, "fsdp", axis=1, tiled=True),
        lax.all_gather(w_out, "fsdp", axis=1, tiled=True),
        lax.all_gather(b_out, "fsdp", axis=1, tiled=True),
    )
    inner_weight = expert_set[0]
    inner_bias = expert_set[1].astype(jnp.float32)
    outer_weight = expert_set[2]
    outer_bias = expert_set[3].astype(jnp.float32)
    own_mask = lax.dynamic_slice_in_dim(key_mask, lax.axis_index("seq") * images, images, 0)
    keep_rows = own_mask.reshape(row_count, 1).astype(jnp.float32)
    usable = (key_mask > 0)[:, None, None, :]
    flat_tokens = tokens.astype(jnp.float32).reshape(row_count, width)
    normed_in = norm_rows(flat_tokens, gain_first, bias_first).astype(jnp.bfloat16)
    mixed_qkv = jnp.dot(normed_in, full_qkv, preferred_element_type=jnp.float32).astype(
        jnp.bfloat16
    )
    mixed_qkv = mixed_qkv.reshape(images, seq_len, 3, HEADS, head_dim)
    head_qkv = lax.all_to_all(mixed_qkv, "seq", split_axis=3, concat_axis=0, tiled=True)
    queries = head_qkv[:, :, 0]
    key_rows = head_qkv[:, :, 1]
    value_rows = head_qkv[:, :, 2]

    def score_block():
        raw = (
            jnp.einsum("gahd,gbhd->ghab", queries, key_rows, preferred_element_type=jnp.float32)
            * scaling
        )
        return jnp.where(usable, raw, masked_score)

    scores = score_block()
    row_top = jnp.max(scores, axis=-1, keepdims=True)
    shifted = jnp.exp(scores - row_top)
    row_total = jnp.sum(shifted, axis=-1, keepdims=True)
    attn_probs = (shifted / row_total).astype(jnp.bfloat16)
    log_total = row_top + jnp.log(row_total)
    head_out = jnp.einsum(
        "ghab,gbhd->gahd", attn_probs, value_rows, preferred_element_type=jnp.float32
    ).astype(jnp.bfloat16)
    attended = lax.all_to_all(head_out, "seq", split_axis=0, concat_axis=2, tiled=True).reshape(
        row_count, width
    )
    middle = (
        flat_tokens + jnp.dot(attended, full_proj, preferred_element_type=jnp.float32) + bias_proj
    )
    normed_mid = norm_rows(middle, gain_second, bias_second).astype(jnp.bfloat16)
    routing = softmax_rows(jnp.dot(normed_mid, full_router, preferred_element_type=jnp.float32))
    chosen = expert_ids.reshape(row_count, 2)
    flat_ids, slot_pos = expert_slots(chosen, experts)
    gating = jnp.take_along_axis(routing, chosen, axis=1)
    buffer = (
        jnp.zeros((experts, CAP, width), jnp.bfloat16)
        .at[flat_ids, slot_pos]
        .set(jnp.repeat(normed_mid, 2, axis=0))
    )
    pre_act = (
        jnp.einsum("ecd,edf->ecf", buffer, inner_weight, preferred_element_type=jnp.float32)
        + inner_bias[:, None, :]
    )
    activated = exact_gelu(pre_act).astype(jnp.bfloat16)
    expert_out = (
        jnp.einsum("ecf,efd->ecd", activated, outer_weight, preferred_element_type=jnp.float32)
        + outer_bias[:, None, :]
    )
    picked = expert_out[flat_ids, slot_pos].reshape(row_count, 2, width)
    mixture = jnp.sum(gating[:, :, None] * picked, axis=1)
    mixed = (keep_rows * (middle + mixture)).astype(jnp.bfloat16).reshape(images, seq_len, width)
    grad_out = cotangent.astype(jnp.float32).reshape(row_count, width) * keep_rows
    grad_gate = jnp.sum(grad_out[:, None, :] * picked, axis=2)
    grad_picked = (
        (gating[:, :, None] * grad_out[:, None, :])
        .astype(jnp.bfloat16)
        .reshape(2 * row_count, width)
    )
    grad_expert_out = (
        jnp.zeros((experts, CAP, width), jnp.bfloat16).at[flat_ids, slot_pos].set(grad_picked)
    )
    grad_outer_bias = jnp.sum(grad_expert_out, axis=1, dtype=jnp.float32)
    hidden_pre = (
        jnp.einsum("ecd,edf->ecf", buffer, inner_weight, preferred_element_type=jnp.float32)
        + inner_bias[:, None, :]
    )
    hidden_act = exact_gelu(hidden_pre).astype(jnp.bfloat16)
    grad_outer_weight = jnp.einsum(
        "ecf,ecd->efd", hidden_act, grad_expert_out, preferred_element_type=jnp.float32
    )
    grad_act = jnp.einsum(
        "ecd,efd->ecf", grad_expert_out, outer_weight, preferred_element_type=jnp.float32
    )
    gelu_pull = jax.vjp(exact_gelu, hidden_pre)[1]
    grad_pre = gelu_pull(grad_act)[0].astype(jnp.bfloat16)
    grad_inner_bias = jnp.sum(grad_pre, axis=1, dtype=jnp.float32)
    grad_inner_weight = jnp.einsum(
        "ecd,ecf->edf", buffer, grad_pre, preferred_element_type=jnp.float32
    )
    grad_buffer = jnp.einsum(
        "ecf,edf->ecd", grad_pre, inner_weight, preferred_element_type=jnp.float32
    )
    grad_rows = jnp.sum(grad_buffer[flat_ids, slot_pos].reshape(row_count, 2, width), axis=1)
    expert_range = jnp.arange(experts, dtype=jnp.int32)[None, None, :]
    grad_route = jnp.sum(
        grad_gate[:, :, None] * (chosen[:, :, None] == expert_range).astype(jnp.float32), axis=1
    )
    grad_logits = (
        routing * (grad_route - jnp.sum(routing * grad_route, axis=-1, keepdims=True))
    ).astype(jnp.bfloat16)
    grad_router = jnp.einsum(
        "nd,ne->de", normed_mid, grad_logits, preferred_element_type=jnp.float32
    )
    grad_normed_mid = grad_rows + jnp.einsum(
        "ne,de->nd", grad_logits, full_router, preferred_element_type=jnp.float32
    )
    second_pull = jax.vjp(norm_rows, middle, gain_second, bias_second)[1]
    grad_mid_norm, grad_gain_second, grad_bias_second = second_pull(grad_normed_mid)
    grad_middle = grad_out + grad_mid_norm
    grad_proj = grad_middle.astype(jnp.bfloat16)
    grad_bias_proj = jnp.sum(grad_proj, axis=0, dtype=jnp.float32)
    grad_proj_weight = jnp.einsum(
        "nd,ne->de", attended, grad_proj, preferred_element_type=jnp.float32
    )
    grad_attended = jnp.einsum(
        "ne,de->nd", grad_proj, full_proj, preferred_element_type=jnp.float32
    ).astype(jnp.bfloat16)
    grad_head_out = lax.all_to_all(
        grad_attended.reshape(images, seq_len, HEADS, head_dim),
        "seq",
        split_axis=2,
        concat_axis=0,
        tiled=True,
    )
    recomputed = jnp.exp(score_block() - log_total)
    grad_values = jnp.einsum(
        "ghab,gahd->gbhd",
        recomputed.astype(jnp.bfloat16),
        grad_head_out,
        preferred_element_type=jnp.float32,
    )
    grad_probs = jnp.einsum(
        "gahd,gbhd->ghab", grad_head_out, value_rows, preferred_element_type=jnp.float32
    )
    grad_scores = (
        recomputed * (grad_probs - jnp.sum(recomputed * grad_probs, axis=-1, keepdims=True))
    ).astype(jnp.bfloat16)
    grad_queries = (
        jnp.einsum("ghab,gbhd->gahd", grad_scores, key_rows, preferred_element_type=jnp.float32)
        * scaling
    )
    grad_keys = (
        jnp.einsum("ghab,gahd->gbhd", grad_scores, queries, preferred_element_type=jnp.float32)
        * scaling
    )
    grad_head_qkv = jnp.stack([grad_queries, grad_keys, grad_values], axis=2).astype(jnp.bfloat16)
    grad_qkv = lax.all_to_all(
        grad_head_qkv, "seq", split_axis=0, concat_axis=3, tiled=True
    ).reshape(row_count, 3 * width)
    grad_qkv_weight = jnp.einsum(
        "nd,ne->de", normed_in, grad_qkv, preferred_element_type=jnp.float32
    )
    grad_normed_in = jnp.einsum("ne,de->nd", grad_qkv, full_qkv, preferred_element_type=jnp.float32)
    first_pull = jax.vjp(norm_rows, flat_tokens, gain_first, bias_first)[1]
    grad_first, grad_gain_first, grad_bias_first = first_pull(grad_normed_in)
    token_grad = (grad_middle + grad_first).astype(jnp.bfloat16).reshape(images, seq_len, width)
    shares = (
        lax.psum_scatter(grad_gain_first, "fsdp", scatter_dimension=0, tiled=True),
        lax.psum_scatter(grad_bias_first, "fsdp", scatter_dimension=0, tiled=True),
        lax.psum_scatter(grad_qkv_weight, "fsdp", scatter_dimension=0, tiled=True),
        lax.psum_scatter(grad_proj_weight, "fsdp", scatter_dimension=0, tiled=True),
        lax.psum_scatter(grad_bias_proj, "fsdp", scatter_dimension=0, tiled=True),
        lax.psum_scatter(grad_gain_second, "fsdp", scatter_dimension=0, tiled=True),
        lax.psum_scatter(grad_bias_second, "fsdp", scatter_dimension=0, tiled=True),
        lax.psum_scatter(grad_router, "fsdp", scatter_dimension=0, tiled=True),
        lax.psum_scatter(grad_inner_weight, "fsdp", scatter_dimension=1, tiled=True),
        lax.psum_scatter(grad_inner_bias, "fsdp", scatter_dimension=1, tiled=True),
        lax.psum_scatter(grad_outer_weight, "fsdp", scatter_dimension=1, tiled=True),
        lax.psum_scatter(grad_outer_bias, "fsdp", scatter_dimension=1, tiled=True),
    )
    parted = (
        lax.psum_scatter(
            shares[0].astype(jnp.bfloat16), "seq", scatter_dimension=0, tiled=True
        ).astype(jnp.float32),
        lax.psum_scatter(
            shares[1].astype(jnp.bfloat16), "seq", scatter_dimension=0, tiled=True
        ).astype(jnp.float32),
        lax.psum_scatter(
            shares[2].astype(jnp.bfloat16), "seq", scatter_dimension=0, tiled=True
        ).astype(jnp.float32),
        lax.psum_scatter(
            shares[3].astype(jnp.bfloat16), "seq", scatter_dimension=0, tiled=True
        ).astype(jnp.float32),
        lax.psum_scatter(
            shares[4].astype(jnp.bfloat16), "seq", scatter_dimension=0, tiled=True
        ).astype(jnp.float32),
        lax.psum_scatter(
            shares[5].astype(jnp.bfloat16), "seq", scatter_dimension=0, tiled=True
        ).astype(jnp.float32),
        lax.psum_scatter(
            shares[6].astype(jnp.bfloat16), "seq", scatter_dimension=0, tiled=True
        ).astype(jnp.float32),
        lax.psum_scatter(
            shares[7].astype(jnp.bfloat16), "seq", scatter_dimension=0, tiled=True
        ).astype(jnp.float32),
        lax.psum_scatter(
            shares[8].astype(jnp.bfloat16), "seq", scatter_dimension=1, tiled=True
        ).astype(jnp.float32),
        lax.psum_scatter(
            shares[9].astype(jnp.bfloat16), "seq", scatter_dimension=1, tiled=True
        ).astype(jnp.float32),
        lax.psum_scatter(
            shares[10].astype(jnp.bfloat16), "seq", scatter_dimension=1, tiled=True
        ).astype(jnp.float32),
        lax.psum_scatter(
            shares[11].astype(jnp.bfloat16), "seq", scatter_dimension=1, tiled=True
        ).astype(jnp.float32),
    )
    totals = (
        lax.all_gather(parted[0].astype(jnp.bfloat16), "seq", axis=0, tiled=True).astype(
            jnp.float32
        ),
        lax.all_gather(parted[1].astype(jnp.bfloat16), "seq", axis=0, tiled=True).astype(
            jnp.float32
        ),
        lax.all_gather(parted[2].astype(jnp.bfloat16), "seq", axis=0, tiled=True).astype(
            jnp.float32
        ),
        lax.all_gather(parted[3].astype(jnp.bfloat16), "seq", axis=0, tiled=True).astype(
            jnp.float32
        ),
        lax.all_gather(parted[4].astype(jnp.bfloat16), "seq", axis=0, tiled=True).astype(
            jnp.float32
        ),
        lax.all_gather(parted[5].astype(jnp.bfloat16), "seq", axis=0, tiled=True).astype(
            jnp.float32
        ),
        lax.all_gather(parted[6].astype(jnp.bfloat16), "seq", axis=0, tiled=True).astype(
            jnp.float32
        ),
        lax.all_gather(parted[7].astype(jnp.bfloat16), "seq", axis=0, tiled=True).astype(
            jnp.float32
        ),
        lax.all_gather(parted[8].astype(jnp.bfloat16), "seq", axis=1, tiled=True).astype(
            jnp.float32
        ),
        lax.all_gather(parted[9].astype(jnp.bfloat16), "seq", axis=1, tiled=True).astype(
            jnp.float32
        ),
        lax.all_gather(parted[10].astype(jnp.bfloat16), "seq", axis=1, tiled=True).astype(
            jnp.float32
        ),
        lax.all_gather(parted[11].astype(jnp.bfloat16), "seq", axis=1, tiled=True).astype(
            jnp.float32
        ),
    )
    return (
        mixed,
        token_grad,
        totals[0],
        totals[1],
        totals[2],
        totals[3],
        totals[4],
        totals[5],
        totals[6],
        totals[7],
        totals[8],
        totals[9],
        totals[10],
        totals[11],
    )


MESH = pl.DeviceIdType.MESH
NT = (((1,), (1,)), ((), ()))
TN = (((0,), (0,)), ((), ()))


def dot(a, b):
    return jnp.dot(a, b, preferred_element_type=jnp.float32)


class Place:
    def __init__(self, planes):
        self.planes = planes
        s, f = lax.axis_index("seq"), lax.axis_index("fsdp")
        self.y, self.c, self.z, self.x = s // 2, s % 2, f // 2, f % 2

    def at(self, y, c, z, x):
        return (y * 2 + c, z * 2 + x)

    def other_core(self):
        return self.at(self.y, 1 - self.c, self.z, self.x)

    def other_x(self):
        return self.at(self.y, self.c, self.z, 1 - self.x)

    def other_y(self):
        return self.at(1 - self.y, self.c, self.z, self.x)

    def level(self, k):
        return self.at(self.y, self.c, lax.rem(self.z + k + self.planes, self.planes), self.x)


def greet(partners):
    barrier = pltpu.get_barrier_semaphore()
    for partner in partners:
        pl.semaphore_signal(barrier, inc=1, device_id=partner, device_id_type=MESH)
    pl.semaphore_wait(barrier, len(partners))


def nearest(place, i):
    level = 0
    for z in range(place.planes):
        order = sorted(range(place.planes), key=lambda other: (abs(other - z), other))
        for at in range(place.planes):
            level = level + jnp.where((place.z == z) & (i == at), order[at], 0)
    return level


def expert_kernel(
    planes,
    own,
    rows,
    real,
    normed_ref,
    grads_all_ref,
    inner_ref,
    outer_all_ref,
    bias_all_ref,
    small_ref,
    mix_out_ref,
    out_ref,
    inner_grad_ref,
    outer_grad_ref,
    bias_grad_ref,
    router_grad_ref,
    grads_ref,
    mix_ref,
    mix_from_core,
    outer_ref,
    inner_t_ref,
    outer_t_ref,
    router_ref,
    router_t_ref,
    tokens,
    part,
    from_core,
    from_x,
    from_z,
    hidden,
    hidden_grad,
    logit_grad,
    inner_acc,
    outer_acc,
    outer_sem,
    grads_sem,
    mix_sem,
    mix_c_send,
    mix_c_recv,
    z_send,
    z_recv,
    x_send,
    x_recv,
    c_send,
    c_recv,
    sum_c_send,
    sum_c_recv,
    sum_x_send,
    sum_x_recv,
    sum_z_send,
    sum_z_recv,
):
    f32, bf16 = jnp.float32, jnp.bfloat16
    place = Place(planes)
    y, c, z, x = place.y, place.c, place.z, place.x
    width = inner_ref.shape[0]
    lanes = inner_ref.shape[1] // own
    first = real % 16

    def remote(src, dst, send, recv, device):
        return pltpu.make_async_remote_copy(
            src_ref=src, dst_ref=dst, send_sem=send, recv_sem=recv, device_id=device, device_id_type=MESH
        )

    def slot(buffer, level, at, count=1):
        return buffer.at[level, pl.ds(at * rows, count * rows)]

    def up_copy(level):
        here = slot(tokens, level, 0)
        return remote(here, here, z_send.at[0, level], z_recv.at[0, level], place.at(y, c, z + 1, x))

    def down_copy(level):
        here = slot(tokens, level, 0)
        return remote(here, here, z_send.at[1, level], z_recv.at[1, level], place.at(y, c, z - 1, x))

    def x_copy(level):
        return remote(
            slot(tokens, level, 0), slot(tokens, level, 2), x_send.at[level], x_recv.at[level], place.other_x()
        )

    def c_copy(level, r):
        return remote(
            slot(tokens, level, 2 * r),
            slot(tokens, level, 2 * r + 1),
            c_send.at[level, r],
            c_recv.at[level, r],
            place.other_core(),
        )

    def sum_c_copy(level, r):
        return remote(
            slot(part, level, 2 * r + 1),
            slot(from_core, level, r),
            sum_c_send.at[level, r],
            sum_c_recv.at[level, r],
            place.other_core(),
        )

    def sum_x_copy(level):
        return remote(
            slot(part, level, 2), from_x.at[level], sum_x_send.at[level], sum_x_recv.at[level], place.other_x()
        )

    def sum_z_copy(level, source):
        return remote(
            slot(part, level, 0),
            from_z.at[source],
            sum_z_send.at[level],
            sum_z_recv.at[source],
            place.at(y, c, level, x),
        )

    partners = [place.other_core(), place.other_x()] + [place.level(k) for k in range(1, planes)]
    greet(partners)
    tokens[z, 0:rows, :] = normed_ref[...]

    @pl.when(z < planes - 1)
    def _():
        up_copy(z).start()

    @pl.when(z > 0)
    def _():
        down_copy(z).start()

    c_copy(z, 0).start()
    x_copy(z).start()
    def grads_load(level):
        return pltpu.make_async_copy(grads_all_ref.at[level], grads_ref.at[level], grads_sem.at[level])

    def mix_c(level, r):
        return remote(
            slot(mix_ref, level, 2 * r + 1),
            slot(mix_from_core, level, r),
            mix_c_send.at[level, r],
            mix_c_recv.at[level, r],
            place.other_core(),
        )

    def mix_store(level, r):
        return pltpu.make_async_copy(
            slot(mix_ref, level, 2 * r), slot(mix_out_ref, level, r), mix_sem.at[level, r]
        )

    def mix_sum(level):
        for r in range(2):
            mix_c(level, r).wait_recv()
            here = slice(2 * r * rows, (2 * r + 1) * rows)
            total = mix_ref[level, here, :].astype(f32)
            total = total + mix_from_core[level, r * rows : (r + 1) * rows, :].astype(f32)
            mix_ref[level, here, :] = total.astype(bf16)
            mix_store(level, r).start()

    for i in range(planes):
        grads_load(nearest(place, (i + 1) % planes)).start()
    loads = [
        pltpu.make_async_copy(
            outer_all_ref.at[c * own + i], outer_ref.at[pl.ds(i * lanes, lanes)], outer_sem.at[i]
        )
        for i in range(own)
    ]
    for load in loads:
        load.start()
    inner_t_ref[...] = jnp.transpose(inner_ref[...])
    place_row = lax.broadcasted_iota(jnp.int32, (128, 128), 0)
    place_lane = lax.broadcasted_iota(jnp.int32, (128, 128), 1)
    take = (place_row - (5 + 2 * own) == place_lane - first) & (place_lane >= first)
    take = take & (place_lane < first + 2 * own)
    router = dot(small_ref[...], take.astype(bf16))
    router_ref[...] = router.astype(bf16)
    router_t_ref[...] = jnp.transpose(router).astype(bf16)
    inner_acc[...] = jnp.zeros_like(inner_acc)
    outer_acc[...] = jnp.zeros_like(outer_acc)
    bias_grad_ref[...] = jnp.zeros_like(bias_grad_ref)
    router_grad_ref[...] = jnp.zeros_like(router_grad_ref)
    for load in loads:
        load.wait()
    outer_t_ref[...] = jnp.transpose(outer_ref[...])

    def hop(h):
        @pl.when(z >= h)
        def _():
            up_copy(z - h).wait_recv()

            @pl.when(z < planes - 1)
            def _():
                up_copy(z - h).start()

            x_copy(z - h).start()
            c_copy(z - h, 0).start()

        @pl.when(z + h < planes)
        def _():
            down_copy(z + h).wait_recv()

            @pl.when(z > 0)
            def _():
                down_copy(z + h).start()

            x_copy(z + h).start()
            c_copy(z + h, 0).start()

    def tiles(level, r):
        here = pl.ds(pl.multiple_of(2 * r * rows, 16), 2 * rows)
        normed, grad_out = tokens[level, here, :], grads_ref[level, here, :]
        select = []
        for t in range(2):
            last = pl.ds(pl.multiple_of((2 * r + t) * rows + real - first, 16), 16)
            chosen = grads_ref[level, last, :256].astype(f32)
            chosen = jnp.concatenate([chosen, jnp.zeros((112, 256), f32)], axis=0)
            select.append(jnp.transpose(chosen)[:rows])
        select = jnp.concatenate(select, axis=0)
        lane = lax.broadcasted_iota(jnp.int32, select.shape, 1)
        named = (lane >= first) & (lane < first + 2 * own)
        select = jnp.where(named, select, 0.0)
        logits = jnp.where(named, dot(normed, router_ref[...]), -1e30)
        routing = jnp.exp(logits - jnp.max(logits, axis=1, keepdims=True))
        routing = routing / jnp.sum(routing, axis=1, keepdims=True)
        gates = routing * select
        gate_grads = jnp.zeros_like(gates)
        all_pre = dot(normed, inner_ref[...])
        all_grad_act = dot(grad_out, outer_t_ref[...])
        for i in range(own):
            mine = lane == first + c * own + i
            units = slice(i * lanes, (i + 1) * lanes)
            gate = jnp.sum(jnp.where(mine, gates, 0.0), axis=1, keepdims=True)
            bias = jnp.where(c == 0, bias_all_ref[i : i + 1, :], bias_all_ref[own + i : own + i + 1, :])
            pre = all_pre[:, units] + bias.astype(f32)
            grad_act = all_grad_act[:, units]
            cdf = 0.5 * (1.0 + lax.erf(pre * (0.5**0.5)))
            act = pre * cdf
            hidden[here, units] = (gate * act).astype(bf16)
            gate_grad = jnp.sum(act * grad_act, axis=1, keepdims=True)
            gate_grads = gate_grads + jnp.where(mine, gate_grad * select, 0.0)
            slope = cdf + pre * jnp.exp(-0.5 * pre * pre) * 0.3989422804014327
            grad_pre = gate * grad_act * slope
            bias_grad_ref[0:1, units] += jnp.sum(grad_pre, axis=0, keepdims=True)
            hidden_grad[here, units] = grad_pre.astype(bf16)
        grad_logits = routing * (gate_grads - jnp.sum(routing * gate_grads, axis=1, keepdims=True))
        logit_grad[here, :] = grad_logits.astype(bf16)
        mix_ref[level, here, :] = dot(hidden[here, :], outer_ref[...]).astype(bf16)
        row_grad = dot(hidden_grad[here, :], inner_t_ref[...])
        row_grad = row_grad + dot(logit_grad[here, :], router_t_ref[...])
        part[level, here, :] = row_grad.astype(bf16)

    def across_sum(level):
        sum_c_copy(level, 1).wait_recv()
        here = slice(2 * rows, 3 * rows)
        total = part[level, here, :].astype(f32) + from_core[level, rows : 2 * rows, :].astype(f32)
        part[level, here, :] = total.astype(bf16)
        sum_x_copy(level).start()

    def level_sum(level):
        sum_c_copy(level, 0).wait_recv()
        sum_x_copy(level).wait_recv()
        total = part[level, 0:rows, :].astype(f32) + from_core[level, 0:rows, :].astype(f32)
        total = total + from_x[level].astype(f32)
        part[level, 0:rows, :] = total.astype(bf16)

    def weight_grads(level):
        for j in range(width // 256):
            some = slice(j * 256, (j + 1) * 256)
            outer_acc[some, :] += lax.dot_general(
                hidden[:, some], grads_ref[level], TN, preferred_element_type=f32
            )
            inner_acc[some, :] += lax.dot_general(
                tokens[level, :, some], hidden_grad[...], TN, preferred_element_type=f32
            )
        router_grad_ref[...] += lax.dot_general(tokens[level], logit_grad[...], TN, preferred_element_type=f32)

    def order(i):
        return nearest(place, jnp.where(i == 0, 1, jnp.where(i == planes - 1, 0, planes - i)))

    def step(i, carry):
        level, before = order(i), order(i - 1)

        def half(s, carry):
            r = jnp.where(i < planes - 2, s, 1 - s)

            @pl.when((i == 0) & (s == 0))
            def _():
                hop(1)

            if planes > 2:
                @pl.when((i == 0) & (s == 1))
                def _():
                    hop(2)

            @pl.when((i == 1) & (s == 0))
            def _():
                for h in range(3, planes):
                    hop(h)

            @pl.when((i > 0) & (s == 1))
            def _():
                level_sum(before)
                sum_z_copy(before, z).start()

            @pl.when(s == 0)
            def _():
                grads_load(level).wait()

            @pl.when(r == 0)
            def _():
                c_copy(level, 0).wait_recv()

            @pl.when(r == 1)
            def _():
                x_copy(level).wait_recv()
                c_copy(level, 1).start()
                c_copy(level, 1).wait_recv()

            tiles(level, r)
            sum_c_copy(level, r).start()
            mix_c(level, r).start()

            @pl.when(r == 1)
            def _():
                across_sum(level)

            return carry

        lax.fori_loop(0, 2, half, 0)
        weight_grads(level)
        mix_sum(level)
        return carry

    lax.fori_loop(0, planes, step, 0)
    level_sum(z)
    inner_grad_ref[...] = inner_acc[...].astype(bf16)
    outer_grad_ref[...] = outer_acc[...].astype(bf16)
    total = part[z, 0:rows, :].astype(f32)
    for k in range(1, planes):
        source = lax.rem(z + k, planes)
        sum_z_copy(z, source).wait_recv()
        total = total + from_z[source].astype(f32)
    out_ref[...] = total
    for level in range(planes):
        mix_store(level, 0).wait()
        mix_store(level, 1).wait()
        mix_c(level, 0).wait_send()
        mix_c(level, 1).wait_send()
        x_copy(level).wait_send()
        c_copy(level, 0).wait_send()
        c_copy(level, 1).wait_send()
        sum_c_copy(level, 0).wait_send()
        sum_c_copy(level, 1).wait_send()
        sum_x_copy(level).wait_send()

        @pl.when(level != z)
        def _():
            sum_z_copy(level, z).wait_send()

        @pl.when((z >= level) & (z < planes - 1))
        def _():
            up_copy(level).wait_send()

        @pl.when((z <= level) & (z > 0))
        def _():
            down_copy(level).wait_send()


def experts_of_the_plane(planes, own, real, normed, grads, inner, outer, bias, small):
    f32, bf16 = jnp.float32, jnp.bfloat16
    rows = normed.shape[0]
    chunk = 4 * rows
    width, units = inner.shape
    shape = jax.ShapeDtypeStruct
    vmem = pl.BlockSpec(memory_space=pltpu.VMEM)
    anywhere = pl.BlockSpec(memory_space=pl.ANY)
    dma = pltpu.SemaphoreType.DMA
    flops = 12 * planes * chunk * width * units
    return pl.pallas_call(
        functools.partial(expert_kernel, planes, own, rows, real),
        out_shape=[
            shape((planes, 2 * rows, width), bf16),
            shape((rows, width), f32),
            shape((width, units), bf16),
            shape((units, width), bf16),
            shape((8, units), f32),
            shape((width, 128), f32),
        ],
        in_specs=[vmem, anywhere, vmem, anywhere, vmem, vmem],
        out_specs=[anywhere] + [vmem] * 5,
        scratch_shapes=[
            pltpu.VMEM((planes, chunk, width), bf16),
            pltpu.VMEM((planes, chunk, width), bf16),
            pltpu.VMEM((planes, 2 * rows, width), bf16),
            pltpu.VMEM((units, width), bf16),
            pltpu.VMEM((units, width), bf16),
            pltpu.VMEM((width, units), bf16),
            pltpu.VMEM((width, 128), bf16),
            pltpu.VMEM((128, width), bf16),
            pltpu.VMEM((planes, chunk, width), bf16),
            pltpu.VMEM((planes, chunk, width), bf16),
            pltpu.VMEM((planes, 2 * rows, width), bf16),
            pltpu.VMEM((planes, rows, width), bf16),
            pltpu.VMEM((planes, rows, width), bf16),
            pltpu.VMEM((chunk, units), bf16),
            pltpu.VMEM((chunk, units), bf16),
            pltpu.VMEM((chunk, 128), bf16),
            pltpu.VMEM((width, units), f32),
            pltpu.VMEM((units, width), f32),
            dma((own,)),
            dma((planes,)),
            dma((planes, 2)),
            dma((planes, 2)),
            dma((planes, 2)),
        ]
        + [dma((2, planes))] * 2
        + [dma((planes,))] * 2
        + [dma((planes, 2))] * 4
        + [dma((planes,))] * 4,
        compiler_params=pltpu.CompilerParams(
            collective_id=1, has_side_effects=True, vmem_limit_bytes=60 * 2**20
        ),
        cost_estimate=pl.CostEstimate(flops=flops, bytes_accessed=40 * 2**20, transcendentals=0),
        name="experts_of_the_plane",
    )(normed, grads, inner, outer, bias, small)


def front_kernel(
    planes,
    heads,
    real,
    tokens_ref,
    mask_ref,
    ids_ref,
    cotangent_ref,
    *refs,
):
    vector_refs, refs = refs[:5], refs[5:]
    (
        router_part_ref,
        outer_bias_ref,
        qkv_part_ref,
    proj_part_ref,
    inner_part_ref,
    small_all,
    w_qkv_out,
    w_proj_out,
    inner_all,
    normed_in_ref,
    qkv_ref,
    attended_ref,
    middle_ref,
    normed_ref,
    grad_ref,
    grads_all,
    wide_ref,
    select_ref,
    keys_ref,
    keep_ref,
    w_qkv_all,
    w_proj_all,
    out_sem,
    up_send,
    up_recv,
    down_send,
    down_recv,
    x_send,
    x_recv,
    c_send,
    c_recv,
    over_send,
    over_recv,
    over_c_send,
    over_c_recv,
    g_z_send,
    g_z_recv,
    g_x_send,
    g_x_recv,
    g_c_send,
    g_c_recv,
    spread_send,
    spread_recv,
    own_sem,
    y_send,
    y_recv,
    ) = refs
    f32, bf16 = jnp.float32, jnp.bfloat16
    place = Place(planes)
    rows, width = wide_ref.shape
    depth = qkv_part_ref.shape[0]
    experts = inner_part_ref.shape[0]
    half = depth // 2
    lanes = inner_part_ref.shape[2] // (2 * planes)
    head_dim = width // heads
    y, c, z, x = place.y, place.c, place.z, place.x
    gathered = [small_all, w_qkv_all, w_proj_all]

    def remote(src, dst, send, recv, device):
        return pltpu.make_async_remote_copy(
            src_ref=src, dst_ref=dst, send_sem=send, recv_sem=recv, device_id=device, device_id_type=MESH
        )

    def block(j, level, across, core, plane):
        start = pl.multiple_of((level * 2 + across) * depth + core * half, 16)
        if j == 0:
            return gathered[j].at[pl.ds(start, half)]
        columns = gathered[j].shape[1] // 2
        return gathered[j].at[pl.ds(start, half), pl.ds(pl.multiple_of(plane * columns, 128), columns)]

    def piece(j, level, across):
        return block(j, level, across, c, y)

    def up_copy(j, level):
        here = piece(j, level, x)
        return remote(here, here, up_send.at[j, level], up_recv.at[j, level], place.at(y, c, z + 1, x))

    def down_copy(j, level):
        here = piece(j, level, x)
        return remote(here, here, down_send.at[j, level], down_recv.at[j, level], place.at(y, c, z - 1, x))

    def x_copy(j, level, across):
        here = piece(j, level, across)
        return remote(here, here, x_send.at[j, level], x_recv.at[j, level], place.other_x())

    def c_copy(j, level, across):
        here = piece(j, level, across)
        at = level * 2 + across
        return remote(here, here, c_send.at[j, at], c_recv.at[j, at], place.other_core())

    def over_copy(j, level, across):
        here = piece(j, level, across)
        at = level * 2 + across
        return remote(here, here, over_send.at[j, at], over_recv.at[j, at], place.other_y())

    def over_c_copy(j, level, across):
        here = block(j, level, across, c, 1 - y)
        at = level * 2 + across
        return remote(here, here, over_c_send.at[j, at], over_c_recv.at[j, at], place.other_core())

    def g_slot(level, at):
        return grads_all.at[level, pl.ds(at * rows, rows)]

    def g_up(level):
        here = g_slot(level, 0)
        return remote(here, here, g_z_send.at[0, level], g_z_recv.at[0, level], place.at(y, c, z + 1, x))

    def g_down(level):
        here = g_slot(level, 0)
        return remote(here, here, g_z_send.at[1, level], g_z_recv.at[1, level], place.at(y, c, z - 1, x))

    def g_x(level):
        return remote(g_slot(level, 0), g_slot(level, 2), g_x_send.at[level], g_x_recv.at[level], place.other_x())

    def g_c(level, r):
        return remote(
            g_slot(level, 2 * r), g_slot(level, 2 * r + 1), g_c_send.at[level, r], g_c_recv.at[level, r], place.other_core()
        )

    def columns_of(f):
        return pl.ds(pl.multiple_of(f * lanes, 128), lanes)

    here_rows = pl.ds(pl.multiple_of((z * 2 + x) * depth, 16), depth)
    my_units = pl.ds(pl.multiple_of(y * lanes, 128), lanes)

    def spread_copy(k, r):
        level, across = lax.rem(z + k, planes), (x + r) % 2
        return remote(
            inner_part_ref.at[c * 2 + y, :, columns_of(level * 2 + across)],
            inner_all.at[here_rows, my_units],
            spread_send.at[k, r],
            spread_recv.at[k, r],
            place.at(y, c, level, across),
        )

    own_copy = pltpu.make_async_copy(
        inner_part_ref.at[c * 2 + y, :, columns_of(z * 2 + x)], inner_all.at[here_rows, my_units], own_sem
    )
    y_copy = remote(inner_all.at[:, my_units], inner_all.at[:, my_units], y_send, y_recv, place.other_y())
    their_units = pl.ds(pl.multiple_of((1 - y) * lanes, 128), lanes)
    from_y = remote(inner_all.at[:, their_units], inner_all.at[:, their_units], y_send, y_recv, place.other_y())

    others = [(k, r) for k in range(planes) for r in range(2) if k or r]
    partners = [place.other_core(), place.other_y()]
    partners += [place.at(y, c, lax.rem(z + k, planes), (x + r) % 2) for k, r in others]
    greet(partners)

    w_qkv_all[here_rows, :] = qkv_part_ref[...]

    def share(j, level, across):
        c_copy(j, level, across).start()
        if j:
            over_copy(j, level, across).start()

    def line(flows):
        @pl.when(z < planes - 1)
        def _():
            for j in flows:
                up_copy(j, z).start()

        @pl.when(z > 0)
        def _():
            for j in flows:
                down_copy(j, z).start()

        for j in flows:
            x_copy(j, z, x).start()

    def hops(flows):
        for h in range(1, planes):
            @pl.when(z >= h)
            def _():
                for j in flows:
                    up_copy(j, z - h).wait_recv()

                    @pl.when(z < planes - 1)
                    def _():
                        up_copy(j, z - h).start()

                    x_copy(j, z - h, x).start()
                    share(j, z - h, x)

            @pl.when(z + h < planes)
            def _():
                for j in flows:
                    down_copy(j, z + h).wait_recv()

                    @pl.when(z > 0)
                    def _():
                        down_copy(j, z + h).start()

                    x_copy(j, z + h, x).start()
                    share(j, z + h, x)

    def arrive(flows):
        for i in range(planes):
            level = nearest(place, i)
            for j in flows:
                x_copy(j, level, 1 - x).wait_recv()
                share(j, level, 1 - x)

    def over_arrive(flows):
        for i in range(planes):
            level = nearest(place, i)
            for j in flows:
                if i:
                    over_copy(j, level, x).wait_recv()
                    over_c_copy(j, level, x).start()
                over_copy(j, level, 1 - x).wait_recv()
                over_c_copy(j, level, 1 - x).start()

    def gather_done(flows):
        for level in range(planes):
            for j in flows:
                c_copy(j, level, 1 - x).wait_recv()
                if j:
                    over_c_copy(j, level, 1 - x).wait_recv()

            @pl.when(level != z)
            def _():
                for j in flows:
                    c_copy(j, level, x).wait_recv()
                    if j:
                        over_c_copy(j, level, x).wait_recv()

    def g_hop(h):
        @pl.when(z >= h)
        def _():
            g_up(z - h).wait_recv()

            @pl.when(z < planes - 1)
            def _():
                g_up(z - h).start()

            g_x(z - h).start()
            g_c(z - h, 0).start()

        @pl.when(z + h < planes)
        def _():
            g_down(z + h).wait_recv()

            @pl.when(z > 0)
            def _():
                g_down(z + h).start()

            g_x(z + h).start()
            g_c(z + h, 0).start()

    line([1])
    lined = [ref[...].astype(f32) for ref in (*vector_refs, outer_bias_ref, router_part_ref)]
    lined = jnp.concatenate(lined, axis=0)
    lined = jnp.concatenate([lined, jnp.zeros((128 - lined.shape[0], depth), f32)], axis=0)
    lined = jnp.concatenate([lined, jnp.zeros((128, 128 - depth), f32)], axis=1)
    small = jnp.transpose(lined)[:depth]
    small_all[here_rows, :] = small.astype(bf16)
    line([0])
    w_proj_all[here_rows, :] = proj_part_ref[...]
    line([2])
    spare = jnp.zeros((rows - real, width), f32)
    values = jnp.concatenate([tokens_ref[...].astype(f32), spare], axis=0)
    wide_ref[...] = values.astype(bf16)
    normal, _ = norm_parts(values)
    mask = mask_ref[pl.ds(y * 2 + c, 1), :].astype(f32)
    keys = jnp.concatenate([mask, jnp.zeros((1, rows - real), f32)], axis=1)
    keys_ref[...] = keys
    keep = lax.broadcasted_iota(jnp.int32, (rows, rows), 0) == lax.broadcasted_iota(jnp.int32, (rows, rows), 1)
    keep = jnp.sum(jnp.where(keep, keys, 0.0), axis=1, keepdims=True)
    keep_ref[...] = keep
    ids = ids_ref[...]
    number = lax.broadcasted_iota(jnp.int32, (8, real), 0)
    chosen = ((number == ids[0:1]) | (number == ids[1:2])).astype(f32)
    chosen = jnp.concatenate([chosen, jnp.zeros((8, width - real), f32)], axis=1)
    select = jnp.concatenate([chosen[:, :256], jnp.zeros((120, 256), f32)], axis=0)
    select_ref[...] = jnp.transpose(select)[:rows].astype(bf16)
    if rows - real > 8:
        chosen = jnp.concatenate([chosen, jnp.zeros((rows - real - 8, width), f32)], axis=0)
    grad_out = cotangent_ref[...].astype(f32) * keep[:real]
    grad_out = jnp.concatenate([grad_out, chosen], axis=0).astype(bf16)
    grad_ref[...] = grad_out
    grads_own = pltpu.make_async_copy(grad_ref, g_slot(z, 0), out_sem.at[2])
    grads_own.start()
    hops([1, 0])
    arrive([1, 0])
    hops([2])
    own_copy.start()
    for k, r in others:
        spread_copy(k, r).start()

    grads_own.wait()

    @pl.when(z < planes - 1)
    def _():
        g_up(z).start()

    @pl.when(z > 0)
    def _():
        g_down(z).start()

    g_x(z).start()
    g_c(z, 0).start()
    arrive([2])
    over_arrive([1])
    gather_done([1, 0])
    qkv_out_copy = pltpu.make_async_copy(w_qkv_all, w_qkv_out, out_sem.at[0])
    qkv_out_copy.start()
    vectors = jnp.transpose(small_all[...].astype(f32))
    normed_in = (normal * vectors[0:1] + vectors[1:2]).astype(bf16)
    normed_in_ref[...] = normed_in
    for j in range(3):
        part = slice(j * width, (j + 1) * width)
        qkv_ref[:, part] = dot(normed_in, w_qkv_all[:, part]).astype(bf16)
    g_hop(1)
    over_arrive([2])
    lane = lax.broadcasted_iota(jnp.int32, (rows, 2 * head_dim), 1)
    usable = keys_ref[...] > 0
    for pair in range(heads // 2):
        if pair == heads // 4:
            g_hop(2)
        at = pair * 2 * head_dim
        queries = qkv_ref[:, at : at + 2 * head_dim]
        keys = qkv_ref[:, width + at : width + at + 2 * head_dim]
        held = qkv_ref[:, 2 * width + at : 2 * width + at + 2 * head_dim]
        outs = []
        for side in range(2):
            only = (lane < head_dim) if side == 0 else (lane >= head_dim)
            scores = lax.dot_general(
                jnp.where(only, queries, 0).astype(bf16), keys, NT, preferred_element_type=f32
            )
            scores = jnp.where(usable, scores * head_dim ** (-0.5), masked_score)
            shifted = jnp.exp(scores - jnp.max(scores, axis=1, keepdims=True))
            probs = (shifted / jnp.sum(shifted, axis=1, keepdims=True)).astype(bf16)
            outs.append(dot(probs, held))
        attended_ref[:, at : at + 2 * head_dim] = jnp.where(lane < head_dim, outs[0], outs[1]).astype(bf16)
    for h in range(3, planes):
        g_hop(h)
    own_copy.wait()
    for k, r in others:
        spread_copy(k, r).wait_recv()
    y_copy.start()
    gather_done([2])
    proj_out_copy = pltpu.make_async_copy(w_proj_all, w_proj_out, out_sem.at[1])
    proj_out_copy.start()
    middle = values + dot(attended_ref[...], w_proj_all[...]) + vectors[2:3]
    middle_ref[...] = middle
    normal_mid, _ = norm_parts(middle)
    normed = normal_mid * vectors[3:4] + vectors[4:5]
    row = lax.broadcasted_iota(jnp.int32, normed.shape, 0)
    normed_ref[...] = jnp.where(row < real, normed, 0.0).astype(bf16)
    for i in range(planes):
        level = nearest(place, i)
        g_x(level).wait_recv()
        g_c(level, 1).start()
    from_y.wait_recv()
    qkv_out_copy.wait()
    proj_out_copy.wait()
    for level in range(planes):
        g_c(level, 0).wait_recv()
        g_c(level, 1).wait_recv()
    y_copy.wait_send()
    for k, r in others:
        spread_copy(k, r).wait_send()
    for level in range(planes):
        g_x(level).wait_send()
        g_c(level, 0).wait_send()
        g_c(level, 1).wait_send()

        @pl.when((z >= level) & (z < planes - 1))
        def _():
            g_up(level).wait_send()

        @pl.when((z <= level) & (z > 0))
        def _():
            g_down(level).wait_send()

    def shared(j, level, across):
        c_copy(j, level, across).wait_send()
        if j:
            over_copy(j, level, across).wait_send()
            over_c_copy(j, level, across).wait_send()

    for j in range(3):
        for level in range(planes):
            x_copy(j, level, x).wait_send()
            shared(j, level, 1 - x)

            @pl.when(level != z)
            def _():
                shared(j, level, x)

            @pl.when((z >= level) & (z < planes - 1))
            def _():
                up_copy(j, level).wait_send()

            @pl.when((z <= level) & (z > 0))
            def _():
                down_copy(j, level).wait_send()


def front(planes, rows, tokens, mask, ids, cotangent, vectors, router, outer_bias, w_qkv, w_proj, w_in):
    f32, bf16 = jnp.float32, jnp.bfloat16
    real, width = tokens.shape
    lanes = w_in.shape[2] // (2 * planes)
    shape = jax.ShapeDtypeStruct
    vmem = pl.BlockSpec(memory_space=pltpu.VMEM)
    anywhere = pl.BlockSpec(memory_space=pl.ANY)
    dma = pltpu.SemaphoreType.DMA
    return pl.pallas_call(
        functools.partial(front_kernel, planes, HEADS, real),
        out_shape=[
            shape((width, 128), bf16),
            shape((width, 3 * width), bf16),
            shape((width, width), bf16),
            shape((width, 2 * lanes), bf16),
            shape((rows, width), bf16),
            shape((rows, 3 * width), bf16),
            shape((rows, width), bf16),
            shape((rows, width), f32),
            shape((rows, width), bf16),
            shape((rows, width), bf16),
            shape((planes, 4 * rows, width), bf16),
            shape((rows, width), bf16),
            shape((rows, 128), bf16),
            shape((1, rows), f32),
            shape((rows, 1), f32),
        ],
        in_specs=[vmem] * (6 + len(vectors)) + [vmem] * 2 + [anywhere],
        out_specs=[vmem] + [anywhere] * 3 + [vmem] * 6 + [anywhere] + [vmem] * 4,
        scratch_shapes=[pltpu.VMEM((width, 3 * width), bf16), pltpu.VMEM((width, width), bf16), dma((3,))]
        + [dma((3, planes))] * 6
        + [dma((3, 2 * planes))] * 6
        + [dma((2, planes))] * 2
        + [dma((planes,))] * 2
        + [dma((planes, 2))] * 4
        + [dma] * 3,
        compiler_params=pltpu.CompilerParams(
            collective_id=2, has_side_effects=True, vmem_limit_bytes=60 * 2**20
        ),
        cost_estimate=pl.CostEstimate(flops=2**32, bytes_accessed=40 * 2**20, transcendentals=0),
        name="dense_weights_and_attention",
    )(tokens, mask, ids, cotangent, *vectors, router, outer_bias, w_qkv, w_proj, w_in)


def back_kernel(planes, heads, own, groups, real, *refs):
    (
        row_grad_ref,
        normed_ref,
        grad_ref,
        middle_ref,
        tokens_ref,
        normed_in_ref,
        qkv_ref,
        attended_ref,
        small_ref,
        w_qkv_all_ref,
        w_proj_ref,
        keys_ref,
        keep_ref,
        select_ref,
        mix_ref,
        inner_ref,
        outer_ref,
        bias_ref,
        router_grad_ref,
    ) = refs[:19]
    mixed_ref, token_grad_ref, qkv_out, proj_out, small_out, inner_out, outer_out, bias_out = refs[19:27]
    refs = refs[27:]
    (
        w_qkv_ref,
        outer_sum,
        grad_attended,
        grad_qkv,
        mix_z,
        mix_from_x,
        mix_from_z,
        inner_from_y,
        inner_sum,
        outer_from_y,
        bias_from_y,
        held,
        held_small,
        from_core,
        from_core_small,
        from_x,
        from_x_small,
        from_z,
        from_z_small,
        plane_sum,
        plane_sum_small,
        from_y,
        from_y_small,
        final,
        final_small,
    ) = refs[:25]
    (
        load_sem,
        outer_own_sem,
        mix_x_send,
        mix_x_recv,
        mix_z_send,
        mix_z_recv,
        inner_y_sem,
        spread_send,
        spread_recv,
        inner_back_sem,
        inner_core_sem,
        outer_y_sem,
        outer_c_sem,
        bias_y_sem,
        bias_c_sem,
        own_sem,
        flow_c_sem,
        flow_x_sem,
        flow_z_send,
        flow_z_recv,
        flow_y_sem,
        flow_end_sem,
    ) = refs[25:]
    f32, bf16 = jnp.float32, jnp.bfloat16
    place = Place(planes)
    y, c, z, x = place.y, place.c, place.z, place.x
    rows, width = middle_ref.shape
    depth = width // (2 * planes)
    half = depth // 2
    lanes = inner_ref.shape[1] // own
    head_dim = width // heads
    pair_width = 2 * head_dim
    small_at = groups + 1

    def remote(src, dst, send, recv, device):
        return pltpu.make_async_remote_copy(
            src_ref=src, dst_ref=dst, send_sem=send, recv_sem=recv, device_id=device, device_id_type=MESH
        )

    def swap(src, dst, sem, device):
        return remote(src, dst, sem.at[0], sem.at[1], device)

    def of_flow(j, many, alone):
        return alone if j == small_at else many.at[j]

    mine, theirs = pl.ds(pl.multiple_of(c * half, 16), half), pl.ds(pl.multiple_of((1 - c) * half, 16), half)

    def flow_c(j):
        source = of_flow(j, held, held_small)
        return swap(
            source.at[:, :, theirs], of_flow(j, from_core, from_core_small), flow_c_sem.at[j], place.other_core()
        )

    def flow_x(j):
        source = of_flow(j, held, held_small)
        return swap(source.at[:, 1 - x, mine], of_flow(j, from_x, from_x_small), flow_x_sem.at[j], place.other_x())

    def flow_z(j, k):
        level = lax.rem(z + k, planes)
        source = of_flow(j, held, held_small)
        return remote(
            source.at[level, x, mine],
            of_flow(j, from_z, from_z_small).at[k],
            flow_z_send.at[j, k],
            flow_z_recv.at[j, k],
            place.level(k),
        )

    def flow_y(j):
        return swap(
            of_flow(j, plane_sum, plane_sum_small),
            of_flow(j, from_y, from_y_small),
            flow_y_sem.at[j],
            place.other_y(),
        )

    def flow_end(j):
        here = of_flow(j, final, final_small).at[mine]
        return swap(here, here, flow_end_sem.at[j], place.other_core())

    def flow_core_sum(j):
        flow_c(j).wait_recv()
        kept = of_flow(j, held, held_small)
        total = kept[:, :, mine, :].astype(f32) + of_flow(j, from_core, from_core_small)[...].astype(f32)
        kept[:, :, mine, :] = total.astype(bf16)
        flow_x(j).start()

    def flow_x_sum(j):
        flow_x(j).wait_recv()
        kept = of_flow(j, held, held_small)
        total = kept[:, x, mine, :].astype(f32) + of_flow(j, from_x, from_x_small)[...].astype(f32)
        kept[:, x, mine, :] = total.astype(bf16)
        for k in range(1, planes):
            flow_z(j, k).start()

    def flow_z_sum(j):
        kept = of_flow(j, held, held_small)
        total = kept[z, x, mine, :].astype(f32)
        for k in range(1, planes):
            flow_z(j, k).wait_recv()
            total = total + of_flow(j, from_z, from_z_small)[k].astype(f32)
        of_flow(j, plane_sum, plane_sum_small)[...] = total.astype(bf16)
        flow_y(j).start()

    def flow_y_sum(j):
        flow_y(j).wait_recv()
        total = of_flow(j, plane_sum, plane_sum_small)[...].astype(f32)
        total = total + of_flow(j, from_y, from_y_small)[...].astype(f32)
        of_flow(j, final, final_small)[mine, :] = total.astype(bf16)
        flow_end(j).start()

    loads = [
        pltpu.make_async_copy(mix_ref.at[:, pl.ds(0, rows)], mix_z, load_sem.at[0]),
        pltpu.make_async_copy(w_qkv_all_ref, w_qkv_ref, load_sem.at[1]),
    ]

    def mix_to_x(level):
        return remote(
            mix_ref.at[level, pl.ds(rows, rows)],
            mix_from_x.at[level],
            mix_x_send.at[level],
            mix_x_recv.at[level],
            place.other_x(),
        )

    def mix_start(k):
        mix_to_x(lax.rem(z + k, planes)).start()

    def mix_to_z(level, source):
        return remote(
            mix_z.at[level], mix_from_z.at[source], mix_z_send.at[level], mix_z_recv.at[source], place.at(y, c, level, x)
        )

    def mix_x_sum(k):
        level = lax.rem(z + k, planes)
        mix_to_x(level).wait_recv()
        mix_z[level] = (mix_z[level].astype(f32) + mix_from_x[level].astype(f32)).astype(bf16)
        if k < planes:
            mix_to_z(level, z).start()

    my_units = pl.ds(pl.multiple_of(y * lanes, 128), lanes)
    their_units = pl.ds(pl.multiple_of((1 - y) * lanes, 128), lanes)
    my_expert, their_expert = c * 2 + y, c * 2 + 1 - y
    my_columns = pl.ds(pl.multiple_of((z * 2 + x) * lanes, 128), lanes)

    def inner_y():
        return swap(inner_ref.at[:, their_units], inner_from_y, inner_y_sem, place.other_y())

    def shard_rows(f):
        return pl.ds(pl.multiple_of(f * depth, 16), depth)

    def spread(k, r):
        level, across = lax.rem(z + k, planes), (x + r) % 2
        return remote(
            inner_sum.at[shard_rows(level * 2 + across)],
            inner_out.at[my_expert, :, my_columns],
            spread_send.at[k, r],
            spread_recv.at[k, r],
            place.at(y, c, level, across),
        )

    own_copy = pltpu.make_async_copy(
        inner_sum.at[shard_rows(z * 2 + x)], inner_out.at[my_expert, :, my_columns], own_sem
    )

    def inner_back():
        here = inner_out.at[my_expert]
        return swap(here, here, inner_back_sem, place.other_y())

    def inner_core(expert, at):
        here = inner_out.at[expert]
        return swap(here, here, inner_core_sem.at[at], place.other_core())

    def outer_y():
        return swap(outer_ref, outer_from_y, outer_y_sem, place.other_y())

    def outer_c():
        return swap(outer_sum, outer_out.at[c], outer_c_sem, place.other_core())

    outer_own = pltpu.make_async_copy(outer_sum, outer_out.at[c], outer_own_sem)

    def bias_y():
        return swap(bias_ref, bias_from_y, bias_y_sem, place.other_y())

    def bias_c():
        here = bias_out.at[c]
        return swap(here, here, bias_c_sem, place.other_core())

    others = [(k, r) for k in range(planes) for r in range(2) if k or r]

    def inner_y_sum():
        inner_y().wait_recv()
        total = inner_ref[:, my_units].astype(f32) + inner_from_y[...].astype(f32)
        inner_sum[...] = total.astype(bf16)
        own_copy.start()
        for k, r in others:
            spread(k, r).start()
        outer_y().start()

    def inner_spread_done():
        own_copy.wait()
        for k, r in others:
            spread(k, r).wait_recv()
        inner_back().start()
        inner_core(my_expert, 0).start()

    def outer_y_sum():
        outer_y().wait_recv()
        total = outer_ref[...].astype(f32) + outer_from_y[...].astype(f32)
        outer_sum[...] = total.astype(bf16)
        outer_own.start()
        outer_c().start()
        bias_y().wait_recv()
        bias_out[c] = bias_ref[...] + bias_from_y[...]
        bias_c().start()

    partners = [place.other_core(), place.other_y()]
    partners += [place.at(y, c, lax.rem(z + k, planes), (x + r) % 2) for k, r in others]
    greet(partners)
    inner_y().start()
    bias_y().start()
    mix_start(1)
    for load in loads:
        load.start()

    vectors = jnp.transpose(small_ref[...].astype(f32))
    gain_first, gain_second = vectors[0:1], vectors[3:4]
    place_row = lax.broadcasted_iota(jnp.int32, (128, 128), 0)
    place_lane = lax.broadcasted_iota(jnp.int32, (128, 128), 1)

    def lanes_from(first):
        take = (place_row == place_lane + first) & (place_lane < 2 * own)
        return dot(small_ref[...], take.astype(bf16)).astype(bf16)

    outer_bias, router = lanes_from(5), lanes_from(5 + 2 * own)
    normed_mid, grad_out = normed_ref[...], grad_ref[...]
    real_row = lax.broadcasted_iota(jnp.int32, grad_out.shape, 0) < real
    grad_out = jnp.where(real_row, grad_out, 0).astype(bf16)
    select = select_ref[...].astype(f32)
    lane = lax.broadcasted_iota(jnp.int32, select.shape, 1)
    logits = jnp.where(lane < 2 * own, dot(normed_mid, router), -1e30)
    routing = jnp.exp(logits - jnp.max(logits, axis=1, keepdims=True))
    routing = routing / jnp.sum(routing, axis=1, keepdims=True)
    gates = routing * select
    bias_gate = select * dot(grad_out, outer_bias)
    bias_logits = routing * (bias_gate - jnp.sum(routing * bias_gate, axis=1, keepdims=True))
    bias_logits = bias_logits.astype(bf16)
    router_grad = lax.dot_general(normed_mid, bias_logits, TN, preferred_element_type=f32)
    router_grad = pltpu.roll(router_grad, 16, 1) + pltpu.roll(router_grad_ref[...], 16 - real % 16, 1)
    outer_bias_grad = lax.dot_general(gates.astype(bf16), grad_out, TN, preferred_element_type=f32)
    grad_normed_mid = row_grad_ref[...] + lax.dot_general(bias_logits, router, NT, preferred_element_type=f32)
    normal_mid, rstd_mid = norm_parts(middle_ref[...])
    gain_second_grad = jnp.sum(grad_normed_mid * normal_mid, axis=0, keepdims=True)
    bias_second_grad = jnp.sum(grad_normed_mid, axis=0, keepdims=True)
    grad_middle = grad_out.astype(f32) + norm_back(grad_normed_mid, normal_mid, rstd_mid, gain_second)
    grad_proj = grad_middle.astype(bf16)
    proj_bias_grad = jnp.sum(grad_proj.astype(f32), axis=0, keepdims=True)
    loads[0].wait()

    def hold(j, value):
        held[j] = value.astype(bf16).reshape(planes, 2, depth, width)
        flow_c(j).start()

    hold(0, lax.dot_general(attended_ref[...], grad_proj, TN, preferred_element_type=f32))
    grad_attended[...] = lax.dot_general(grad_proj, w_proj_ref[...], NT, preferred_element_type=f32).astype(bf16)
    flow_core_sum(0)

    pair_lane = lax.broadcasted_iota(jnp.int32, (rows, pair_width), 1)
    usable = keys_ref[...] > 0
    scaling = head_dim ** (-0.5)
    group_width = width // groups

    def pair_back(pair):
        at = pair * pair_width
        group, inside = at // group_width, at % group_width
        queries = qkv_ref[:, at : at + pair_width]
        keys = qkv_ref[:, width + at : width + at + pair_width]
        values = qkv_ref[:, 2 * width + at : 2 * width + at + pair_width]
        grads = grad_attended[:, at : at + pair_width]
        found = []
        for side in range(2):
            only = (pair_lane < head_dim) if side == 0 else (pair_lane >= head_dim)
            some_queries = jnp.where(only, queries, 0).astype(bf16)
            some_grads = jnp.where(only, grads, 0).astype(bf16)
            scores = lax.dot_general(some_queries, keys, NT, preferred_element_type=f32)
            scores = jnp.where(usable, scores * scaling, masked_score)
            shifted = jnp.exp(scores - jnp.max(scores, axis=1, keepdims=True))
            probs = shifted / jnp.sum(shifted, axis=1, keepdims=True)
            grad_probs = lax.dot_general(some_grads, values, NT, preferred_element_type=f32)
            grad_scores = probs * (grad_probs - jnp.sum(probs * grad_probs, axis=1, keepdims=True))
            grad_scores = grad_scores.astype(bf16)
            found.append(
                (
                    dot(grad_scores, keys),
                    lax.dot_general(grad_scores, some_queries, TN, preferred_element_type=f32),
                    lax.dot_general(probs.astype(bf16), some_grads, TN, preferred_element_type=f32),
                )
            )
        grad_queries = jnp.where(pair_lane < head_dim, found[0][0], found[1][0]) * scaling
        grad_keys = (found[0][1] + found[1][1]) * scaling
        grad_values = found[0][2] + found[1][2]
        for part, value in enumerate((grad_queries, grad_keys, grad_values)):
            start = part * group_width + inside
            grad_qkv[group, :, start : start + pair_width] = value.astype(bf16)

    def group_back(group):
        per_group = heads // 2 // groups
        for pair in range(group * per_group, (group + 1) * per_group):
            pair_back(pair)
        hold(
            1 + group,
            lax.dot_general(normed_in_ref[...], grad_qkv[group], TN, preferred_element_type=f32),
        )

    group_back(0)
    mix_start(2)
    inner_y_sum()
    flow_core_sum(1)
    mix_x_sum(1)
    for group in range(1, groups):
        group_back(group)
        flow_core_sum(1 + group)
        if group == 1:
            flow_x_sum(0)
            mix_x_sum(2)
    if groups == 1:
        flow_x_sum(0)
        mix_x_sum(2)

    loads[1].wait()
    grad_normed_in = jnp.zeros((rows, width), f32)
    for group in range(groups):
        for part in range(3):
            grad_normed_in = grad_normed_in + lax.dot_general(
                grad_qkv[group, :, part * group_width : (part + 1) * group_width],
                w_qkv_ref[:, part * width + group * group_width : part * width + (group + 1) * group_width],
                NT,
                preferred_element_type=f32,
            )
    normal_first, rstd_first = norm_parts(tokens_ref[...].astype(f32))
    gain_first_grad = jnp.sum(grad_normed_in * normal_first, axis=0, keepdims=True)
    bias_first_grad = jnp.sum(grad_normed_in, axis=0, keepdims=True)
    token_grad = grad_middle + norm_back(grad_normed_in, normal_first, rstd_first, gain_first)
    token_grad_ref[...] = token_grad.astype(bf16)[:real]
    vector_rows = jnp.concatenate(
        [
            gain_first_grad,
            bias_first_grad,
            proj_bias_grad,
            gain_second_grad,
            bias_second_grad,
            jnp.zeros((3, width), f32),
            outer_bias_grad[:8],
            jnp.zeros((112, width), f32),
        ],
        axis=0,
    )
    vector_grads = jnp.transpose(vector_rows) + router_grad
    held_small[...] = vector_grads.astype(bf16).reshape(planes, 2, depth, 128)
    flow_c(small_at).start()
    flow_core_sum(small_at)
    inner_spread_done()
    for group in range(groups - 1):
        flow_x_sum(1 + group)
    mix_start(3)
    flow_x_sum(groups)
    for k in range(4, planes + 1):
        mix_start(k)
    flow_x_sum(small_at)
    outer_y_sum()
    for k in range(3, planes):
        mix_x_sum(k)
    flow_z_sum(0)
    flow_y_sum(0)
    for group in range(groups):
        flow_z_sum(1 + group)
    flow_z_sum(small_at)
    inner_back().wait_recv()
    inner_core(their_expert, 1).start()
    mix_x_sum(planes)
    mixture = mix_z[z].astype(f32) + dot(gates.astype(bf16), jnp.transpose(outer_bias.astype(f32)).astype(bf16))
    for k in range(1, planes):
        source = lax.rem(z + k, planes)
        mix_to_z(z, source).wait_recv()
        mixture = mixture + mix_from_z[source].astype(f32)
    mixed = (keep_ref[...] * (middle_ref[...] + mixture)).astype(bf16)
    mixed_ref[...] = mixed[:real]
    for group in range(groups):
        flow_y_sum(1 + group)
    flow_y_sum(small_at)

    def arrived(j):
        here = of_flow(j, final, final_small).at[theirs]
        swap(here, here, flow_end_sem.at[j], place.other_core()).wait_recv()

    arrived(0)
    proj_out[...] = final[0]
    for group in range(groups):
        arrived(1 + group)
        for part in range(3):
            start = part * width + group * group_width
            qkv_out[:, start : start + group_width] = final[
                1 + group, :, part * group_width : (part + 1) * group_width
            ]
    arrived(small_at)
    small_out[...] = jnp.transpose(
        jnp.concatenate([final_small[...].astype(f32), jnp.zeros((128 - depth, 128), f32)], axis=0)
    )
    outer_own.wait()
    outer_c().wait_recv()
    bias_theirs = bias_out.at[1 - c]
    swap(bias_theirs, bias_theirs, bias_c_sem, place.other_core()).wait_recv()
    for at, expert in enumerate(((1 - c) * 2 + y, (1 - c) * 2 + 1 - y)):
        inner_core(expert, at).wait_recv()

    inner_y().wait_send()
    inner_back().wait_send()
    inner_core(my_expert, 0).wait_send()
    inner_core(their_expert, 1).wait_send()
    outer_y().wait_send()
    outer_c().wait_send()
    bias_y().wait_send()
    bias_c().wait_send()
    for k, r in others:
        spread(k, r).wait_send()
    for k in range(1, planes + 1):
        level = lax.rem(z + k, planes)
        mix_to_x(level).wait_send()
        if k < planes:
            mix_to_z(level, z).wait_send()
    for j in range(groups + 2):
        flow_c(j).wait_send()
        flow_x(j).wait_send()
        for k in range(1, planes):
            flow_z(j, k).wait_send()
        flow_y(j).wait_send()
        flow_end(j).wait_send()


def back(planes, own, real, *args):
    f32, bf16 = jnp.float32, jnp.bfloat16
    (
        row_grad,
        normed_mid,
        grad_out,
        middle,
        tokens,
        normed_in,
        qkv,
        attended,
        small,
        w_qkv,
        w_proj,
        keys,
        keep,
        select,
        mix_parts,
        inner_grad,
        outer_grad,
        bias_grad,
        router_grad,
    ) = args
    rows, width = middle.shape
    depth = width // (2 * planes)
    half = depth // 2
    lanes = inner_grad.shape[1] // own
    tall = outer_grad.shape[0]
    pairs = HEADS // 2
    groups = 3 if pairs % 3 == 0 and (pairs // 3) * 2 * (width // HEADS) % 128 == 0 else 1
    flows = groups + 1
    shape = jax.ShapeDtypeStruct
    vmem = pl.BlockSpec(memory_space=pltpu.VMEM)
    anywhere = pl.BlockSpec(memory_space=pl.ANY)
    dma = pltpu.SemaphoreType.DMA

    def both(*dims):
        return [pltpu.VMEM((flows, *dims, width), bf16), pltpu.VMEM((*dims, 128), bf16)]

    return pl.pallas_call(
        functools.partial(back_kernel, planes, HEADS, own, groups, real),
        out_shape=[
            shape((real, width), bf16),
            shape((real, width), bf16),
            shape((depth, 3 * width), bf16),
            shape((depth, width), bf16),
            shape((128, 128), f32),
            shape((2 * own, depth, 2 * planes * lanes), bf16),
            shape((2, tall, width), bf16),
            shape((2, *bias_grad.shape), f32),
        ],
        in_specs=[vmem] * 9 + [anywhere] + [vmem] * 4 + [anywhere] + [vmem] * 4,
        out_specs=[vmem] * 5 + [anywhere] * 2 + [vmem],
        scratch_shapes=[
            pltpu.VMEM((width, 3 * width), bf16),
            pltpu.VMEM((tall, width), bf16),
            pltpu.VMEM((rows, width), bf16),
            pltpu.VMEM((groups, rows, 3 * width // groups), bf16),
            pltpu.VMEM((planes, rows, width), bf16),
            pltpu.VMEM((planes, rows, width), bf16),
            pltpu.VMEM((planes, rows, width), bf16),
            pltpu.VMEM((width, lanes), bf16),
            pltpu.VMEM((width, lanes), bf16),
            pltpu.VMEM((tall, width), bf16),
            pltpu.VMEM(bias_grad.shape, f32),
        ]
        + both(planes, 2, depth)
        + both(planes, 2, half)
        + both(planes, half)
        + both(planes, half)
        + both(half)
        + both(half)
        + both(depth)
        + [dma((2,)), dma]
        + [dma((planes,))] * 4
        + [dma((2,))]
        + [dma((planes, 2))] * 2
        + [dma((2,)), dma((2, 2)), dma((2,)), dma((2,)), dma((2,)), dma((2,)), dma]
        + [dma((flows + 1, 2))] * 2
        + [dma((flows + 1, planes))] * 2
        + [dma((flows + 1, 2))] * 2,
        compiler_params=pltpu.CompilerParams(
            collective_id=3, has_side_effects=True, vmem_limit_bytes=60 * 2**20
        ),
        cost_estimate=pl.CostEstimate(flops=2**33, bytes_accessed=40 * 2**20, transcendentals=0),
        name="attention_backward_and_sums",
    )(*args)


def finish_kernel(
    depth,
    experts,
    qkv_ref,
    proj_ref,
    rows_ref,
    inner_ref,
    outer_ref,
    mixed_ref,
    token_grad_ref,
    qkv_out,
    proj_out,
    inner_out,
    outer_out,
    mixed_out,
    token_grad_out,
    router_out,
    outer_bias_out,
    *vector_outs,
):
    f32 = jnp.float32

    @pl.when(pl.program_id(0) == 0)
    def _():
        for i, out in enumerate(vector_outs):
            out[...] = rows_ref[i : i + 1, :depth]
        outer_bias_out[...] = rows_ref[8 : 8 + experts, :depth]
        router_out[...] = rows_ref[16 : 16 + experts, :depth]
        qkv_out[...] = qkv_ref[...].astype(f32)
        proj_out[...] = proj_ref[...].astype(f32)
        mixed_out[...] = mixed_ref[...]
        token_grad_out[...] = token_grad_ref[...]

    inner_out[...] = inner_ref[...].astype(f32)
    outer_out[...] = outer_ref[...].astype(f32)


def finish(qkv, proj, vectors, inner, outer, mixed, token_grad):
    f32 = jnp.float32
    experts, depth, _ = inner.shape
    shape = jax.ShapeDtypeStruct

    def whole(array):
        return pl.BlockSpec(array.shape, lambda i, rank=len(array.shape): (0,) * rank)

    def one(array):
        return pl.BlockSpec((1, *array.shape[1:]), lambda i: (i, 0, 0))

    outs = [
        shape(qkv.shape, f32),
        shape(proj.shape, f32),
        shape(inner.shape, f32),
        shape(outer.shape, f32),
        shape(mixed.shape, mixed.dtype),
        shape(token_grad.shape, token_grad.dtype),
        shape((experts, depth), f32),
        shape((experts, depth), f32),
    ] + [shape((1, depth), f32)] * 5
    return pl.pallas_call(
        functools.partial(finish_kernel, depth, experts),
        out_shape=outs,
        grid=(experts,),
        in_specs=[whole(qkv), whole(proj), whole(vectors), one(inner), one(outer), whole(mixed), whole(token_grad)],
        out_specs=[whole(outs[0]), whole(outs[1]), one(outs[2]), one(outs[3])] + [whole(out) for out in outs[4:]],
        compiler_params=pltpu.CompilerParams(vmem_limit_bytes=62 * 2**20),
        name="results_in_float32",
    )(qkv, proj, vectors, inner, outer, mixed, token_grad)


def norm_parts(values):
    center = values - jnp.mean(values, axis=-1, keepdims=True)
    rstd = lax.rsqrt(jnp.mean(center * center, axis=-1, keepdims=True) + epsilon)
    return center * rstd, rstd


def norm_back(grad, normal, rstd, gain):
    scaled = grad * gain
    return rstd * (
        scaled
        - jnp.mean(scaled, axis=-1, keepdims=True)
        - normal * jnp.mean(scaled * normal, axis=-1, keepdims=True)
    )


def move_tokens_plan(
    tokens,
    key_mask,
    expert_ids,
    cotangent,
    norm1_gain,
    norm1_bias,
    w_qkv,
    w_proj,
    proj_bias,
    norm2_gain,
    norm2_bias,
    w_router,
    w_in,
    b_in,
    w_out,
    b_out,
):
    f32 = jnp.float32
    _, rows, width = tokens.shape
    experts, depth, hidden = w_in.shape
    slice_width = w_out.shape[1]
    planes = hidden // slice_width // 2
    own = experts // 2
    padded = (rows + experts + 15) // 16 * 16
    vectors = [v[None] for v in (norm1_gain, norm1_bias, proj_bias, norm2_gain, norm2_bias)]
    fronts = front(
        planes,
        padded,
        tokens[0],
        key_mask,
        expert_ids[0].T,
        cotangent[0],
        vectors,
        w_router.T,
        b_out,
        w_qkv,
        w_proj,
        w_in,
    )
    small, full_qkv, full_proj, inner, normed_in, qkv, attended, middle = fronts[:8]
    normed_mid, grad_out, all_grad_out, wide, select, keys, keep = fronts[8:]
    mix_parts, row_grad, inner_grad, outer_grad, bias_grad, router_grad = experts_of_the_plane(
        planes, own, rows, normed_mid, all_grad_out, inner, w_out, b_in, small
    )
    mixed, token_grad, qkv_grad, proj_grad, vector_grads, inner_grad, outer_grad, bias_grad = back(
        planes,
        own,
        rows,
        row_grad,
        normed_mid,
        grad_out,
        middle,
        wide,
        normed_in,
        qkv,
        attended,
        small,
        full_qkv,
        full_proj,
        keys,
        keep,
        select,
        mix_parts,
        inner_grad,
        outer_grad,
        bias_grad,
        router_grad,
    )
    outer_grad = outer_grad.reshape(experts, slice_width, width)
    finished = finish(qkv_grad, proj_grad, vector_grads, inner_grad, outer_grad, mixed, token_grad)
    qkv_grad, proj_grad, inner_grad, outer_grad, mixed, token_grad, router_grad, outer_bias_grad = finished[:8]
    vector_grads = [row.reshape(depth) for row in finished[8:]]
    return (
        mixed[None],
        token_grad[None],
        vector_grads[0],
        vector_grads[1],
        qkv_grad,
        proj_grad,
        vector_grads[2],
        vector_grads[3],
        vector_grads[4],
        router_grad.T,
        inner_grad,
        bias_grad[:, 0].reshape(experts, slice_width),
        outer_grad,
        outer_bias_grad,
    )


def solution(mesh):
    n_seq, n_fsdp = mesh.shape["seq"], mesh.shape["fsdp"]

    def per_device(*args):
        tokens, w_in, w_out = args[0], args[12], args[14]
        experts, _, hidden = w_in.shape
        lanes = hidden // n_fsdp
        whole_tiles = lanes % 128 == 0 and tokens.shape[2] % 256 == 0 and w_in.shape[1] % 32 == 0 and 2 * lanes <= tokens.shape[2]
        if n_seq == 4 and experts == n_seq and n_fsdp >= 6 and n_fsdp % 2 == 0 and tokens.shape[0] == 1 and whole_tiles:
            return move_tokens_plan(*args)
        return gather_weights_plan(*args)

    return jax.shard_map(
        per_device,
        mesh=mesh,
        in_specs=(
            P(("fsdp", "seq"), None, None),
            P("fsdp", None),
            P(("fsdp", "seq"), None, None),
            P(("fsdp", "seq"), None, None),
            P("fsdp"),
            P("fsdp"),
            P("fsdp", None),
            P("fsdp", None),
            P("fsdp"),
            P("fsdp"),
            P("fsdp"),
            P("fsdp", None),
            P(None, "fsdp", None),
            P(None, "fsdp"),
            P(None, "fsdp", None),
            P(None, "fsdp"),
        ),
        out_specs=(
            P(("fsdp", "seq"), None, None),
            P(("fsdp", "seq"), None, None),
            P("fsdp"),
            P("fsdp"),
            P("fsdp", None),
            P("fsdp", None),
            P("fsdp"),
            P("fsdp"),
            P("fsdp"),
            P("fsdp", None),
            P(None, "fsdp", None),
            P(None, "fsdp"),
            P(None, "fsdp", None),
            P(None, "fsdp"),
        ),
        check_vma=False,
    )
```

```python
import functools

import jax
import jax.numpy as jnp
from jax import lax
from jax.experimental import pallas as pl
from jax.experimental.pallas import tpu as pltpu
from jax.sharding import PartitionSpec as P

HEADS = 12
CAP = 142


epsilon = 1e-06
masked_score = -1e30


def norm_rows(values, gain, offset):
    center = values - jnp.mean(values, axis=-1, keepdims=True)
    spread = jnp.mean(center * center, axis=-1, keepdims=True)
    return center * lax.rsqrt(spread + epsilon) * gain + offset


def softmax_rows(values):
    shifted = jnp.exp(values - jnp.max(values, axis=-1, keepdims=True))
    return shifted / jnp.sum(shifted, axis=-1, keepdims=True)


def exact_gelu(values):
    return jax.nn.gelu(values, approximate=False)


def expert_slots(chosen, experts):
    flat_ids = chosen.reshape(-1)
    onehot = (flat_ids[:, None] == jnp.arange(experts, dtype=jnp.int32)[None, :]).astype(jnp.int32)
    ranks = jnp.cumsum(onehot, axis=0, dtype=jnp.int32)
    slot_pos = jnp.sum(onehot * ranks, axis=1, dtype=jnp.int32) - 1
    return (flat_ids, slot_pos)


def gather_weights_plan(
    tokens,
    key_mask,
    expert_ids,
    cotangent,
    norm1_gain,
    norm1_bias,
    w_qkv,
    w_proj,
    proj_bias,
    norm2_gain,
    norm2_bias,
    w_router,
    w_in,
    b_in,
    w_out,
    b_out,
):
    images, seq_len, width = tokens.shape
    experts = w_in.shape[0]
    head_dim = width // HEADS
    scaling = head_dim ** (-0.5)
    row_count = images * seq_len
    dense_set = (
        lax.all_gather(norm1_gain, "fsdp", axis=0, tiled=True),
        lax.all_gather(norm1_bias, "fsdp", axis=0, tiled=True),
        lax.all_gather(w_qkv, "fsdp", axis=0, tiled=True),
        lax.all_gather(w_proj, "fsdp", axis=0, tiled=True),
        lax.all_gather(proj_bias, "fsdp", axis=0, tiled=True),
        lax.all_gather(norm2_gain, "fsdp", axis=0, tiled=True),
        lax.all_gather(norm2_bias, "fsdp", axis=0, tiled=True),
        lax.all_gather(w_router, "fsdp", axis=0, tiled=True),
    )
    gain_first = dense_set[0].astype(jnp.float32)
    bias_first = dense_set[1].astype(jnp.float32)
    full_qkv = dense_set[2]
    full_proj = dense_set[3]
    bias_proj = dense_set[4].astype(jnp.float32)
    gain_second = dense_set[5].astype(jnp.float32)
    bias_second = dense_set[6].astype(jnp.float32)
    full_router = dense_set[7]
    expert_set = (
        lax.all_gather(w_in, "fsdp", axis=1, tiled=True),
        lax.all_gather(b_in, "fsdp", axis=1, tiled=True),
        lax.all_gather(w_out, "fsdp", axis=1, tiled=True),
        lax.all_gather(b_out, "fsdp", axis=1, tiled=True),
    )
    inner_weight = expert_set[0]
    inner_bias = expert_set[1].astype(jnp.float32)
    outer_weight = expert_set[2]
    outer_bias = expert_set[3].astype(jnp.float32)
    own_mask = lax.dynamic_slice_in_dim(key_mask, lax.axis_index("seq") * images, images, 0)
    keep_rows = own_mask.reshape(row_count, 1).astype(jnp.float32)
    usable = (key_mask > 0)[:, None, None, :]
    flat_tokens = tokens.astype(jnp.float32).reshape(row_count, width)
    normed_in = norm_rows(flat_tokens, gain_first, bias_first).astype(jnp.bfloat16)
    mixed_qkv = jnp.dot(normed_in, full_qkv, preferred_element_type=jnp.float32).astype(
        jnp.bfloat16
    )
    mixed_qkv = mixed_qkv.reshape(images, seq_len, 3, HEADS, head_dim)
    head_qkv = lax.all_to_all(mixed_qkv, "seq", split_axis=3, concat_axis=0, tiled=True)
    queries = head_qkv[:, :, 0]
    key_rows = head_qkv[:, :, 1]
    value_rows = head_qkv[:, :, 2]

    def score_block():
        raw = (
            jnp.einsum("gahd,gbhd->ghab", queries, key_rows, preferred_element_type=jnp.float32)
            * scaling
        )
        return jnp.where(usable, raw, masked_score)

    scores = score_block()
    row_top = jnp.max(scores, axis=-1, keepdims=True)
    shifted = jnp.exp(scores - row_top)
    row_total = jnp.sum(shifted, axis=-1, keepdims=True)
    attn_probs = (shifted / row_total).astype(jnp.bfloat16)
    log_total = row_top + jnp.log(row_total)
    head_out = jnp.einsum(
        "ghab,gbhd->gahd", attn_probs, value_rows, preferred_element_type=jnp.float32
    ).astype(jnp.bfloat16)
    attended = lax.all_to_all(head_out, "seq", split_axis=0, concat_axis=2, tiled=True).reshape(
        row_count, width
    )
    middle = (
        flat_tokens + jnp.dot(attended, full_proj, preferred_element_type=jnp.float32) + bias_proj
    )
    normed_mid = norm_rows(middle, gain_second, bias_second).astype(jnp.bfloat16)
    routing = softmax_rows(jnp.dot(normed_mid, full_router, preferred_element_type=jnp.float32))
    chosen = expert_ids.reshape(row_count, 2)
    flat_ids, slot_pos = expert_slots(chosen, experts)
    gating = jnp.take_along_axis(routing, chosen, axis=1)
    buffer = (
        jnp.zeros((experts, CAP, width), jnp.bfloat16)
        .at[flat_ids, slot_pos]
        .set(jnp.repeat(normed_mid, 2, axis=0))
    )
    pre_act = (
        jnp.einsum("ecd,edf->ecf", buffer, inner_weight, preferred_element_type=jnp.float32)
        + inner_bias[:, None, :]
    )
    activated = exact_gelu(pre_act).astype(jnp.bfloat16)
    expert_out = (
        jnp.einsum("ecf,efd->ecd", activated, outer_weight, preferred_element_type=jnp.float32)
        + outer_bias[:, None, :]
    )
    picked = expert_out[flat_ids, slot_pos].reshape(row_count, 2, width)
    mixture = jnp.sum(gating[:, :, None] * picked, axis=1)
    mixed = (keep_rows * (middle + mixture)).astype(jnp.bfloat16).reshape(images, seq_len, width)
    grad_out = cotangent.astype(jnp.float32).reshape(row_count, width) * keep_rows
    grad_gate = jnp.sum(grad_out[:, None, :] * picked, axis=2)
    grad_picked = (
        (gating[:, :, None] * grad_out[:, None, :])
        .astype(jnp.bfloat16)
        .reshape(2 * row_count, width)
    )
    grad_expert_out = (
        jnp.zeros((experts, CAP, width), jnp.bfloat16).at[flat_ids, slot_pos].set(grad_picked)
    )
    grad_outer_bias = jnp.sum(grad_expert_out, axis=1, dtype=jnp.float32)
    hidden_pre = (
        jnp.einsum("ecd,edf->ecf", buffer, inner_weight, preferred_element_type=jnp.float32)
        + inner_bias[:, None, :]
    )
    hidden_act = exact_gelu(hidden_pre).astype(jnp.bfloat16)
    grad_outer_weight = jnp.einsum(
        "ecf,ecd->efd", hidden_act, grad_expert_out, preferred_element_type=jnp.float32
    )
    grad_act = jnp.einsum(
        "ecd,efd->ecf", grad_expert_out, outer_weight, preferred_element_type=jnp.float32
    )
    gelu_pull = jax.vjp(exact_gelu, hidden_pre)[1]
    grad_pre = gelu_pull(grad_act)[0].astype(jnp.bfloat16)
    grad_inner_bias = jnp.sum(grad_pre, axis=1, dtype=jnp.float32)
    grad_inner_weight = jnp.einsum(
        "ecd,ecf->edf", buffer, grad_pre, preferred_element_type=jnp.float32
    )
    grad_buffer = jnp.einsum(
        "ecf,edf->ecd", grad_pre, inner_weight, preferred_element_type=jnp.float32
    )
    grad_rows = jnp.sum(grad_buffer[flat_ids, slot_pos].reshape(row_count, 2, width), axis=1)
    expert_range = jnp.arange(experts, dtype=jnp.int32)[None, None, :]
    grad_route = jnp.sum(
        grad_gate[:, :, None] * (chosen[:, :, None] == expert_range).astype(jnp.float32), axis=1
    )
    grad_logits = (
        routing * (grad_route - jnp.sum(routing * grad_route, axis=-1, keepdims=True))
    ).astype(jnp.bfloat16)
    grad_router = jnp.einsum(
        "nd,ne->de", normed_mid, grad_logits, preferred_element_type=jnp.float32
    )
    grad_normed_mid = grad_rows + jnp.einsum(
        "ne,de->nd", grad_logits, full_router, preferred_element_type=jnp.float32
    )
    second_pull = jax.vjp(norm_rows, middle, gain_second, bias_second)[1]
    grad_mid_norm, grad_gain_second, grad_bias_second = second_pull(grad_normed_mid)
    grad_middle = grad_out + grad_mid_norm
    grad_proj = grad_middle.astype(jnp.bfloat16)
    grad_bias_proj = jnp.sum(grad_proj, axis=0, dtype=jnp.float32)
    grad_proj_weight = jnp.einsum(
        "nd,ne->de", attended, grad_proj, preferred_element_type=jnp.float32
    )
    grad_attended = jnp.einsum(
        "ne,de->nd", grad_proj, full_proj, preferred_element_type=jnp.float32
    ).astype(jnp.bfloat16)
    grad_head_out = lax.all_to_all(
        grad_attended.reshape(images, seq_len, HEADS, head_dim),
        "seq",
        split_axis=2,
        concat_axis=0,
        tiled=True,
    )
    recomputed = jnp.exp(score_block() - log_total)
    grad_values = jnp.einsum(
        "ghab,gahd->gbhd",
        recomputed.astype(jnp.bfloat16),
        grad_head_out,
        preferred_element_type=jnp.float32,
    )
    grad_probs = jnp.einsum(
        "gahd,gbhd->ghab", grad_head_out, value_rows, preferred_element_type=jnp.float32
    )
    grad_scores = (
        recomputed * (grad_probs - jnp.sum(recomputed * grad_probs, axis=-1, keepdims=True))
    ).astype(jnp.bfloat16)
    grad_queries = (
        jnp.einsum("ghab,gbhd->gahd", grad_scores, key_rows, preferred_element_type=jnp.float32)
        * scaling
    )
    grad_keys = (
        jnp.einsum("ghab,gahd->gbhd", grad_scores, queries, preferred_element_type=jnp.float32)
        * scaling
    )
    grad_head_qkv = jnp.stack([grad_queries, grad_keys, grad_values], axis=2).astype(jnp.bfloat16)
    grad_qkv = lax.all_to_all(
        grad_head_qkv, "seq", split_axis=0, concat_axis=3, tiled=True
    ).reshape(row_count, 3 * width)
    grad_qkv_weight = jnp.einsum(
        "nd,ne->de", normed_in, grad_qkv, preferred_element_type=jnp.float32
    )
    grad_normed_in = jnp.einsum("ne,de->nd", grad_qkv, full_qkv, preferred_element_type=jnp.float32)
    first_pull = jax.vjp(norm_rows, flat_tokens, gain_first, bias_first)[1]
    grad_first, grad_gain_first, grad_bias_first = first_pull(grad_normed_in)
    token_grad = (grad_middle + grad_first).astype(jnp.bfloat16).reshape(images, seq_len, width)
    shares = (
        lax.psum_scatter(grad_gain_first, "fsdp", scatter_dimension=0, tiled=True),
        lax.psum_scatter(grad_bias_first, "fsdp", scatter_dimension=0, tiled=True),
        lax.psum_scatter(grad_qkv_weight, "fsdp", scatter_dimension=0, tiled=True),
        lax.psum_scatter(grad_proj_weight, "fsdp", scatter_dimension=0, tiled=True),
        lax.psum_scatter(grad_bias_proj, "fsdp", scatter_dimension=0, tiled=True),
        lax.psum_scatter(grad_gain_second, "fsdp", scatter_dimension=0, tiled=True),
        lax.psum_scatter(grad_bias_second, "fsdp", scatter_dimension=0, tiled=True),
        lax.psum_scatter(grad_router, "fsdp", scatter_dimension=0, tiled=True),
        lax.psum_scatter(grad_inner_weight, "fsdp", scatter_dimension=1, tiled=True),
        lax.psum_scatter(grad_inner_bias, "fsdp", scatter_dimension=1, tiled=True),
        lax.psum_scatter(grad_outer_weight, "fsdp", scatter_dimension=1, tiled=True),
        lax.psum_scatter(grad_outer_bias, "fsdp", scatter_dimension=1, tiled=True),
    )
    parted = (
        lax.psum_scatter(
            shares[0].astype(jnp.bfloat16), "seq", scatter_dimension=0, tiled=True
        ).astype(jnp.float32),
        lax.psum_scatter(
            shares[1].astype(jnp.bfloat16), "seq", scatter_dimension=0, tiled=True
        ).astype(jnp.float32),
        lax.psum_scatter(
            shares[2].astype(jnp.bfloat16), "seq", scatter_dimension=0, tiled=True
        ).astype(jnp.float32),
        lax.psum_scatter(
            shares[3].astype(jnp.bfloat16), "seq", scatter_dimension=0, tiled=True
        ).astype(jnp.float32),
        lax.psum_scatter(
            shares[4].astype(jnp.bfloat16), "seq", scatter_dimension=0, tiled=True
        ).astype(jnp.float32),
        lax.psum_scatter(
            shares[5].astype(jnp.bfloat16), "seq", scatter_dimension=0, tiled=True
        ).astype(jnp.float32),
        lax.psum_scatter(
            shares[6].astype(jnp.bfloat16), "seq", scatter_dimension=0, tiled=True
        ).astype(jnp.float32),
        lax.psum_scatter(
            shares[7].astype(jnp.bfloat16), "seq", scatter_dimension=0, tiled=True
        ).astype(jnp.float32),
        lax.psum_scatter(
            shares[8].astype(jnp.bfloat16), "seq", scatter_dimension=1, tiled=True
        ).astype(jnp.float32),
        lax.psum_scatter(
            shares[9].astype(jnp.bfloat16), "seq", scatter_dimension=1, tiled=True
        ).astype(jnp.float32),
        lax.psum_scatter(
            shares[10].astype(jnp.bfloat16), "seq", scatter_dimension=1, tiled=True
        ).astype(jnp.float32),
        lax.psum_scatter(
            shares[11].astype(jnp.bfloat16), "seq", scatter_dimension=1, tiled=True
        ).astype(jnp.float32),
    )
    totals = (
        lax.all_gather(parted[0].astype(jnp.bfloat16), "seq", axis=0, tiled=True).astype(
            jnp.float32
        ),
        lax.all_gather(parted[1].astype(jnp.bfloat16), "seq", axis=0, tiled=True).astype(
            jnp.float32
        ),
        lax.all_gather(parted[2].astype(jnp.bfloat16), "seq", axis=0, tiled=True).astype(
            jnp.float32
        ),
        lax.all_gather(parted[3].astype(jnp.bfloat16), "seq", axis=0, tiled=True).astype(
            jnp.float32
        ),
        lax.all_gather(parted[4].astype(jnp.bfloat16), "seq", axis=0, tiled=True).astype(
            jnp.float32
        ),
        lax.all_gather(parted[5].astype(jnp.bfloat16), "seq", axis=0, tiled=True).astype(
            jnp.float32
        ),
        lax.all_gather(parted[6].astype(jnp.bfloat16), "seq", axis=0, tiled=True).astype(
            jnp.float32
        ),
        lax.all_gather(parted[7].astype(jnp.bfloat16), "seq", axis=0, tiled=True).astype(
            jnp.float32
        ),
        lax.all_gather(parted[8].astype(jnp.bfloat16), "seq", axis=1, tiled=True).astype(
            jnp.float32
        ),
        lax.all_gather(parted[9].astype(jnp.bfloat16), "seq", axis=1, tiled=True).astype(
            jnp.float32
        ),
        lax.all_gather(parted[10].astype(jnp.bfloat16), "seq", axis=1, tiled=True).astype(
            jnp.float32
        ),
        lax.all_gather(parted[11].astype(jnp.bfloat16), "seq", axis=1, tiled=True).astype(
            jnp.float32
        ),
    )
    return (
        mixed,
        token_grad,
        totals[0],
        totals[1],
        totals[2],
        totals[3],
        totals[4],
        totals[5],
        totals[6],
        totals[7],
        totals[8],
        totals[9],
        totals[10],
        totals[11],
    )


MESH = pl.DeviceIdType.MESH
NT = (((1,), (1,)), ((), ()))
TN = (((0,), (0,)), ((), ()))


def dot(a, b):
    return jnp.dot(a, b, preferred_element_type=jnp.float32)


class Place:
    def __init__(self, planes):
        self.planes = planes
        s, f = lax.axis_index("seq"), lax.axis_index("fsdp")
        self.y, self.c, self.z, self.x = s // 2, s % 2, f // 2, f % 2

    def at(self, y, c, z, x):
        return (y * 2 + c, z * 2 + x)

    def other_core(self):
        return self.at(self.y, 1 - self.c, self.z, self.x)

    def other_x(self):
        return self.at(self.y, self.c, self.z, 1 - self.x)

    def other_y(self):
        return self.at(1 - self.y, self.c, self.z, self.x)

    def level(self, k):
        return self.at(self.y, self.c, lax.rem(self.z + k + self.planes, self.planes), self.x)


def greet(partners):
    barrier = pltpu.get_barrier_semaphore()
    for partner in partners:
        pl.semaphore_signal(barrier, inc=1, device_id=partner, device_id_type=MESH)
    pl.semaphore_wait(barrier, len(partners))


def nearest(place, i):
    level = 0
    for z in range(place.planes):
        order = sorted(range(place.planes), key=lambda other: (abs(other - z), other))
        for at in range(place.planes):
            level = level + jnp.where((place.z == z) & (i == at), order[at], 0)
    return level


def expert_kernel(
    planes,
    own,
    rows,
    real,
    normed_ref,
    grads_all_ref,
    inner_ref,
    outer_all_ref,
    bias_all_ref,
    small_ref,
    mix_out_ref,
    out_ref,
    inner_grad_ref,
    outer_grad_ref,
    bias_grad_ref,
    router_grad_ref,
    grads_ref,
    mix_ref,
    mix_from_core,
    outer_ref,
    inner_t_ref,
    outer_t_ref,
    router_ref,
    router_t_ref,
    tokens,
    part,
    from_core,
    from_x,
    from_z,
    hidden,
    hidden_grad,
    logit_grad,
    inner_acc,
    outer_acc,
    outer_sem,
    grads_sem,
    mix_sem,
    mix_c_send,
    mix_c_recv,
    z_send,
    z_recv,
    x_send,
    x_recv,
    c_send,
    c_recv,
    sum_c_send,
    sum_c_recv,
    sum_x_send,
    sum_x_recv,
    sum_z_send,
    sum_z_recv,
):
    f32, bf16 = jnp.float32, jnp.bfloat16
    place = Place(planes)
    y, c, z, x = place.y, place.c, place.z, place.x
    width = inner_ref.shape[0]
    lanes = inner_ref.shape[1] // own
    first = real % 16

    def remote(src, dst, send, recv, device):
        return pltpu.make_async_remote_copy(
            src_ref=src, dst_ref=dst, send_sem=send, recv_sem=recv, device_id=device, device_id_type=MESH
        )

    def slot(buffer, level, at, count=1):
        return buffer.at[level, pl.ds(at * rows, count * rows)]

    def up_copy(level):
        here = slot(tokens, level, 0)
        return remote(here, here, z_send.at[0, level], z_recv.at[0, level], place.at(y, c, z + 1, x))

    def down_copy(level):
        here = slot(tokens, level, 0)
        return remote(here, here, z_send.at[1, level], z_recv.at[1, level], place.at(y, c, z - 1, x))

    def x_copy(level):
        return remote(
            slot(tokens, level, 0), slot(tokens, level, 2), x_send.at[level], x_recv.at[level], place.other_x()
        )

    def c_copy(level, r):
        return remote(
            slot(tokens, level, 2 * r),
            slot(tokens, level, 2 * r + 1),
            c_send.at[level, r],
            c_recv.at[level, r],
            place.other_core(),
        )

    def sum_c_copy(level, r):
        return remote(
            slot(part, level, 2 * r + 1),
            slot(from_core, level, r),
            sum_c_send.at[level, r],
            sum_c_recv.at[level, r],
            place.other_core(),
        )

    def sum_x_copy(level):
        return remote(
            slot(part, level, 2), from_x.at[level], sum_x_send.at[level], sum_x_recv.at[level], place.other_x()
        )

    def sum_z_copy(level, source):
        return remote(
            slot(part, level, 0),
            from_z.at[source],
            sum_z_send.at[level],
            sum_z_recv.at[source],
            place.at(y, c, level, x),
        )

    partners = [place.other_core(), place.other_x()] + [place.level(k) for k in range(1, planes)]
    greet(partners)
    tokens[z, 0:rows, :] = normed_ref[...]

    @pl.when(z < planes - 1)
    def _():
        up_copy(z).start()

    @pl.when(z > 0)
    def _():
        down_copy(z).start()

    c_copy(z, 0).start()
    x_copy(z).start()
    def grads_load(level):
        return pltpu.make_async_copy(grads_all_ref.at[level], grads_ref.at[level], grads_sem.at[level])

    def mix_c(level, r):
        return remote(
            slot(mix_ref, level, 2 * r + 1),
            slot(mix_from_core, level, r),
            mix_c_send.at[level, r],
            mix_c_recv.at[level, r],
            place.other_core(),
        )

    def mix_store(level, r):
        return pltpu.make_async_copy(
            slot(mix_ref, level, 2 * r), slot(mix_out_ref, level, r), mix_sem.at[level, r]
        )

    def mix_sum(level):
        for r in range(2):
            mix_c(level, r).wait_recv()
            here = slice(2 * r * rows, (2 * r + 1) * rows)
            total = mix_ref[level, here, :].astype(f32)
            total = total + mix_from_core[level, r * rows : (r + 1) * rows, :].astype(f32)
            mix_ref[level, here, :] = total.astype(bf16)
            mix_store(level, r).start()

    for i in range(planes):
        grads_load(nearest(place, (i + 1) % planes)).start()
    loads = [
        pltpu.make_async_copy(
            outer_all_ref.at[c * own + i], outer_ref.at[pl.ds(i * lanes, lanes)], outer_sem.at[i]
        )
        for i in range(own)
    ]
    for load in loads:
        load.start()
    inner_t_ref[...] = jnp.transpose(inner_ref[...])
    place_row = lax.broadcasted_iota(jnp.int32, (128, 128), 0)
    place_lane = lax.broadcasted_iota(jnp.int32, (128, 128), 1)
    take = (place_row - (5 + 2 * own) == place_lane - first) & (place_lane >= first)
    take = take & (place_lane < first + 2 * own)
    router = dot(small_ref[...], take.astype(bf16))
    router_ref[...] = router.astype(bf16)
    router_t_ref[...] = jnp.transpose(router).astype(bf16)
    inner_acc[...] = jnp.zeros_like(inner_acc)
    outer_acc[...] = jnp.zeros_like(outer_acc)
    bias_grad_ref[...] = jnp.zeros_like(bias_grad_ref)
    router_grad_ref[...] = jnp.zeros_like(router_grad_ref)
    for load in loads:
        load.wait()
    outer_t_ref[...] = jnp.transpose(outer_ref[...])

    def hop(h):
        @pl.when(z >= h)
        def _():
            up_copy(z - h).wait_recv()

            @pl.when(z < planes - 1)
            def _():
                up_copy(z - h).start()

            x_copy(z - h).start()
            c_copy(z - h, 0).start()

        @pl.when(z + h < planes)
        def _():
            down_copy(z + h).wait_recv()

            @pl.when(z > 0)
            def _():
                down_copy(z + h).start()

            x_copy(z + h).start()
            c_copy(z + h, 0).start()

    def tiles(level, r):
        here = pl.ds(pl.multiple_of(2 * r * rows, 16), 2 * rows)
        normed, grad_out = tokens[level, here, :], grads_ref[level, here, :]
        select = []
        for t in range(2):
            last = pl.ds(pl.multiple_of((2 * r + t) * rows + real - first, 16), 16)
            chosen = grads_ref[level, last, :256].astype(f32)
            chosen = jnp.concatenate([chosen, jnp.zeros((112, 256), f32)], axis=0)
            select.append(jnp.transpose(chosen)[:rows])
        select = jnp.concatenate(select, axis=0)
        lane = lax.broadcasted_iota(jnp.int32, select.shape, 1)
        named = (lane >= first) & (lane < first + 2 * own)
        select = jnp.where(named, select, 0.0)
        logits = jnp.where(named, dot(normed, router_ref[...]), -1e30)
        routing = jnp.exp(logits - jnp.max(logits, axis=1, keepdims=True))
        routing = routing / jnp.sum(routing, axis=1, keepdims=True)
        gates = routing * select
        gate_grads = jnp.zeros_like(gates)
        all_pre = dot(normed, inner_ref[...])
        all_grad_act = dot(grad_out, outer_t_ref[...])
        for i in range(own):
            mine = lane == first + c * own + i
            units = slice(i * lanes, (i + 1) * lanes)
            gate = jnp.sum(jnp.where(mine, gates, 0.0), axis=1, keepdims=True)
            bias = jnp.where(c == 0, bias_all_ref[i : i + 1, :], bias_all_ref[own + i : own + i + 1, :])
            pre = all_pre[:, units] + bias.astype(f32)
            grad_act = all_grad_act[:, units]
            cdf = 0.5 * (1.0 + lax.erf(pre * (0.5**0.5)))
            act = pre * cdf
            hidden[here, units] = (gate * act).astype(bf16)
            gate_grad = jnp.sum(act * grad_act, axis=1, keepdims=True)
            gate_grads = gate_grads + jnp.where(mine, gate_grad * select, 0.0)
            slope = cdf + pre * jnp.exp(-0.5 * pre * pre) * 0.3989422804014327
            grad_pre = gate * grad_act * slope
            bias_grad_ref[0:1, units] += jnp.sum(grad_pre, axis=0, keepdims=True)
            hidden_grad[here, units] = grad_pre.astype(bf16)
        grad_logits = routing * (gate_grads - jnp.sum(routing * gate_grads, axis=1, keepdims=True))
        logit_grad[here, :] = grad_logits.astype(bf16)
        mix_ref[level, here, :] = dot(hidden[here, :], outer_ref[...]).astype(bf16)
        row_grad = dot(hidden_grad[here, :], inner_t_ref[...])
        row_grad = row_grad + dot(logit_grad[here, :], router_t_ref[...])
        part[level, here, :] = row_grad.astype(bf16)

    def across_sum(level):
        sum_c_copy(level, 1).wait_recv()
        here = slice(2 * rows, 3 * rows)
        total = part[level, here, :].astype(f32) + from_core[level, rows : 2 * rows, :].astype(f32)
        part[level, here, :] = total.astype(bf16)
        sum_x_copy(level).start()

    def level_sum(level):
        sum_c_copy(level, 0).wait_recv()
        sum_x_copy(level).wait_recv()
        total = part[level, 0:rows, :].astype(f32) + from_core[level, 0:rows, :].astype(f32)
        total = total + from_x[level].astype(f32)
        part[level, 0:rows, :] = total.astype(bf16)

    def weight_grads(level):
        for j in range(width // 256):
            some = slice(j * 256, (j + 1) * 256)
            outer_acc[some, :] += lax.dot_general(
                hidden[:, some], grads_ref[level], TN, preferred_element_type=f32
            )
            inner_acc[some, :] += lax.dot_general(
                tokens[level, :, some], hidden_grad[...], TN, preferred_element_type=f32
            )
        router_grad_ref[...] += lax.dot_general(tokens[level], logit_grad[...], TN, preferred_element_type=f32)

    def order(i):
        return nearest(place, jnp.where(i == 0, 1, jnp.where(i == planes - 1, 0, planes - i)))

    def step(i, carry):
        level, before = order(i), order(i - 1)

        def half(s, carry):
            r = jnp.where(i < planes - 2, s, 1 - s)

            @pl.when((i == 0) & (s == 0))
            def _():
                hop(1)

            if planes > 2:
                @pl.when((i == 0) & (s == 1))
                def _():
                    hop(2)

            @pl.when((i == 1) & (s == 0))
            def _():
                for h in range(3, planes):
                    hop(h)

            @pl.when((i > 0) & (s == 1))
            def _():
                level_sum(before)
                sum_z_copy(before, z).start()

            @pl.when(s == 0)
            def _():
                grads_load(level).wait()

            @pl.when(r == 0)
            def _():
                c_copy(level, 0).wait_recv()

            @pl.when(r == 1)
            def _():
                x_copy(level).wait_recv()
                c_copy(level, 1).start()
                c_copy(level, 1).wait_recv()

            tiles(level, r)
            sum_c_copy(level, r).start()
            mix_c(level, r).start()

            @pl.when(r == 1)
            def _():
                across_sum(level)

            return carry

        lax.fori_loop(0, 2, half, 0)
        weight_grads(level)
        mix_sum(level)
        return carry

    lax.fori_loop(0, planes, step, 0)
    level_sum(z)
    inner_grad_ref[...] = inner_acc[...].astype(bf16)
    outer_grad_ref[...] = outer_acc[...].astype(bf16)
    total = part[z, 0:rows, :].astype(f32)
    for k in range(1, planes):
        source = lax.rem(z + k, planes)
        sum_z_copy(z, source).wait_recv()
        total = total + from_z[source].astype(f32)
    out_ref[...] = total
    for level in range(planes):
        mix_store(level, 0).wait()
        mix_store(level, 1).wait()
        mix_c(level, 0).wait_send()
        mix_c(level, 1).wait_send()
        x_copy(level).wait_send()
        c_copy(level, 0).wait_send()
        c_copy(level, 1).wait_send()
        sum_c_copy(level, 0).wait_send()
        sum_c_copy(level, 1).wait_send()
        sum_x_copy(level).wait_send()

        @pl.when(level != z)
        def _():
            sum_z_copy(level, z).wait_send()

        @pl.when((z >= level) & (z < planes - 1))
        def _():
            up_copy(level).wait_send()

        @pl.when((z <= level) & (z > 0))
        def _():
            down_copy(level).wait_send()


def experts_of_the_plane(planes, own, real, normed, grads, inner, outer, bias, small):
    f32, bf16 = jnp.float32, jnp.bfloat16
    rows = normed.shape[0]
    chunk = 4 * rows
    width, units = inner.shape
    shape = jax.ShapeDtypeStruct
    vmem = pl.BlockSpec(memory_space=pltpu.VMEM)
    anywhere = pl.BlockSpec(memory_space=pl.ANY)
    dma = pltpu.SemaphoreType.DMA
    flops = 12 * planes * chunk * width * units
    return pl.pallas_call(
        functools.partial(expert_kernel, planes, own, rows, real),
        out_shape=[
            shape((planes, 2 * rows, width), bf16),
            shape((rows, width), f32),
            shape((width, units), bf16),
            shape((units, width), bf16),
            shape((8, units), f32),
            shape((width, 128), f32),
        ],
        in_specs=[vmem, anywhere, vmem, anywhere, vmem, vmem],
        out_specs=[anywhere] + [vmem] * 5,
        scratch_shapes=[
            pltpu.VMEM((planes, chunk, width), bf16),
            pltpu.VMEM((planes, chunk, width), bf16),
            pltpu.VMEM((planes, 2 * rows, width), bf16),
            pltpu.VMEM((units, width), bf16),
            pltpu.VMEM((units, width), bf16),
            pltpu.VMEM((width, units), bf16),
            pltpu.VMEM((width, 128), bf16),
            pltpu.VMEM((128, width), bf16),
            pltpu.VMEM((planes, chunk, width), bf16),
            pltpu.VMEM((planes, chunk, width), bf16),
            pltpu.VMEM((planes, 2 * rows, width), bf16),
            pltpu.VMEM((planes, rows, width), bf16),
            pltpu.VMEM((planes, rows, width), bf16),
            pltpu.VMEM((chunk, units), bf16),
            pltpu.VMEM((chunk, units), bf16),
            pltpu.VMEM((chunk, 128), bf16),
            pltpu.VMEM((width, units), f32),
            pltpu.VMEM((units, width), f32),
            dma((own,)),
            dma((planes,)),
            dma((planes, 2)),
            dma((planes, 2)),
            dma((planes, 2)),
        ]
        + [dma((2, planes))] * 2
        + [dma((planes,))] * 2
        + [dma((planes, 2))] * 4
        + [dma((planes,))] * 4,
        compiler_params=pltpu.CompilerParams(
            collective_id=1, has_side_effects=True, vmem_limit_bytes=60 * 2**20
        ),
        cost_estimate=pl.CostEstimate(flops=flops, bytes_accessed=40 * 2**20, transcendentals=0),
        name="experts_of_the_plane",
    )(normed, grads, inner, outer, bias, small)


def front_kernel(
    planes,
    heads,
    real,
    tokens_ref,
    mask_ref,
    ids_ref,
    cotangent_ref,
    *refs,
):
    vector_refs, refs = refs[:5], refs[5:]
    (
        router_part_ref,
        outer_bias_ref,
        qkv_part_ref,
    proj_part_ref,
    inner_part_ref,
    small_all,
    w_qkv_out,
    w_proj_out,
    inner_all,
    normed_in_ref,
    qkv_ref,
    attended_ref,
    middle_ref,
    normed_ref,
    grad_ref,
    grads_all,
    wide_ref,
    select_ref,
    keys_ref,
    keep_ref,
    w_qkv_all,
    w_proj_all,
    out_sem,
    up_send,
    up_recv,
    down_send,
    down_recv,
    x_send,
    x_recv,
    c_send,
    c_recv,
    over_send,
    over_recv,
    over_c_send,
    over_c_recv,
    g_z_send,
    g_z_recv,
    g_x_send,
    g_x_recv,
    g_c_send,
    g_c_recv,
    spread_send,
    spread_recv,
    own_sem,
    y_send,
    y_recv,
    ) = refs
    f32, bf16 = jnp.float32, jnp.bfloat16
    place = Place(planes)
    rows, width = wide_ref.shape
    depth = qkv_part_ref.shape[0]
    experts = inner_part_ref.shape[0]
    half = depth // 2
    lanes = inner_part_ref.shape[2] // (2 * planes)
    head_dim = width // heads
    y, c, z, x = place.y, place.c, place.z, place.x
    gathered = [small_all, w_qkv_all, w_proj_all]

    def remote(src, dst, send, recv, device):
        return pltpu.make_async_remote_copy(
            src_ref=src, dst_ref=dst, send_sem=send, recv_sem=recv, device_id=device, device_id_type=MESH
        )

    def block(j, level, across, core, plane):
        start = pl.multiple_of((level * 2 + across) * depth + core * half, 16)
        if j == 0:
            return gathered[j].at[pl.ds(start, half)]
        columns = gathered[j].shape[1] // 2
        return gathered[j].at[pl.ds(start, half), pl.ds(pl.multiple_of(plane * columns, 128), columns)]

    def piece(j, level, across):
        return block(j, level, across, c, y)

    def up_copy(j, level):
        here = piece(j, level, x)
        return remote(here, here, up_send.at[j, level], up_recv.at[j, level], place.at(y, c, z + 1, x))

    def down_copy(j, level):
        here = piece(j, level, x)
        return remote(here, here, down_send.at[j, level], down_recv.at[j, level], place.at(y, c, z - 1, x))

    def x_copy(j, level, across):
        here = piece(j, level, across)
        return remote(here, here, x_send.at[j, level], x_recv.at[j, level], place.other_x())

    def c_copy(j, level, across):
        here = piece(j, level, across)
        at = level * 2 + across
        return remote(here, here, c_send.at[j, at], c_recv.at[j, at], place.other_core())

    def over_copy(j, level, across):
        here = piece(j, level, across)
        at = level * 2 + across
        return remote(here, here, over_send.at[j, at], over_recv.at[j, at], place.other_y())

    def over_c_copy(j, level, across):
        here = block(j, level, across, c, 1 - y)
        at = level * 2 + across
        return remote(here, here, over_c_send.at[j, at], over_c_recv.at[j, at], place.other_core())

    def g_slot(level, at):
        return grads_all.at[level, pl.ds(at * rows, rows)]

    def g_up(level):
        here = g_slot(level, 0)
        return remote(here, here, g_z_send.at[0, level], g_z_recv.at[0, level], place.at(y, c, z + 1, x))

    def g_down(level):
        here = g_slot(level, 0)
        return remote(here, here, g_z_send.at[1, level], g_z_recv.at[1, level], place.at(y, c, z - 1, x))

    def g_x(level):
        return remote(g_slot(level, 0), g_slot(level, 2), g_x_send.at[level], g_x_recv.at[level], place.other_x())

    def g_c(level, r):
        return remote(
            g_slot(level, 2 * r), g_slot(level, 2 * r + 1), g_c_send.at[level, r], g_c_recv.at[level, r], place.other_core()
        )

    def columns_of(f):
        return pl.ds(pl.multiple_of(f * lanes, 128), lanes)

    here_rows = pl.ds(pl.multiple_of((z * 2 + x) * depth, 16), depth)
    my_units = pl.ds(pl.multiple_of(y * lanes, 128), lanes)

    def spread_copy(k, r):
        level, across = lax.rem(z + k, planes), (x + r) % 2
        return remote(
            inner_part_ref.at[c * 2 + y, :, columns_of(level * 2 + across)],
            inner_all.at[here_rows, my_units],
            spread_send.at[k, r],
            spread_recv.at[k, r],
            place.at(y, c, level, across),
        )

    own_copy = pltpu.make_async_copy(
        inner_part_ref.at[c * 2 + y, :, columns_of(z * 2 + x)], inner_all.at[here_rows, my_units], own_sem
    )
    y_copy = remote(inner_all.at[:, my_units], inner_all.at[:, my_units], y_send, y_recv, place.other_y())
    their_units = pl.ds(pl.multiple_of((1 - y) * lanes, 128), lanes)
    from_y = remote(inner_all.at[:, their_units], inner_all.at[:, their_units], y_send, y_recv, place.other_y())

    others = [(k, r) for k in range(planes) for r in range(2) if k or r]
    partners = [place.other_core(), place.other_y()]
    partners += [place.at(y, c, lax.rem(z + k, planes), (x + r) % 2) for k, r in others]
    greet(partners)

    w_qkv_all[here_rows, :] = qkv_part_ref[...]

    def share(j, level, across):
        c_copy(j, level, across).start()
        if j:
            over_copy(j, level, across).start()

    def line(flows):
        @pl.when(z < planes - 1)
        def _():
            for j in flows:
                up_copy(j, z).start()

        @pl.when(z > 0)
        def _():
            for j in flows:
                down_copy(j, z).start()

        for j in flows:
            x_copy(j, z, x).start()

    def hops(flows):
        for h in range(1, planes):
            @pl.when(z >= h)
            def _():
                for j in flows:
                    up_copy(j, z - h).wait_recv()

                    @pl.when(z < planes - 1)
                    def _():
                        up_copy(j, z - h).start()

                    x_copy(j, z - h, x).start()
                    share(j, z - h, x)

            @pl.when(z + h < planes)
            def _():
                for j in flows:
                    down_copy(j, z + h).wait_recv()

                    @pl.when(z > 0)
                    def _():
                        down_copy(j, z + h).start()

                    x_copy(j, z + h, x).start()
                    share(j, z + h, x)

    def arrive(flows):
        for i in range(planes):
            level = nearest(place, i)
            for j in flows:
                x_copy(j, level, 1 - x).wait_recv()
                share(j, level, 1 - x)

    def over_arrive(flows):
        for i in range(planes):
            level = nearest(place, i)
            for j in flows:
                if i:
                    over_copy(j, level, x).wait_recv()
                    over_c_copy(j, level, x).start()
                over_copy(j, level, 1 - x).wait_recv()
                over_c_copy(j, level, 1 - x).start()

    def gather_done(flows):
        for level in range(planes):
            for j in flows:
                c_copy(j, level, 1 - x).wait_recv()
                if j:
                    over_c_copy(j, level, 1 - x).wait_recv()

            @pl.when(level != z)
            def _():
                for j in flows:
                    c_copy(j, level, x).wait_recv()
                    if j:
                        over_c_copy(j, level, x).wait_recv()

    def g_hop(h):
        @pl.when(z >= h)
        def _():
            g_up(z - h).wait_recv()

            @pl.when(z < planes - 1)
            def _():
                g_up(z - h).start()

            g_x(z - h).start()
            g_c(z - h, 0).start()

        @pl.when(z + h < planes)
        def _():
            g_down(z + h).wait_recv()

            @pl.when(z > 0)
            def _():
                g_down(z + h).start()

            g_x(z + h).start()
            g_c(z + h, 0).start()

    line([1])
    lined = [ref[...].astype(f32) for ref in (*vector_refs, outer_bias_ref, router_part_ref)]
    lined = jnp.concatenate(lined, axis=0)
    lined = jnp.concatenate([lined, jnp.zeros((128 - lined.shape[0], depth), f32)], axis=0)
    lined = jnp.concatenate([lined, jnp.zeros((128, 128 - depth), f32)], axis=1)
    small = jnp.transpose(lined)[:depth]
    small_all[here_rows, :] = small.astype(bf16)
    line([0])
    w_proj_all[here_rows, :] = proj_part_ref[...]
    line([2])
    spare = jnp.zeros((rows - real, width), f32)
    values = jnp.concatenate([tokens_ref[...].astype(f32), spare], axis=0)
    wide_ref[...] = values.astype(bf16)
    normal, _ = norm_parts(values)
    mask = mask_ref[pl.ds(y * 2 + c, 1), :].astype(f32)
    keys = jnp.concatenate([mask, jnp.zeros((1, rows - real), f32)], axis=1)
    keys_ref[...] = keys
    keep = lax.broadcasted_iota(jnp.int32, (rows, rows), 0) == lax.broadcasted_iota(jnp.int32, (rows, rows), 1)
    keep = jnp.sum(jnp.where(keep, keys, 0.0), axis=1, keepdims=True)
    keep_ref[...] = keep
    ids = ids_ref[...]
    number = lax.broadcasted_iota(jnp.int32, (8, real), 0)
    chosen = ((number == ids[0:1]) | (number == ids[1:2])).astype(f32)
    chosen = jnp.concatenate([chosen, jnp.zeros((8, width - real), f32)], axis=1)
    select = jnp.concatenate([chosen[:, :256], jnp.zeros((120, 256), f32)], axis=0)
    select_ref[...] = jnp.transpose(select)[:rows].astype(bf16)
    if rows - real > 8:
        chosen = jnp.concatenate([chosen, jnp.zeros((rows - real - 8, width), f32)], axis=0)
    grad_out = cotangent_ref[...].astype(f32) * keep[:real]
    grad_out = jnp.concatenate([grad_out, chosen], axis=0).astype(bf16)
    grad_ref[...] = grad_out
    grads_own = pltpu.make_async_copy(grad_ref, g_slot(z, 0), out_sem.at[2])
    grads_own.start()
    hops([1, 0])
    arrive([1, 0])
    hops([2])
    own_copy.start()
    for k, r in others:
        spread_copy(k, r).start()

    grads_own.wait()

    @pl.when(z < planes - 1)
    def _():
        g_up(z).start()

    @pl.when(z > 0)
    def _():
        g_down(z).start()

    g_x(z).start()
    g_c(z, 0).start()
    arrive([2])
    over_arrive([1])
    gather_done([1, 0])
    qkv_out_copy = pltpu.make_async_copy(w_qkv_all, w_qkv_out, out_sem.at[0])
    qkv_out_copy.start()
    vectors = jnp.transpose(small_all[...].astype(f32))
    normed_in = (normal * vectors[0:1] + vectors[1:2]).astype(bf16)
    normed_in_ref[...] = normed_in
    for j in range(3):
        part = slice(j * width, (j + 1) * width)
        qkv_ref[:, part] = dot(normed_in, w_qkv_all[:, part]).astype(bf16)
    g_hop(1)
    over_arrive([2])
    lane = lax.broadcasted_iota(jnp.int32, (rows, 2 * head_dim), 1)
    usable = keys_ref[...] > 0
    for pair in range(heads // 2):
        if pair == heads // 4:
            g_hop(2)
        at = pair * 2 * head_dim
        queries = qkv_ref[:, at : at + 2 * head_dim]
        keys = qkv_ref[:, width + at : width + at + 2 * head_dim]
        held = qkv_ref[:, 2 * width + at : 2 * width + at + 2 * head_dim]
        outs = []
        for side in range(2):
            only = (lane < head_dim) if side == 0 else (lane >= head_dim)
            scores = lax.dot_general(
                jnp.where(only, queries, 0).astype(bf16), keys, NT, preferred_element_type=f32
            )
            scores = jnp.where(usable, scores * head_dim ** (-0.5), masked_score)
            shifted = jnp.exp(scores - jnp.max(scores, axis=1, keepdims=True))
            probs = (shifted / jnp.sum(shifted, axis=1, keepdims=True)).astype(bf16)
            outs.append(dot(probs, held))
        attended_ref[:, at : at + 2 * head_dim] = jnp.where(lane < head_dim, outs[0], outs[1]).astype(bf16)
    for h in range(3, planes):
        g_hop(h)
    own_copy.wait()
    for k, r in others:
        spread_copy(k, r).wait_recv()
    y_copy.start()
    gather_done([2])
    proj_out_copy = pltpu.make_async_copy(w_proj_all, w_proj_out, out_sem.at[1])
    proj_out_copy.start()
    middle = values + dot(attended_ref[...], w_proj_all[...]) + vectors[2:3]
    middle_ref[...] = middle
    normal_mid, _ = norm_parts(middle)
    normed = normal_mid * vectors[3:4] + vectors[4:5]
    row = lax.broadcasted_iota(jnp.int32, normed.shape, 0)
    normed_ref[...] = jnp.where(row < real, normed, 0.0).astype(bf16)
    for i in range(planes):
        level = nearest(place, i)
        g_x(level).wait_recv()
        g_c(level, 1).start()
    from_y.wait_recv()
    qkv_out_copy.wait()
    proj_out_copy.wait()
    for level in range(planes):
        g_c(level, 0).wait_recv()
        g_c(level, 1).wait_recv()
    y_copy.wait_send()
    for k, r in others:
        spread_copy(k, r).wait_send()
    for level in range(planes):
        g_x(level).wait_send()
        g_c(level, 0).wait_send()
        g_c(level, 1).wait_send()

        @pl.when((z >= level) & (z < planes - 1))
        def _():
            g_up(level).wait_send()

        @pl.when((z <= level) & (z > 0))
        def _():
            g_down(level).wait_send()

    def shared(j, level, across):
        c_copy(j, level, across).wait_send()
        if j:
            over_copy(j, level, across).wait_send()
            over_c_copy(j, level, across).wait_send()

    for j in range(3):
        for level in range(planes):
            x_copy(j, level, x).wait_send()
            shared(j, level, 1 - x)

            @pl.when(level != z)
            def _():
                shared(j, level, x)

            @pl.when((z >= level) & (z < planes - 1))
            def _():
                up_copy(j, level).wait_send()

            @pl.when((z <= level) & (z > 0))
            def _():
                down_copy(j, level).wait_send()


def front(planes, rows, tokens, mask, ids, cotangent, vectors, router, outer_bias, w_qkv, w_proj, w_in):
    f32, bf16 = jnp.float32, jnp.bfloat16
    real, width = tokens.shape
    lanes = w_in.shape[2] // (2 * planes)
    shape = jax.ShapeDtypeStruct
    vmem = pl.BlockSpec(memory_space=pltpu.VMEM)
    anywhere = pl.BlockSpec(memory_space=pl.ANY)
    dma = pltpu.SemaphoreType.DMA
    return pl.pallas_call(
        functools.partial(front_kernel, planes, HEADS, real),
        out_shape=[
            shape((width, 128), bf16),
            shape((width, 3 * width), bf16),
            shape((width, width), bf16),
            shape((width, 2 * lanes), bf16),
            shape((rows, width), bf16),
            shape((rows, 3 * width), bf16),
            shape((rows, width), bf16),
            shape((rows, width), f32),
            shape((rows, width), bf16),
            shape((rows, width), bf16),
            shape((planes, 4 * rows, width), bf16),
            shape((rows, width), bf16),
            shape((rows, 128), bf16),
            shape((1, rows), f32),
            shape((rows, 1), f32),
        ],
        in_specs=[vmem] * (6 + len(vectors)) + [vmem] * 2 + [anywhere],
        out_specs=[vmem] + [anywhere] * 3 + [vmem] * 6 + [anywhere] + [vmem] * 4,
        scratch_shapes=[pltpu.VMEM((width, 3 * width), bf16), pltpu.VMEM((width, width), bf16), dma((3,))]
        + [dma((3, planes))] * 6
        + [dma((3, 2 * planes))] * 6
        + [dma((2, planes))] * 2
        + [dma((planes,))] * 2
        + [dma((planes, 2))] * 4
        + [dma] * 3,
        compiler_params=pltpu.CompilerParams(
            collective_id=2, has_side_effects=True, vmem_limit_bytes=60 * 2**20
        ),
        cost_estimate=pl.CostEstimate(flops=2**32, bytes_accessed=40 * 2**20, transcendentals=0),
        name="dense_weights_and_attention",
    )(tokens, mask, ids, cotangent, *vectors, router, outer_bias, w_qkv, w_proj, w_in)


def back_kernel(planes, heads, own, groups, real, *refs):
    (
        row_grad_ref,
        normed_ref,
        grad_ref,
        middle_ref,
        tokens_ref,
        normed_in_ref,
        qkv_ref,
        attended_ref,
        small_ref,
        w_qkv_all_ref,
        w_proj_ref,
        keys_ref,
        keep_ref,
        select_ref,
        mix_ref,
        inner_ref,
        outer_ref,
        bias_ref,
        router_grad_ref,
    ) = refs[:19]
    mixed_ref, token_grad_ref, qkv_out, proj_out, small_out, inner_out, outer_out, bias_out = refs[19:27]
    refs = refs[27:]
    (
        w_qkv_ref,
        outer_sum,
        grad_attended,
        grad_qkv,
        mix_z,
        mix_from_x,
        mix_from_z,
        inner_from_y,
        inner_sum,
        outer_from_y,
        bias_from_y,
        held,
        held_small,
        from_core,
        from_core_small,
        from_x,
        from_x_small,
        from_z,
        from_z_small,
        plane_sum,
        plane_sum_small,
        from_y,
        from_y_small,
        final,
        final_small,
    ) = refs[:25]
    (
        load_sem,
        outer_own_sem,
        mix_x_send,
        mix_x_recv,
        mix_z_send,
        mix_z_recv,
        inner_y_sem,
        spread_send,
        spread_recv,
        inner_back_sem,
        inner_core_sem,
        outer_y_sem,
        outer_c_sem,
        bias_y_sem,
        bias_c_sem,
        own_sem,
        flow_c_sem,
        flow_x_sem,
        flow_z_send,
        flow_z_recv,
        flow_y_sem,
        flow_end_sem,
    ) = refs[25:]
    f32, bf16 = jnp.float32, jnp.bfloat16
    place = Place(planes)
    y, c, z, x = place.y, place.c, place.z, place.x
    rows, width = middle_ref.shape
    depth = width // (2 * planes)
    half = depth // 2
    lanes = inner_ref.shape[1] // own
    head_dim = width // heads
    pair_width = 2 * head_dim
    small_at = groups + 1

    def remote(src, dst, send, recv, device):
        return pltpu.make_async_remote_copy(
            src_ref=src, dst_ref=dst, send_sem=send, recv_sem=recv, device_id=device, device_id_type=MESH
        )

    def swap(src, dst, sem, device):
        return remote(src, dst, sem.at[0], sem.at[1], device)

    def of_flow(j, many, alone):
        return alone if j == small_at else many.at[j]

    mine, theirs = pl.ds(pl.multiple_of(c * half, 16), half), pl.ds(pl.multiple_of((1 - c) * half, 16), half)

    def flow_c(j):
        source = of_flow(j, held, held_small)
        return swap(
            source.at[:, :, theirs], of_flow(j, from_core, from_core_small), flow_c_sem.at[j], place.other_core()
        )

    def flow_x(j):
        source = of_flow(j, held, held_small)
        return swap(source.at[:, 1 - x, mine], of_flow(j, from_x, from_x_small), flow_x_sem.at[j], place.other_x())

    def flow_z(j, k):
        level = lax.rem(z + k, planes)
        source = of_flow(j, held, held_small)
        return remote(
            source.at[level, x, mine],
            of_flow(j, from_z, from_z_small).at[k],
            flow_z_send.at[j, k],
            flow_z_recv.at[j, k],
            place.level(k),
        )

    def flow_y(j):
        return swap(
            of_flow(j, plane_sum, plane_sum_small),
            of_flow(j, from_y, from_y_small),
            flow_y_sem.at[j],
            place.other_y(),
        )

    def flow_end(j):
        here = of_flow(j, final, final_small).at[mine]
        return swap(here, here, flow_end_sem.at[j], place.other_core())

    def flow_core_sum(j):
        flow_c(j).wait_recv()
        kept = of_flow(j, held, held_small)
        total = kept[:, :, mine, :].astype(f32) + of_flow(j, from_core, from_core_small)[...].astype(f32)
        kept[:, :, mine, :] = total.astype(bf16)
        flow_x(j).start()

    def flow_x_sum(j):
        flow_x(j).wait_recv()
        kept = of_flow(j, held, held_small)
        total = kept[:, x, mine, :].astype(f32) + of_flow(j, from_x, from_x_small)[...].astype(f32)
        kept[:, x, mine, :] = total.astype(bf16)
        for k in range(1, planes):
            flow_z(j, k).start()

    def flow_z_sum(j):
        kept = of_flow(j, held, held_small)
        total = kept[z, x, mine, :].astype(f32)
        for k in range(1, planes):
            flow_z(j, k).wait_recv()
            total = total + of_flow(j, from_z, from_z_small)[k].astype(f32)
        of_flow(j, plane_sum, plane_sum_small)[...] = total.astype(bf16)
        flow_y(j).start()

    def flow_y_sum(j):
        flow_y(j).wait_recv()
        total = of_flow(j, plane_sum, plane_sum_small)[...].astype(f32)
        total = total + of_flow(j, from_y, from_y_small)[...].astype(f32)
        of_flow(j, final, final_small)[mine, :] = total.astype(bf16)
        flow_end(j).start()

    loads = [
        pltpu.make_async_copy(mix_ref.at[:, pl.ds(0, rows)], mix_z, load_sem.at[0]),
        pltpu.make_async_copy(w_qkv_all_ref, w_qkv_ref, load_sem.at[1]),
    ]

    def mix_to_x(level):
        return remote(
            mix_ref.at[level, pl.ds(rows, rows)],
            mix_from_x.at[level],
            mix_x_send.at[level],
            mix_x_recv.at[level],
            place.other_x(),
        )

    def mix_start(k):
        mix_to_x(lax.rem(z + k, planes)).start()

    def mix_to_z(level, source):
        return remote(
            mix_z.at[level], mix_from_z.at[source], mix_z_send.at[level], mix_z_recv.at[source], place.at(y, c, level, x)
        )

    def mix_x_sum(k):
        level = lax.rem(z + k, planes)
        mix_to_x(level).wait_recv()
        mix_z[level] = (mix_z[level].astype(f32) + mix_from_x[level].astype(f32)).astype(bf16)
        if k < planes:
            mix_to_z(level, z).start()

    my_units = pl.ds(pl.multiple_of(y * lanes, 128), lanes)
    their_units = pl.ds(pl.multiple_of((1 - y) * lanes, 128), lanes)
    my_expert, their_expert = c * 2 + y, c * 2 + 1 - y
    my_columns = pl.ds(pl.multiple_of((z * 2 + x) * lanes, 128), lanes)

    def inner_y():
        return swap(inner_ref.at[:, their_units], inner_from_y, inner_y_sem, place.other_y())

    def shard_rows(f):
        return pl.ds(pl.multiple_of(f * depth, 16), depth)

    def spread(k, r):
        level, across = lax.rem(z + k, planes), (x + r) % 2
        return remote(
            inner_sum.at[shard_rows(level * 2 + across)],
            inner_out.at[my_expert, :, my_columns],
            spread_send.at[k, r],
            spread_recv.at[k, r],
            place.at(y, c, level, across),
        )

    own_copy = pltpu.make_async_copy(
        inner_sum.at[shard_rows(z * 2 + x)], inner_out.at[my_expert, :, my_columns], own_sem
    )

    def inner_back():
        here = inner_out.at[my_expert]
        return swap(here, here, inner_back_sem, place.other_y())

    def inner_core(expert, at):
        here = inner_out.at[expert]
        return swap(here, here, inner_core_sem.at[at], place.other_core())

    def outer_y():
        return swap(outer_ref, outer_from_y, outer_y_sem, place.other_y())

    def outer_c():
        return swap(outer_sum, outer_out.at[c], outer_c_sem, place.other_core())

    outer_own = pltpu.make_async_copy(outer_sum, outer_out.at[c], outer_own_sem)

    def bias_y():
        return swap(bias_ref, bias_from_y, bias_y_sem, place.other_y())

    def bias_c():
        here = bias_out.at[c]
        return swap(here, here, bias_c_sem, place.other_core())

    others = [(k, r) for k in range(planes) for r in range(2) if k or r]

    def inner_y_sum():
        inner_y().wait_recv()
        total = inner_ref[:, my_units].astype(f32) + inner_from_y[...].astype(f32)
        inner_sum[...] = total.astype(bf16)
        own_copy.start()
        for k, r in others:
            spread(k, r).start()
        outer_y().start()

    def inner_spread_done():
        own_copy.wait()
        for k, r in others:
            spread(k, r).wait_recv()
        inner_back().start()
        inner_core(my_expert, 0).start()

    def outer_y_sum():
        outer_y().wait_recv()
        total = outer_ref[...].astype(f32) + outer_from_y[...].astype(f32)
        outer_sum[...] = total.astype(bf16)
        outer_own.start()
        outer_c().start()
        bias_y().wait_recv()
        bias_out[c] = bias_ref[...] + bias_from_y[...]
        bias_c().start()

    partners = [place.other_core(), place.other_y()]
    partners += [place.at(y, c, lax.rem(z + k, planes), (x + r) % 2) for k, r in others]
    greet(partners)
    inner_y().start()
    bias_y().start()
    mix_start(1)
    for load in loads:
        load.start()

    vectors = jnp.transpose(small_ref[...].astype(f32))
    gain_first, gain_second = vectors[0:1], vectors[3:4]
    place_row = lax.broadcasted_iota(jnp.int32, (128, 128), 0)
    place_lane = lax.broadcasted_iota(jnp.int32, (128, 128), 1)

    def lanes_from(first):
        take = (place_row == place_lane + first) & (place_lane < 2 * own)
        return dot(small_ref[...], take.astype(bf16)).astype(bf16)

    outer_bias, router = lanes_from(5), lanes_from(5 + 2 * own)
    normed_mid, grad_out = normed_ref[...], grad_ref[...]
    real_row = lax.broadcasted_iota(jnp.int32, grad_out.shape, 0) < real
    grad_out = jnp.where(real_row, grad_out, 0).astype(bf16)
    select = select_ref[...].astype(f32)
    lane = lax.broadcasted_iota(jnp.int32, select.shape, 1)
    logits = jnp.where(lane < 2 * own, dot(normed_mid, router), -1e30)
    routing = jnp.exp(logits - jnp.max(logits, axis=1, keepdims=True))
    routing = routing / jnp.sum(routing, axis=1, keepdims=True)
    gates = routing * select
    bias_gate = select * dot(grad_out, outer_bias)
    bias_logits = routing * (bias_gate - jnp.sum(routing * bias_gate, axis=1, keepdims=True))
    bias_logits = bias_logits.astype(bf16)
    router_grad = lax.dot_general(normed_mid, bias_logits, TN, preferred_element_type=f32)
    router_grad = pltpu.roll(router_grad, 16, 1) + pltpu.roll(router_grad_ref[...], 16 - real % 16, 1)
    outer_bias_grad = lax.dot_general(gates.astype(bf16), grad_out, TN, preferred_element_type=f32)
    grad_normed_mid = row_grad_ref[...] + lax.dot_general(bias_logits, router, NT, preferred_element_type=f32)
    normal_mid, rstd_mid = norm_parts(middle_ref[...])
    gain_second_grad = jnp.sum(grad_normed_mid * normal_mid, axis=0, keepdims=True)
    bias_second_grad = jnp.sum(grad_normed_mid, axis=0, keepdims=True)
    grad_middle = grad_out.astype(f32) + norm_back(grad_normed_mid, normal_mid, rstd_mid, gain_second)
    grad_proj = grad_middle.astype(bf16)
    proj_bias_grad = jnp.sum(grad_proj.astype(f32), axis=0, keepdims=True)
    loads[0].wait()

    def hold(j, value):
        held[j] = value.astype(bf16).reshape(planes, 2, depth, width)
        flow_c(j).start()

    hold(0, lax.dot_general(attended_ref[...], grad_proj, TN, preferred_element_type=f32))
    grad_attended[...] = lax.dot_general(grad_proj, w_proj_ref[...], NT, preferred_element_type=f32).astype(bf16)
    flow_core_sum(0)

    pair_lane = lax.broadcasted_iota(jnp.int32, (rows, pair_width), 1)
    usable = keys_ref[...] > 0
    scaling = head_dim ** (-0.5)
    group_width = width // groups

    def pair_back(pair):
        at = pair * pair_width
        group, inside = at // group_width, at % group_width
        queries = qkv_ref[:, at : at + pair_width]
        keys = qkv_ref[:, width + at : width + at + pair_width]
        values = qkv_ref[:, 2 * width + at : 2 * width + at + pair_width]
        grads = grad_attended[:, at : at + pair_width]
        found = []
        for side in range(2):
            only = (pair_lane < head_dim) if side == 0 else (pair_lane >= head_dim)
            some_queries = jnp.where(only, queries, 0).astype(bf16)
            some_grads = jnp.where(only, grads, 0).astype(bf16)
            scores = lax.dot_general(some_queries, keys, NT, preferred_element_type=f32)
            scores = jnp.where(usable, scores * scaling, masked_score)
            shifted = jnp.exp(scores - jnp.max(scores, axis=1, keepdims=True))
            probs = shifted / jnp.sum(shifted, axis=1, keepdims=True)
            grad_probs = lax.dot_general(some_grads, values, NT, preferred_element_type=f32)
            grad_scores = probs * (grad_probs - jnp.sum(probs * grad_probs, axis=1, keepdims=True))
            grad_scores = grad_scores.astype(bf16)
            found.append(
                (
                    dot(grad_scores, keys),
                    lax.dot_general(grad_scores, some_queries, TN, preferred_element_type=f32),
                    lax.dot_general(probs.astype(bf16), some_grads, TN, preferred_element_type=f32),
                )
            )
        grad_queries = jnp.where(pair_lane < head_dim, found[0][0], found[1][0]) * scaling
        grad_keys = (found[0][1] + found[1][1]) * scaling
        grad_values = found[0][2] + found[1][2]
        for part, value in enumerate((grad_queries, grad_keys, grad_values)):
            start = part * group_width + inside
            grad_qkv[group, :, start : start + pair_width] = value.astype(bf16)

    def group_back(group):
        per_group = heads // 2 // groups
        for pair in range(group * per_group, (group + 1) * per_group):
            pair_back(pair)
        hold(
            1 + group,
            lax.dot_general(normed_in_ref[...], grad_qkv[group], TN, preferred_element_type=f32),
        )

    group_back(0)
    mix_start(2)
    inner_y_sum()
    flow_core_sum(1)
    mix_x_sum(1)
    for group in range(1, groups):
        group_back(group)
        flow_core_sum(1 + group)
        if group == 1:
            flow_x_sum(0)
            mix_x_sum(2)
    if groups == 1:
        flow_x_sum(0)
        mix_x_sum(2)

    loads[1].wait()
    grad_normed_in = jnp.zeros((rows, width), f32)
    for group in range(groups):
        for part in range(3):
            grad_normed_in = grad_normed_in + lax.dot_general(
                grad_qkv[group, :, part * group_width : (part + 1) * group_width],
                w_qkv_ref[:, part * width + group * group_width : part * width + (group + 1) * group_width],
                NT,
                preferred_element_type=f32,
            )
    normal_first, rstd_first = norm_parts(tokens_ref[...].astype(f32))
    gain_first_grad = jnp.sum(grad_normed_in * normal_first, axis=0, keepdims=True)
    bias_first_grad = jnp.sum(grad_normed_in, axis=0, keepdims=True)
    token_grad = grad_middle + norm_back(grad_normed_in, normal_first, rstd_first, gain_first)
    token_grad_ref[...] = token_grad.astype(bf16)[:real]
    vector_rows = jnp.concatenate(
        [
            gain_first_grad,
            bias_first_grad,
            proj_bias_grad,
            gain_second_grad,
            bias_second_grad,
            jnp.zeros((3, width), f32),
            outer_bias_grad[:8],
            jnp.zeros((112, width), f32),
        ],
        axis=0,
    )
    vector_grads = jnp.transpose(vector_rows) + router_grad
    held_small[...] = vector_grads.astype(bf16).reshape(planes, 2, depth, 128)
    flow_c(small_at).start()
    flow_core_sum(small_at)
    inner_spread_done()
    for group in range(groups - 1):
        flow_x_sum(1 + group)
    mix_start(3)
    flow_x_sum(groups)
    for k in range(4, planes + 1):
        mix_start(k)
    flow_x_sum(small_at)
    outer_y_sum()
    for k in range(3, planes):
        mix_x_sum(k)
    flow_z_sum(0)
    flow_y_sum(0)
    for group in range(groups):
        flow_z_sum(1 + group)
    flow_z_sum(small_at)
    inner_back().wait_recv()
    inner_core(their_expert, 1).start()
    mix_x_sum(planes)
    mixture = mix_z[z].astype(f32) + dot(gates.astype(bf16), jnp.transpose(outer_bias.astype(f32)).astype(bf16))
    for k in range(1, planes):
        source = lax.rem(z + k, planes)
        mix_to_z(z, source).wait_recv()
        mixture = mixture + mix_from_z[source].astype(f32)
    mixed = (keep_ref[...] * (middle_ref[...] + mixture)).astype(bf16)
    mixed_ref[...] = mixed[:real]
    for group in range(groups):
        flow_y_sum(1 + group)
    flow_y_sum(small_at)

    def arrived(j):
        here = of_flow(j, final, final_small).at[theirs]
        swap(here, here, flow_end_sem.at[j], place.other_core()).wait_recv()

    arrived(0)
    proj_out[...] = final[0]
    for group in range(groups):
        arrived(1 + group)
        for part in range(3):
            start = part * width + group * group_width
            qkv_out[:, start : start + group_width] = final[
                1 + group, :, part * group_width : (part + 1) * group_width
            ]
    arrived(small_at)
    small_out[...] = jnp.transpose(
        jnp.concatenate([final_small[...].astype(f32), jnp.zeros((128 - depth, 128), f32)], axis=0)
    )
    outer_own.wait()
    outer_c().wait_recv()
    bias_theirs = bias_out.at[1 - c]
    swap(bias_theirs, bias_theirs, bias_c_sem, place.other_core()).wait_recv()
    for at, expert in enumerate(((1 - c) * 2 + y, (1 - c) * 2 + 1 - y)):
        inner_core(expert, at).wait_recv()

    inner_y().wait_send()
    inner_back().wait_send()
    inner_core(my_expert, 0).wait_send()
    inner_core(their_expert, 1).wait_send()
    outer_y().wait_send()
    outer_c().wait_send()
    bias_y().wait_send()
    bias_c().wait_send()
    for k, r in others:
        spread(k, r).wait_send()
    for k in range(1, planes + 1):
        level = lax.rem(z + k, planes)
        mix_to_x(level).wait_send()
        if k < planes:
            mix_to_z(level, z).wait_send()
    for j in range(groups + 2):
        flow_c(j).wait_send()
        flow_x(j).wait_send()
        for k in range(1, planes):
            flow_z(j, k).wait_send()
        flow_y(j).wait_send()
        flow_end(j).wait_send()


def back(planes, own, real, *args):
    f32, bf16 = jnp.float32, jnp.bfloat16
    (
        row_grad,
        normed_mid,
        grad_out,
        middle,
        tokens,
        normed_in,
        qkv,
        attended,
        small,
        w_qkv,
        w_proj,
        keys,
        keep,
        select,
        mix_parts,
        inner_grad,
        outer_grad,
        bias_grad,
        router_grad,
    ) = args
    rows, width = middle.shape
    depth = width // (2 * planes)
    half = depth // 2
    lanes = inner_grad.shape[1] // own
    tall = outer_grad.shape[0]
    pairs = HEADS // 2
    groups = 3 if pairs % 3 == 0 and (pairs // 3) * 2 * (width // HEADS) % 128 == 0 else 1
    flows = groups + 1
    shape = jax.ShapeDtypeStruct
    vmem = pl.BlockSpec(memory_space=pltpu.VMEM)
    anywhere = pl.BlockSpec(memory_space=pl.ANY)
    dma = pltpu.SemaphoreType.DMA

    def both(*dims):
        return [pltpu.VMEM((flows, *dims, width), bf16), pltpu.VMEM((*dims, 128), bf16)]

    return pl.pallas_call(
        functools.partial(back_kernel, planes, HEADS, own, groups, real),
        out_shape=[
            shape((real, width), bf16),
            shape((real, width), bf16),
            shape((depth, 3 * width), bf16),
            shape((depth, width), bf16),
            shape((128, 128), f32),
            shape((2 * own, depth, 2 * planes * lanes), bf16),
            shape((2, tall, width), bf16),
            shape((2, *bias_grad.shape), f32),
        ],
        in_specs=[vmem] * 9 + [anywhere] + [vmem] * 4 + [anywhere] + [vmem] * 4,
        out_specs=[vmem] * 5 + [anywhere] * 2 + [vmem],
        scratch_shapes=[
            pltpu.VMEM((width, 3 * width), bf16),
            pltpu.VMEM((tall, width), bf16),
            pltpu.VMEM((rows, width), bf16),
            pltpu.VMEM((groups, rows, 3 * width // groups), bf16),
            pltpu.VMEM((planes, rows, width), bf16),
            pltpu.VMEM((planes, rows, width), bf16),
            pltpu.VMEM((planes, rows, width), bf16),
            pltpu.VMEM((width, lanes), bf16),
            pltpu.VMEM((width, lanes), bf16),
            pltpu.VMEM((tall, width), bf16),
            pltpu.VMEM(bias_grad.shape, f32),
        ]
        + both(planes, 2, depth)
        + both(planes, 2, half)
        + both(planes, half)
        + both(planes, half)
        + both(half)
        + both(half)
        + both(depth)
        + [dma((2,)), dma]
        + [dma((planes,))] * 4
        + [dma((2,))]
        + [dma((planes, 2))] * 2
        + [dma((2,)), dma((2, 2)), dma((2,)), dma((2,)), dma((2,)), dma((2,)), dma]
        + [dma((flows + 1, 2))] * 2
        + [dma((flows + 1, planes))] * 2
        + [dma((flows + 1, 2))] * 2,
        compiler_params=pltpu.CompilerParams(
            collective_id=3, has_side_effects=True, vmem_limit_bytes=60 * 2**20
        ),
        cost_estimate=pl.CostEstimate(flops=2**33, bytes_accessed=40 * 2**20, transcendentals=0),
        name="attention_backward_and_sums",
    )(*args)


def finish_kernel(
    depth,
    experts,
    qkv_ref,
    proj_ref,
    rows_ref,
    inner_ref,
    outer_ref,
    mixed_ref,
    token_grad_ref,
    bias_ref,
    qkv_out,
    proj_out,
    inner_out,
    outer_out,
    mixed_out,
    token_grad_out,
    router_out,
    outer_bias_out,
    bias_out,
    *vector_outs,
):
    f32 = jnp.float32

    @pl.when(pl.program_id(0) == 0)
    def _():
        for i, out in enumerate(vector_outs):
            out[...] = rows_ref[i : i + 1, :depth]
        outer_bias_out[...] = rows_ref[8 : 8 + experts, :depth]
        router_out[...] = rows_ref[16 : 16 + experts, :depth]
        qkv_out[...] = qkv_ref[...].astype(f32)
        proj_out[...] = proj_ref[...].astype(f32)
        lanes = bias_out.shape[1]
        for e in range(experts):
            at = e % (experts // 2) * lanes
            bias_out[e : e + 1, :] = bias_ref[e // (experts // 2), 0:1, at : at + lanes]
        mixed_out[...] = mixed_ref[...]
        token_grad_out[...] = token_grad_ref[...]

    inner_out[...] = inner_ref[...].astype(f32)
    outer_out[...] = outer_ref[...].astype(f32)


def finish(qkv, proj, vectors, inner, outer, mixed, token_grad, bias):
    f32 = jnp.float32
    experts, depth, _ = inner.shape
    shape = jax.ShapeDtypeStruct

    def whole(array):
        return pl.BlockSpec(array.shape, lambda i, rank=len(array.shape): (0,) * rank)

    def one(array):
        return pl.BlockSpec((1, *array.shape[1:]), lambda i: (i, 0, 0))

    outs = [
        shape(qkv.shape, f32),
        shape(proj.shape, f32),
        shape(inner.shape, f32),
        shape(outer.shape, f32),
        shape(mixed.shape, mixed.dtype),
        shape(token_grad.shape, token_grad.dtype),
        shape((experts, depth), f32),
        shape((experts, depth), f32),
        shape((experts, outer.shape[1]), f32),
    ] + [shape((1, depth), f32)] * 5
    return pl.pallas_call(
        functools.partial(finish_kernel, depth, experts),
        out_shape=outs,
        grid=(experts,),
        in_specs=[whole(qkv), whole(proj), whole(vectors), one(inner), one(outer)]
        + [whole(mixed), whole(token_grad), whole(bias)],
        out_specs=[whole(outs[0]), whole(outs[1]), one(outs[2]), one(outs[3])] + [whole(out) for out in outs[4:]],
        compiler_params=pltpu.CompilerParams(vmem_limit_bytes=62 * 2**20),
        name="results_in_float32",
    )(qkv, proj, vectors, inner, outer, mixed, token_grad, bias)


def norm_parts(values):
    center = values - jnp.mean(values, axis=-1, keepdims=True)
    rstd = lax.rsqrt(jnp.mean(center * center, axis=-1, keepdims=True) + epsilon)
    return center * rstd, rstd


def norm_back(grad, normal, rstd, gain):
    scaled = grad * gain
    return rstd * (
        scaled
        - jnp.mean(scaled, axis=-1, keepdims=True)
        - normal * jnp.mean(scaled * normal, axis=-1, keepdims=True)
    )


def move_tokens_plan(
    tokens,
    key_mask,
    expert_ids,
    cotangent,
    norm1_gain,
    norm1_bias,
    w_qkv,
    w_proj,
    proj_bias,
    norm2_gain,
    norm2_bias,
    w_router,
    w_in,
    b_in,
    w_out,
    b_out,
):
    f32 = jnp.float32
    _, rows, width = tokens.shape
    experts, depth, hidden = w_in.shape
    slice_width = w_out.shape[1]
    planes = hidden // slice_width // 2
    own = experts // 2
    padded = (rows + experts + 15) // 16 * 16
    vectors = [v[None] for v in (norm1_gain, norm1_bias, proj_bias, norm2_gain, norm2_bias)]
    fronts = front(
        planes,
        padded,
        tokens[0],
        key_mask,
        expert_ids[0].T,
        cotangent[0],
        vectors,
        w_router.T,
        b_out,
        w_qkv,
        w_proj,
        w_in,
    )
    small, full_qkv, full_proj, inner, normed_in, qkv, attended, middle = fronts[:8]
    normed_mid, grad_out, all_grad_out, wide, select, keys, keep = fronts[8:]
    mix_parts, row_grad, inner_grad, outer_grad, bias_grad, router_grad = experts_of_the_plane(
        planes, own, rows, normed_mid, all_grad_out, inner, w_out, b_in, small
    )
    mixed, token_grad, qkv_grad, proj_grad, vector_grads, inner_grad, outer_grad, bias_grad = back(
        planes,
        own,
        rows,
        row_grad,
        normed_mid,
        grad_out,
        middle,
        wide,
        normed_in,
        qkv,
        attended,
        small,
        full_qkv,
        full_proj,
        keys,
        keep,
        select,
        mix_parts,
        inner_grad,
        outer_grad,
        bias_grad,
        router_grad,
    )
    outer_grad = outer_grad.reshape(experts, slice_width, width)
    finished = finish(
        qkv_grad, proj_grad, vector_grads, inner_grad, outer_grad, mixed, token_grad, bias_grad
    )
    qkv_grad, proj_grad, inner_grad, outer_grad, mixed, token_grad, router_grad, outer_bias_grad = finished[:8]
    bias_grad = finished[8]
    vector_grads = [row.reshape(depth) for row in finished[9:]]
    return (
        mixed[None],
        token_grad[None],
        vector_grads[0],
        vector_grads[1],
        qkv_grad,
        proj_grad,
        vector_grads[2],
        vector_grads[3],
        vector_grads[4],
        router_grad.T,
        inner_grad,
        bias_grad,
        outer_grad,
        outer_bias_grad,
    )


def solution(mesh):
    n_seq, n_fsdp = mesh.shape["seq"], mesh.shape["fsdp"]

    def per_device(*args):
        tokens, w_in, w_out = args[0], args[12], args[14]
        experts, _, hidden = w_in.shape
        lanes = hidden // n_fsdp
        whole_tiles = lanes % 128 == 0 and tokens.shape[2] % 256 == 0 and w_in.shape[1] % 32 == 0 and 2 * lanes <= tokens.shape[2]
        if n_seq == 4 and experts == n_seq and n_fsdp >= 6 and n_fsdp % 2 == 0 and tokens.shape[0] == 1 and whole_tiles:
            return move_tokens_plan(*args)
        return gather_weights_plan(*args)

    return jax.shard_map(
        per_device,
        mesh=mesh,
        in_specs=(
            P(("fsdp", "seq"), None, None),
            P("fsdp", None),
            P(("fsdp", "seq"), None, None),
            P(("fsdp", "seq"), None, None),
            P("fsdp"),
            P("fsdp"),
            P("fsdp", None),
            P("fsdp", None),
            P("fsdp"),
            P("fsdp"),
            P("fsdp"),
            P("fsdp", None),
            P(None, "fsdp", None),
            P(None, "fsdp"),
            P(None, "fsdp", None),
            P(None, "fsdp"),
        ),
        out_specs=(
            P(("fsdp", "seq"), None, None),
            P(("fsdp", "seq"), None, None),
            P("fsdp"),
            P("fsdp"),
            P("fsdp", None),
            P("fsdp", None),
            P("fsdp"),
            P("fsdp"),
            P("fsdp"),
            P("fsdp", None),
            P(None, "fsdp", None),
            P(None, "fsdp"),
            P(None, "fsdp", None),
            P(None, "fsdp"),
        ),
        check_vma=False,
    )
```

```python
import functools

import jax
import jax.numpy as jnp
from jax import lax
from jax.experimental import pallas as pl
from jax.experimental.pallas import tpu as pltpu
from jax.sharding import PartitionSpec as P

HEADS = 12
CAP = 142


epsilon = 1e-06
masked_score = -1e30


def norm_rows(values, gain, offset):
    center = values - jnp.mean(values, axis=-1, keepdims=True)
    spread = jnp.mean(center * center, axis=-1, keepdims=True)
    return center * lax.rsqrt(spread + epsilon) * gain + offset


def softmax_rows(values):
    shifted = jnp.exp(values - jnp.max(values, axis=-1, keepdims=True))
    return shifted / jnp.sum(shifted, axis=-1, keepdims=True)


def exact_gelu(values):
    return jax.nn.gelu(values, approximate=False)


def expert_slots(chosen, experts):
    flat_ids = chosen.reshape(-1)
    onehot = (flat_ids[:, None] == jnp.arange(experts, dtype=jnp.int32)[None, :]).astype(jnp.int32)
    ranks = jnp.cumsum(onehot, axis=0, dtype=jnp.int32)
    slot_pos = jnp.sum(onehot * ranks, axis=1, dtype=jnp.int32) - 1
    return (flat_ids, slot_pos)


def gather_weights_plan(
    tokens,
    key_mask,
    expert_ids,
    cotangent,
    norm1_gain,
    norm1_bias,
    w_qkv,
    w_proj,
    proj_bias,
    norm2_gain,
    norm2_bias,
    w_router,
    w_in,
    b_in,
    w_out,
    b_out,
):
    images, seq_len, width = tokens.shape
    experts = w_in.shape[0]
    head_dim = width // HEADS
    scaling = head_dim ** (-0.5)
    row_count = images * seq_len
    dense_set = (
        lax.all_gather(norm1_gain, "fsdp", axis=0, tiled=True),
        lax.all_gather(norm1_bias, "fsdp", axis=0, tiled=True),
        lax.all_gather(w_qkv, "fsdp", axis=0, tiled=True),
        lax.all_gather(w_proj, "fsdp", axis=0, tiled=True),
        lax.all_gather(proj_bias, "fsdp", axis=0, tiled=True),
        lax.all_gather(norm2_gain, "fsdp", axis=0, tiled=True),
        lax.all_gather(norm2_bias, "fsdp", axis=0, tiled=True),
        lax.all_gather(w_router, "fsdp", axis=0, tiled=True),
    )
    gain_first = dense_set[0].astype(jnp.float32)
    bias_first = dense_set[1].astype(jnp.float32)
    full_qkv = dense_set[2]
    full_proj = dense_set[3]
    bias_proj = dense_set[4].astype(jnp.float32)
    gain_second = dense_set[5].astype(jnp.float32)
    bias_second = dense_set[6].astype(jnp.float32)
    full_router = dense_set[7]
    expert_set = (
        lax.all_gather(w_in, "fsdp", axis=1, tiled=True),
        lax.all_gather(b_in, "fsdp", axis=1, tiled=True),
        lax.all_gather(w_out, "fsdp", axis=1, tiled=True),
        lax.all_gather(b_out, "fsdp", axis=1, tiled=True),
    )
    inner_weight = expert_set[0]
    inner_bias = expert_set[1].astype(jnp.float32)
    outer_weight = expert_set[2]
    outer_bias = expert_set[3].astype(jnp.float32)
    own_mask = lax.dynamic_slice_in_dim(key_mask, lax.axis_index("seq") * images, images, 0)
    keep_rows = own_mask.reshape(row_count, 1).astype(jnp.float32)
    usable = (key_mask > 0)[:, None, None, :]
    flat_tokens = tokens.astype(jnp.float32).reshape(row_count, width)
    normed_in = norm_rows(flat_tokens, gain_first, bias_first).astype(jnp.bfloat16)
    mixed_qkv = jnp.dot(normed_in, full_qkv, preferred_element_type=jnp.float32).astype(
        jnp.bfloat16
    )
    mixed_qkv = mixed_qkv.reshape(images, seq_len, 3, HEADS, head_dim)
    head_qkv = lax.all_to_all(mixed_qkv, "seq", split_axis=3, concat_axis=0, tiled=True)
    queries = head_qkv[:, :, 0]
    key_rows = head_qkv[:, :, 1]
    value_rows = head_qkv[:, :, 2]

    def score_block():
        raw = (
            jnp.einsum("gahd,gbhd->ghab", queries, key_rows, preferred_element_type=jnp.float32)
            * scaling
        )
        return jnp.where(usable, raw, masked_score)

    scores = score_block()
    row_top = jnp.max(scores, axis=-1, keepdims=True)
    shifted = jnp.exp(scores - row_top)
    row_total = jnp.sum(shifted, axis=-1, keepdims=True)
    attn_probs = (shifted / row_total).astype(jnp.bfloat16)
    log_total = row_top + jnp.log(row_total)
    head_out = jnp.einsum(
        "ghab,gbhd->gahd", attn_probs, value_rows, preferred_element_type=jnp.float32
    ).astype(jnp.bfloat16)
    attended = lax.all_to_all(head_out, "seq", split_axis=0, concat_axis=2, tiled=True).reshape(
        row_count, width
    )
    middle = (
        flat_tokens + jnp.dot(attended, full_proj, preferred_element_type=jnp.float32) + bias_proj
    )
    normed_mid = norm_rows(middle, gain_second, bias_second).astype(jnp.bfloat16)
    routing = softmax_rows(jnp.dot(normed_mid, full_router, preferred_element_type=jnp.float32))
    chosen = expert_ids.reshape(row_count, 2)
    flat_ids, slot_pos = expert_slots(chosen, experts)
    gating = jnp.take_along_axis(routing, chosen, axis=1)
    buffer = (
        jnp.zeros((experts, CAP, width), jnp.bfloat16)
        .at[flat_ids, slot_pos]
        .set(jnp.repeat(normed_mid, 2, axis=0))
    )
    pre_act = (
        jnp.einsum("ecd,edf->ecf", buffer, inner_weight, preferred_element_type=jnp.float32)
        + inner_bias[:, None, :]
    )
    activated = exact_gelu(pre_act).astype(jnp.bfloat16)
    expert_out = (
        jnp.einsum("ecf,efd->ecd", activated, outer_weight, preferred_element_type=jnp.float32)
        + outer_bias[:, None, :]
    )
    picked = expert_out[flat_ids, slot_pos].reshape(row_count, 2, width)
    mixture = jnp.sum(gating[:, :, None] * picked, axis=1)
    mixed = (keep_rows * (middle + mixture)).astype(jnp.bfloat16).reshape(images, seq_len, width)
    grad_out = cotangent.astype(jnp.float32).reshape(row_count, width) * keep_rows
    grad_gate = jnp.sum(grad_out[:, None, :] * picked, axis=2)
    grad_picked = (
        (gating[:, :, None] * grad_out[:, None, :])
        .astype(jnp.bfloat16)
        .reshape(2 * row_count, width)
    )
    grad_expert_out = (
        jnp.zeros((experts, CAP, width), jnp.bfloat16).at[flat_ids, slot_pos].set(grad_picked)
    )
    grad_outer_bias = jnp.sum(grad_expert_out, axis=1, dtype=jnp.float32)
    hidden_pre = (
        jnp.einsum("ecd,edf->ecf", buffer, inner_weight, preferred_element_type=jnp.float32)
        + inner_bias[:, None, :]
    )
    hidden_act = exact_gelu(hidden_pre).astype(jnp.bfloat16)
    grad_outer_weight = jnp.einsum(
        "ecf,ecd->efd", hidden_act, grad_expert_out, preferred_element_type=jnp.float32
    )
    grad_act = jnp.einsum(
        "ecd,efd->ecf", grad_expert_out, outer_weight, preferred_element_type=jnp.float32
    )
    gelu_pull = jax.vjp(exact_gelu, hidden_pre)[1]
    grad_pre = gelu_pull(grad_act)[0].astype(jnp.bfloat16)
    grad_inner_bias = jnp.sum(grad_pre, axis=1, dtype=jnp.float32)
    grad_inner_weight = jnp.einsum(
        "ecd,ecf->edf", buffer, grad_pre, preferred_element_type=jnp.float32
    )
    grad_buffer = jnp.einsum(
        "ecf,edf->ecd", grad_pre, inner_weight, preferred_element_type=jnp.float32
    )
    grad_rows = jnp.sum(grad_buffer[flat_ids, slot_pos].reshape(row_count, 2, width), axis=1)
    expert_range = jnp.arange(experts, dtype=jnp.int32)[None, None, :]
    grad_route = jnp.sum(
        grad_gate[:, :, None] * (chosen[:, :, None] == expert_range).astype(jnp.float32), axis=1
    )
    grad_logits = (
        routing * (grad_route - jnp.sum(routing * grad_route, axis=-1, keepdims=True))
    ).astype(jnp.bfloat16)
    grad_router = jnp.einsum(
        "nd,ne->de", normed_mid, grad_logits, preferred_element_type=jnp.float32
    )
    grad_normed_mid = grad_rows + jnp.einsum(
        "ne,de->nd", grad_logits, full_router, preferred_element_type=jnp.float32
    )
    second_pull = jax.vjp(norm_rows, middle, gain_second, bias_second)[1]
    grad_mid_norm, grad_gain_second, grad_bias_second = second_pull(grad_normed_mid)
    grad_middle = grad_out + grad_mid_norm
    grad_proj = grad_middle.astype(jnp.bfloat16)
    grad_bias_proj = jnp.sum(grad_proj, axis=0, dtype=jnp.float32)
    grad_proj_weight = jnp.einsum(
        "nd,ne->de", attended, grad_proj, preferred_element_type=jnp.float32
    )
    grad_attended = jnp.einsum(
        "ne,de->nd", grad_proj, full_proj, preferred_element_type=jnp.float32
    ).astype(jnp.bfloat16)
    grad_head_out = lax.all_to_all(
        grad_attended.reshape(images, seq_len, HEADS, head_dim),
        "seq",
        split_axis=2,
        concat_axis=0,
        tiled=True,
    )
    recomputed = jnp.exp(score_block() - log_total)
    grad_values = jnp.einsum(
        "ghab,gahd->gbhd",
        recomputed.astype(jnp.bfloat16),
        grad_head_out,
        preferred_element_type=jnp.float32,
    )
    grad_probs = jnp.einsum(
        "gahd,gbhd->ghab", grad_head_out, value_rows, preferred_element_type=jnp.float32
    )
    grad_scores = (
        recomputed * (grad_probs - jnp.sum(recomputed * grad_probs, axis=-1, keepdims=True))
    ).astype(jnp.bfloat16)
    grad_queries = (
        jnp.einsum("ghab,gbhd->gahd", grad_scores, key_rows, preferred_element_type=jnp.float32)
        * scaling
    )
    grad_keys = (
        jnp.einsum("ghab,gahd->gbhd", grad_scores, queries, preferred_element_type=jnp.float32)
        * scaling
    )
    grad_head_qkv = jnp.stack([grad_queries, grad_keys, grad_values], axis=2).astype(jnp.bfloat16)
    grad_qkv = lax.all_to_all(
        grad_head_qkv, "seq", split_axis=0, concat_axis=3, tiled=True
    ).reshape(row_count, 3 * width)
    grad_qkv_weight = jnp.einsum(
        "nd,ne->de", normed_in, grad_qkv, preferred_element_type=jnp.float32
    )
    grad_normed_in = jnp.einsum("ne,de->nd", grad_qkv, full_qkv, preferred_element_type=jnp.float32)
    first_pull = jax.vjp(norm_rows, flat_tokens, gain_first, bias_first)[1]
    grad_first, grad_gain_first, grad_bias_first = first_pull(grad_normed_in)
    token_grad = (grad_middle + grad_first).astype(jnp.bfloat16).reshape(images, seq_len, width)
    shares = (
        lax.psum_scatter(grad_gain_first, "fsdp", scatter_dimension=0, tiled=True),
        lax.psum_scatter(grad_bias_first, "fsdp", scatter_dimension=0, tiled=True),
        lax.psum_scatter(grad_qkv_weight, "fsdp", scatter_dimension=0, tiled=True),
        lax.psum_scatter(grad_proj_weight, "fsdp", scatter_dimension=0, tiled=True),
        lax.psum_scatter(grad_bias_proj, "fsdp", scatter_dimension=0, tiled=True),
        lax.psum_scatter(grad_gain_second, "fsdp", scatter_dimension=0, tiled=True),
        lax.psum_scatter(grad_bias_second, "fsdp", scatter_dimension=0, tiled=True),
        lax.psum_scatter(grad_router, "fsdp", scatter_dimension=0, tiled=True),
        lax.psum_scatter(grad_inner_weight, "fsdp", scatter_dimension=1, tiled=True),
        lax.psum_scatter(grad_inner_bias, "fsdp", scatter_dimension=1, tiled=True),
        lax.psum_scatter(grad_outer_weight, "fsdp", scatter_dimension=1, tiled=True),
        lax.psum_scatter(grad_outer_bias, "fsdp", scatter_dimension=1, tiled=True),
    )
    parted = (
        lax.psum_scatter(
            shares[0].astype(jnp.bfloat16), "seq", scatter_dimension=0, tiled=True
        ).astype(jnp.float32),
        lax.psum_scatter(
            shares[1].astype(jnp.bfloat16), "seq", scatter_dimension=0, tiled=True
        ).astype(jnp.float32),
        lax.psum_scatter(
            shares[2].astype(jnp.bfloat16), "seq", scatter_dimension=0, tiled=True
        ).astype(jnp.float32),
        lax.psum_scatter(
            shares[3].astype(jnp.bfloat16), "seq", scatter_dimension=0, tiled=True
        ).astype(jnp.float32),
        lax.psum_scatter(
            shares[4].astype(jnp.bfloat16), "seq", scatter_dimension=0, tiled=True
        ).astype(jnp.float32),
        lax.psum_scatter(
            shares[5].astype(jnp.bfloat16), "seq", scatter_dimension=0, tiled=True
        ).astype(jnp.float32),
        lax.psum_scatter(
            shares[6].astype(jnp.bfloat16), "seq", scatter_dimension=0, tiled=True
        ).astype(jnp.float32),
        lax.psum_scatter(
            shares[7].astype(jnp.bfloat16), "seq", scatter_dimension=0, tiled=True
        ).astype(jnp.float32),
        lax.psum_scatter(
            shares[8].astype(jnp.bfloat16), "seq", scatter_dimension=1, tiled=True
        ).astype(jnp.float32),
        lax.psum_scatter(
            shares[9].astype(jnp.bfloat16), "seq", scatter_dimension=1, tiled=True
        ).astype(jnp.float32),
        lax.psum_scatter(
            shares[10].astype(jnp.bfloat16), "seq", scatter_dimension=1, tiled=True
        ).astype(jnp.float32),
        lax.psum_scatter(
            shares[11].astype(jnp.bfloat16), "seq", scatter_dimension=1, tiled=True
        ).astype(jnp.float32),
    )
    totals = (
        lax.all_gather(parted[0].astype(jnp.bfloat16), "seq", axis=0, tiled=True).astype(
            jnp.float32
        ),
        lax.all_gather(parted[1].astype(jnp.bfloat16), "seq", axis=0, tiled=True).astype(
            jnp.float32
        ),
        lax.all_gather(parted[2].astype(jnp.bfloat16), "seq", axis=0, tiled=True).astype(
            jnp.float32
        ),
        lax.all_gather(parted[3].astype(jnp.bfloat16), "seq", axis=0, tiled=True).astype(
            jnp.float32
        ),
        lax.all_gather(parted[4].astype(jnp.bfloat16), "seq", axis=0, tiled=True).astype(
            jnp.float32
        ),
        lax.all_gather(parted[5].astype(jnp.bfloat16), "seq", axis=0, tiled=True).astype(
            jnp.float32
        ),
        lax.all_gather(parted[6].astype(jnp.bfloat16), "seq", axis=0, tiled=True).astype(
            jnp.float32
        ),
        lax.all_gather(parted[7].astype(jnp.bfloat16), "seq", axis=0, tiled=True).astype(
            jnp.float32
        ),
        lax.all_gather(parted[8].astype(jnp.bfloat16), "seq", axis=1, tiled=True).astype(
            jnp.float32
        ),
        lax.all_gather(parted[9].astype(jnp.bfloat16), "seq", axis=1, tiled=True).astype(
            jnp.float32
        ),
        lax.all_gather(parted[10].astype(jnp.bfloat16), "seq", axis=1, tiled=True).astype(
            jnp.float32
        ),
        lax.all_gather(parted[11].astype(jnp.bfloat16), "seq", axis=1, tiled=True).astype(
            jnp.float32
        ),
    )
    return (
        mixed,
        token_grad,
        totals[0],
        totals[1],
        totals[2],
        totals[3],
        totals[4],
        totals[5],
        totals[6],
        totals[7],
        totals[8],
        totals[9],
        totals[10],
        totals[11],
    )


MESH = pl.DeviceIdType.MESH
NT = (((1,), (1,)), ((), ()))
TN = (((0,), (0,)), ((), ()))


def dot(a, b):
    return jnp.dot(a, b, preferred_element_type=jnp.float32)


class Place:
    def __init__(self, planes):
        self.planes = planes
        s, f = lax.axis_index("seq"), lax.axis_index("fsdp")
        self.y, self.c, self.z, self.x = s // 2, s % 2, f // 2, f % 2

    def at(self, y, c, z, x):
        return (y * 2 + c, z * 2 + x)

    def other_core(self):
        return self.at(self.y, 1 - self.c, self.z, self.x)

    def other_x(self):
        return self.at(self.y, self.c, self.z, 1 - self.x)

    def other_y(self):
        return self.at(1 - self.y, self.c, self.z, self.x)

    def level(self, k):
        return self.at(self.y, self.c, lax.rem(self.z + k + self.planes, self.planes), self.x)


def greet(partners):
    barrier = pltpu.get_barrier_semaphore()
    for partner in partners:
        pl.semaphore_signal(barrier, inc=1, device_id=partner, device_id_type=MESH)
    pl.semaphore_wait(barrier, len(partners))


def nearest(place, i):
    level = 0
    for z in range(place.planes):
        order = sorted(range(place.planes), key=lambda other: (abs(other - z), other))
        for at in range(place.planes):
            level = level + jnp.where((place.z == z) & (i == at), order[at], 0)
    return level


def expert_kernel(
    planes,
    own,
    rows,
    real,
    normed_ref,
    grads_all_ref,
    inner_ref,
    outer_all_ref,
    bias_all_ref,
    small_ref,
    mix_out_ref,
    out_ref,
    inner_grad_ref,
    outer_grad_ref,
    bias_grad_ref,
    router_grad_ref,
    grads_ref,
    mix_ref,
    mix_from_core,
    outer_ref,
    inner_t_ref,
    outer_t_ref,
    router_ref,
    router_t_ref,
    tokens,
    part,
    from_core,
    from_x,
    from_z,
    hidden,
    hidden_grad,
    logit_grad,
    inner_acc,
    outer_acc,
    outer_sem,
    grads_sem,
    mix_sem,
    mix_c_send,
    mix_c_recv,
    z_send,
    z_recv,
    x_send,
    x_recv,
    c_send,
    c_recv,
    sum_c_send,
    sum_c_recv,
    sum_x_send,
    sum_x_recv,
    sum_z_send,
    sum_z_recv,
):
    f32, bf16 = jnp.float32, jnp.bfloat16
    place = Place(planes)
    y, c, z, x = place.y, place.c, place.z, place.x
    width = inner_ref.shape[0]
    lanes = inner_ref.shape[1] // own
    first = real % 16

    def remote(src, dst, send, recv, device):
        return pltpu.make_async_remote_copy(
            src_ref=src, dst_ref=dst, send_sem=send, recv_sem=recv, device_id=device, device_id_type=MESH
        )

    def slot(buffer, level, at, count=1):
        return buffer.at[level, pl.ds(at * rows, count * rows)]

    def up_copy(level):
        here = slot(tokens, level, 0)
        return remote(here, here, z_send.at[0, level], z_recv.at[0, level], place.at(y, c, z + 1, x))

    def down_copy(level):
        here = slot(tokens, level, 0)
        return remote(here, here, z_send.at[1, level], z_recv.at[1, level], place.at(y, c, z - 1, x))

    def x_copy(level):
        return remote(
            slot(tokens, level, 0), slot(tokens, level, 2), x_send.at[level], x_recv.at[level], place.other_x()
        )

    def c_copy(level, r):
        return remote(
            slot(tokens, level, 2 * r),
            slot(tokens, level, 2 * r + 1),
            c_send.at[level, r],
            c_recv.at[level, r],
            place.other_core(),
        )

    def sum_c_copy(level, r):
        return remote(
            slot(part, level, 2 * r + 1),
            slot(from_core, level, r),
            sum_c_send.at[level, r],
            sum_c_recv.at[level, r],
            place.other_core(),
        )

    def sum_x_copy(level):
        return remote(
            slot(part, level, 2), from_x.at[level], sum_x_send.at[level], sum_x_recv.at[level], place.other_x()
        )

    def sum_z_copy(level, source):
        return remote(
            slot(part, level, 0),
            from_z.at[source],
            sum_z_send.at[level],
            sum_z_recv.at[source],
            place.at(y, c, level, x),
        )

    partners = [place.other_core(), place.other_x()] + [place.level(k) for k in range(1, planes)]
    greet(partners)
    tokens[z, 0:rows, :] = normed_ref[...]

    @pl.when(z < planes - 1)
    def _():
        up_copy(z).start()

    @pl.when(z > 0)
    def _():
        down_copy(z).start()

    c_copy(z, 0).start()
    x_copy(z).start()
    def grads_load(level):
        return pltpu.make_async_copy(grads_all_ref.at[level], grads_ref.at[level], grads_sem.at[level])

    def mix_c(level, r):
        return remote(
            slot(mix_ref, level, 2 * r + 1),
            slot(mix_from_core, level, r),
            mix_c_send.at[level, r],
            mix_c_recv.at[level, r],
            place.other_core(),
        )

    def mix_store(level, r):
        return pltpu.make_async_copy(
            slot(mix_ref, level, 2 * r), slot(mix_out_ref, level, r), mix_sem.at[level, r]
        )

    def mix_sum(level):
        for r in range(2):
            mix_c(level, r).wait_recv()
            here = slice(2 * r * rows, (2 * r + 1) * rows)
            total = mix_ref[level, here, :].astype(f32)
            total = total + mix_from_core[level, r * rows : (r + 1) * rows, :].astype(f32)
            mix_ref[level, here, :] = total.astype(bf16)
            mix_store(level, r).start()

    for i in range(planes):
        grads_load(nearest(place, (i + 1) % planes)).start()
    loads = [
        pltpu.make_async_copy(
            outer_all_ref.at[c * own + i], outer_ref.at[pl.ds(i * lanes, lanes)], outer_sem.at[i]
        )
        for i in range(own)
    ]
    for load in loads:
        load.start()
    inner_t_ref[...] = jnp.transpose(inner_ref[...])
    place_row = lax.broadcasted_iota(jnp.int32, (128, 128), 0)
    place_lane = lax.broadcasted_iota(jnp.int32, (128, 128), 1)
    take = (place_row - (5 + 2 * own) == place_lane - first) & (place_lane >= first)
    take = take & (place_lane < first + 2 * own)
    router = dot(small_ref[...], take.astype(bf16))
    router_ref[...] = router.astype(bf16)
    router_t_ref[...] = jnp.transpose(router).astype(bf16)
    inner_acc[...] = jnp.zeros_like(inner_acc)
    outer_acc[...] = jnp.zeros_like(outer_acc)
    bias_grad_ref[...] = jnp.zeros_like(bias_grad_ref)
    router_grad_ref[...] = jnp.zeros_like(router_grad_ref)
    for load in loads:
        load.wait()
    outer_t_ref[...] = jnp.transpose(outer_ref[...])

    def hop(h):
        @pl.when(z >= h)
        def _():
            up_copy(z - h).wait_recv()

            @pl.when(z < planes - 1)
            def _():
                up_copy(z - h).start()

            x_copy(z - h).start()
            c_copy(z - h, 0).start()

        @pl.when(z + h < planes)
        def _():
            down_copy(z + h).wait_recv()

            @pl.when(z > 0)
            def _():
                down_copy(z + h).start()

            x_copy(z + h).start()
            c_copy(z + h, 0).start()

    def tiles(level, r):
        here = pl.ds(pl.multiple_of(2 * r * rows, 16), 2 * rows)
        normed, grad_out = tokens[level, here, :], grads_ref[level, here, :]
        select = []
        for t in range(2):
            last = pl.ds(pl.multiple_of((2 * r + t) * rows + real - first, 16), 16)
            chosen = grads_ref[level, last, :256].astype(f32)
            chosen = jnp.concatenate([chosen, jnp.zeros((112, 256), f32)], axis=0)
            select.append(jnp.transpose(chosen)[:rows])
        select = jnp.concatenate(select, axis=0)
        lane = lax.broadcasted_iota(jnp.int32, select.shape, 1)
        named = (lane >= first) & (lane < first + 2 * own)
        select = jnp.where(named, select, 0.0)
        logits = jnp.where(named, dot(normed, router_ref[...]), -1e30)
        routing = jnp.exp(logits - jnp.max(logits, axis=1, keepdims=True))
        routing = routing / jnp.sum(routing, axis=1, keepdims=True)
        gates = routing * select
        gate_grads = jnp.zeros_like(gates)
        all_pre = dot(normed, inner_ref[...])
        all_grad_act = dot(grad_out, outer_t_ref[...])
        for i in range(own):
            mine = lane == first + c * own + i
            units = slice(i * lanes, (i + 1) * lanes)
            gate = jnp.sum(jnp.where(mine, gates, 0.0), axis=1, keepdims=True)
            bias = jnp.where(c == 0, bias_all_ref[i : i + 1, :], bias_all_ref[own + i : own + i + 1, :])
            pre = all_pre[:, units] + bias.astype(f32)
            grad_act = all_grad_act[:, units]
            cdf = 0.5 * (1.0 + lax.erf(pre * (0.5**0.5)))
            act = pre * cdf
            hidden[here, units] = (gate * act).astype(bf16)
            gate_grad = jnp.sum(act * grad_act, axis=1, keepdims=True)
            gate_grads = gate_grads + jnp.where(mine, gate_grad * select, 0.0)
            slope = cdf + pre * jnp.exp(-0.5 * pre * pre) * 0.3989422804014327
            grad_pre = gate * grad_act * slope
            bias_grad_ref[0:1, units] += jnp.sum(grad_pre, axis=0, keepdims=True)
            hidden_grad[here, units] = grad_pre.astype(bf16)
        grad_logits = routing * (gate_grads - jnp.sum(routing * gate_grads, axis=1, keepdims=True))
        logit_grad[here, :] = grad_logits.astype(bf16)
        mix_ref[level, here, :] = dot(hidden[here, :], outer_ref[...]).astype(bf16)
        row_grad = dot(hidden_grad[here, :], inner_t_ref[...])
        row_grad = row_grad + dot(logit_grad[here, :], router_t_ref[...])
        part[level, here, :] = row_grad.astype(bf16)

    def across_sum(level):
        sum_c_copy(level, 1).wait_recv()
        here = slice(2 * rows, 3 * rows)
        total = part[level, here, :].astype(f32) + from_core[level, rows : 2 * rows, :].astype(f32)
        part[level, here, :] = total.astype(bf16)
        sum_x_copy(level).start()

    def level_sum(level):
        sum_c_copy(level, 0).wait_recv()
        sum_x_copy(level).wait_recv()
        total = part[level, 0:rows, :].astype(f32) + from_core[level, 0:rows, :].astype(f32)
        total = total + from_x[level].astype(f32)
        part[level, 0:rows, :] = total.astype(bf16)

    def weight_grads(level):
        for j in range(width // 256):
            some = slice(j * 256, (j + 1) * 256)
            outer_acc[some, :] += lax.dot_general(
                hidden[:, some], grads_ref[level], TN, preferred_element_type=f32
            )
            inner_acc[some, :] += lax.dot_general(
                tokens[level, :, some], hidden_grad[...], TN, preferred_element_type=f32
            )
        router_grad_ref[...] += lax.dot_general(tokens[level], logit_grad[...], TN, preferred_element_type=f32)

    def order(i):
        return nearest(place, jnp.where(i == 0, 1, jnp.where(i == planes - 1, 0, planes - i)))

    def step(i, carry):
        level, before = order(i), order(i - 1)

        def half(s, carry):
            r = jnp.where(i < planes - 2, s, 1 - s)

            @pl.when((i == 0) & (s == 0))
            def _():
                hop(1)

            if planes > 2:
                @pl.when((i == 0) & (s == 1))
                def _():
                    hop(2)

            @pl.when((i == 1) & (s == 0))
            def _():
                for h in range(3, planes):
                    hop(h)

            @pl.when((i > 0) & (s == 1))
            def _():
                level_sum(before)
                sum_z_copy(before, z).start()

            @pl.when(s == 0)
            def _():
                grads_load(level).wait()

            @pl.when(r == 0)
            def _():
                c_copy(level, 0).wait_recv()

            @pl.when(r == 1)
            def _():
                x_copy(level).wait_recv()
                c_copy(level, 1).start()
                c_copy(level, 1).wait_recv()

            tiles(level, r)
            sum_c_copy(level, r).start()
            mix_c(level, r).start()

            @pl.when(r == 1)
            def _():
                across_sum(level)

            return carry

        lax.fori_loop(0, 2, half, 0)
        weight_grads(level)
        mix_sum(level)
        return carry

    lax.fori_loop(0, planes, step, 0)
    level_sum(z)
    inner_grad_ref[...] = inner_acc[...].astype(bf16)
    outer_grad_ref[...] = outer_acc[...].astype(bf16)
    total = part[z, 0:rows, :].astype(f32)
    for k in range(1, planes):
        source = lax.rem(z + k, planes)
        sum_z_copy(z, source).wait_recv()
        total = total + from_z[source].astype(f32)
    out_ref[...] = total
    for level in range(planes):
        mix_store(level, 0).wait()
        mix_store(level, 1).wait()
        mix_c(level, 0).wait_send()
        mix_c(level, 1).wait_send()
        x_copy(level).wait_send()
        c_copy(level, 0).wait_send()
        c_copy(level, 1).wait_send()
        sum_c_copy(level, 0).wait_send()
        sum_c_copy(level, 1).wait_send()
        sum_x_copy(level).wait_send()

        @pl.when(level != z)
        def _():
            sum_z_copy(level, z).wait_send()

        @pl.when((z >= level) & (z < planes - 1))
        def _():
            up_copy(level).wait_send()

        @pl.when((z <= level) & (z > 0))
        def _():
            down_copy(level).wait_send()


def experts_of_the_plane(planes, own, real, normed, grads, inner, outer, bias, small):
    f32, bf16 = jnp.float32, jnp.bfloat16
    rows = normed.shape[0]
    chunk = 4 * rows
    width, units = inner.shape
    shape = jax.ShapeDtypeStruct
    vmem = pl.BlockSpec(memory_space=pltpu.VMEM)
    anywhere = pl.BlockSpec(memory_space=pl.ANY)
    dma = pltpu.SemaphoreType.DMA
    flops = 12 * planes * chunk * width * units
    return pl.pallas_call(
        functools.partial(expert_kernel, planes, own, rows, real),
        out_shape=[
            shape((planes, 2 * rows, width), bf16),
            shape((rows, width), f32),
            shape((width, units), bf16),
            shape((units, width), bf16),
            shape((8, units), f32),
            shape((width, 128), f32),
        ],
        in_specs=[vmem, anywhere, vmem, anywhere, vmem, vmem],
        out_specs=[anywhere] + [vmem] * 5,
        scratch_shapes=[
            pltpu.VMEM((planes, chunk, width), bf16),
            pltpu.VMEM((planes, chunk, width), bf16),
            pltpu.VMEM((planes, 2 * rows, width), bf16),
            pltpu.VMEM((units, width), bf16),
            pltpu.VMEM((units, width), bf16),
            pltpu.VMEM((width, units), bf16),
            pltpu.VMEM((width, 128), bf16),
            pltpu.VMEM((128, width), bf16),
            pltpu.VMEM((planes, chunk, width), bf16),
            pltpu.VMEM((planes, chunk, width), bf16),
            pltpu.VMEM((planes, 2 * rows, width), bf16),
            pltpu.VMEM((planes, rows, width), bf16),
            pltpu.VMEM((planes, rows, width), bf16),
            pltpu.VMEM((chunk, units), bf16),
            pltpu.VMEM((chunk, units), bf16),
            pltpu.VMEM((chunk, 128), bf16),
            pltpu.VMEM((width, units), f32),
            pltpu.VMEM((units, width), f32),
            dma((own,)),
            dma((planes,)),
            dma((planes, 2)),
            dma((planes, 2)),
            dma((planes, 2)),
        ]
        + [dma((2, planes))] * 2
        + [dma((planes,))] * 2
        + [dma((planes, 2))] * 4
        + [dma((planes,))] * 4,
        compiler_params=pltpu.CompilerParams(
            collective_id=1, has_side_effects=True, vmem_limit_bytes=60 * 2**20
        ),
        cost_estimate=pl.CostEstimate(flops=flops, bytes_accessed=40 * 2**20, transcendentals=0),
        name="experts_of_the_plane",
    )(normed, grads, inner, outer, bias, small)


def front_kernel(
    planes,
    heads,
    real,
    tokens_ref,
    mask_ref,
    ids_ref,
    cotangent_ref,
    *refs,
):
    vector_refs, refs = refs[:5], refs[5:]
    (
        router_part_ref,
        outer_bias_ref,
        qkv_part_ref,
    proj_part_ref,
    inner_part_ref,
    small_all,
    w_qkv_out,
    w_proj_out,
    inner_all,
    normed_in_ref,
    qkv_ref,
    attended_ref,
    middle_ref,
    normed_ref,
    grad_ref,
    grads_all,
    wide_ref,
    select_ref,
    keys_ref,
    keep_ref,
    w_qkv_all,
    w_proj_all,
    out_sem,
    up_send,
    up_recv,
    down_send,
    down_recv,
    x_send,
    x_recv,
    c_send,
    c_recv,
    over_send,
    over_recv,
    over_c_send,
    over_c_recv,
    g_z_send,
    g_z_recv,
    g_x_send,
    g_x_recv,
    g_c_send,
    g_c_recv,
    spread_send,
    spread_recv,
    own_sem,
    y_send,
    y_recv,
    ) = refs
    f32, bf16 = jnp.float32, jnp.bfloat16
    place = Place(planes)
    rows, width = wide_ref.shape
    depth = qkv_part_ref.shape[0]
    experts = inner_part_ref.shape[0]
    half = depth // 2
    lanes = inner_part_ref.shape[2] // (2 * planes)
    head_dim = width // heads
    y, c, z, x = place.y, place.c, place.z, place.x
    gathered = [small_all, w_qkv_all, w_proj_all]

    def remote(src, dst, send, recv, device):
        return pltpu.make_async_remote_copy(
            src_ref=src, dst_ref=dst, send_sem=send, recv_sem=recv, device_id=device, device_id_type=MESH
        )

    def block(j, level, across, core, plane):
        start = pl.multiple_of((level * 2 + across) * depth + core * half, 16)
        if j == 0:
            return gathered[j].at[pl.ds(start, half)]
        columns = gathered[j].shape[1] // 2
        return gathered[j].at[pl.ds(start, half), pl.ds(pl.multiple_of(plane * columns, 128), columns)]

    def piece(j, level, across):
        return block(j, level, across, c, y)

    def up_copy(j, level):
        here = piece(j, level, x)
        return remote(here, here, up_send.at[j, level], up_recv.at[j, level], place.at(y, c, z + 1, x))

    def down_copy(j, level):
        here = piece(j, level, x)
        return remote(here, here, down_send.at[j, level], down_recv.at[j, level], place.at(y, c, z - 1, x))

    def x_copy(j, level, across):
        here = piece(j, level, across)
        return remote(here, here, x_send.at[j, level], x_recv.at[j, level], place.other_x())

    def c_copy(j, level, across):
        here = piece(j, level, across)
        at = level * 2 + across
        return remote(here, here, c_send.at[j, at], c_recv.at[j, at], place.other_core())

    def over_copy(j, level, across):
        here = piece(j, level, across)
        at = level * 2 + across
        return remote(here, here, over_send.at[j, at], over_recv.at[j, at], place.other_y())

    def over_c_copy(j, level, across):
        here = block(j, level, across, c, 1 - y)
        at = level * 2 + across
        return remote(here, here, over_c_send.at[j, at], over_c_recv.at[j, at], place.other_core())

    def g_slot(level, at):
        return grads_all.at[level, pl.ds(at * rows, rows)]

    def g_up(level):
        here = g_slot(level, 0)
        return remote(here, here, g_z_send.at[0, level], g_z_recv.at[0, level], place.at(y, c, z + 1, x))

    def g_down(level):
        here = g_slot(level, 0)
        return remote(here, here, g_z_send.at[1, level], g_z_recv.at[1, level], place.at(y, c, z - 1, x))

    def g_x(level):
        return remote(g_slot(level, 0), g_slot(level, 2), g_x_send.at[level], g_x_recv.at[level], place.other_x())

    def g_c(level, r):
        return remote(
            g_slot(level, 2 * r), g_slot(level, 2 * r + 1), g_c_send.at[level, r], g_c_recv.at[level, r], place.other_core()
        )

    def columns_of(f):
        return pl.ds(pl.multiple_of(f * lanes, 128), lanes)

    here_rows = pl.ds(pl.multiple_of((z * 2 + x) * depth, 16), depth)
    my_units = pl.ds(pl.multiple_of(y * lanes, 128), lanes)

    def spread_copy(k, r):
        level, across = lax.rem(z + k, planes), (x + r) % 2
        return remote(
            inner_part_ref.at[c * 2 + y, :, columns_of(level * 2 + across)],
            inner_all.at[here_rows, my_units],
            spread_send.at[k, r],
            spread_recv.at[k, r],
            place.at(y, c, level, across),
        )

    own_copy = pltpu.make_async_copy(
        inner_part_ref.at[c * 2 + y, :, columns_of(z * 2 + x)], inner_all.at[here_rows, my_units], own_sem
    )
    y_copy = remote(inner_all.at[:, my_units], inner_all.at[:, my_units], y_send, y_recv, place.other_y())
    their_units = pl.ds(pl.multiple_of((1 - y) * lanes, 128), lanes)
    from_y = remote(inner_all.at[:, their_units], inner_all.at[:, their_units], y_send, y_recv, place.other_y())

    others = [(k, r) for k in range(planes) for r in range(2) if k or r]
    partners = [place.other_core(), place.other_y()]
    partners += [place.at(y, c, lax.rem(z + k, planes), (x + r) % 2) for k, r in others]
    greet(partners)

    w_qkv_all[here_rows, :] = qkv_part_ref[...]

    def share(j, level, across):
        c_copy(j, level, across).start()
        if j:
            over_copy(j, level, across).start()

    def line(flows):
        @pl.when(z < planes - 1)
        def _():
            for j in flows:
                up_copy(j, z).start()

        @pl.when(z > 0)
        def _():
            for j in flows:
                down_copy(j, z).start()

        for j in flows:
            x_copy(j, z, x).start()

    def hops(flows):
        for h in range(1, planes):
            @pl.when(z >= h)
            def _():
                for j in flows:
                    up_copy(j, z - h).wait_recv()

                    @pl.when(z < planes - 1)
                    def _():
                        up_copy(j, z - h).start()

                    x_copy(j, z - h, x).start()
                    share(j, z - h, x)

            @pl.when(z + h < planes)
            def _():
                for j in flows:
                    down_copy(j, z + h).wait_recv()

                    @pl.when(z > 0)
                    def _():
                        down_copy(j, z + h).start()

                    x_copy(j, z + h, x).start()
                    share(j, z + h, x)

    def arrive(flows):
        for i in range(planes):
            level = nearest(place, i)
            for j in flows:
                x_copy(j, level, 1 - x).wait_recv()
                share(j, level, 1 - x)

    def over_arrive(flows):
        for i in range(planes):
            level = nearest(place, i)
            for j in flows:
                if i:
                    over_copy(j, level, x).wait_recv()
                    over_c_copy(j, level, x).start()
                over_copy(j, level, 1 - x).wait_recv()
                over_c_copy(j, level, 1 - x).start()

    def gather_done(flows):
        for level in range(planes):
            for j in flows:
                c_copy(j, level, 1 - x).wait_recv()
                if j:
                    over_c_copy(j, level, 1 - x).wait_recv()

            @pl.when(level != z)
            def _():
                for j in flows:
                    c_copy(j, level, x).wait_recv()
                    if j:
                        over_c_copy(j, level, x).wait_recv()

    def g_hop(h):
        @pl.when(z >= h)
        def _():
            g_up(z - h).wait_recv()

            @pl.when(z < planes - 1)
            def _():
                g_up(z - h).start()

            g_x(z - h).start()
            g_c(z - h, 0).start()

        @pl.when(z + h < planes)
        def _():
            g_down(z + h).wait_recv()

            @pl.when(z > 0)
            def _():
                g_down(z + h).start()

            g_x(z + h).start()
            g_c(z + h, 0).start()

    line([1])
    lined = [ref[...].astype(f32) for ref in (*vector_refs, outer_bias_ref, router_part_ref)]
    lined = jnp.concatenate(lined, axis=0)
    lined = jnp.concatenate([lined, jnp.zeros((128 - lined.shape[0], depth), f32)], axis=0)
    lined = jnp.concatenate([lined, jnp.zeros((128, 128 - depth), f32)], axis=1)
    small = jnp.transpose(lined)[:depth]
    small_all[here_rows, :] = small.astype(bf16)
    line([0])
    w_proj_all[here_rows, :] = proj_part_ref[...]
    line([2])
    spare = jnp.zeros((rows - real, width), f32)
    values = jnp.concatenate([tokens_ref[...].astype(f32), spare], axis=0)
    wide_ref[...] = values.astype(bf16)
    normal, _ = norm_parts(values)
    mask = mask_ref[pl.ds(y * 2 + c, 1), :].astype(f32)
    keys = jnp.concatenate([mask, jnp.zeros((1, rows - real), f32)], axis=1)
    keys_ref[...] = keys
    keep = lax.broadcasted_iota(jnp.int32, (rows, rows), 0) == lax.broadcasted_iota(jnp.int32, (rows, rows), 1)
    keep = jnp.sum(jnp.where(keep, keys, 0.0), axis=1, keepdims=True)
    keep_ref[...] = keep
    ids = ids_ref[...]
    number = lax.broadcasted_iota(jnp.int32, (8, real), 0)
    chosen = ((number == ids[0:1]) | (number == ids[1:2])).astype(f32)
    chosen = jnp.concatenate([chosen, jnp.zeros((8, width - real), f32)], axis=1)
    select = jnp.concatenate([chosen[:, :256], jnp.zeros((120, 256), f32)], axis=0)
    select_ref[...] = jnp.transpose(select)[:rows].astype(bf16)
    if rows - real > 8:
        chosen = jnp.concatenate([chosen, jnp.zeros((rows - real - 8, width), f32)], axis=0)
    grad_out = cotangent_ref[...].astype(f32) * keep[:real]
    grad_out = jnp.concatenate([grad_out, chosen], axis=0).astype(bf16)
    grad_ref[...] = grad_out
    grads_own = pltpu.make_async_copy(grad_ref, g_slot(z, 0), out_sem.at[2])
    grads_own.start()
    hops([1, 0])
    arrive([1, 0])
    hops([2])
    own_copy.start()
    for k, r in others:
        spread_copy(k, r).start()

    grads_own.wait()

    @pl.when(z < planes - 1)
    def _():
        g_up(z).start()

    @pl.when(z > 0)
    def _():
        g_down(z).start()

    g_x(z).start()
    g_c(z, 0).start()
    arrive([2])
    over_arrive([1])
    gather_done([1, 0])
    qkv_out_copy = pltpu.make_async_copy(w_qkv_all, w_qkv_out, out_sem.at[0])
    qkv_out_copy.start()
    vectors = jnp.transpose(small_all[...].astype(f32))
    normed_in = (normal * vectors[0:1] + vectors[1:2]).astype(bf16)
    normed_in_ref[...] = normed_in
    for j in range(3):
        part = slice(j * width, (j + 1) * width)
        qkv_ref[:, part] = dot(normed_in, w_qkv_all[:, part]).astype(bf16)
    g_hop(1)
    over_arrive([2])
    lane = lax.broadcasted_iota(jnp.int32, (rows, 2 * head_dim), 1)
    usable = keys_ref[...] > 0
    for pair in range(heads // 2):
        if pair == heads // 4:
            g_hop(2)
        at = pair * 2 * head_dim
        queries = qkv_ref[:, at : at + 2 * head_dim]
        keys = qkv_ref[:, width + at : width + at + 2 * head_dim]
        held = qkv_ref[:, 2 * width + at : 2 * width + at + 2 * head_dim]
        outs = []
        for side in range(2):
            only = (lane < head_dim) if side == 0 else (lane >= head_dim)
            scores = lax.dot_general(
                jnp.where(only, queries, 0).astype(bf16), keys, NT, preferred_element_type=f32
            )
            scores = jnp.where(usable, scores * head_dim ** (-0.5), masked_score)
            shifted = jnp.exp(scores - jnp.max(scores, axis=1, keepdims=True))
            probs = (shifted / jnp.sum(shifted, axis=1, keepdims=True)).astype(bf16)
            outs.append(dot(probs, held))
        attended_ref[:, at : at + 2 * head_dim] = jnp.where(lane < head_dim, outs[0], outs[1]).astype(bf16)
    for h in range(3, planes):
        g_hop(h)
    own_copy.wait()
    for k, r in others:
        spread_copy(k, r).wait_recv()
    y_copy.start()
    gather_done([2])
    proj_out_copy = pltpu.make_async_copy(w_proj_all, w_proj_out, out_sem.at[1])
    proj_out_copy.start()
    middle = values + dot(attended_ref[...], w_proj_all[...]) + vectors[2:3]
    middle_ref[...] = middle
    normal_mid, _ = norm_parts(middle)
    normed = normal_mid * vectors[3:4] + vectors[4:5]
    row = lax.broadcasted_iota(jnp.int32, normed.shape, 0)
    normed_ref[...] = jnp.where(row < real, normed, 0.0).astype(bf16)
    for i in range(planes):
        level = nearest(place, i)
        g_x(level).wait_recv()
        g_c(level, 1).start()
    from_y.wait_recv()
    qkv_out_copy.wait()
    proj_out_copy.wait()
    for level in range(planes):
        g_c(level, 0).wait_recv()
        g_c(level, 1).wait_recv()
    y_copy.wait_send()
    for k, r in others:
        spread_copy(k, r).wait_send()
    for level in range(planes):
        g_x(level).wait_send()
        g_c(level, 0).wait_send()
        g_c(level, 1).wait_send()

        @pl.when((z >= level) & (z < planes - 1))
        def _():
            g_up(level).wait_send()

        @pl.when((z <= level) & (z > 0))
        def _():
            g_down(level).wait_send()

    def shared(j, level, across):
        c_copy(j, level, across).wait_send()
        if j:
            over_copy(j, level, across).wait_send()
            over_c_copy(j, level, across).wait_send()

    for j in range(3):
        for level in range(planes):
            x_copy(j, level, x).wait_send()
            shared(j, level, 1 - x)

            @pl.when(level != z)
            def _():
                shared(j, level, x)

            @pl.when((z >= level) & (z < planes - 1))
            def _():
                up_copy(j, level).wait_send()

            @pl.when((z <= level) & (z > 0))
            def _():
                down_copy(j, level).wait_send()


def front(planes, rows, tokens, mask, ids, cotangent, vectors, router, outer_bias, w_qkv, w_proj, w_in):
    f32, bf16 = jnp.float32, jnp.bfloat16
    real, width = tokens.shape
    lanes = w_in.shape[2] // (2 * planes)
    shape = jax.ShapeDtypeStruct
    vmem = pl.BlockSpec(memory_space=pltpu.VMEM)
    anywhere = pl.BlockSpec(memory_space=pl.ANY)
    dma = pltpu.SemaphoreType.DMA
    return pl.pallas_call(
        functools.partial(front_kernel, planes, HEADS, real),
        out_shape=[
            shape((width, 128), bf16),
            shape((width, 3 * width), bf16),
            shape((width, width), bf16),
            shape((width, 2 * lanes), bf16),
            shape((rows, width), bf16),
            shape((rows, 3 * width), bf16),
            shape((rows, width), bf16),
            shape((rows, width), f32),
            shape((rows, width), bf16),
            shape((rows, width), bf16),
            shape((planes, 4 * rows, width), bf16),
            shape((rows, width), bf16),
            shape((rows, 128), bf16),
            shape((1, rows), f32),
            shape((rows, 1), f32),
        ],
        in_specs=[vmem] * (6 + len(vectors)) + [vmem] * 2 + [anywhere],
        out_specs=[vmem] + [anywhere] * 3 + [vmem] * 6 + [anywhere] + [vmem] * 4,
        scratch_shapes=[pltpu.VMEM((width, 3 * width), bf16), pltpu.VMEM((width, width), bf16), dma((3,))]
        + [dma((3, planes))] * 6
        + [dma((3, 2 * planes))] * 6
        + [dma((2, planes))] * 2
        + [dma((planes,))] * 2
        + [dma((planes, 2))] * 4
        + [dma] * 3,
        compiler_params=pltpu.CompilerParams(
            collective_id=2, has_side_effects=True, vmem_limit_bytes=60 * 2**20
        ),
        cost_estimate=pl.CostEstimate(flops=2**32, bytes_accessed=40 * 2**20, transcendentals=0),
        name="dense_weights_and_attention",
    )(tokens, mask, ids, cotangent, *vectors, router, outer_bias, w_qkv, w_proj, w_in)


def back_kernel(planes, heads, own, groups, real, *refs):
    (
        row_grad_ref,
        normed_ref,
        grad_ref,
        middle_ref,
        tokens_ref,
        normed_in_ref,
        qkv_ref,
        attended_ref,
        small_ref,
        w_qkv_all_ref,
        w_proj_ref,
        keys_ref,
        keep_ref,
        select_ref,
        mix_ref,
        inner_ref,
        outer_ref,
        bias_ref,
        router_grad_ref,
    ) = refs[:19]
    mixed_ref, token_grad_ref, qkv_out, proj_out, small_out, inner_out, outer_out, bias_out = refs[19:27]
    refs = refs[27:]
    (
        w_qkv_ref,
        outer_sum,
        grad_attended,
        grad_qkv,
        mix_z,
        mix_from_x,
        mix_from_z,
        inner_from_y,
        inner_sum,
        outer_from_y,
        bias_from_y,
        held,
        held_small,
        from_core,
        from_core_small,
        from_x,
        from_x_small,
        from_z,
        from_z_small,
        plane_sum,
        plane_sum_small,
        from_y,
        from_y_small,
        final,
        final_small,
    ) = refs[:25]
    (
        load_sem,
        outer_own_sem,
        mix_x_send,
        mix_x_recv,
        mix_z_send,
        mix_z_recv,
        inner_y_sem,
        spread_send,
        spread_recv,
        inner_back_sem,
        inner_core_sem,
        outer_y_sem,
        outer_c_sem,
        bias_y_sem,
        bias_c_sem,
        own_sem,
        flow_c_sem,
        flow_x_sem,
        flow_z_send,
        flow_z_recv,
        flow_y_sem,
        flow_end_sem,
    ) = refs[25:]
    f32, bf16 = jnp.float32, jnp.bfloat16
    place = Place(planes)
    y, c, z, x = place.y, place.c, place.z, place.x
    rows, width = middle_ref.shape
    depth = width // (2 * planes)
    half = depth // 2
    lanes = inner_ref.shape[1] // own
    head_dim = width // heads
    pair_width = 2 * head_dim
    small_at = groups + 1

    def remote(src, dst, send, recv, device):
        return pltpu.make_async_remote_copy(
            src_ref=src, dst_ref=dst, send_sem=send, recv_sem=recv, device_id=device, device_id_type=MESH
        )

    def swap(src, dst, sem, device):
        return remote(src, dst, sem.at[0], sem.at[1], device)

    def of_flow(j, many, alone):
        return alone if j == small_at else many.at[j]

    mine, theirs = pl.ds(pl.multiple_of(c * half, 16), half), pl.ds(pl.multiple_of((1 - c) * half, 16), half)

    def flow_c(j):
        source = of_flow(j, held, held_small)
        return swap(
            source.at[:, :, theirs], of_flow(j, from_core, from_core_small), flow_c_sem.at[j], place.other_core()
        )

    def flow_x(j):
        source = of_flow(j, held, held_small)
        return swap(source.at[:, 1 - x, mine], of_flow(j, from_x, from_x_small), flow_x_sem.at[j], place.other_x())

    def flow_z(j, k):
        level = lax.rem(z + k, planes)
        source = of_flow(j, held, held_small)
        return remote(
            source.at[level, x, mine],
            of_flow(j, from_z, from_z_small).at[k],
            flow_z_send.at[j, k],
            flow_z_recv.at[j, k],
            place.level(k),
        )

    def flow_y(j):
        return swap(
            of_flow(j, plane_sum, plane_sum_small),
            of_flow(j, from_y, from_y_small),
            flow_y_sem.at[j],
            place.other_y(),
        )

    def flow_end(j):
        here = of_flow(j, final, final_small).at[mine]
        return swap(here, here, flow_end_sem.at[j], place.other_core())

    def flow_core_sum(j):
        flow_c(j).wait_recv()
        kept = of_flow(j, held, held_small)
        total = kept[:, :, mine, :].astype(f32) + of_flow(j, from_core, from_core_small)[...].astype(f32)
        kept[:, :, mine, :] = total.astype(bf16)
        flow_x(j).start()

    def flow_x_sum(j):
        flow_x(j).wait_recv()
        kept = of_flow(j, held, held_small)
        total = kept[:, x, mine, :].astype(f32) + of_flow(j, from_x, from_x_small)[...].astype(f32)
        kept[:, x, mine, :] = total.astype(bf16)
        for k in range(1, planes):
            flow_z(j, k).start()

    def flow_z_sum(j):
        kept = of_flow(j, held, held_small)
        total = kept[z, x, mine, :].astype(f32)
        for k in range(1, planes):
            flow_z(j, k).wait_recv()
            total = total + of_flow(j, from_z, from_z_small)[k].astype(f32)
        of_flow(j, plane_sum, plane_sum_small)[...] = total.astype(bf16)
        flow_y(j).start()

    def flow_y_sum(j):
        flow_y(j).wait_recv()
        total = of_flow(j, plane_sum, plane_sum_small)[...].astype(f32)
        total = total + of_flow(j, from_y, from_y_small)[...].astype(f32)
        of_flow(j, final, final_small)[mine, :] = total.astype(bf16)
        flow_end(j).start()

    loads = [
        pltpu.make_async_copy(mix_ref.at[:, pl.ds(0, rows)], mix_z, load_sem.at[0]),
        pltpu.make_async_copy(w_qkv_all_ref, w_qkv_ref, load_sem.at[1]),
    ]

    def mix_to_x(level):
        return remote(
            mix_ref.at[level, pl.ds(rows, rows)],
            mix_from_x.at[level],
            mix_x_send.at[level],
            mix_x_recv.at[level],
            place.other_x(),
        )

    def mix_start(k):
        mix_to_x(lax.rem(z + k, planes)).start()

    def mix_to_z(level, source):
        return remote(
            mix_z.at[level], mix_from_z.at[source], mix_z_send.at[level], mix_z_recv.at[source], place.at(y, c, level, x)
        )

    def mix_x_sum(k):
        level = lax.rem(z + k, planes)
        mix_to_x(level).wait_recv()
        mix_z[level] = (mix_z[level].astype(f32) + mix_from_x[level].astype(f32)).astype(bf16)
        if k < planes:
            mix_to_z(level, z).start()

    my_units = pl.ds(pl.multiple_of(y * lanes, 128), lanes)
    their_units = pl.ds(pl.multiple_of((1 - y) * lanes, 128), lanes)
    my_expert, their_expert = c * 2 + y, c * 2 + 1 - y
    my_columns = pl.ds(pl.multiple_of((z * 2 + x) * lanes, 128), lanes)

    def inner_y():
        return swap(inner_ref.at[:, their_units], inner_from_y, inner_y_sem, place.other_y())

    def shard_rows(f):
        return pl.ds(pl.multiple_of(f * depth, 16), depth)

    def spread(k, r):
        level, across = lax.rem(z + k, planes), (x + r) % 2
        return remote(
            inner_sum.at[shard_rows(level * 2 + across)],
            inner_out.at[my_expert, :, my_columns],
            spread_send.at[k, r],
            spread_recv.at[k, r],
            place.at(y, c, level, across),
        )

    own_copy = pltpu.make_async_copy(
        inner_sum.at[shard_rows(z * 2 + x)], inner_out.at[my_expert, :, my_columns], own_sem
    )

    def inner_back():
        here = inner_out.at[my_expert]
        return swap(here, here, inner_back_sem, place.other_y())

    def inner_core(expert, at):
        here = inner_out.at[expert]
        return swap(here, here, inner_core_sem.at[at], place.other_core())

    def outer_y():
        return swap(outer_ref, outer_from_y, outer_y_sem, place.other_y())

    def outer_c():
        return swap(outer_sum, outer_out.at[c], outer_c_sem, place.other_core())

    outer_own = pltpu.make_async_copy(outer_sum, outer_out.at[c], outer_own_sem)

    def bias_y():
        return swap(bias_ref, bias_from_y, bias_y_sem, place.other_y())

    def bias_c():
        here = bias_out.at[c]
        return swap(here, here, bias_c_sem, place.other_core())

    others = [(k, r) for k in range(planes) for r in range(2) if k or r]

    def inner_y_sum():
        inner_y().wait_recv()
        total = inner_ref[:, my_units].astype(f32) + inner_from_y[...].astype(f32)
        inner_sum[...] = total.astype(bf16)
        own_copy.start()
        for k, r in others:
            spread(k, r).start()
        outer_y().start()

    def inner_spread_done():
        own_copy.wait()
        for k, r in others:
            spread(k, r).wait_recv()
        inner_back().start()
        inner_core(my_expert, 0).start()

    def outer_y_sum():
        outer_y().wait_recv()
        total = outer_ref[...].astype(f32) + outer_from_y[...].astype(f32)
        outer_sum[...] = total.astype(bf16)
        outer_own.start()
        outer_c().start()
        bias_y().wait_recv()
        bias_out[c] = bias_ref[...] + bias_from_y[...]
        bias_c().start()

    partners = [place.other_core(), place.other_y()]
    partners += [place.at(y, c, lax.rem(z + k, planes), (x + r) % 2) for k, r in others]
    greet(partners)
    inner_y().start()
    bias_y().start()
    mix_start(1)
    for load in loads:
        load.start()

    vectors = jnp.transpose(small_ref[...].astype(f32))
    gain_first, gain_second = vectors[0:1], vectors[3:4]
    place_row = lax.broadcasted_iota(jnp.int32, (128, 128), 0)
    place_lane = lax.broadcasted_iota(jnp.int32, (128, 128), 1)

    def lanes_from(first):
        take = (place_row == place_lane + first) & (place_lane < 2 * own)
        return dot(small_ref[...], take.astype(bf16)).astype(bf16)

    outer_bias, router = lanes_from(5), lanes_from(5 + 2 * own)
    normed_mid, grad_out = normed_ref[...], grad_ref[...]
    real_row = lax.broadcasted_iota(jnp.int32, grad_out.shape, 0) < real
    grad_out = jnp.where(real_row, grad_out, 0).astype(bf16)
    select = select_ref[...].astype(f32)
    lane = lax.broadcasted_iota(jnp.int32, select.shape, 1)
    logits = jnp.where(lane < 2 * own, dot(normed_mid, router), -1e30)
    routing = jnp.exp(logits - jnp.max(logits, axis=1, keepdims=True))
    routing = routing / jnp.sum(routing, axis=1, keepdims=True)
    gates = routing * select
    bias_gate = select * dot(grad_out, outer_bias)
    bias_logits = routing * (bias_gate - jnp.sum(routing * bias_gate, axis=1, keepdims=True))
    bias_logits = bias_logits.astype(bf16)
    router_grad = lax.dot_general(normed_mid, bias_logits, TN, preferred_element_type=f32)
    router_grad = pltpu.roll(router_grad, 16, 1) + pltpu.roll(router_grad_ref[...], 16 - real % 16, 1)
    outer_bias_grad = lax.dot_general(gates.astype(bf16), grad_out, TN, preferred_element_type=f32)
    grad_normed_mid = row_grad_ref[...] + lax.dot_general(bias_logits, router, NT, preferred_element_type=f32)
    normal_mid, rstd_mid = norm_parts(middle_ref[...])
    gain_second_grad = jnp.sum(grad_normed_mid * normal_mid, axis=0, keepdims=True)
    bias_second_grad = jnp.sum(grad_normed_mid, axis=0, keepdims=True)
    grad_middle = grad_out.astype(f32) + norm_back(grad_normed_mid, normal_mid, rstd_mid, gain_second)
    grad_proj = grad_middle.astype(bf16)
    proj_bias_grad = jnp.sum(grad_proj.astype(f32), axis=0, keepdims=True)
    loads[0].wait()

    def hold(j, value):
        held[j] = value.astype(bf16).reshape(planes, 2, depth, width)
        flow_c(j).start()

    hold(0, lax.dot_general(attended_ref[...], grad_proj, TN, preferred_element_type=f32))
    grad_attended[...] = lax.dot_general(grad_proj, w_proj_ref[...], NT, preferred_element_type=f32).astype(bf16)
    flow_core_sum(0)

    pair_lane = lax.broadcasted_iota(jnp.int32, (rows, pair_width), 1)
    usable = keys_ref[...] > 0
    scaling = head_dim ** (-0.5)
    group_width = width // groups

    def pair_back(pair):
        at = pair * pair_width
        group, inside = at // group_width, at % group_width
        queries = qkv_ref[:, at : at + pair_width]
        keys = qkv_ref[:, width + at : width + at + pair_width]
        values = qkv_ref[:, 2 * width + at : 2 * width + at + pair_width]
        grads = grad_attended[:, at : at + pair_width]
        found = []
        for side in range(2):
            only = (pair_lane < head_dim) if side == 0 else (pair_lane >= head_dim)
            some_queries = jnp.where(only, queries, 0).astype(bf16)
            some_grads = jnp.where(only, grads, 0).astype(bf16)
            scores = lax.dot_general(some_queries, keys, NT, preferred_element_type=f32)
            scores = jnp.where(usable, scores * scaling, masked_score)
            shifted = jnp.exp(scores - jnp.max(scores, axis=1, keepdims=True))
            probs = shifted / jnp.sum(shifted, axis=1, keepdims=True)
            grad_probs = lax.dot_general(some_grads, values, NT, preferred_element_type=f32)
            grad_scores = probs * (grad_probs - jnp.sum(probs * grad_probs, axis=1, keepdims=True))
            grad_scores = grad_scores.astype(bf16)
            found.append(
                (
                    dot(grad_scores, keys),
                    lax.dot_general(grad_scores, some_queries, TN, preferred_element_type=f32),
                    lax.dot_general(probs.astype(bf16), some_grads, TN, preferred_element_type=f32),
                )
            )
        grad_queries = jnp.where(pair_lane < head_dim, found[0][0], found[1][0]) * scaling
        grad_keys = (found[0][1] + found[1][1]) * scaling
        grad_values = found[0][2] + found[1][2]
        for part, value in enumerate((grad_queries, grad_keys, grad_values)):
            start = part * group_width + inside
            grad_qkv[group, :, start : start + pair_width] = value.astype(bf16)

    def group_back(group):
        per_group = heads // 2 // groups
        for pair in range(group * per_group, (group + 1) * per_group):
            pair_back(pair)
        hold(
            1 + group,
            lax.dot_general(normed_in_ref[...], grad_qkv[group], TN, preferred_element_type=f32),
        )

    group_back(0)
    mix_start(2)
    inner_y_sum()
    flow_core_sum(1)
    mix_x_sum(1)
    for group in range(1, groups):
        group_back(group)
        flow_core_sum(1 + group)
        if group == 1:
            flow_x_sum(0)
            mix_x_sum(2)
    if groups == 1:
        flow_x_sum(0)
        mix_x_sum(2)

    loads[1].wait()
    grad_normed_in = jnp.zeros((rows, width), f32)
    for group in range(groups):
        for part in range(3):
            grad_normed_in = grad_normed_in + lax.dot_general(
                grad_qkv[group, :, part * group_width : (part + 1) * group_width],
                w_qkv_ref[:, part * width + group * group_width : part * width + (group + 1) * group_width],
                NT,
                preferred_element_type=f32,
            )
    normal_first, rstd_first = norm_parts(tokens_ref[...].astype(f32))
    gain_first_grad = jnp.sum(grad_normed_in * normal_first, axis=0, keepdims=True)
    bias_first_grad = jnp.sum(grad_normed_in, axis=0, keepdims=True)
    token_grad = grad_middle + norm_back(grad_normed_in, normal_first, rstd_first, gain_first)
    token_grad_ref[...] = token_grad.astype(bf16)[:real]
    vector_rows = jnp.concatenate(
        [
            gain_first_grad,
            bias_first_grad,
            proj_bias_grad,
            gain_second_grad,
            bias_second_grad,
            jnp.zeros((3, width), f32),
            outer_bias_grad[:8],
            jnp.zeros((112, width), f32),
        ],
        axis=0,
    )
    vector_grads = jnp.transpose(vector_rows) + router_grad
    held_small[...] = vector_grads.astype(bf16).reshape(planes, 2, depth, 128)
    flow_c(small_at).start()
    flow_core_sum(small_at)
    inner_spread_done()
    for group in range(groups - 1):
        flow_x_sum(1 + group)
    mix_start(3)
    flow_x_sum(groups)
    for k in range(4, planes + 1):
        mix_start(k)
    flow_x_sum(small_at)
    outer_y_sum()
    for k in range(3, planes):
        mix_x_sum(k)
    flow_z_sum(0)
    flow_y_sum(0)
    for group in range(groups):
        flow_z_sum(1 + group)
    flow_z_sum(small_at)
    inner_back().wait_recv()
    inner_core(their_expert, 1).start()
    mix_x_sum(planes)
    mixture = mix_z[z].astype(f32) + dot(gates.astype(bf16), jnp.transpose(outer_bias.astype(f32)).astype(bf16))
    for k in range(1, planes):
        source = lax.rem(z + k, planes)
        mix_to_z(z, source).wait_recv()
        mixture = mixture + mix_from_z[source].astype(f32)
    mixed = (keep_ref[...] * (middle_ref[...] + mixture)).astype(bf16)
    mixed_ref[...] = mixed[:real]
    for group in range(groups):
        flow_y_sum(1 + group)
    flow_y_sum(small_at)

    def arrived(j):
        here = of_flow(j, final, final_small).at[theirs]
        swap(here, here, flow_end_sem.at[j], place.other_core()).wait_recv()

    arrived(0)
    proj_out[...] = final[0]
    for group in range(groups):
        arrived(1 + group)
        for part in range(3):
            start = part * width + group * group_width
            qkv_out[:, start : start + group_width] = final[
                1 + group, :, part * group_width : (part + 1) * group_width
            ]
    arrived(small_at)
    small_out[...] = jnp.transpose(
        jnp.concatenate([final_small[...].astype(f32), jnp.zeros((128 - depth, 128), f32)], axis=0)
    )
    outer_own.wait()
    outer_c().wait_recv()
    bias_theirs = bias_out.at[1 - c]
    swap(bias_theirs, bias_theirs, bias_c_sem, place.other_core()).wait_recv()
    for at, expert in enumerate(((1 - c) * 2 + y, (1 - c) * 2 + 1 - y)):
        inner_core(expert, at).wait_recv()

    inner_y().wait_send()
    inner_back().wait_send()
    inner_core(my_expert, 0).wait_send()
    inner_core(their_expert, 1).wait_send()
    outer_y().wait_send()
    outer_c().wait_send()
    bias_y().wait_send()
    bias_c().wait_send()
    for k, r in others:
        spread(k, r).wait_send()
    for k in range(1, planes + 1):
        level = lax.rem(z + k, planes)
        mix_to_x(level).wait_send()
        if k < planes:
            mix_to_z(level, z).wait_send()
    for j in range(groups + 2):
        flow_c(j).wait_send()
        flow_x(j).wait_send()
        for k in range(1, planes):
            flow_z(j, k).wait_send()
        flow_y(j).wait_send()
        flow_end(j).wait_send()


def back(planes, own, real, *args):
    f32, bf16 = jnp.float32, jnp.bfloat16
    (
        row_grad,
        normed_mid,
        grad_out,
        middle,
        tokens,
        normed_in,
        qkv,
        attended,
        small,
        w_qkv,
        w_proj,
        keys,
        keep,
        select,
        mix_parts,
        inner_grad,
        outer_grad,
        bias_grad,
        router_grad,
    ) = args
    rows, width = middle.shape
    depth = width // (2 * planes)
    half = depth // 2
    lanes = inner_grad.shape[1] // own
    tall = outer_grad.shape[0]
    pairs = HEADS // 2
    groups = 3 if pairs % 3 == 0 and (pairs // 3) * 2 * (width // HEADS) % 128 == 0 else 1
    flows = groups + 1
    shape = jax.ShapeDtypeStruct
    vmem = pl.BlockSpec(memory_space=pltpu.VMEM)
    anywhere = pl.BlockSpec(memory_space=pl.ANY)
    dma = pltpu.SemaphoreType.DMA

    def both(*dims):
        return [pltpu.VMEM((flows, *dims, width), bf16), pltpu.VMEM((*dims, 128), bf16)]

    return pl.pallas_call(
        functools.partial(back_kernel, planes, HEADS, own, groups, real),
        out_shape=[
            shape((real, width), bf16),
            shape((real, width), bf16),
            shape((depth, 3 * width), bf16),
            shape((depth, width), bf16),
            shape((128, 128), f32),
            shape((2 * own, depth, 2 * planes * lanes), bf16),
            shape((2, tall, width), bf16),
            shape((2, *bias_grad.shape), f32),
        ],
        in_specs=[vmem] * 9 + [anywhere] + [vmem] * 4 + [anywhere] + [vmem] * 4,
        out_specs=[vmem] * 5 + [anywhere] * 2 + [vmem],
        scratch_shapes=[
            pltpu.VMEM((width, 3 * width), bf16),
            pltpu.VMEM((tall, width), bf16),
            pltpu.VMEM((rows, width), bf16),
            pltpu.VMEM((groups, rows, 3 * width // groups), bf16),
            pltpu.VMEM((planes, rows, width), bf16),
            pltpu.VMEM((planes, rows, width), bf16),
            pltpu.VMEM((planes, rows, width), bf16),
            pltpu.VMEM((width, lanes), bf16),
            pltpu.VMEM((width, lanes), bf16),
            pltpu.VMEM((tall, width), bf16),
            pltpu.VMEM(bias_grad.shape, f32),
        ]
        + both(planes, 2, depth)
        + both(planes, 2, half)
        + both(planes, half)
        + both(planes, half)
        + both(half)
        + both(half)
        + both(depth)
        + [dma((2,)), dma]
        + [dma((planes,))] * 4
        + [dma((2,))]
        + [dma((planes, 2))] * 2
        + [dma((2,)), dma((2, 2)), dma((2,)), dma((2,)), dma((2,)), dma((2,)), dma]
        + [dma((flows + 1, 2))] * 2
        + [dma((flows + 1, planes))] * 2
        + [dma((flows + 1, 2))] * 2,
        compiler_params=pltpu.CompilerParams(
            collective_id=3, has_side_effects=True, vmem_limit_bytes=60 * 2**20
        ),
        cost_estimate=pl.CostEstimate(flops=2**33, bytes_accessed=40 * 2**20, transcendentals=0),
        name="attention_backward_and_sums",
    )(*args)


def finish_kernel(
    depth,
    experts,
    qkv_ref,
    proj_ref,
    rows_ref,
    inner_ref,
    outer_ref,
    mixed_ref,
    token_grad_ref,
    bias_ref,
    qkv_out,
    proj_out,
    inner_out,
    outer_out,
    mixed_out,
    token_grad_out,
    router_out,
    outer_bias_out,
    bias_out,
    *vector_outs,
):
    f32 = jnp.float32

    @pl.when(pl.program_id(0) == 0)
    def _():
        for i, out in enumerate(vector_outs):
            out[...] = rows_ref[i : i + 1, :depth]
        outer_bias_out[...] = rows_ref[8 : 8 + experts, :depth]
        router_out[...] = rows_ref[16 : 16 + experts, :depth]
        qkv_out[...] = qkv_ref[...].astype(f32)
        proj_out[...] = proj_ref[...].astype(f32)
        lanes = bias_out.shape[1]
        for e in range(experts):
            at = e % (experts // 2) * lanes
            bias_out[e : e + 1, :] = bias_ref[e // (experts // 2), 0:1, at : at + lanes]
        mixed_out[...] = mixed_ref[...]
        token_grad_out[...] = token_grad_ref[...]

    inner_out[...] = inner_ref[...].astype(f32)
    outer_out[...] = outer_ref[...].astype(f32)


def finish(qkv, proj, vectors, inner, outer, mixed, token_grad, bias):
    f32 = jnp.float32
    experts, depth, _ = inner.shape
    shape = jax.ShapeDtypeStruct

    def whole(array):
        return pl.BlockSpec(array.shape, lambda i, rank=len(array.shape): (0,) * rank)

    def one(array):
        return pl.BlockSpec((1, array.shape[1] // 2, array.shape[2]), lambda i: (i // 2, i % 2, 0))

    outs = [
        shape(qkv.shape, f32),
        shape(proj.shape, f32),
        shape(inner.shape, f32),
        shape(outer.shape, f32),
        shape(mixed.shape, mixed.dtype),
        shape(token_grad.shape, token_grad.dtype),
        shape((experts, depth), f32),
        shape((experts, depth), f32),
        shape((experts, outer.shape[1]), f32),
    ] + [shape((1, depth), f32)] * 5
    return pl.pallas_call(
        functools.partial(finish_kernel, depth, experts),
        out_shape=outs,
        grid=(2 * experts,),
        in_specs=[whole(qkv), whole(proj), whole(vectors), one(inner), one(outer)]
        + [whole(mixed), whole(token_grad), whole(bias)],
        out_specs=[whole(outs[0]), whole(outs[1]), one(outs[2]), one(outs[3])] + [whole(out) for out in outs[4:]],
        compiler_params=pltpu.CompilerParams(vmem_limit_bytes=62 * 2**20),
        name="results_in_float32",
    )(qkv, proj, vectors, inner, outer, mixed, token_grad, bias)


def norm_parts(values):
    center = values - jnp.mean(values, axis=-1, keepdims=True)
    rstd = lax.rsqrt(jnp.mean(center * center, axis=-1, keepdims=True) + epsilon)
    return center * rstd, rstd


def norm_back(grad, normal, rstd, gain):
    scaled = grad * gain
    return rstd * (
        scaled
        - jnp.mean(scaled, axis=-1, keepdims=True)
        - normal * jnp.mean(scaled * normal, axis=-1, keepdims=True)
    )


def move_tokens_plan(
    tokens,
    key_mask,
    expert_ids,
    cotangent,
    norm1_gain,
    norm1_bias,
    w_qkv,
    w_proj,
    proj_bias,
    norm2_gain,
    norm2_bias,
    w_router,
    w_in,
    b_in,
    w_out,
    b_out,
):
    f32 = jnp.float32
    _, rows, width = tokens.shape
    experts, depth, hidden = w_in.shape
    slice_width = w_out.shape[1]
    planes = hidden // slice_width // 2
    own = experts // 2
    padded = (rows + experts + 15) // 16 * 16
    vectors = [v[None] for v in (norm1_gain, norm1_bias, proj_bias, norm2_gain, norm2_bias)]
    fronts = front(
        planes,
        padded,
        tokens[0],
        key_mask,
        expert_ids[0].T,
        cotangent[0],
        vectors,
        w_router.T,
        b_out,
        w_qkv,
        w_proj,
        w_in,
    )
    small, full_qkv, full_proj, inner, normed_in, qkv, attended, middle = fronts[:8]
    normed_mid, grad_out, all_grad_out, wide, select, keys, keep = fronts[8:]
    mix_parts, row_grad, inner_grad, outer_grad, bias_grad, router_grad = experts_of_the_plane(
        planes, own, rows, normed_mid, all_grad_out, inner, w_out, b_in, small
    )
    mixed, token_grad, qkv_grad, proj_grad, vector_grads, inner_grad, outer_grad, bias_grad = back(
        planes,
        own,
        rows,
        row_grad,
        normed_mid,
        grad_out,
        middle,
        wide,
        normed_in,
        qkv,
        attended,
        small,
        full_qkv,
        full_proj,
        keys,
        keep,
        select,
        mix_parts,
        inner_grad,
        outer_grad,
        bias_grad,
        router_grad,
    )
    outer_grad = outer_grad.reshape(experts, slice_width, width)
    finished = finish(
        qkv_grad, proj_grad, vector_grads, inner_grad, outer_grad, mixed, token_grad, bias_grad
    )
    qkv_grad, proj_grad, inner_grad, outer_grad, mixed, token_grad, router_grad, outer_bias_grad = finished[:8]
    bias_grad = finished[8]
    vector_grads = [row.reshape(depth) for row in finished[9:]]
    return (
        mixed[None],
        token_grad[None],
        vector_grads[0],
        vector_grads[1],
        qkv_grad,
        proj_grad,
        vector_grads[2],
        vector_grads[3],
        vector_grads[4],
        router_grad.T,
        inner_grad,
        bias_grad,
        outer_grad,
        outer_bias_grad,
    )


def solution(mesh):
    n_seq, n_fsdp = mesh.shape["seq"], mesh.shape["fsdp"]

    def per_device(*args):
        tokens, w_in, w_out = args[0], args[12], args[14]
        experts, _, hidden = w_in.shape
        lanes = hidden // n_fsdp
        whole_tiles = lanes % 128 == 0 and tokens.shape[2] % 256 == 0 and w_in.shape[1] % 32 == 0 and 2 * lanes <= tokens.shape[2]
        if n_seq == 4 and experts == n_seq and n_fsdp >= 6 and n_fsdp % 2 == 0 and tokens.shape[0] == 1 and whole_tiles:
            return move_tokens_plan(*args)
        return gather_weights_plan(*args)

    return jax.shard_map(
        per_device,
        mesh=mesh,
        in_specs=(
            P(("fsdp", "seq"), None, None),
            P("fsdp", None),
            P(("fsdp", "seq"), None, None),
            P(("fsdp", "seq"), None, None),
            P("fsdp"),
            P("fsdp"),
            P("fsdp", None),
            P("fsdp", None),
            P("fsdp"),
            P("fsdp"),
            P("fsdp"),
            P("fsdp", None),
            P(None, "fsdp", None),
            P(None, "fsdp"),
            P(None, "fsdp", None),
            P(None, "fsdp"),
        ),
        out_specs=(
            P(("fsdp", "seq"), None, None),
            P(("fsdp", "seq"), None, None),
            P("fsdp"),
            P("fsdp"),
            P("fsdp", None),
            P("fsdp", None),
            P("fsdp"),
            P("fsdp"),
            P("fsdp"),
            P("fsdp", None),
            P(None, "fsdp", None),
            P(None, "fsdp"),
            P(None, "fsdp", None),
            P(None, "fsdp"),
        ),
        check_vma=False,
    )
```
